32 devices in a mesh: fsdp: 16 (over z, y, core), seq: 2 (over x).
Axes of the slice: x: 2, y: 2, z: 4, core: 2. Of those that a mesh axis runs over, the one named last changes fastest.
Arguments:
- layer_input: bfloat16 [16, 1024, 768], P('fsdp', 'seq'), may hold values from -6 to 6
- query_weight: bfloat16 [768, 768], P('fsdp'), may hold values from -0.109375 to 0.109375
- key_weight: bfloat16 [768, 768], P('fsdp'), may hold values from -0.109375 to 0.109375
- value_weight: bfloat16 [768, 768], P('fsdp'), may hold values from -0.21875 to 0.21875
- output_weight: bfloat16 [768, 768], P('fsdp'), may hold values from -1.75 to 1.75
- expand_weight: bfloat16 [768, 3072], P('fsdp'), may hold values from -0.21875 to 0.21875
- contract_weight: bfloat16 [3072, 768], P('fsdp'), may hold values from -0.109375 to 0.109375
- attention_gain: bfloat16 [768], P('fsdp'), may hold values from 0.5 to 1.5
- feedforward_gain: bfloat16 [768], P('fsdp'), may hold values from 0.5 to 1.5
- bias_table: bfloat16 [32, 12], P('fsdp'), may hold values from -4 to 4
- valid_len: int32 [16], P('fsdp'), may hold values from 257 to 1024, as said below
- instr_len: int32 [16], P('fsdp'), may hold values from 1 to 256
- pair_flag: int32 [16], P('fsdp'), may hold values from 0 to 1
- cotangent: bfloat16 [16, 1024, 768], P('fsdp', 'seq'), may hold values from -6 to 6
Outputs:
- layer_output: bfloat16 [16, 1024, 768], P('fsdp', 'seq')
- input_grad: bfloat16 [16, 1024, 768], P('fsdp', 'seq')
- attention_gain_grad: float32 [768], P('fsdp')
- feedforward_gain_grad: float32 [768], P('fsdp')
- query_grad: float32 [768, 768], P('fsdp')
- key_grad: float32 [768, 768], P('fsdp')
- value_grad: float32 [768, 768], P('fsdp')
- output_grad: float32 [768, 768], P('fsdp')
- expand_grad: float32 [768, 3072], P('fsdp')
- contract_grad: float32 [3072, 768], P('fsdp')
- bias_grad: float32 [32, 12], P('fsdp')
The draws below stay inside these ranges and needn't reach their ends.
Inputs may be any that keep to these rules, and one draw needn't show every extreme that they name: `valid_len`: in every aligned block of 1 row (the rows of one fsdp index) at least one row has more than 512 tokens; at least one row of all has all 1024 tokens; every row has more than 256 tokens.
All inputs are finite; a program needn't handle non-finite values.
Results may differ from the reference program's by a relative error of at most 0.02.
Values may be sent and summed in bfloat16 or wider, within the bound.
No kernel may reach another device: no remote copies, remote signals or barrier semaphores. Data moves between devices by JAX's collectives and lax.ppermute only.
A program may use at most 256 MiB of HBM per device.

```python
import jax
import jax.numpy as jnp
from jax import lax

D = 768
HEADS = 12
FF = 3072
BUCKETS = 32
LEN = 1024
ROWS_DEV = 1
ROWS = 16
N_SEQ = 2


def draw_valid_len(key, part):
    key = jax.random.fold_in(key, 11)
    first_key, second_key, third_key, fourth_key = jax.random.split(key, 4)
    base = jax.random.randint(first_key, (ROWS,), LEN // 4 + 1, LEN + 1)
    picked = jax.random.randint(second_key, (ROWS // ROWS_DEV,), 0, ROWS_DEV)
    long_len = jax.random.randint(third_key, (ROWS,), LEN - LEN // N_SEQ + 1, LEN + 1)
    full_row = jax.random.randint(fourth_key, (), 0, ROWS)
    index = jnp.arange(ROWS, dtype=jnp.int32)
    within = index % ROWS_DEV
    chosen = jnp.repeat(picked, ROWS_DEV)
    lengths = jnp.where(within == chosen, long_len, base)
    return jnp.where(index == full_row, LEN, lengths).astype(jnp.int32)


def plant(entries, rng, least, high):
    dims = entries.shape
    index_at = [jax.random.randint(jax.random.fold_in(rng, axis), (), 0, dims[axis]) for axis in range(len(dims))]
    entries = entries.at[tuple(index_at)].set(least)
    longest = dims.index(max(dims))
    index_at[longest] = (index_at[longest] + 1) % dims[longest]
    return entries.at[tuple(index_at)].set(high)


def block_scale(key, dims, pieces, least, top_value):
    gain, own = 1.0, jax.random.fold_in(key, 6)
    for position, shards_of in pieces:
        heights = jnp.exp(jax.random.uniform(jax.random.fold_in(own, position), (shards_of,), jnp.float32, least / len(pieces), top_value / len(pieces)))
        gain = gain * jnp.repeat(heights, dims[position] // shards_of).reshape([-1 if axis == position else 1 for axis in range(len(dims))])
    return gain


def bell_draw(stream_key, dims, spread, reach, shards=(), kind=jnp.bfloat16):
    entries = spread * jax.random.normal(stream_key, dims, jnp.float32)
    if shards:
        entries = entries * block_scale(stream_key, dims, shards, -0.22, 0.18)
    return jnp.clip(entries, -reach, reach).astype(kind)


def setup_inputs(seed: int = 0) -> dict:
    seeds = jax.random.split(jax.random.key(seed), 15)
    layer_input = bell_draw(seeds[0], (ROWS, LEN, D), 1.0, 6.0, ((0, 16), (1, 2)))
    query_weight = bell_draw(seeds[1], (D, D), (4 * D) ** -0.5, 0.109375, ((0, 16),))
    key_weight = bell_draw(seeds[2], (D, D), (4 * D) ** -0.5, 0.109375, ((0, 16),))
    value_weight = bell_draw(seeds[3], (D, D), D ** -0.5, 0.21875, ((0, 16),))
    output_weight = bell_draw(seeds[4], (D, D), (max(D // 64, 1)) ** -0.5, 1.75, ((0, 16),))
    expand_weight = bell_draw(seeds[5], (D, FF), D ** -0.5, 0.21875, ((0, 16),))
    contract_weight = bell_draw(seeds[6], (FF, D), FF ** -0.5, 0.109375, ((0, 16),))
    attention_gain = jnp.clip(1.0 + 0.1 * jax.random.normal(seeds[7], (D,), jnp.float32), 0.5, 1.5).astype(jnp.bfloat16)
    feedforward_gain = jnp.clip(1.0 + 0.1 * jax.random.normal(seeds[8], (D,), jnp.float32), 0.5, 1.5).astype(jnp.bfloat16)
    bias_table = bell_draw(seeds[9], (BUCKETS, HEADS), 1.0, 4.0, ((0, 16),))
    valid_len = draw_valid_len(jax.random.fold_in(seeds[14], 71), 0)
    instr_len = plant(jax.random.randint(seeds[11], (ROWS,), 1, LEN // 4 + 1), jax.random.fold_in(seeds[11], 1), 1, (LEN // 4 + 1) - 1).astype(jnp.int32)
    pair_flag = plant(jax.random.randint(seeds[12], (ROWS,), 0, 2), jax.random.fold_in(seeds[12], 1), 0, 1).astype(jnp.int32)
    cotangent = bell_draw(seeds[13], (ROWS, LEN, D), 1.0, 6.0, ((0, 16), (1, 2)))
    return dict(layer_input=layer_input, query_weight=query_weight, key_weight=key_weight, value_weight=value_weight, output_weight=output_weight, expand_weight=expand_weight, contract_weight=contract_weight, attention_gain=attention_gain, feedforward_gain=feedforward_gain, bias_table=bias_table, valid_len=valid_len, instr_len=instr_len, pair_flag=pair_flag, cotangent=cotangent)


EPS = 1e-06
far_edges = (12, 16, 23, 32, 46, 64, 91)

@jax.custom_vjp
def low(v):
    return lax.optimization_barrier(v.astype(jnp.bfloat16)).astype(jnp.float32)

@jax.custom_vjp
def low_back(v):
    return v

def low_keep(v):
    return (low(v), None)

def low_pass(kept, grad):
    return (grad,)

def back_keep(v):
    return (v, None)

def back_low(kept, grad):
    return (low(grad),)
low.defvjp(low_keep, low_pass)
low_back.defvjp(back_keep, back_low)

def bucket_table(query_pos, key_pos):
    offset = key_pos[None, :] - query_pos[:, None]
    distance = jnp.abs(offset)
    beyond = jnp.zeros_like(distance)
    for far_edge in far_edges:
        beyond = beyond + (distance >= far_edge).astype(jnp.int32)
    nearby = jnp.where(distance < 8, distance, 8 + beyond)
    return (nearby + 16 * (offset > 0).astype(jnp.int32)).astype(jnp.int32)

def visible_keys(query_pos, key_pos, valid_len, instr_len, pair_flag):
    in_valid = key_pos[None, None, :] < valid_len[:, None, None]
    guarded = (pair_flag[:, None, None] == 1) & (query_pos[None, :, None] < instr_len[:, None, None]) & (key_pos[None, None, :] >= instr_len[:, None, None])
    return in_valid & jnp.logical_not(guarded)

def rms_scale(values):
    return lax.rsqrt(lax.optimization_barrier(jnp.mean(values * values, axis=-1, keepdims=True)) + EPS)

def layer_rows(params, rows_in, valid_len, instr_len, pair_flag, buckets):
    query_w, key_w, value_w, output_w, expand_w, contract_w, gain_one, gain_two, table = params
    highest = lax.Precision.HIGHEST
    row_count, length, model_width = rows_in.shape
    head_count = table.shape[1]
    positions = jnp.arange(length, dtype=jnp.int32)
    visible = visible_keys(positions, positions, valid_len, instr_len, pair_flag)
    normed_one = low(rows_in * rms_scale(rows_in) * gain_one)

    def project(weight):
        made = low_back(low(jnp.einsum('rtd,de->rte', normed_one, weight, precision=highest)))
        return made.reshape(row_count, length, head_count, model_width // head_count)
    queries = project(query_w)
    key_vectors = project(key_w)
    values = project(value_w)
    raw_scores = low_back(jnp.einsum('rihe,rjhe->rhij', queries, key_vectors, precision=highest))
    rel_bias = jnp.transpose(table[buckets], (2, 0, 1))
    scores = jnp.where(visible[:, None], raw_scores + rel_bias[None], -1000000000.0)
    row_peak = lax.optimization_barrier(jnp.max(scores, axis=-1, keepdims=True))
    log_total = row_peak + jnp.log(lax.optimization_barrier(jnp.sum(jnp.exp(scores - row_peak), axis=-1, keepdims=True)))
    probs_low = low(jnp.exp(scores - log_total))
    attended = jnp.einsum('rhij,rjhe->rihe', probs_low, values, precision=highest).reshape(row_count, length, model_width)
    attended = low_back(low(attended))
    branch = low_back(jnp.einsum('rtd,de->rte', attended, output_w, precision=highest))
    middle = rows_in + branch
    normed_two = low(middle * rms_scale(middle) * gain_two)
    hidden_pre = low_back(jnp.einsum('rtd,df->rtf', normed_two, expand_w, precision=highest))
    hidden = low(jax.nn.gelu(hidden_pre, approximate=True))
    return middle + low_back(jnp.einsum('rtf,fd->rtd', hidden, contract_w, precision=highest))

def reference(layer_input, query_weight, key_weight, value_weight, output_weight, expand_weight, contract_weight, attention_gain, feedforward_gain, bias_table, valid_len, instr_len, pair_flag, cotangent):
    params = tuple((member.astype(jnp.float32) for member in (query_weight, key_weight, value_weight, output_weight, expand_weight, contract_weight, attention_gain, feedforward_gain, bias_table)))
    positions = jnp.arange(LEN, dtype=jnp.int32)
    buckets = bucket_table(positions, positions)
    group_size = 2 if ROWS % 2 == 0 else 1
    group_count = ROWS // group_size

    def forward(whole_input, weights):
        stacked = (whole_input.reshape(group_count, group_size, LEN, D), valid_len.reshape(group_count, group_size), instr_len.reshape(group_count, group_size), pair_flag.reshape(group_count, group_size))
        runner = jax.checkpoint(lambda member: layer_rows(weights, member[0], member[1], member[2], member[3], buckets))
        return lax.map(runner, stacked).reshape(ROWS, LEN, D)
    result, pullback = jax.vjp(forward, layer_input.astype(jnp.float32), params)
    grad_input, grad_params = pullback(cotangent.astype(jnp.float32))
    return (result.astype(jnp.bfloat16), grad_input.astype(jnp.bfloat16), grad_params[6], grad_params[7], grad_params[0], grad_params[1], grad_params[2], grad_params[3], grad_params[4], grad_params[5], grad_params[8])
```

```python
import functools

import jax
import jax.numpy as jnp
from jax import lax
from jax.experimental import pallas as pl
from jax.experimental.pallas import tpu as pltpu
from jax.sharding import PartitionSpec as P

f32 = jnp.float32
bf16 = jnp.bfloat16
BUCKETS = 32
EPS = 1e-06
far_edges = (12, 16, 23, 32, 46, 64, 91)
HIDDEN = -(2.0**30)
VMEM = 56 * 1024 * 1024
ANY = pl.BlockSpec(memory_space=pl.ANY)
FULL = pl.BlockSpec(memory_space=pltpu.VMEM)
SCALARS = pl.BlockSpec(memory_space=pltpu.SMEM)


def dot(left, right, left_dim, right_dim):
    return lax.dot_general(
        left, right, (((left_dim,), (right_dim,)), ((), ())), preferred_element_type=f32
    )


def params():
    return pltpu.CompilerParams(vmem_limit_bytes=VMEM)


def cost(flops, byte_count, exps=0):
    return pl.CostEstimate(flops=flops, bytes_accessed=byte_count, transcendentals=exps)


def bucket_of(offset):
    distance = jnp.abs(offset)
    beyond = jnp.zeros_like(distance)
    for far_edge in far_edges:
        beyond = beyond + (distance >= far_edge).astype(jnp.int32)
    nearby = jnp.where(distance < 8, distance, 8 + beyond)
    return nearby + 16 * (offset > 0).astype(jnp.int32)


def iota(shape, dim):
    return lax.broadcasted_iota(jnp.int32, shape, dim)


def place_blocks(place, near, far, dest, sems):
    z, y, c = place[0], place[1], place[2]
    copies = []
    for turn in range(4):
        for dy in range(2):
            owner = ((jnp.bitwise_xor(z, turn) * 2) + jnp.bitwise_xor(y, dy)) * 2
            for other, source in enumerate((near, far)):
                row = pl.multiple_of((owner + jnp.bitwise_xor(c, other)) * 48, 16)
                index = turn * 2 + dy
                copy = pltpu.make_async_copy(
                    source.at[index], dest.at[pl.ds(row, 48)], sems.at[len(copies)]
                )
                copy.start()
                copies.append(copy)
    return copies


def place_tokens(x, near, far, dest, sems, count):
    copies = []
    for other, source in enumerate((near, far)):
        row = pl.multiple_of(jnp.bitwise_xor(x, other) * count, count)
        copy = pltpu.make_async_copy(source, dest.at[pl.ds(row, count)], sems.at[other])
        copy.start()
        copies.append(copy)
    return copies


def project_kernel(place, x_near, x_far, w_near, w_far, qkv, normed, small, xs, w, sems, xsems):
    tokens = place_tokens(place[3], x_near, x_far, xs, xsems, 512)
    blocks = place_blocks(place, w_near, w_far, w, sems)
    for copy in tokens + blocks:
        copy.wait()
    side = w[:, 1152:1280].astype(f32).T
    small[...] = side[:8]
    gain = side[0:1]
    for row in range(0, 1024, 256):
        wide = xs[row : row + 256].astype(f32)
        scale = lax.rsqrt(jnp.mean(wide * wide, axis=-1, keepdims=True) + EPS)
        normed[row : row + 256] = (wide * scale * gain).astype(bf16)
    for col in range(0, 1152, 384):
        made = dot(w[:, col : col + 384], normed[...], 0, 1)
        qkv[col : col + 384] = made.astype(bf16)


def project(place, x_near, x_far, w_near, w_far):
    return pl.pallas_call(
        project_kernel,
        out_shape=(
            jax.ShapeDtypeStruct((1152, 1024), bf16),
            jax.ShapeDtypeStruct((1024, 768), bf16),
            jax.ShapeDtypeStruct((8, 768), f32),
        ),
        in_specs=[SCALARS, ANY, ANY, ANY, ANY],
        out_specs=(FULL, FULL, FULL),
        scratch_shapes=[
            pltpu.VMEM((1024, 768), bf16),
            pltpu.VMEM((768, 1280), bf16),
            pltpu.SemaphoreType.DMA((16,)),
            pltpu.SemaphoreType.DMA((2,)),
        ],
        compiler_params=params(),
        cost_estimate=cost(2 * 1024 * 768 * 1152, 9_000_000),
        name="project",
    )(place, x_near, x_far, w_near, w_far)


def attend_kernel(scal, table, q, k, v, out, kept, inverse, ka, kt, qt, vt, s0, s1, tile, which):
    head = pl.program_id(0)
    first, valid, instr, pair = scal[0], scal[1], scal[2], scal[3]

    @pl.when(head == 0)
    def _():
        which[...] = bucket_of(iota((384, 128), 0) - 128 - iota((384, 128), 1))
        kt[64:128] = jnp.zeros((64, 1024), bf16)
        qt[64:128] = jnp.zeros((64, 512), bf16)
        row = iota((16, 1024), 0)
        key = iota((16, 1024), 1)
        extra = jnp.where(row < 8, (key // 128 == row).astype(f32), 0.0)
        extra = jnp.where(row == 8, jnp.where(key >= valid, HIDDEN, 0.0), extra)
        extra = jnp.where(row == 9, (key >= instr).astype(f32), extra)
        kt[64:80] = extra.astype(bf16)
        vt[64:80] = jnp.where(row == 0, 1.0, 0.0).astype(bf16)

    buckets = which[...]
    bias = jnp.zeros((384, 128), f32)
    for bucket in range(BUCKETS):
        bias = jnp.where(buckets == bucket, table[head, bucket], bias)
    tile[...] = bias
    row = iota((16, 512), 0)
    query = iota((16, 512), 1) + first
    block = query // 128
    extra = jnp.where(row <= block - 2, table[head, 15], 0.0)
    extra = jnp.where(row >= block + 2, table[head, 31], extra)
    extra = jnp.where(row == 8, 1.0, extra)
    guarded = (query < instr) & (pair == 1)
    extra = jnp.where(row == 9, jnp.where(guarded, HIDDEN, 0.0), extra)
    extra = jnp.where(row > 9, 0.0, extra)
    qt[64:80] = extra.astype(bf16)
    qt[0:64] = q[...]
    kt[0:64] = k[...]
    vt[0:64] = v[...]
    ka[...] = kt[...].T
    for part, s in enumerate((s0, s1)):
        lanes = slice(part * 256, part * 256 + 256)
        s[128:1152] = dot(ka[...], qt[:, lanes], 1, 0)
        for half in range(2):
            base = pl.multiple_of(first + (part * 2 + half) * 128, 128)
            cols = slice(half * 128, half * 128 + 128)
            s[pl.ds(base, 384), cols] = s[pl.ds(base, 384), cols] + tile[...]
        scores = s[128:1152]
        peak = jnp.max(scores, axis=0, keepdims=True)
        weights = jnp.exp(scores - peak).astype(bf16)
        kept[0, :, lanes] = weights
        summed = dot(vt[...], weights, 1, 0)
        share = 1.0 / summed[64:65]
        out[:, lanes] = (summed[0:64] * share).astype(bf16)
        inverse[0, :, lanes] = share


def attend(scal, table, qkv, half):
    heads = 6
    grid = pltpu.PrefetchScalarGridSpec(
        num_scalar_prefetch=1,
        grid=(heads,),
        in_specs=[
            SCALARS,
            pl.BlockSpec((64, 512), lambda h, s: (h, s[0] // 512)),
            pl.BlockSpec((64, 1024), lambda h, s: (6 + h, 0)),
            pl.BlockSpec((64, 1024), lambda h, s: (12 + h, 0)),
        ],
        out_specs=(
            pl.BlockSpec((64, 512), lambda h, s: (h, 0)),
            pl.BlockSpec((1, 1024, 512), lambda h, s: (h, 0, 0)),
            pl.BlockSpec((1, 1, 512), lambda h, s: (h, 0, 0)),
        ),
        scratch_shapes=[
            pltpu.VMEM((1024, 128), bf16),
            pltpu.VMEM((128, 1024), bf16),
            pltpu.VMEM((128, 512), bf16),
            pltpu.VMEM((80, 1024), bf16),
            pltpu.VMEM((1280, 256), f32),
            pltpu.VMEM((1280, 256), f32),
            pltpu.VMEM((384, 128), f32),
            pltpu.VMEM((384, 128), jnp.int32),
        ],
    )
    return pl.pallas_call(
        attend_kernel,
        out_shape=(
            jax.ShapeDtypeStruct((384, 512), bf16),
            jax.ShapeDtypeStruct((heads, 1024, 512), bf16),
            jax.ShapeDtypeStruct((heads, 1, 512), f32),
        ),
        grid_spec=grid,
        compiler_params=params(),
        cost_estimate=cost(heads * 1024 * 512 * 512, 10_000_000, heads * 1024 * 512),
        name="attend_" + half,
    )(scal, table, qkv, qkv, qkv)


def attend_back_kernel(
    carried, scal, grad, out, inverse, q, k, v, kept, *refs
):
    if carried:
        dk_in, dv_in, band_in, far_in, *refs = refs
    dq, dk, dv, band, far, va, vt, kt, gt, ds = refs
    head = pl.program_id(0)
    first = scal[0]

    @pl.when(head == 0)
    def _():
        row = iota((16, 1024), 0)
        key = iota((16, 1024), 1)
        vt[64:128] = jnp.zeros((64, 1024), bf16)
        vt[64:80] = jnp.where(row < 2, 1.0, 0.0).astype(bf16)
        kt[64:80] = jnp.where(row < 8, (key // 128 == row).astype(f32), 0.0).astype(bf16)
        gt[64:128] = jnp.zeros((64, 512), bf16)
        ds[0:128] = jnp.zeros((128, 512), bf16)
        ds[1152:1280] = jnp.zeros((128, 512), bf16)

    share = inverse[0]
    scaled = grad[...].astype(f32) * share
    delta = jnp.sum(scaled * out[...].astype(f32), axis=0, keepdims=True)
    high = delta.astype(bf16).astype(f32)
    row = iota((16, 512), 0)
    extra = jnp.where(row == 0, -high, jnp.where(row == 1, high - delta, 0.0))
    gt[64:80] = extra.astype(bf16)
    gt[0:64] = scaled.astype(bf16)
    vt[0:64] = v[...]
    kt[0:64] = k[...]
    va[...] = vt[...].T
    for row_at in range(0, 1024, 256):
        rows = slice(row_at, row_at + 256)
        pull = dot(va[rows], gt[...], 1, 0)
        ds[128 + row_at : 384 + row_at] = (kept[0, rows] * pull).astype(bf16)
    made = dot(kt[...], ds[128:1152], 1, 0)
    dq[...] = made[0:64].astype(bf16)
    block = (iota((8, 512), 1) + first) // 128
    key_block = iota((8, 512), 0)
    totals = made[64:72]
    left = jnp.sum(jnp.where(key_block <= block - 2, totals, 0.0), axis=0, keepdims=True)
    right = jnp.sum(jnp.where(key_block >= block + 2, totals, 0.0), axis=0, keepdims=True)
    sides = jnp.concatenate([left, right, jnp.zeros((6, 512), f32)], axis=0)
    far[0] = sides + far_in[0] if carried else sides
    dv_made = dot(gt[0:64], kept[0], 1, 1)
    dk_made = dot(q[...], ds[128:1152], 1, 1)
    near = None
    for part in range(4):
        base = pl.multiple_of(first + part * 128, 128)
        window = ds[pl.ds(base, 384), part * 128 : part * 128 + 128].astype(f32)
        near = window if near is None else near + window
    if carried:
        dk[...] = (dk_made + dk_in[...]).astype(bf16)
        dv[...] = (dv_made + dv_in[...]).astype(bf16)
        band[0] = near + band_in[0]
    else:
        dk[...] = dk_made
        dv[...] = dv_made
        band[0] = near


def attend_back(scal, grad, out, inverse, qkv, kept, carry, half):
    heads = 6
    rows512 = pl.BlockSpec((64, 512), lambda h, s: (h, 0))
    rows1024 = pl.BlockSpec((64, 1024), lambda h, s: (h, 0))
    band_spec = pl.BlockSpec((1, 384, 128), lambda h, s: (h, 0, 0))
    in_specs = [
        rows512,
        rows512,
        pl.BlockSpec((1, 1, 512), lambda h, s: (h, 0, 0)),
        pl.BlockSpec((64, 512), lambda h, s: (h, s[0] // 512)),
        pl.BlockSpec((64, 1024), lambda h, s: (6 + h, 0)),
        pl.BlockSpec((64, 1024), lambda h, s: (12 + h, 0)),
        pl.BlockSpec((1, 1024, 512), lambda h, s: (h, 0, 0)),
    ]
    far_spec = pl.BlockSpec((1, 8, 512), lambda h, s: (h, 0, 0))
    if carry:
        in_specs += [rows1024, rows1024, band_spec, far_spec]
    wide = bf16 if carry else f32
    grid = pltpu.PrefetchScalarGridSpec(
        num_scalar_prefetch=1,
        grid=(heads,),
        in_specs=in_specs,
        out_specs=(
            rows512,
            rows1024,
            rows1024,
            band_spec,
            far_spec,
        ),
        scratch_shapes=[
            pltpu.VMEM((1024, 128), bf16),
            pltpu.VMEM((128, 1024), bf16),
            pltpu.VMEM((80, 1024), bf16),
            pltpu.VMEM((128, 512), bf16),
            pltpu.VMEM((1280, 512), bf16),
        ],
    )
    return pl.pallas_call(
        functools.partial(attend_back_kernel, bool(carry)),
        out_shape=(
            jax.ShapeDtypeStruct((384, 512), bf16),
            jax.ShapeDtypeStruct((384, 1024), wide),
            jax.ShapeDtypeStruct((384, 1024), wide),
            jax.ShapeDtypeStruct((heads, 384, 128), f32),
            jax.ShapeDtypeStruct((heads, 8, 512), f32),
        ),
        grid_spec=grid,
        compiler_params=params(),
        cost_estimate=cost(heads * 1024 * 512 * 1024, 12_000_000),
        name="attend_back_" + half,
    )(scal, grad, out, inverse, qkv, qkv, qkv, kept, *carry)


def gelu_both(wide):
    square = wide * wide
    inner = 0.7978845608 * wide * (1.0 + 0.044715 * square)
    bend = jnp.tanh(inner)
    half = 0.5 * (1.0 + bend)
    slope = 0.7978845608 * (1.0 + 3 * 0.044715 * square)
    return (wide * half, half + 0.5 * wide * (1.0 - bend * bend) * slope)


def forward_kernel(
    place, att_near, att_far, x, cot, small, near0, near1, far0, far1, nearx0, nearx1, farx0, farx1,
    hidden_hbm, pre_hbm, contract_hbm, middle, normed, branch_low, middle_grad, att, near_grad,
    far_grad, gain_grad,
    w_out, w_up, w_down, hidden, pre, normed_grad, pulled, sems, att_sems, out_sems,
):
    z, y, c, xs = place[0], place[1], place[2], place[3]
    att_copies = []
    for other, source in enumerate((att_near, att_far)):
        row = pl.multiple_of(jnp.bitwise_xor(xs, other) * 384, 128)
        copy = pltpu.make_async_copy(source, att.at[pl.ds(row, 384)], att_sems.at[other])
        copy.start()
        att_copies.append(copy)
    groups = ([], [], [])
    for turn in range(4):
        for dy in range(2):
            owner = ((jnp.bitwise_xor(z, turn) * 2) + jnp.bitwise_xor(y, dy)) * 2
            index = (turn % 2) * 2 + dy
            for other in range(2):
                main = ((near0, near1), (far0, far1))[other][turn // 2]
                side = ((nearx0, nearx1), (farx0, farx1))[other][turn // 2]
                who = owner + jnp.bitwise_xor(c, other)
                row = pl.multiple_of(who * 48, 16)
                pieces = (
                    (0, main.at[index, 4], w_out.at[pl.ds(row, 48)]),
                    (1, main.at[index, 0:4], w_up.at[:, pl.ds(row, 48)]),
                    (2, main.at[index, 5:7], w_down.at[pl.ds(who * 4 + xs * 2, 2)]),
                    (2, side.at[index], w_down.at[pl.ds(who * 4 + (1 - xs) * 2, 2)]),
                )
                for at, (group, source, dest) in enumerate(pieces):
                    sem = sems.at[at, turn * 4 + dy * 2 + other]
                    groups[group].append(pltpu.make_async_copy(source, dest, sem))
    for group in groups:
        for copy in group:
            copy.start()
    for copy in att_copies + groups[0]:
        copy.wait()
    gain = small[1:2]
    wide = x[...].astype(f32) + dot(att[...], w_out[...], 0, 0)
    middle[...] = wide
    scale = lax.rsqrt(jnp.mean(wide * wide, axis=-1, keepdims=True) + EPS)
    normed[...] = (wide * scale * gain).astype(bf16)
    for group in groups[1:]:
        for copy in group:
            copy.wait()
    keep = pltpu.make_async_copy(w_down, contract_hbm, out_sems.at[0])
    keep.start()
    normed_grad[...] = jnp.zeros_like(normed_grad)

    def chunk(j, carry):
        pulled[...] = dot(cot[...], w_down[pl.ds(j * 16, 16)].reshape(768, 768), 1, 1)
        value, slope = gelu_both(dot(normed[...], w_up[j], 1, 0))
        hidden[j] = value.astype(bf16)
        low = (pulled[...] * slope).astype(bf16)
        pre[j] = low
        normed_grad[...] += dot(low, w_up[j], 1, 1)
        return carry

    lax.fori_loop(0, 4, chunk, 0)
    first = pltpu.make_async_copy(hidden, hidden_hbm, out_sems.at[1])
    second = pltpu.make_async_copy(pre, pre_hbm, out_sems.at[2])
    first.start()
    second.start()
    wide = middle[...]
    scale = lax.rsqrt(jnp.mean(wide * wide, axis=-1, keepdims=True) + EPS)
    unit = wide * scale
    incoming = normed_grad[...]
    gain_grad[...] = jnp.sum(incoming * unit, axis=0, keepdims=True)
    direct = incoming * gain
    inward = scale * (direct - unit * jnp.mean(direct * unit, axis=-1, keepdims=True))
    grad = cot[...].astype(f32) + inward
    middle_grad[...] = grad
    low = grad.astype(bf16)
    branch_low[...] = low
    for other, dest in enumerate((near_grad, far_grad)):
        row = pl.multiple_of(jnp.bitwise_xor(xs, other) * 384, 128)
        dest[...] = dot(w_out[pl.ds(row, 384)], low, 1, 1).astype(bf16)
    keep.wait()
    first.wait()
    second.wait()


def forward(place, att_near, att_far, x, cot, small, blocks):
    tokens = jax.ShapeDtypeStruct((512, 768), bf16)
    wide = jax.ShapeDtypeStruct((512, 768), f32)
    half = jax.ShapeDtypeStruct((384, 512), bf16)
    return pl.pallas_call(
        forward_kernel,
        out_shape=(
            jax.ShapeDtypeStruct((4, 512, 768), bf16),
            jax.ShapeDtypeStruct((4, 512, 768), bf16),
            jax.ShapeDtypeStruct((64, 48, 768), bf16),
            wide,
            tokens,
            tokens,
            wide,
            jax.ShapeDtypeStruct((768, 512), bf16),
            half,
            half,
            jax.ShapeDtypeStruct((1, 768), f32),
        ),
        in_specs=[SCALARS, ANY, ANY, FULL, FULL, FULL] + [ANY] * 8,
        out_specs=(ANY, ANY, ANY) + (FULL,) * 8,
        scratch_shapes=[
            pltpu.VMEM((768, 768), bf16),
            pltpu.VMEM((4, 768, 768), bf16),
            pltpu.VMEM((64, 48, 768), bf16),
            pltpu.VMEM((4, 512, 768), bf16),
            pltpu.VMEM((4, 512, 768), bf16),
            pltpu.VMEM((512, 768), f32),
            pltpu.VMEM((512, 768), f32),
            pltpu.SemaphoreType.DMA((4, 16)),
            pltpu.SemaphoreType.DMA((2,)),
            pltpu.SemaphoreType.DMA((3,)),
        ],
        compiler_params=params(),
        cost_estimate=cost(8_500_000_000, 20_000_000, 512 * 3072),
        name="forward",
    )(place, att_near, att_far, x, cot, small, *blocks)


def pick(made, core, near, far, index):
    first, second = made
    near[index] = jnp.where(core == 0, first, second)
    far[index] = jnp.where(core == 0, second, first)


def contract_grad_kernel(place, hidden, cot, near, far):
    made = dot(hidden[0], cot[...], 0, 0).astype(bf16).reshape(2, 4, 48, 768)
    pick((made[0], made[1]), place[2], near, far, 0)


def contract_weight_grad(place, hidden, cot):
    shape = jax.ShapeDtypeStruct((8, 4, 48, 768), bf16)
    spec = pl.BlockSpec((1, 4, 48, 768), lambda j: (j, 0, 0, 0))
    return pl.pallas_call(
        contract_grad_kernel,
        out_shape=(shape, shape),
        grid=(8,),
        in_specs=[
            SCALARS,
            pl.BlockSpec((1, 512, 384), lambda j: (j // 2, 0, j % 2)),
            pl.BlockSpec((512, 768), lambda j: (0, 0)),
        ],
        out_specs=(spec, spec),
        compiler_params=params(),
        cost_estimate=cost(2 * 512 * 3072 * 768, 9_000_000),
        name="contract_weight_grad",
    )(place, hidden, cot)


def expand_grad_kernel(place, normed, pre, att, branch, hidden, contract, middle, near, far, result, total):
    step = pl.program_id(0)

    def store(made):
        made = made.astype(bf16).reshape(8, 2, 48, 768)
        near[:, 0] = jnp.where(place[2] == 0, made[:, 0], made[:, 1])
        far[:, 0] = jnp.where(place[2] == 0, made[:, 1], made[:, 0])

    @pl.when(step < 4)
    def _():
        store(dot(normed[...], pre[0], 0, 0))

    @pl.when(step == 4)
    def _():
        store(dot(att[...], branch[...], 1, 0))

    @pl.when(step == 0)
    def _():
        total[...] = middle[...]

    @pl.when(step < 4)
    def _():
        total[...] += dot(hidden[0], contract[...].reshape(768, 768), 1, 0)

    @pl.when(step == 4)
    def _():
        result[...] = total[...].astype(bf16)


def expand_weight_grad(place, normed, pre, att, branch, hidden, contract, middle):
    shape = jax.ShapeDtypeStruct((8, 5, 48, 768), bf16)
    spec = pl.BlockSpec((8, 1, 48, 768), lambda j: (0, j, 0, 0))
    chunk = pl.BlockSpec((1, 512, 768), lambda j: (jnp.minimum(j, 3), 0, 0))
    whole = pl.BlockSpec((512, 768), lambda j: (0, 0))
    return pl.pallas_call(
        expand_grad_kernel,
        out_shape=(shape, shape, jax.ShapeDtypeStruct((512, 768), bf16)),
        grid=(5,),
        in_specs=[
            SCALARS,
            whole,
            chunk,
            pl.BlockSpec((768, 512), lambda j: (0, 0)),
            whole,
            chunk,
            pl.BlockSpec((16, 48, 768), lambda j: (jnp.minimum(j, 3), 0, 0)),
            whole,
        ],
        out_specs=(spec, spec, whole),
        scratch_shapes=[pltpu.VMEM((512, 768), f32)],
        compiler_params=params(),
        cost_estimate=cost(2 * 512 * 768 * (6144 + 768), 24_000_000),
        name="expand_weight_grad",
    )(place, normed, pre, att, branch, hidden, contract, middle)


def project_back_kernel(
    place, x_near, x_far, w_near, w_far, small, normed, dq_near, dq_far, dk, dv, band, far, gain_two,
    g_near, g_far, part_near, part_far, xs, w, grad, gains, sems, xsems, qsems,
):
    x, core = place[3], place[2]
    tokens = place_tokens(x, x_near, x_far, xs, xsems, 512)
    blocks = place_blocks(place, w_near, w_far, w, sems)
    moves = []
    for other, source in enumerate((dq_near, dq_far)):
        lane = pl.multiple_of(jnp.bitwise_xor(x, other) * 512, 128)
        moves.append(pltpu.make_async_copy(source, grad.at[0:384, pl.ds(lane, 512)], qsems.at[other]))
    moves.append(pltpu.make_async_copy(dk, grad.at[384:768], qsems.at[2]))
    moves.append(pltpu.make_async_copy(dv, grad.at[768:1152], qsems.at[3]))
    for copy in moves:
        copy.start()
    for copy in moves + blocks + tokens:
        copy.wait()
    gain_total = jnp.zeros((1, 768), f32)
    for other, dest in ((1, part_far), (0, part_near)):
        start = pl.multiple_of(jnp.bitwise_xor(x, other) * 512, 512)
        part = dot(grad[:, pl.ds(start, 512)], w[:, 0:1152], 0, 1)
        dest[...] = part.astype(bf16)
        wide = xs[pl.ds(start, 512)].astype(f32)
        scale = lax.rsqrt(jnp.mean(wide * wide, axis=-1, keepdims=True) + EPS)
        gain_total = gain_total + jnp.sum(part * (wide * scale), axis=0, keepdims=True)
    buckets = bucket_of(iota((384, 128), 0) - 128 - iota((384, 128), 1))
    lane = iota((1, 128), 1)
    rows = []
    for head in range(6):
        sums = jnp.zeros((1, 128), f32)
        here = band[head]
        for bucket in range(BUCKETS):
            if bucket == 16:
                continue
            some = jnp.sum(jnp.where(buckets == bucket, here, 0.0))
            if bucket in (15, 31):
                some = some + jnp.sum(far[head, bucket // 16])
            sums = jnp.where(lane == bucket, some, sums)
        rows.append(sums)
    bias = jnp.concatenate(rows + [jnp.zeros((2, 128), f32)], axis=0)
    owner_row = iota((768, 128), 0)
    spot = owner_row % 48
    bucket_at = (owner_row // 48) * 2 + spot // 6
    chosen = jnp.where((iota((768, 128), 1) == bucket_at) & (spot < 12), 1.0, 0.0)
    per_head = lax.dot_general(
        chosen, bias, (((1,), (1,)), ((), ())),
        precision=lax.Precision.HIGHEST, preferred_element_type=f32,
    )
    pattern = (iota((768, 8), 1) == (iota((768, 8), 0) % 48) % 6).astype(f32)
    bias_column = jnp.sum(per_head * pattern, axis=1, keepdims=True)
    gains[...] = jnp.zeros((8, 768), f32)
    gains[0:1] = gain_total
    gains[1:2] = gain_two[...]
    columns = jnp.concatenate([gains[...], jnp.zeros((120, 768), f32)], axis=0).T
    side = jnp.where(iota((768, 128), 1) == 2, bias_column, columns)

    def store(made, low, high):
        made = made.astype(bf16).reshape(8, 2, 48, high - low)
        g_near[:, :, low:high] = jnp.where(core == 0, made[:, 0], made[:, 1])
        g_far[:, :, low:high] = jnp.where(core == 0, made[:, 1], made[:, 0])

    for col in range(0, 1152, 384):
        store(dot(normed[...], grad[col : col + 384], 0, 1), col, col + 384)
    store(side, 1152, 1280)


def project_back(place, x_near, x_far, w_near, w_far, small, normed, dq_near, dq_far, dk, dv, band, far, gain_two):
    owned = jax.ShapeDtypeStruct((8, 48, 1280), bf16)
    part = jax.ShapeDtypeStruct((512, 768), bf16)
    return pl.pallas_call(
        project_back_kernel,
        out_shape=(owned, owned, part, part),
        in_specs=[SCALARS, ANY, ANY, ANY, ANY, FULL, FULL, ANY, ANY, ANY, ANY, FULL, FULL, FULL],
        out_specs=(FULL,) * 4,
        scratch_shapes=[
            pltpu.VMEM((1024, 768), bf16),
            pltpu.VMEM((768, 1280), bf16),
            pltpu.VMEM((1152, 1024), bf16),
            pltpu.VMEM((8, 768), f32),
            pltpu.SemaphoreType.DMA((16,)),
            pltpu.SemaphoreType.DMA((2,)),
            pltpu.SemaphoreType.DMA((4,)),
        ],
        compiler_params=params(),
        cost_estimate=cost(4 * 1024 * 768 * 1152, 16_000_000),
        name="project_back",
    )(place, x_near, x_far, w_near, w_far, small, normed, dq_near, dq_far, dk, dv, band, far, gain_two)


def input_grad_kernel(x, small, near, far, middle_grad, result):
    for row in range(0, 512, 256):
        rows = slice(row, row + 256)
        wide = x[rows].astype(f32)
        scale = lax.rsqrt(jnp.mean(wide * wide, axis=-1, keepdims=True) + EPS)
        unit = wide * scale
        direct = (near[rows].astype(f32) + far[rows].astype(f32)) * small[0:1]
        inward = scale * (direct - unit * jnp.mean(direct * unit, axis=-1, keepdims=True))
        result[rows] = (middle_grad[rows] + inward).astype(bf16)


def input_grad(x, small, near, far, middle_grad):
    return pl.pallas_call(
        input_grad_kernel,
        out_shape=jax.ShapeDtypeStruct((512, 768), bf16),
        in_specs=[FULL] * 5,
        out_specs=FULL,
        compiler_params=params(),
        cost_estimate=cost(512 * 768 * 20, 6_000_000),
        name="input_grad",
    )(x, small, near, far, middle_grad)


def swap(array, axis, bit):
    count = lax.axis_size(axis)
    return lax.ppermute(array, axis, [(i, i ^ bit) for i in range(count)])


CORE, Y, Z = 1, 2, 4


def take(array, index, axis):
    return lax.dynamic_index_in_dim(array, index, axis, keepdims=False)


def added(parts):
    total = parts[0].astype(f32)
    for part in parts[1:]:
        total = total + part.astype(f32)
    return total


def trade(parts, axis, index, mesh_axis, bit):
    sent = added([take(part, 1 - index, axis) for part in parts]).astype(bf16)
    return [take(part, index, axis) for part in parts] + [swap(sent, mesh_axis, bit)]


def trade_z(parts, z):
    got = []
    for turn in range(1, 4):
        sent = added([take(part, z ^ turn, 0) for part in parts]).astype(bf16)
        got.append(swap(sent, "fsdp", Z * turn))
    return added([take(part, z, 0) for part in parts] + got)


def both(array):
    low = lax.optimization_barrier(array.astype(bf16))
    return low, swap(low, "seq", 1)


def local_split(
    layer_input, query_weight, key_weight, value_weight, output_weight, expand_weight,
    contract_weight, attention_gain, feedforward_gain, bias_table, valid_len, instr_len, pair_flag,
    cotangent,
):
    owner, x = lax.axis_index("fsdp"), lax.axis_index("seq")
    z, y, c = owner // 4, (owner // 2) % 2, owner % 2
    place = jnp.stack([z, y, c, x]).astype(jnp.int32)
    tokens, cot = layer_input[0], cotangent[0]

    def columns(weight):
        return lax.dynamic_slice(weight, (0, 384 * x), (48, 384))

    table_column = jnp.pad(bias_table.reshape(24, 1), ((0, 24), (0, 0)))
    side = jnp.concatenate(
        [attention_gain[:, None], feedforward_gain[:, None], table_column], axis=1
    )
    shard = jnp.concatenate(
        [columns(query_weight), columns(key_weight), columns(value_weight), jnp.pad(side, ((0, 0), (0, 125)))],
        axis=1,
    )
    x_far = swap(tokens, "seq", 1)
    along = [shard] + [swap(shard, "fsdp", Z * turn) for turn in range(1, 4)]
    across = [swap(block, "fsdp", Y) for block in along]
    w_near = jnp.stack([block for pair in zip(along, across) for block in pair])
    w_far = swap(w_near, "fsdp", CORE)

    half = lax.dynamic_slice(contract_weight, (96 * x, 0), (96, 768)).reshape(2, 48, 768)
    shard = jnp.concatenate(
        [expand_weight.reshape(48, 4, 768).transpose(1, 0, 2), output_weight[None], half], axis=0
    )
    shard, _ = lax.optimization_barrier((shard, along[3]))
    zs = [shard] + [swap(shard, "fsdp", Z * turn) for turn in range(1, 4)]
    ys = [swap(block, "fsdp", Y) for block in zs]
    near, near_x, far, far_x = [], [], [], []
    for group in range(2):
        at = 2 * group
        blocks = jnp.stack([zs[at], ys[at], zs[at + 1], ys[at + 1]])
        side_blocks = swap(blocks[:, 5:7], "seq", 1)
        near.append(blocks)
        near_x.append(side_blocks)
        far.append(swap(blocks, "fsdp", CORE))
        far_x.append(swap(side_blocks, "fsdp", CORE))

    qkv, normed, small = project(place, tokens, x_far, w_near, w_far)
    table = small[2].reshape(16, 48)[:, :24].reshape(32, 12).T
    table = jnp.pad(lax.dynamic_slice(table, (6 * x, 0), (6, 32)), ((0, 2), (0, 0)))
    lens = jnp.stack([valid_len[0], instr_len[0], pair_flag[0]])
    mine = jnp.concatenate([(x * 512).astype(jnp.int32)[None], lens])
    theirs = jnp.concatenate([((1 - x) * 512).astype(jnp.int32)[None], lens])
    out_theirs, kept_theirs, inverse_theirs = attend(theirs, table, qkv, "theirs")
    out_got = swap(out_theirs, "seq", 1)
    out_mine, kept_mine, inverse_mine = attend(mine, table, qkv, "mine")

    (
        hidden, pre, contract, middle, normed_two, branch_low, middle_grad, att, grad_mine, grad_sent, gain_two,
    ) = forward(place, out_mine, out_got, tokens, cot, small, near + far + near_x + far_x)
    grad_theirs = swap(grad_sent, "seq", 1)

    a_near, a_far = contract_weight_grad(place, hidden, cot)
    a_parts = [part.reshape(4, 2, 2, 2, 48, 768) for part in (a_near, swap(a_far, "fsdp", CORE))]
    b_near, b_far, layer_output = expand_weight_grad(
        place, normed_two, pre, att, branch_low, hidden, contract, middle
    )
    b_parts = [part.reshape(4, 2, 5, 48, 768) for part in (b_near, swap(b_far, "fsdp", CORE))]

    dq_mine, dk, dv, band, far_sum = attend_back(
        mine, grad_mine, out_mine, inverse_mine, qkv, kept_mine, (), "mine"
    )
    a_parts = trade(a_parts, 2, x, "seq", 1)
    b_parts = trade(b_parts, 1, y, "fsdp", Y)
    dq_theirs, dk, dv, band, far_sum = attend_back(
        theirs, grad_theirs, out_theirs, inverse_theirs, qkv, kept_theirs, (dk, dv, band, far_sum), "theirs"
    )
    a_parts = trade(a_parts, 1, y, "fsdp", Y)
    g_near, g_far, part_near, part_far = project_back(
        place, tokens, x_far, w_near, w_far, small, normed, dq_mine, dq_theirs, dk, dv, band, far_sum, gain_two
    )
    part_got = swap(part_far, "seq", 1)
    g_parts = [part.reshape(4, 2, 48, 1280) for part in (g_near, swap(g_far, "fsdp", CORE))]
    g_parts = trade(g_parts, 1, y, "fsdp", Y)

    b_low, b_other = both(trade_z(b_parts, z))
    b_sum = b_low.astype(f32) + b_other.astype(f32)
    expand_sum = b_sum[:4].transpose(1, 0, 2).reshape(48, 3072)
    output_sum = b_sum[4]
    a_low, a_other = both(trade_z(a_parts, z))
    first, second = jnp.where(x == 0, a_low, a_other), jnp.where(x == 0, a_other, a_low)
    contract_sum = jnp.concatenate([first, second], axis=0).reshape(192, 768).astype(f32)

    result = input_grad(tokens, small, part_near, part_got, middle_grad)
    g_low, g_other = both(trade_z(g_parts, z))
    first, second = jnp.where(x == 0, g_low, g_other), jnp.where(x == 0, g_other, g_low)
    grads = [
        jnp.concatenate([first[:, at : at + 384], second[:, at : at + 384]], axis=1).astype(f32)
        for at in (0, 384, 768)
    ]
    gains = g_low[:, 1152:1154].astype(f32) + g_other[:, 1152:1154].astype(f32)
    bias_grad = jnp.concatenate(
        [first[:12, 1154].reshape(2, 6), second[:12, 1154].reshape(2, 6)], axis=1
    ).astype(f32)
    return (
        layer_output[None], result[None], gains[:, 0], gains[:, 1], *grads,
        output_sum, expand_sum, contract_sum, bias_grad,
    )


def bucket_table(query_pos, key_pos):
    offset = key_pos[None, :] - query_pos[:, None]
    distance = jnp.abs(offset)
    beyond = jnp.zeros_like(distance)
    for far_edge in far_edges:
        beyond = beyond + (distance >= far_edge).astype(jnp.int32)
    nearby = jnp.where(distance < 8, distance, 8 + beyond)
    return nearby + 16 * (offset > 0).astype(jnp.int32)


def visible_keys(query_pos, key_pos, valid_len, instr_len, pair_flag):
    in_valid = key_pos[None, None, :] < valid_len[:, None, None]
    guarded = (
        (pair_flag[:, None, None] == 1)
        & (query_pos[None, :, None] < instr_len[:, None, None])
        & (key_pos[None, None, :] >= instr_len[:, None, None])
    )
    return in_valid & jnp.logical_not(guarded)


def rms_scale(values):
    return lax.rsqrt(jnp.mean(values * values, axis=-1, keepdims=True) + EPS)


def norm_back(values, scale, gain, grad_out):
    normed = values * scale
    grad_normed = grad_out * gain
    grad_values = scale * (
        grad_normed - normed * jnp.mean(grad_normed * normed, axis=-1, keepdims=True)
    )
    return (grad_values, jnp.sum(grad_out * normed, axis=(0, 1)))


def gelu_tanh(values):
    return jax.nn.gelu(values, approximate=True)


def local(
    layer_input,
    query_weight,
    key_weight,
    value_weight,
    output_weight,
    expand_weight,
    contract_weight,
    attention_gain,
    feedforward_gain,
    bias_table,
    valid_len,
    instr_len,
    pair_flag,
    cotangent,
):
    f32 = jnp.float32
    bf16 = jnp.bfloat16
    row_count, local_len, model_width = layer_input.shape
    head_count = bias_table.shape[1]
    head_size = model_width // head_count
    full_len = local_len * lax.axis_size("seq")
    local_start = lax.axis_index("seq") * local_len
    query_pos = local_start + jnp.arange(local_len, dtype=jnp.int32)
    key_pos = jnp.arange(full_len, dtype=jnp.int32)
    buckets = bucket_table(query_pos, key_pos)
    onehot = buckets[:, :, None] == jnp.arange(BUCKETS, dtype=jnp.int32)[None, None, :]
    visible = visible_keys(query_pos, key_pos, valid_len, instr_len, pair_flag)
    input_wide = layer_input.astype(f32)

    def attend_probs(queries, key_heads, table_full):
        rel_bias = jnp.einsum(
            "ijb,bh->hij", onehot.astype(bf16), table_full, preferred_element_type=f32
        )
        raw_scores = jnp.einsum("rihe,rjhe->rhij", queries, key_heads, preferred_element_type=f32)
        scores = jnp.where(visible[:, None], raw_scores + rel_bias[None], -1000000000.0)
        row_peak = jnp.max(scores, axis=-1, keepdims=True)
        log_total = row_peak + jnp.log(jnp.sum(jnp.exp(scores - row_peak), axis=-1, keepdims=True))
        return (jnp.exp(scores - log_total), log_total[..., 0])

    def forward(weights):
        (
            query_full,
            key_full,
            value_full,
            output_full,
            expand_full,
            contract_full,
            gain_one,
            gain_two,
            table_full,
        ) = weights
        scale_one = rms_scale(input_wide)
        normed_low = (input_wide * scale_one * gain_one.astype(f32)).astype(bf16)

        def project(weight):
            return jnp.einsum("rtd,de->rte", normed_low, weight, preferred_element_type=f32).astype(
                bf16
            )

        query_low = project(query_full)
        key_low = project(key_full)
        value_low = project(value_full)
        key_all, value_all = (
            lax.all_gather(key_low, "seq", axis=1, tiled=True),
            lax.all_gather(value_low, "seq", axis=1, tiled=True),
        )
        queries = query_low.reshape(row_count, local_len, head_count, head_size)
        key_heads = key_all.reshape(row_count, full_len, head_count, head_size)
        value_heads = value_all.reshape(row_count, full_len, head_count, head_size)
        probs, log_total = attend_probs(queries, key_heads, table_full)
        probs_low = probs.astype(bf16)
        attended = jnp.einsum("rhij,rjhe->rihe", probs_low, value_heads, preferred_element_type=f32)
        attended = attended.reshape(row_count, local_len, model_width).astype(bf16)
        middle = input_wide + jnp.einsum(
            "rtd,de->rte", attended, output_full, preferred_element_type=f32
        )
        scale_two = rms_scale(middle)
        normed_two = (middle * scale_two * gain_two.astype(f32)).astype(bf16)
        hidden_pre = jnp.einsum("rtd,df->rtf", normed_two, expand_full, preferred_element_type=f32)
        hidden_low = gelu_tanh(hidden_pre).astype(bf16)
        result = middle + jnp.einsum(
            "rtf,fd->rtd", hidden_low, contract_full, preferred_element_type=f32
        )
        return (
            result,
            scale_one,
            normed_low,
            queries,
            key_heads,
            value_heads,
            probs,
            probs_low,
            log_total,
            attended,
            middle,
            scale_two,
            normed_two,
            hidden_pre,
            hidden_low,
        )

    stored = forward(
        (
            lax.all_gather(query_weight, "fsdp", axis=0, tiled=True),
            lax.all_gather(key_weight, "fsdp", axis=0, tiled=True),
            lax.all_gather(value_weight, "fsdp", axis=0, tiled=True),
            lax.all_gather(output_weight, "fsdp", axis=0, tiled=True),
            lax.all_gather(expand_weight, "fsdp", axis=0, tiled=True),
            lax.all_gather(contract_weight, "fsdp", axis=0, tiled=True),
            lax.all_gather(attention_gain, "fsdp", axis=0, tiled=True),
            lax.all_gather(feedforward_gain, "fsdp", axis=0, tiled=True),
            lax.all_gather(bias_table, "fsdp", axis=0, tiled=True),
        )
    )
    layer_output = stored[0].astype(bf16)
    gathered = (
        lax.all_gather(query_weight, "fsdp", axis=0, tiled=True),
        lax.all_gather(key_weight, "fsdp", axis=0, tiled=True),
        lax.all_gather(value_weight, "fsdp", axis=0, tiled=True),
        lax.all_gather(output_weight, "fsdp", axis=0, tiled=True),
        lax.all_gather(expand_weight, "fsdp", axis=0, tiled=True),
        lax.all_gather(contract_weight, "fsdp", axis=0, tiled=True),
        lax.all_gather(attention_gain, "fsdp", axis=0, tiled=True),
        lax.all_gather(feedforward_gain, "fsdp", axis=0, tiled=True),
        lax.all_gather(bias_table, "fsdp", axis=0, tiled=True),
    )
    kept = forward(gathered)
    (
        unused,
        scale_one,
        normed_low,
        queries,
        key_heads,
        value_heads,
        probs,
        probs_low,
        log_total,
        attended,
        middle,
        scale_two,
        normed_two,
        hidden_pre,
        hidden_low,
    ) = kept
    (
        query_full,
        key_full,
        value_full,
        output_full,
        expand_full,
        contract_full,
        gain_one,
        gain_two,
        table_full,
    ) = gathered
    gain_one_wide = gain_one.astype(f32)
    gain_two_wide = gain_two.astype(f32)
    contract_grad = jnp.einsum("rtf,rtd->fd", hidden_low, cotangent, preferred_element_type=f32)
    grad_hidden = jnp.einsum("rtd,fd->rtf", cotangent, contract_full, preferred_element_type=f32)
    gelu_pull = jax.vjp(gelu_tanh, hidden_pre)[1]
    grad_pre = gelu_pull(grad_hidden)[0].astype(bf16)
    expand_grad = jnp.einsum("rtd,rtf->df", normed_two, grad_pre, preferred_element_type=f32)
    grad_normed_two = jnp.einsum("rtf,df->rtd", grad_pre, expand_full, preferred_element_type=f32)
    grad_middle_norm, gain_two_grad = norm_back(middle, scale_two, gain_two_wide, grad_normed_two)
    grad_middle = cotangent.astype(f32) + grad_middle_norm
    grad_branch = grad_middle.astype(bf16)
    output_grad = jnp.einsum("rtd,rte->de", attended, grad_branch, preferred_element_type=f32)
    grad_attended = jnp.einsum(
        "rte,de->rtd", grad_branch, output_full, preferred_element_type=f32
    ).astype(bf16)
    grad_attended = grad_attended.reshape(row_count, local_len, head_count, head_size)
    grad_probs = jnp.einsum(
        "rihe,rjhe->rhij", grad_attended, value_heads, preferred_element_type=f32
    )
    row_delta = jnp.sum(probs * grad_probs, axis=-1)
    grad_scores = probs * (grad_probs - row_delta[..., None])
    bias_part = jnp.einsum(
        "hij,ijb->bh",
        jnp.sum(grad_scores, axis=0),
        onehot.astype(f32),
        precision=lax.Precision.HIGHEST,
    )
    scores_low = grad_scores.astype(bf16)
    grad_queries = jnp.einsum("rhij,rjhe->rihe", scores_low, key_heads, preferred_element_type=f32)
    grad_queries = grad_queries.reshape(row_count, local_len, model_width).astype(bf16)
    value_partial = jnp.einsum(
        "rhij,rihe->rjhe", probs_low, grad_attended, preferred_element_type=f32
    ).reshape(row_count, full_len, model_width)
    key_partial = jnp.einsum(
        "rhij,rihe->rjhe", scores_low, queries, preferred_element_type=f32
    ).reshape(row_count, full_len, model_width)
    key_summed, value_summed = (
        lax.psum_scatter(
            key_partial.astype(jnp.bfloat16), "seq", scatter_dimension=1, tiled=True
        ).astype(jnp.float32),
        lax.psum_scatter(
            value_partial.astype(jnp.bfloat16), "seq", scatter_dimension=1, tiled=True
        ).astype(jnp.float32),
    )
    grad_keys = key_summed.astype(bf16)
    grad_values = value_summed.astype(bf16)
    query_part = jnp.einsum("rtd,rte->de", normed_low, grad_queries, preferred_element_type=f32)
    key_part = jnp.einsum("rtd,rte->de", normed_low, grad_keys, preferred_element_type=f32)
    value_part = jnp.einsum("rtd,rte->de", normed_low, grad_values, preferred_element_type=f32)
    grad_normed_one = jnp.einsum(
        "rte,de->rtd", grad_queries, query_full, preferred_element_type=f32
    )
    grad_normed_one = grad_normed_one + jnp.einsum(
        "rte,de->rtd", grad_keys, key_full, preferred_element_type=f32
    )
    grad_normed_one = grad_normed_one + jnp.einsum(
        "rte,de->rtd", grad_values, value_full, preferred_element_type=f32
    )
    grad_input_norm, gain_one_grad = norm_back(
        input_wide, scale_one, gain_one_wide, grad_normed_one
    )
    input_grad = (grad_middle + grad_input_norm).astype(bf16)
    owned = (
        lax.psum_scatter(
            query_part.astype(jnp.bfloat16), "fsdp", scatter_dimension=0, tiled=True
        ).astype(jnp.float32),
        lax.psum_scatter(
            key_part.astype(jnp.bfloat16), "fsdp", scatter_dimension=0, tiled=True
        ).astype(jnp.float32),
        lax.psum_scatter(
            value_part.astype(jnp.bfloat16), "fsdp", scatter_dimension=0, tiled=True
        ).astype(jnp.float32),
        lax.psum_scatter(
            output_grad.astype(jnp.bfloat16), "fsdp", scatter_dimension=0, tiled=True
        ).astype(jnp.float32),
        lax.psum_scatter(
            expand_grad.astype(jnp.bfloat16), "fsdp", scatter_dimension=0, tiled=True
        ).astype(jnp.float32),
        lax.psum_scatter(
            contract_grad.astype(jnp.bfloat16), "fsdp", scatter_dimension=0, tiled=True
        ).astype(jnp.float32),
        lax.psum_scatter(
            gain_one_grad.astype(jnp.bfloat16), "fsdp", scatter_dimension=0, tiled=True
        ).astype(jnp.float32),
        lax.psum_scatter(
            gain_two_grad.astype(jnp.bfloat16), "fsdp", scatter_dimension=0, tiled=True
        ).astype(jnp.float32),
        lax.psum_scatter(
            bias_part.astype(jnp.bfloat16), "fsdp", scatter_dimension=0, tiled=True
        ).astype(jnp.float32),
    )
    summed = (
        lax.psum(owned[0].astype(jnp.bfloat16), "seq").astype(jnp.float32),
        lax.psum(owned[1].astype(jnp.bfloat16), "seq").astype(jnp.float32),
        lax.psum(owned[2].astype(jnp.bfloat16), "seq").astype(jnp.float32),
        lax.psum(owned[3].astype(jnp.bfloat16), "seq").astype(jnp.float32),
        lax.psum(owned[4].astype(jnp.bfloat16), "seq").astype(jnp.float32),
        lax.psum(owned[5].astype(jnp.bfloat16), "seq").astype(jnp.float32),
        lax.psum(owned[6].astype(jnp.bfloat16), "seq").astype(jnp.float32),
        lax.psum(owned[7].astype(jnp.bfloat16), "seq").astype(jnp.float32),
        lax.psum(owned[8].astype(jnp.bfloat16), "seq").astype(jnp.float32),
    )
    (
        query_grad,
        key_grad,
        value_grad,
        output_sum,
        expand_sum,
        contract_sum,
        gain_one_sum,
        gain_two_sum,
        bias_grad,
    ) = summed
    return (
        layer_output,
        input_grad,
        gain_one_sum,
        gain_two_sum,
        query_grad,
        key_grad,
        value_grad,
        output_sum,
        expand_sum,
        contract_sum,
        bias_grad,
    )


def solution(mesh):
    in_specs = (
        P("fsdp", "seq", None),
        P("fsdp", None),
        P("fsdp", None),
        P("fsdp", None),
        P("fsdp", None),
        P("fsdp", None),
        P("fsdp", None),
        P("fsdp"),
        P("fsdp"),
        P("fsdp", None),
        P("fsdp"),
        P("fsdp"),
        P("fsdp"),
        P("fsdp", "seq", None),
    )
    out_specs = (
        P("fsdp", "seq", None),
        P("fsdp", "seq", None),
        P("fsdp"),
        P("fsdp"),
        P("fsdp", None),
        P("fsdp", None),
        P("fsdp", None),
        P("fsdp", None),
        P("fsdp", None),
        P("fsdp", None),
        P("fsdp", None),
    )
    split = mesh.shape["fsdp"] == 16 and mesh.shape["seq"] == 2
    step = local_split if split else local
    return jax.shard_map(step, mesh=mesh, in_specs=in_specs, out_specs=out_specs, check_vma=False)
```

```python
import functools
import itertools
import math

import jax
import jax.numpy as jnp
from jax import lax
from jax.experimental import pallas as pl
from jax.experimental.pallas import tpu as pltpu
from jax.sharding import PartitionSpec as P

f32 = jnp.float32
bf16 = jnp.bfloat16
BUCKETS = 32
EPS = 1e-06
far_edges = (12, 16, 23, 32, 46, 64, 91)
HIDDEN = -(2.0**30)
VMEM = 56 * 1024 * 1024
ANY = pl.BlockSpec(memory_space=pl.ANY)
FULL = pl.BlockSpec(memory_space=pltpu.VMEM)
SCALARS = pl.BlockSpec(memory_space=pltpu.SMEM)


def dot(left, right, left_dim, right_dim):
    return lax.dot_general(
        left, right, (((left_dim,), (right_dim,)), ((), ())), preferred_element_type=f32
    )


def params():
    return pltpu.CompilerParams(vmem_limit_bytes=VMEM)


def cost(flops, byte_count, exps=0):
    return pl.CostEstimate(flops=flops // 1000, bytes_accessed=byte_count // 1000, transcendentals=exps // 1000)


def bucket_of(offset):
    distance = jnp.abs(offset)
    beyond = jnp.zeros_like(distance)
    for far_edge in far_edges:
        beyond = beyond + (distance >= far_edge).astype(jnp.int32)
    nearby = jnp.where(distance < 8, distance, 8 + beyond)
    return nearby + 16 * (offset > 0).astype(jnp.int32)


def iota(shape, dim):
    return lax.broadcasted_iota(jnp.int32, shape, dim)


def narrow_kernel(place, q, k, v, gain_one, gain_two, table, out, side, sems):
    x = place[3]
    column = pl.multiple_of(x * 384, 128)
    copies = []
    for at, weight in enumerate((q, k, v)):
        source = weight.at[:, pl.ds(column, 384)]
        copy = pltpu.make_async_copy(source, out.at[:, at * 384 : at * 384 + 384], sems.at[at])
        copy.start()
        copies.append(copy)
    side[...] = jnp.zeros((8, 128), f32)
    side[0:1, 0:48] = gain_one[...].astype(f32)
    side[1:2, 0:48] = gain_two[...].astype(f32)
    side[2:3, 0:12] = table[0:1].astype(f32)
    side[2:3, 12:24] = table[1:2].astype(f32)
    wide = jnp.concatenate([side[...], jnp.zeros((120, 128), f32)], axis=0).T
    out[:, 1152:1280] = wide[0:48].astype(bf16)
    for copy in copies:
        copy.wait()


def narrow_shard(place, q, k, v, gain_one, gain_two, table):
    return pl.pallas_call(
        narrow_kernel,
        out_shape=jax.ShapeDtypeStruct((48, 1280), bf16),
        in_specs=[SCALARS, ANY, ANY, ANY, FULL, FULL, FULL],
        out_specs=FULL,
        scratch_shapes=[pltpu.VMEM((8, 128), f32), pltpu.SemaphoreType.DMA((3,))],
        compiler_params=params(),
        cost_estimate=cost(1000, 250_000),
        name="narrow_shard",
    )(place, q, k, v, gain_one.reshape(1, 48), gain_two.reshape(1, 48), table)


def wide_kernel(place, expand, output, contract, out, side, sems):
    x = place[3]
    pieces = [(expand.at[:, at * 768 : at * 768 + 768], out.at[at]) for at in range(4)]
    pieces.append((output, out.at[4]))
    for at in range(2):
        row = pl.multiple_of(x * 96 + at * 48, 16)
        pieces.append((contract.at[pl.ds(row, 48)], out.at[5 + at]))
        row = pl.multiple_of((1 - x) * 96 + at * 48, 16)
        pieces.append((contract.at[pl.ds(row, 48)], side.at[at]))
    copies = [pltpu.make_async_copy(*piece, sems.at[at]) for at, piece in enumerate(pieces)]
    for copy in copies:
        copy.start()
    for copy in copies:
        copy.wait()


def wide_shard(place, expand, output, contract):
    return pl.pallas_call(
        wide_kernel,
        out_shape=(
            jax.ShapeDtypeStruct((7, 48, 768), bf16), jax.ShapeDtypeStruct((2, 48, 768), bf16),
        ),
        in_specs=[SCALARS, ANY, ANY, ANY],
        out_specs=(FULL, FULL),
        scratch_shapes=[pltpu.SemaphoreType.DMA((9,))],
        compiler_params=params(),
        cost_estimate=cost(1000, 900_000),
        name="wide_shard",
    )(place, expand, output, contract)


def eight(blocks):
    own, across, along, both = blocks
    return [own, across] + [ref.at[at] for at in range(3) for ref in (along, both)]


def place_blocks(place, near, far, dest, sems):
    z, y, c = place[0], place[1], place[2]
    copies = []
    near, far = eight(near), eight(far)
    for turn in range(4):
        for dy in range(2):
            owner = ((jnp.bitwise_xor(z, turn) * 2) + jnp.bitwise_xor(y, dy)) * 2
            for other, source in enumerate((near, far)):
                row = pl.multiple_of((owner + jnp.bitwise_xor(c, other)) * 48, 16)
                copy = pltpu.make_async_copy(
                    source[turn * 2 + dy], dest.at[pl.ds(row, 48)], sems.at[len(copies)]
                )
                copy.start()
                copies.append(copy)
    return copies


def place_tokens(x, near, far, dest, sems, count):
    copies = []
    for other, source in enumerate((near, far)):
        row = pl.multiple_of(jnp.bitwise_xor(x, other) * count, count)
        copy = pltpu.make_async_copy(source, dest.at[pl.ds(row, count)], sems.at[other])
        copy.start()
        copies.append(copy)
    return copies


def first_query(place, mine):
    return (place[3] if mine else 1 - place[3]) * 512


def project_kernel(place, x_near, x_far, *refs):
    w_near, w_far, refs = refs[:4], refs[4:8], refs[8:]
    qkv, normed, small, table, tiles, xs, w, sems, xsems = refs
    tokens = place_tokens(place[3], x_near, x_far, xs, xsems, 512)
    blocks = place_blocks(place, w_near, w_far, w, sems)
    for copy in tokens + blocks:
        copy.wait()
    side = w[:, 1152:1280].astype(f32).T
    small[...] = side[:8]
    gain = side[0:1]
    row = iota((768, 128), 0)
    spot = row % 48
    bucket = (row // 48) * 2 + spot // 12
    kept = (iota((768, 128), 1) == bucket) & (spot < 24)
    values = jnp.where(kept, w[:, 1154:1155].astype(f32), 0.0).astype(bf16)
    head = iota((8, 768), 0)
    chosen = ((iota((8, 768), 1) % 48) % 12 == place[3] * 6 + head) & (head < 6)
    made = dot(chosen.astype(bf16), values, 1, 0)
    table[...] = made
    lane = iota((128, 512), 1)
    spread = (bucket_of(jnp.where(lane < 128, -128 - lane, 384 - lane)) == iota((128, 512), 0)).astype(bf16)
    turned = dot(made.astype(bf16), spread, 1, 0)
    for head in range(6):
        for block, (low, high) in enumerate(((384, 0), (256, 384), (128, 256))):
            parts = [turned[head : head + 1, at : at + 128] for at in (low, high)]
            wide = jnp.broadcast_to(jnp.concatenate(parts, axis=1), (128, 256))
            rolled = pltpu.roll(wide, 0, 1, stride=1, stride_axis=0)
            tiles[head, block * 128 : block * 128 + 128] = rolled[:, 128:256]
    for row in range(0, 1024, 256):
        wide = xs[row : row + 256].astype(f32)
        scale = lax.rsqrt(jnp.mean(wide * wide, axis=-1, keepdims=True) + EPS)
        normed[row : row + 256] = (wide * scale * gain).astype(bf16)
    for col in range(0, 1152, 384):
        made = dot(w[:, col : col + 384], normed[...], 0, 1)
        qkv[col : col + 384] = made.astype(bf16)


def project(place, x_near, x_far, w_near, w_far):
    return pl.pallas_call(
        project_kernel,
        out_shape=(
            jax.ShapeDtypeStruct((1152, 1024), bf16),
            jax.ShapeDtypeStruct((1024, 768), bf16),
            jax.ShapeDtypeStruct((8, 768), f32),
            jax.ShapeDtypeStruct((8, 128), f32),
            jax.ShapeDtypeStruct((6, 384, 128), f32),
        ),
        in_specs=[SCALARS] + [ANY] * 10,
        out_specs=(FULL,) * 5,
        scratch_shapes=[
            pltpu.VMEM((1024, 768), bf16),
            pltpu.VMEM((768, 1280), bf16),
            pltpu.SemaphoreType.DMA((16,)),
            pltpu.SemaphoreType.DMA((2,)),
        ],
        compiler_params=params(),
        cost_estimate=cost(2 * 1024 * 768 * 1152, 9_000_000),
        name="project",
    )(place, x_near, x_far, *w_near, *w_far)


def attend_kernel(mine, place, table, tile, q, k, v, out, kept, inverse, ka, kt, qt, vt, s):
    head = pl.program_id(0)
    first, valid, instr, pair = first_query(place, mine), place[4], place[5], place[6]

    @pl.when(head == 0)
    def _():
        kt[64:128] = jnp.zeros((64, 1024), bf16)
        qt[64:128] = jnp.zeros((64, 512), bf16)
        row = iota((16, 1024), 0)
        key = iota((16, 1024), 1)
        extra = jnp.where(row < 8, (key // 128 == row).astype(f32), 0.0)
        extra = jnp.where(row == 8, jnp.where(key >= valid, HIDDEN, 0.0), extra)
        extra = jnp.where(row == 9, (key >= instr).astype(f32), extra)
        kt[64:80] = extra.astype(bf16)
        vt[64:80] = jnp.where(row == 0, 1.0, 0.0).astype(bf16)

    row = iota((16, 512), 0)
    query = iota((16, 512), 1) + first
    block = query // 128
    extra = jnp.where(row <= block - 2, table[head, 15], 0.0)
    extra = jnp.where(row >= block + 2, table[head, 31], extra)
    extra = jnp.where(row == 8, 1.0, extra)
    guarded = (query < instr) & (pair == 1)
    extra = jnp.where(row == 9, jnp.where(guarded, HIDDEN, 0.0), extra)
    extra = jnp.where(row > 9, 0.0, extra)
    qt[64:80] = extra.astype(bf16)
    qt[0:64] = q[...]
    kt[0:64] = k[...]
    vt[0:64] = v[...]
    ka[...] = kt[...].T
    s[128:1152] = dot(ka[...], qt[...], 1, 0)
    for part in range(4):
        base = pl.multiple_of(first + part * 128, 128)
        cols = slice(part * 128, part * 128 + 128)
        s[pl.ds(base, 384), cols] = s[pl.ds(base, 384), cols] + tile[0]
    scores = s[128:1152]
    peak = jnp.max(scores, axis=0, keepdims=True)
    weights = jnp.exp(scores - peak).astype(bf16)
    kept[0] = weights
    summed = dot(vt[...], weights, 1, 0)
    share = 1.0 / summed[64:65]
    out[...] = (summed[0:64] * share).astype(bf16)
    inverse[0] = share


def attend(place, table, tiles, qkv, mine):
    half = (lambda s: s[3]) if mine else (lambda s: 1 - s[3])
    grid = pltpu.PrefetchScalarGridSpec(
        num_scalar_prefetch=1,
        grid=(6,),
        in_specs=[
            SCALARS,
            pl.BlockSpec((1, 384, 128), lambda h, s: (h, 0, 0)),
            pl.BlockSpec((64, 512), lambda h, s: (h, half(s))),
            pl.BlockSpec((64, 1024), lambda h, s: (6 + h, 0)),
            pl.BlockSpec((64, 1024), lambda h, s: (12 + h, 0)),
        ],
        out_specs=(
            pl.BlockSpec((64, 512), lambda h, s: (h, 0)),
            pl.BlockSpec((1, 1024, 512), lambda h, s: (h, 0, 0)),
            pl.BlockSpec((1, 1, 512), lambda h, s: (h, 0, 0)),
        ),
        scratch_shapes=[
            pltpu.VMEM((1024, 128), bf16),
            pltpu.VMEM((128, 1024), bf16),
            pltpu.VMEM((128, 512), bf16),
            pltpu.VMEM((80, 1024), bf16),
            pltpu.VMEM((1280, 512), f32),
        ],
    )
    return pl.pallas_call(
        functools.partial(attend_kernel, mine),
        out_shape=(
            jax.ShapeDtypeStruct((384, 512), bf16),
            jax.ShapeDtypeStruct((6, 1024, 512), bf16),
            jax.ShapeDtypeStruct((6, 1, 512), f32),
        ),
        grid_spec=grid,
        compiler_params=params(),
        cost_estimate=cost(6 * 1024 * 512 * 512, 10_000_000, 6 * 1024 * 512),
        name="attend_mine" if mine else "attend_theirs",
    )(place, table, tiles, qkv, qkv, qkv)


def attend_back_kernel(carried, mine, place, grad, out, inverse, q, k, v, kept, *refs):
    if carried:
        dk_in, dv_in, band_in, far_in, *refs = refs
    dq, dk, dv, band, far, va, vt, kt, gt, ds = refs
    first = first_query(place, mine)

    @pl.when(pl.program_id(0) == 0)
    def _():
        row = iota((16, 1024), 0)
        key = iota((16, 1024), 1)
        vt[64:128] = jnp.zeros((64, 1024), bf16)
        vt[64:80] = jnp.where(row < 2, 1.0, 0.0).astype(bf16)
        kt[64:80] = jnp.where(row < 8, (key // 128 == row).astype(f32), 0.0).astype(bf16)
        gt[64:128] = jnp.zeros((64, 512), bf16)
        ds[0:128] = jnp.zeros((128, 512), bf16)
        ds[1152:1280] = jnp.zeros((128, 512), bf16)

    share = inverse[0]
    scaled = grad[...].astype(f32) * share
    delta = jnp.sum(scaled * out[...].astype(f32), axis=0, keepdims=True)
    high = delta.astype(bf16).astype(f32)
    row = iota((16, 512), 0)
    extra = jnp.where(row == 0, -high, jnp.where(row == 1, high - delta, 0.0))
    gt[64:80] = extra.astype(bf16)
    gt[0:64] = scaled.astype(bf16)
    vt[0:64] = v[...]
    kt[0:64] = k[...]
    va[...] = vt[...].T
    for row_at in range(0, 1024, 256):
        rows = slice(row_at, row_at + 256)
        pull = dot(va[rows], gt[...], 1, 0)
        ds[128 + row_at : 384 + row_at] = (kept[0, rows] * pull).astype(bf16)
    made = dot(kt[...], ds[128:1152], 1, 0)
    dq[...] = made[0:64].astype(bf16)
    block = (iota((8, 512), 1) + first) // 128
    key_block = iota((8, 512), 0)
    totals = made[64:72]
    left = jnp.sum(jnp.where(key_block <= block - 2, totals, 0.0), axis=0, keepdims=True)
    right = jnp.sum(jnp.where(key_block >= block + 2, totals, 0.0), axis=0, keepdims=True)
    sides = jnp.concatenate([left, right, jnp.zeros((6, 512), f32)], axis=0)
    far[0] = sides + far_in[0] if carried else sides
    dv_made = dot(gt[0:64], kept[0], 1, 1)
    dk_made = dot(q[...], ds[128:1152], 1, 1)
    near = None
    for part in range(4):
        base = pl.multiple_of(first + part * 128, 128)
        window = ds[pl.ds(base, 384), part * 128 : part * 128 + 128].astype(f32)
        near = window if near is None else near + window
    if carried:
        dk[...] = (dk_made + dk_in[...]).astype(bf16)
        dv[...] = (dv_made + dv_in[...]).astype(bf16)
        band[0] = near + band_in[0]
    else:
        dk[...] = dk_made
        dv[...] = dv_made
        band[0] = near


def attend_back(place, grad, out, inverse, qkv, kept, carry, mine, start, count):
    half = (lambda s: s[3]) if mine else (lambda s: 1 - s[3])
    whole = lambda h, s: (start + h, 0)
    whole3 = lambda h, s: (start + h, 0, 0)
    rows1024 = pl.BlockSpec((64, 1024), lambda h, s: (h, 0))
    band_spec = pl.BlockSpec((1, 384, 128), lambda h, s: (h, 0, 0))
    far_spec = pl.BlockSpec((1, 8, 512), lambda h, s: (h, 0, 0))
    in_specs = [
        pl.BlockSpec((64, 512), whole),
        pl.BlockSpec((64, 512), whole),
        pl.BlockSpec((1, 1, 512), whole3),
        pl.BlockSpec((64, 512), lambda h, s: (start + h, half(s))),
        pl.BlockSpec((64, 1024), lambda h, s: (start + 6 + h, 0)),
        pl.BlockSpec((64, 1024), lambda h, s: (start + 12 + h, 0)),
        pl.BlockSpec((1, 1024, 512), whole3),
    ]
    if carry:
        in_specs += [rows1024, rows1024, band_spec, far_spec]
    wide = bf16 if carry else f32
    grid = pltpu.PrefetchScalarGridSpec(
        num_scalar_prefetch=1,
        grid=(count,),
        in_specs=in_specs,
        out_specs=(pl.BlockSpec((64, 512), lambda h, s: (h, 0)), rows1024, rows1024, band_spec, far_spec),
        scratch_shapes=[
            pltpu.VMEM((1024, 128), bf16),
            pltpu.VMEM((128, 1024), bf16),
            pltpu.VMEM((80, 1024), bf16),
            pltpu.VMEM((128, 512), bf16),
            pltpu.VMEM((1280, 512), bf16),
        ],
    )
    return pl.pallas_call(
        functools.partial(attend_back_kernel, bool(carry), mine),
        out_shape=(
            jax.ShapeDtypeStruct((64 * count, 512), bf16),
            jax.ShapeDtypeStruct((64 * count, 1024), wide),
            jax.ShapeDtypeStruct((64 * count, 1024), wide),
            jax.ShapeDtypeStruct((count, 384, 128), f32),
            jax.ShapeDtypeStruct((count, 8, 512), f32),
        ),
        grid_spec=grid,
        compiler_params=params(),
        cost_estimate=cost(count * 1024 * 512 * 1024, 6_000_000),
        name=("attend_back_mine_" if mine else "attend_back_theirs_") + str(start),
    )(place, grad, out, inverse, qkv, qkv, qkv, kept, *carry)


def gelu_both(wide):
    square = wide * wide
    inner = 0.7978845608 * wide * (1.0 + 0.044715 * square)
    bend = jnp.tanh(inner)
    half = 0.5 * (1.0 + bend)
    slope = 0.7978845608 * (1.0 + 3 * 0.044715 * square)
    return (wide * half, half + 0.5 * wide * (1.0 - bend * bend) * slope)


BLOCKS = (
    lambda s: s[0], lambda s: s[1], lambda s: s[2].at[0], lambda s: s[3].at[0],
    lambda s: s[2].at[1], lambda s: s[3].at[1], lambda s: s[4], lambda s: s[5],
)
SIDES = (
    lambda s: s[0], lambda s: s[1].at[2], lambda s: s[1].at[0], lambda s: s[3].at[0],
    lambda s: s[1].at[1], lambda s: s[3].at[1], lambda s: s[2], lambda s: s[4],
)


def forward_kernel(
    place, att_near, att_far, x, cot, small, *refs
):
    nears, fars, near_sides, far_sides, refs = refs[:6], refs[6:12], refs[12:17], refs[17:22], refs[22:]
    nears, fars = ([get(blocks) for get in BLOCKS] for blocks in (nears, fars))
    near_sides, far_sides = ([get(sides) for get in SIDES] for sides in (near_sides, far_sides))
    (
        hidden_hbm, pre_hbm, result, normed, branch_low, middle_grad, att, near_grad, far_grad,
        w_out, w_up, w_down, hidden, pre, normed_grad, pulled, middle, total, sems, att_sems, out_sems,
    ) = refs
    z, y, c, xs = place[0], place[1], place[2], place[3]
    att_copies = []
    for other, source in enumerate((att_near, att_far)):
        row = pl.multiple_of(jnp.bitwise_xor(xs, other) * 384, 128)
        copy = pltpu.make_async_copy(source, att.at[pl.ds(row, 384)], att_sems.at[other])
        copy.start()
        att_copies.append(copy)
    groups = ([], [], [])
    for turn in range(4):
        for dy in range(2):
            owner = ((jnp.bitwise_xor(z, turn) * 2) + jnp.bitwise_xor(y, dy)) * 2
            for other in range(2):
                main = (nears, fars)[other][turn * 2 + dy]
                side = (near_sides, far_sides)[other][turn * 2 + dy]
                who = owner + jnp.bitwise_xor(c, other)
                row = pl.multiple_of(who * 48, 16)
                pieces = (
                    (0, main.at[4], w_out.at[pl.ds(row, 48)]),
                    (1, main.at[0:4], w_up.at[:, pl.ds(row, 48)]),
                    (2, main.at[5:7], w_down.at[pl.ds(who * 4 + xs * 2, 2)]),
                    (2, side, w_down.at[pl.ds(who * 4 + (1 - xs) * 2, 2)]),
                )
                for at, (group, source, dest) in enumerate(pieces):
                    sem = sems.at[at, turn * 4 + dy * 2 + other]
                    groups[group].append(pltpu.make_async_copy(source, dest, sem))
    for group in groups:
        for copy in group:
            copy.start()
    for copy in att_copies + groups[0]:
        copy.wait()
    gain = small[1:2]
    wide = x[...].astype(f32) + dot(att[...], w_out[...], 0, 0)
    middle[...] = wide
    scale = lax.rsqrt(jnp.mean(wide * wide, axis=-1, keepdims=True) + EPS)
    normed[...] = (wide * scale * gain).astype(bf16)
    for group in groups[1:]:
        for copy in group:
            copy.wait()
    total[...] = wide
    normed_grad[...] = jnp.zeros_like(normed_grad)

    def chunk(j, carry):
        down = w_down[pl.ds(j * 16, 16)].reshape(768, 768)
        pulled[...] = dot(cot[...], down, 1, 1)
        value, slope = gelu_both(dot(normed[...], w_up[j], 1, 0))
        hidden[j] = value.astype(bf16)
        total[...] += dot(hidden[j], down, 1, 0)
        low = (pulled[...] * slope).astype(bf16)
        pre[j] = low
        normed_grad[...] += dot(low, w_up[j], 1, 1)
        return carry

    lax.fori_loop(0, 4, chunk, 0)
    first = pltpu.make_async_copy(hidden, hidden_hbm, out_sems.at[1])
    second = pltpu.make_async_copy(pre, pre_hbm, out_sems.at[2])
    first.start()
    second.start()
    wide = middle[...]
    scale = lax.rsqrt(jnp.mean(wide * wide, axis=-1, keepdims=True) + EPS)
    unit = wide * scale
    incoming = normed_grad[...]
    direct = incoming * gain
    inward = scale * (direct - unit * jnp.mean(direct * unit, axis=-1, keepdims=True))
    grad = cot[...].astype(f32) + inward
    middle_grad[...] = grad
    low = grad.astype(bf16)
    branch_low[...] = low
    for other, dest in enumerate((near_grad, far_grad)):
        row = pl.multiple_of(jnp.bitwise_xor(xs, other) * 384, 128)
        dest[...] = dot(w_out[pl.ds(row, 384)], low, 1, 1).astype(bf16)
    result[...] = total[...].astype(bf16)
    first.wait()
    second.wait()


def forward(place, att_near, att_far, x, cot, small, blocks, sides):
    tokens = jax.ShapeDtypeStruct((512, 768), bf16)
    wide = jax.ShapeDtypeStruct((512, 768), f32)
    half = jax.ShapeDtypeStruct((384, 512), bf16)
    return pl.pallas_call(
        forward_kernel,
        out_shape=(
            jax.ShapeDtypeStruct((4, 512, 768), bf16),
            jax.ShapeDtypeStruct((4, 512, 768), bf16),
            tokens,
            tokens,
            tokens,
            wide,
            jax.ShapeDtypeStruct((768, 512), bf16),
            half,
            half,
        ),
        in_specs=[SCALARS, ANY, ANY, FULL, FULL, FULL] + [ANY] * 22,
        out_specs=(ANY, ANY) + (FULL,) * 7,
        scratch_shapes=[
            pltpu.VMEM((768, 768), bf16),
            pltpu.VMEM((4, 768, 768), bf16),
            pltpu.VMEM((64, 48, 768), bf16),
            pltpu.VMEM((4, 512, 768), bf16),
            pltpu.VMEM((4, 512, 768), bf16),
            pltpu.VMEM((512, 768), f32),
            pltpu.VMEM((512, 768), f32),
            pltpu.VMEM((512, 768), f32),
            pltpu.VMEM((512, 768), f32),
            pltpu.SemaphoreType.DMA((4, 16)),
            pltpu.SemaphoreType.DMA((2,)),
            pltpu.SemaphoreType.DMA((3,)),
        ],
        compiler_params=params(),
        cost_estimate=cost(8_500_000_000, 20_000_000, 512 * 3072),
        name="forward",
    )(place, att_near, att_far, x, cot, small, *blocks, *sides)


def contract_grad_kernel(place, hidden, cot, near, far):
    made = dot(hidden[0], cot[...], 0, 0).astype(bf16).reshape(2, 2, 4, 48, 768)
    near[...] = jnp.where(place[2] == 0, made[:, 0], made[:, 1])
    far[...] = jnp.where(place[2] == 0, made[:, 1], made[:, 0])


def contract_weight_grad(place, hidden, cot):
    shape = jax.ShapeDtypeStruct((8, 4, 48, 768), bf16)
    spec = pl.BlockSpec((2, 4, 48, 768), lambda j: (j, 0, 0, 0))
    return pl.pallas_call(
        contract_grad_kernel,
        out_shape=(shape, shape),
        grid=(4,),
        in_specs=[
            SCALARS,
            pl.BlockSpec((1, 512, 768), lambda j: (j, 0, 0)),
            pl.BlockSpec((512, 768), lambda j: (0, 0)),
        ],
        out_specs=(spec, spec),
        compiler_params=params(),
        cost_estimate=cost(2 * 512 * 3072 * 768, 9_000_000),
        name="contract_weight_grad",
    )(place, hidden, cot)


def expand_grad_kernel(place, normed, pre, att, branch, near, far):
    step = pl.program_id(0)

    def store(made):
        made = made.astype(bf16).reshape(8, 2, 48, 768)
        near[:, 0] = jnp.where(place[2] == 0, made[:, 0], made[:, 1])
        far[:, 0] = jnp.where(place[2] == 0, made[:, 1], made[:, 0])

    @pl.when(step < 4)
    def _():
        store(dot(normed[...], pre[0], 0, 0))

    @pl.when(step == 4)
    def _():
        store(dot(att[...], branch[...], 1, 0))


def expand_weight_grad(place, normed, pre, att, branch):
    shape = jax.ShapeDtypeStruct((8, 5, 48, 768), bf16)
    spec = pl.BlockSpec((8, 1, 48, 768), lambda j: (0, j, 0, 0))
    whole = pl.BlockSpec((512, 768), lambda j: (0, 0))
    return pl.pallas_call(
        expand_grad_kernel,
        out_shape=(shape, shape),
        grid=(5,),
        in_specs=[
            SCALARS,
            whole,
            pl.BlockSpec((1, 512, 768), lambda j: (jnp.minimum(j, 3), 0, 0)),
            pl.BlockSpec((768, 512), lambda j: (0, 0)),
            whole,
        ],
        out_specs=(spec, spec),
        compiler_params=params(),
        cost_estimate=cost(2 * 512 * 768 * 3840, 12_000_000),
        name="expand_weight_grad",
    )(place, normed, pre, att, branch)


GROUPS = ((0, 4), (4, 2))


def place_grads(x, group, pieces, grad, rows, sems):
    dq_near, dq_far, dk, dv = pieces
    size = 64 * GROUPS[group][1]
    moves = []
    for other, source in enumerate((dq_near, dq_far)):
        lane = pl.multiple_of(jnp.bitwise_xor(x, other) * 512, 128)
        moves.append((source, grad.at[rows[0] : rows[0] + size, pl.ds(lane, 512)]))
    moves.append((dk, grad.at[rows[1] : rows[1] + size]))
    moves.append((dv, grad.at[rows[2] : rows[2] + size]))
    copies = [pltpu.make_async_copy(*move, sems.at[group, at]) for at, move in enumerate(moves)]
    for copy in copies:
        copy.start()
    return copies


def bias_sums(band, far):
    flip = (iota((128, 128), 0) + iota((128, 128), 1) == 127).astype(f32)
    total = None
    heads = band.shape[0]
    for block in range(3):
        rows = []
        for head in range(heads):
            here = lax.dot_general(
                flip, band[head, block * 128 : block * 128 + 128], (((1,), (0,)), ((), ())),
                precision=lax.Precision.HIGHEST, preferred_element_type=f32,
            )
            wide = jnp.concatenate([here, jnp.zeros((128, 128), f32)], axis=1)
            rolled = pltpu.roll(wide, 0, 1, stride=1, stride_axis=0)
            rows.append(jnp.sum(rolled, axis=0, keepdims=True))
        diagonals = jnp.concatenate(rows + [jnp.zeros((8 - heads, 256), f32)], axis=0)
        offset = block * 128 - 1 - iota((256, 128), 0)
        spread = (bucket_of(offset) == iota((256, 128), 1)).astype(f32)
        made = lax.dot_general(
            diagonals, spread, (((1,), (0,)), ((), ())),
            precision=lax.Precision.HIGHEST, preferred_element_type=f32,
        )
        total = made if total is None else total + made
    lane = iota((1, 128), 1)
    rows = []
    for head in range(heads):
        sums = jnp.sum(far[head], axis=1, keepdims=True)
        rows.append(jnp.where(lane == 15, sums[0:1], jnp.where(lane == 31, sums[1:2], 0.0)))
    return total + jnp.concatenate(rows + [jnp.zeros((8 - heads, 128), f32)], axis=0)


def weight_grad_kernel(group, place, normed, *refs):
    pieces, (band, far_sum), refs = refs[:4], refs[4:6], refs[6:]
    if group == 1:
        bias, near, far, grad, sems = refs
    else:
        near, far, bias, grad, sems = refs
    core = place[2]
    size = 64 * GROUPS[group][1]
    copies = place_grads(place[3], group, pieces, grad, (0, size, 2 * size), sems)

    def store(made, low, high):
        made = made.astype(bf16).reshape(8, 2, 48, high - low)
        near[:, :, low:high] = jnp.where(core == 0, made[:, 0], made[:, 1])
        far[:, :, low:high] = jnp.where(core == 0, made[:, 1], made[:, 0])

    sums = bias_sums(band, far_sum)
    if group == 0:
        bias[...] = sums
    else:
        whole = jnp.concatenate([bias[0:4], sums[0:4]], axis=0)
        spot = iota((768, 128), 0) % 48
        bucket = (iota((768, 128), 0) // 48) * 2 + spot // 6
        chosen = jnp.where((iota((768, 128), 1) == bucket) & (spot < 12), 1.0, 0.0)
        per_head = lax.dot_general(
            chosen, whole, (((1,), (1,)), ((), ())),
            precision=lax.Precision.HIGHEST, preferred_element_type=f32,
        )
        pattern = (iota((768, 8), 1) == (iota((768, 8), 0) % 48) % 6).astype(f32)
        column = jnp.sum(per_head * pattern, axis=1, keepdims=True)
        store(jnp.where(iota((768, 128), 1) == 0, column, 0.0), 3 * size, 3 * size + 128)
    for copy in copies:
        copy.wait()
    store(dot(normed[...], grad[...], 0, 1), 0, 3 * size)


def weight_grad(place, normed, group, pieces, rest):
    columns = 192 * GROUPS[group][1]
    owned = jax.ShapeDtypeStruct((8, 48, columns + 128 * group), bf16)
    out_shape = (owned, owned) + ((jax.ShapeDtypeStruct((8, 128), f32),) if group == 0 else ())
    return pl.pallas_call(
        functools.partial(weight_grad_kernel, group),
        out_shape=out_shape,
        in_specs=[SCALARS, FULL] + [ANY] * 4 + [FULL] * len(rest),
        out_specs=(FULL,) * len(out_shape),
        scratch_shapes=[pltpu.VMEM((columns, 1024), bf16), pltpu.SemaphoreType.DMA((2, 4))],
        compiler_params=params(),
        cost_estimate=cost(2 * 1024 * 768 * columns, 6_000_000),
        name="weight_grad_" + str(group),
    )(place, normed, *pieces, *rest)


def project_back_kernel(place, *refs):
    w_near, w_far, refs = refs[:4], refs[4:8], refs[8:]
    pieces, refs = (refs[0:4], refs[4:8]), refs[8:]
    part_near, part_far, w, grad, sems, qsems = refs
    x = place[3]
    copies = place_blocks(place, w_near, w_far, w, sems)
    for group, (start, _) in enumerate(GROUPS):
        rows = [start * 64 + at for at in (0, 384, 768)]
        copies += place_grads(x, group, pieces[group], grad, rows, qsems)
    for copy in copies:
        copy.wait()
    for other, dest in ((1, part_far), (0, part_near)):
        start = pl.multiple_of(jnp.bitwise_xor(x, other) * 512, 512)
        dest[...] = dot(grad[:, pl.ds(start, 512)], w[:, 0:1152], 0, 1).astype(bf16)


def project_back(place, w_near, w_far, pieces):
    part = jax.ShapeDtypeStruct((512, 768), bf16)
    return pl.pallas_call(
        project_back_kernel,
        out_shape=(part, part),
        in_specs=[SCALARS] + [ANY] * 16,
        out_specs=(FULL,) * 2,
        scratch_shapes=[
            pltpu.VMEM((768, 1280), bf16),
            pltpu.VMEM((1152, 1024), bf16),
            pltpu.SemaphoreType.DMA((16,)),
            pltpu.SemaphoreType.DMA((2, 4)),
        ],
        compiler_params=params(),
        cost_estimate=cost(2 * 1024 * 768 * 1152, 10_000_000),
        name="project_back",
    )(place, *w_near, *w_far, *pieces[0], *pieces[1])


def finish_kernel(place, near, far, g0_near, g0_far, g1_near, g1_far, qw, kw, vw, gain, contract, q, k, v, gain_grad, bias):
    swapped = place[3] == 1

    def ordered(near, far):
        near, far = near[...].astype(f32), far[...].astype(f32)
        return jnp.where(swapped, far, near), jnp.where(swapped, near, far)

    for half, wide in enumerate(ordered(near, far)):
        for at in range(2):
            row = half * 96 + at * 48
            contract[row : row + 48] = wide[at]
    (a0, b0), (a1, b1) = ordered(g0_near, g0_far), ordered(g1_near, g1_far)
    for at, dest in enumerate((q, k, v)):
        for half, (wide, thin) in enumerate(((a0, a1), (b0, b1))):
            dest[:, half * 384 : half * 384 + 256] = wide[:, at * 256 : at * 256 + 256]
            dest[:, half * 384 + 256 : half * 384 + 384] = thin[:, at * 128 : at * 128 + 128]
    joint = q[...] * qw[...].astype(f32) + k[...] * kw[...].astype(f32) + v[...] * vw[...].astype(f32)
    summed = jnp.broadcast_to(jnp.sum(joint, axis=1, keepdims=True), (48, 128))
    blank = jnp.zeros((80, 128), f32)
    turned = jnp.concatenate([summed, blank], axis=0).T
    gain_grad[...] = turned[0:1, 0:48] / gain[...].astype(f32)
    first = jnp.concatenate([a1[:, 384:512], blank], axis=0).T
    second = jnp.concatenate([b1[:, 384:512], blank], axis=0).T
    for row in range(2):
        cols = slice(row * 6, row * 6 + 6)
        bias[row : row + 1, 0:6] = first[0:1, cols]
        bias[row : row + 1, 6:12] = second[0:1, cols]


def finish(place, near, far, g0_near, g0_far, g1_near, g1_far, qw, kw, vw, gain):
    full = jax.ShapeDtypeStruct((48, 768), f32)
    return pl.pallas_call(
        finish_kernel,
        out_shape=(
            jax.ShapeDtypeStruct((192, 768), f32),
            full, full, full, jax.ShapeDtypeStruct((1, 48), f32), jax.ShapeDtypeStruct((2, 12), f32),
        ),
        in_specs=[SCALARS] + [FULL] * 10,
        out_specs=(FULL,) * 6,
        compiler_params=params(),
        cost_estimate=cost(1000, 1_000_000),
        name="finish",
    )(place, near, far, g0_near, g0_far, g1_near, g1_far, qw, kw, vw, gain.reshape(1, 48))


def finish_wide_kernel(place, near, far, up, gain, expand, output, gain_grad):
    summed = near[...].astype(f32) + far[...].astype(f32)
    joint = jnp.zeros((48, 768), f32)
    for at in range(4):
        cols = slice(at * 768, at * 768 + 768)
        expand[:, cols] = summed[at]
        joint = joint + summed[at] * up[:, cols].astype(f32)
    output[...] = summed[4]
    column = jnp.broadcast_to(jnp.sum(joint, axis=1, keepdims=True), (48, 128))
    turned = jnp.concatenate([column, jnp.zeros((80, 128), f32)], axis=0).T
    gain_grad[...] = turned[0:1, 0:48] / gain[...].astype(f32)


def finish_wide(place, near, far, up, gain):
    return pl.pallas_call(
        finish_wide_kernel,
        out_shape=(
            jax.ShapeDtypeStruct((48, 3072), f32), jax.ShapeDtypeStruct((48, 768), f32), jax.ShapeDtypeStruct((1, 48), f32),
        ),
        in_specs=[SCALARS] + [FULL] * 4,
        out_specs=(FULL,) * 3,
        compiler_params=params(),
        cost_estimate=cost(1000, 2_000_000),
        name="finish_wide",
    )(place, near, far, up, gain.reshape(1, 48))


def input_grad_kernel(place, x, small, near, far, middle_grad, result):
    for row in range(0, 512, 256):
        rows = slice(row, row + 256)
        wide = x[rows].astype(f32)
        scale = lax.rsqrt(jnp.mean(wide * wide, axis=-1, keepdims=True) + EPS)
        unit = wide * scale
        direct = (near[rows].astype(f32) + far[rows].astype(f32)) * small[0:1]
        inward = scale * (direct - unit * jnp.mean(direct * unit, axis=-1, keepdims=True))
        result[rows] = (middle_grad[rows] + inward).astype(bf16)


def input_grad(place, x, small, near, far, middle_grad):
    return pl.pallas_call(
        input_grad_kernel,
        out_shape=jax.ShapeDtypeStruct((512, 768), bf16),
        in_specs=[SCALARS] + [FULL] * 5,
        out_specs=FULL,
        compiler_params=params(),
        cost_estimate=cost(512 * 768 * 20, 6_000_000),
        name="input_grad",
    )(place, x, small, near, far, middle_grad)


def swap(array, axis, bit):
    count = lax.axis_size(axis)
    return lax.ppermute(array, axis, [(i, i ^ bit) for i in range(count)])


def swap_both(array):
    pairs = [(i * 2 + j, (i ^ Y) * 2 + 1 - j) for i in range(lax.axis_size("fsdp")) for j in range(2)]
    return lax.ppermute(array, ("fsdp", "seq"), pairs)


CORE, Y, Z = 1, 2, 4


def after(value, *others):
    return lax.optimization_barrier((value, *others))[0]


class Line:
    def __init__(self, place):
        self.place = place

    def wait(self, *arrays):
        self.place = after(self.place, *arrays)

    def run(self, kernel, *args):
        made = kernel(self.place, *args)
        self.wait(jax.tree.leaves(made)[0])
        return made


def gather_part(part, own, now):
    array, dims, gone = part
    for axis in reversed(range(len(dims))):
        if dims[axis] == now:
            array = lax.dynamic_index_in_dim(array, 1 - own[now], axis, keepdims=False)
        elif dims[axis] in gone:
            array = lax.dynamic_index_in_dim(array, own[dims[axis]], axis, keepdims=False)
    return array.astype(f32)


def total(line, parts, own, now=None):
    arrays = after([array for array, _, _ in parts], line.place)
    made = None
    for array, (_, dims, gone) in zip(arrays, parts):
        term = gather_part((array, dims, gone), own, now)
        made = term if made is None else made + term
    made = lax.optimization_barrier(made.astype(bf16))
    line.wait(made)
    return made


def keep(parts, now, got):
    _, dims, gone = parts[0]
    left = tuple(dim for dim in dims if dim not in gone and dim != now)
    return [(a, d, g + (now,)) for a, d, g in parts] + [(got, left, ())]


def local_split(
    layer_input, query_weight, key_weight, value_weight, output_weight, expand_weight,
    contract_weight, attention_gain, feedforward_gain, bias_table, valid_len, instr_len, pair_flag,
    cotangent,
):
    owner, x = lax.axis_index("fsdp"), lax.axis_index("seq")
    z, y, c = owner // 4, (owner // 2) % 2, owner % 2
    place = jnp.stack([z, y, c, x, valid_len[0], instr_len[0], pair_flag[0]]).astype(jnp.int32)
    line = Line(place)
    tokens, cot = layer_input[0], cotangent[0]

    def by_z(array):
        return swap(array, "fsdp", Z)

    def by_zz(array):
        return swap(array, "fsdp", 2 * Z)

    def by_y(array):
        return swap(array, "fsdp", Y)

    def by_core(array):
        return swap(array, "fsdp", CORE)

    def by_x(array):
        return swap(array, "seq", 1)

    shard = line.run(
        narrow_shard, query_weight, key_weight, value_weight, attention_gain, feedforward_gain, bias_table
    )
    a2, a3, a1, b0 = by_zz(shard), swap(shard, "fsdp", 3 * Z), by_z(shard), by_y(shard)
    x_far = by_x(tokens)
    rest, own_side = line.run(wide_shard, expand_weight, output_weight, contract_weight)
    a1, a2, a3, rest = lax.optimization_barrier((a1, a2, a3, rest))
    along = jnp.stack([a1, a2, a3])
    across = by_y(along)
    z2, z1 = by_zz(rest), by_z(rest)
    w_near = [shard, b0, along, across]
    x_far, across, rest = lax.optimization_barrier((x_far, across, rest))
    y0 = by_y(rest)
    w_far = [by_core(block) for block in w_near]

    qkv, normed, small, table, tiles = line.run(project, tokens, x_far, w_near, w_far)
    line.place, z1, z2, y0 = lax.optimization_barrier((line.place, z1, z2, y0))
    z12 = jnp.stack([z1, z2])
    z3, y12 = by_z(z2), by_y(z12)
    sides = jnp.stack([z1[5:], z2[5:], y0[5:]])
    sides_a = by_x(sides)
    line.wait(sides, z12)
    out_theirs, kept_theirs, inverse_theirs = line.run(attend, table, tiles, qkv, False)
    line.place, z3, sides_a, out_theirs = lax.optimization_barrier((line.place, z3, sides_a, out_theirs))
    y3 = by_y(z3)
    out_got = by_x(out_theirs)
    sides_b = by_x(z3[5:])
    out_mine, kept_mine, inverse_mine = line.run(attend, table, tiles, qkv, True)
    out_mine, y12, out_got, sides_b, rest, own_side, y0, z12, z3, sides_a = lax.optimization_barrier(
        (out_mine, y12, out_got, sides_b, rest, own_side, y0, z12, z3, sides_a)
    )
    sides_c = by_x(y12[:, 5:])
    far = [by_core(block) for block in (rest, y0, z12, z3, y12)]
    far[3], far[4] = far[4], far[3]
    y3, sides_c = lax.optimization_barrier((y3, sides_c))
    sides_d = by_x(y3[5:])
    near, near_sides = [rest, y0, z12, y12, z3, y3], [own_side, sides_a, sides_b, sides_c, sides_d]
    far, far_sides = far + [by_core(y3)], [by_core(side) for side in near_sides]
    (
        hidden, pre, layer_output, normed_two, branch_low, middle_grad, att, grad_mine, grad_sent,
    ) = line.run(forward, out_mine, out_got, tokens, cot, small, near + far, near_sides + far_sides)
    grad_theirs = by_x(grad_sent)

    def parts(near, far_got, *left):
        dims = ("high", "low", "y") + left
        sizes = {"high": 2, "low": 2, "y": 2, "x": 2}
        rest = near.size // (8 * 48 * near.shape[-1] * (2 if "x" in left else 1))
        shape = tuple(sizes.get(dim, rest) for dim in dims) + (48, near.shape[-1])
        return [(near.reshape(shape), dims, ()), (far_got.reshape(shape), dims, ())]

    own = {"high": z // 2, "low": z % 2, "y": y, "x": x}
    b_near, b_far = line.run(expand_weight_grad, normed_two, pre, att, branch_low)
    b_parts = parts(b_near, by_core(b_far), "n")
    a_near, a_far = line.run(contract_weight_grad, hidden, cot)
    a_parts = parts(a_near, by_core(a_far), "x", "n")

    def back_mine(place, group):
        return attend_back(place, grad_mine, out_mine, inverse_mine, qkv, kept_mine, (), True, *GROUPS[group])

    def back_theirs(place, group, carry):
        return attend_back(
            place, grad_theirs, out_theirs, inverse_theirs, qkv, kept_theirs, carry[1:], False, *GROUPS[group]
        )

    mine0 = line.run(back_mine, 0)
    line.wait(grad_theirs)
    b_parts = keep(b_parts, "y", by_y(total(line, b_parts, own, "y")))
    a_parts = keep(a_parts, "x", by_x(total(line, a_parts, own, "x")))
    theirs0 = line.run(back_theirs, 0, mine0)
    pieces0 = (mine0[0], *theirs0[:3])
    g_near, g_far, bias0 = line.run(weight_grad, normed, 0, pieces0, theirs0[3:])
    g_parts = parts(g_near, by_core(g_far))
    mine1 = line.run(back_mine, 1)
    b_parts = keep(b_parts, "low", by_z(total(line, b_parts, own, "low")))
    a_parts = keep(a_parts, "y", by_y(total(line, a_parts, own, "y")))
    g_parts = keep(g_parts, "y", by_y(total(line, g_parts, own, "y")))
    theirs1 = line.run(back_theirs, 1, mine1)
    pieces1 = (mine1[0], *theirs1[:3])
    h_near, h_far = line.run(weight_grad, normed, 1, pieces1, (*theirs1[3:], bias0))
    h_parts = parts(h_near, by_core(h_far))
    b_parts = keep(b_parts, "high", by_zz(total(line, b_parts, own, "high")))
    part_near, part_far = line.run(project_back, w_near, w_far, (pieces0, pieces1))
    part_got = by_x(part_far)
    arrays = after([array.reshape(4, 2, 48, 512) for array, _, _ in h_parts], line.place)

    def for_owner(turn, dy):
        terms = []
        for array in arrays:
            along_z = lax.dynamic_index_in_dim(array, z ^ turn, 0, keepdims=False)
            terms.append(lax.dynamic_index_in_dim(along_z, y ^ dy, 0, keepdims=False).astype(f32))
        return terms[0] + terms[1]

    turns = [(turn, dy) for turn in range(4) for dy in range(2)][1:]
    sends = lax.optimization_barrier([for_owner(*turn).astype(bf16) for turn in turns])
    line.wait(*sends)
    h_got = [swap(sent, "fsdp", Z * turn + Y * dy) for (turn, dy), sent in zip(turns, sends)]
    a_parts = keep(a_parts, "low", by_z(total(line, a_parts, own, "low")))
    g_parts = keep(g_parts, "low", by_z(total(line, g_parts, own, "low")))
    b_low = total(line, b_parts, own)
    b_other = by_x(b_low)
    line.wait(*h_got)
    arrays, h_got = lax.optimization_barrier((arrays, h_got))
    made = for_owner(0, 0)
    for got in h_got:
        made = made + got.astype(f32)
    h_low = lax.optimization_barrier(made.astype(bf16))
    line.wait(h_low)
    h_other = by_x(h_low)
    a_parts = keep(a_parts, "high", by_zz(total(line, a_parts, own, "high")))
    g_parts = keep(g_parts, "high", by_zz(total(line, g_parts, own, "high")))
    result = line.run(input_grad, tokens, small, part_near, part_got, middle_grad)
    a_low, g_low = total(line, a_parts, own), total(line, g_parts, own)
    a_other, g_other = by_x(a_low), by_x(g_low)
    expand_sum, output_sum, gain_two = line.run(finish_wide, b_low, b_other, expand_weight, feedforward_gain)
    contract_sum, *grads, gain_one, bias_grad = line.run(
        finish, a_low, a_other, g_low, g_other, h_low, h_other, query_weight, key_weight, value_weight, attention_gain
    )
    return (
        layer_output[None], result[None], gain_one[0], gain_two[0], *grads,
        output_sum, expand_sum, contract_sum, bias_grad,
    )


def bucket_table(query_pos, key_pos):
    offset = key_pos[None, :] - query_pos[:, None]
    distance = jnp.abs(offset)
    beyond = jnp.zeros_like(distance)
    for far_edge in far_edges:
        beyond = beyond + (distance >= far_edge).astype(jnp.int32)
    nearby = jnp.where(distance < 8, distance, 8 + beyond)
    return nearby + 16 * (offset > 0).astype(jnp.int32)


def visible_keys(query_pos, key_pos, valid_len, instr_len, pair_flag):
    in_valid = key_pos[None, None, :] < valid_len[:, None, None]
    guarded = (
        (pair_flag[:, None, None] == 1)
        & (query_pos[None, :, None] < instr_len[:, None, None])
        & (key_pos[None, None, :] >= instr_len[:, None, None])
    )
    return in_valid & jnp.logical_not(guarded)


def rms_scale(values):
    return lax.rsqrt(jnp.mean(values * values, axis=-1, keepdims=True) + EPS)


def norm_back(values, scale, gain, grad_out):
    normed = values * scale
    grad_normed = grad_out * gain
    grad_values = scale * (
        grad_normed - normed * jnp.mean(grad_normed * normed, axis=-1, keepdims=True)
    )
    return (grad_values, jnp.sum(grad_out * normed, axis=(0, 1)))


def gelu_tanh(values):
    return jax.nn.gelu(values, approximate=True)


def local(
    layer_input,
    query_weight,
    key_weight,
    value_weight,
    output_weight,
    expand_weight,
    contract_weight,
    attention_gain,
    feedforward_gain,
    bias_table,
    valid_len,
    instr_len,
    pair_flag,
    cotangent,
):
    f32 = jnp.float32
    bf16 = jnp.bfloat16
    row_count, local_len, model_width = layer_input.shape
    head_count = bias_table.shape[1]
    head_size = model_width // head_count
    full_len = local_len * lax.axis_size("seq")
    local_start = lax.axis_index("seq") * local_len
    query_pos = local_start + jnp.arange(local_len, dtype=jnp.int32)
    key_pos = jnp.arange(full_len, dtype=jnp.int32)
    buckets = bucket_table(query_pos, key_pos)
    onehot = buckets[:, :, None] == jnp.arange(BUCKETS, dtype=jnp.int32)[None, None, :]
    visible = visible_keys(query_pos, key_pos, valid_len, instr_len, pair_flag)
    input_wide = layer_input.astype(f32)

    def attend_probs(queries, key_heads, table_full):
        rel_bias = jnp.einsum(
            "ijb,bh->hij", onehot.astype(bf16), table_full, preferred_element_type=f32
        )
        raw_scores = jnp.einsum("rihe,rjhe->rhij", queries, key_heads, preferred_element_type=f32)
        scores = jnp.where(visible[:, None], raw_scores + rel_bias[None], -1000000000.0)
        row_peak = jnp.max(scores, axis=-1, keepdims=True)
        log_total = row_peak + jnp.log(jnp.sum(jnp.exp(scores - row_peak), axis=-1, keepdims=True))
        return (jnp.exp(scores - log_total), log_total[..., 0])

    def forward(weights):
        (
            query_full,
            key_full,
            value_full,
            output_full,
            expand_full,
            contract_full,
            gain_one,
            gain_two,
            table_full,
        ) = weights
        scale_one = rms_scale(input_wide)
        normed_low = (input_wide * scale_one * gain_one.astype(f32)).astype(bf16)

        def project(weight):
            return jnp.einsum("rtd,de->rte", normed_low, weight, preferred_element_type=f32).astype(
                bf16
            )

        query_low = project(query_full)
        key_low = project(key_full)
        value_low = project(value_full)
        key_all, value_all = (
            lax.all_gather(key_low, "seq", axis=1, tiled=True),
            lax.all_gather(value_low, "seq", axis=1, tiled=True),
        )
        queries = query_low.reshape(row_count, local_len, head_count, head_size)
        key_heads = key_all.reshape(row_count, full_len, head_count, head_size)
        value_heads = value_all.reshape(row_count, full_len, head_count, head_size)
        probs, log_total = attend_probs(queries, key_heads, table_full)
        probs_low = probs.astype(bf16)
        attended = jnp.einsum("rhij,rjhe->rihe", probs_low, value_heads, preferred_element_type=f32)
        attended = attended.reshape(row_count, local_len, model_width).astype(bf16)
        middle = input_wide + jnp.einsum(
            "rtd,de->rte", attended, output_full, preferred_element_type=f32
        )
        scale_two = rms_scale(middle)
        normed_two = (middle * scale_two * gain_two.astype(f32)).astype(bf16)
        hidden_pre = jnp.einsum("rtd,df->rtf", normed_two, expand_full, preferred_element_type=f32)
        hidden_low = gelu_tanh(hidden_pre).astype(bf16)
        result = middle + jnp.einsum(
            "rtf,fd->rtd", hidden_low, contract_full, preferred_element_type=f32
        )
        return (
            result,
            scale_one,
            normed_low,
            queries,
            key_heads,
            value_heads,
            probs,
            probs_low,
            log_total,
            attended,
            middle,
            scale_two,
            normed_two,
            hidden_pre,
            hidden_low,
        )

    stored = forward(
        (
            lax.all_gather(query_weight, "fsdp", axis=0, tiled=True),
            lax.all_gather(key_weight, "fsdp", axis=0, tiled=True),
            lax.all_gather(value_weight, "fsdp", axis=0, tiled=True),
            lax.all_gather(output_weight, "fsdp", axis=0, tiled=True),
            lax.all_gather(expand_weight, "fsdp", axis=0, tiled=True),
            lax.all_gather(contract_weight, "fsdp", axis=0, tiled=True),
            lax.all_gather(attention_gain, "fsdp", axis=0, tiled=True),
            lax.all_gather(feedforward_gain, "fsdp", axis=0, tiled=True),
            lax.all_gather(bias_table, "fsdp", axis=0, tiled=True),
        )
    )
    layer_output = stored[0].astype(bf16)
    gathered = (
        lax.all_gather(query_weight, "fsdp", axis=0, tiled=True),
        lax.all_gather(key_weight, "fsdp", axis=0, tiled=True),
        lax.all_gather(value_weight, "fsdp", axis=0, tiled=True),
        lax.all_gather(output_weight, "fsdp", axis=0, tiled=True),
        lax.all_gather(expand_weight, "fsdp", axis=0, tiled=True),
        lax.all_gather(contract_weight, "fsdp", axis=0, tiled=True),
        lax.all_gather(attention_gain, "fsdp", axis=0, tiled=True),
        lax.all_gather(feedforward_gain, "fsdp", axis=0, tiled=True),
        lax.all_gather(bias_table, "fsdp", axis=0, tiled=True),
    )
    kept = forward(gathered)
    (
        unused,
        scale_one,
        normed_low,
        queries,
        key_heads,
        value_heads,
        probs,
        probs_low,
        log_total,
        attended,
        middle,
        scale_two,
        normed_two,
        hidden_pre,
        hidden_low,
    ) = kept
    (
        query_full,
        key_full,
        value_full,
        output_full,
        expand_full,
        contract_full,
        gain_one,
        gain_two,
        table_full,
    ) = gathered
    gain_one_wide = gain_one.astype(f32)
    gain_two_wide = gain_two.astype(f32)
    contract_grad = jnp.einsum("rtf,rtd->fd", hidden_low, cotangent, preferred_element_type=f32)
    grad_hidden = jnp.einsum("rtd,fd->rtf", cotangent, contract_full, preferred_element_type=f32)
    gelu_pull = jax.vjp(gelu_tanh, hidden_pre)[1]
    grad_pre = gelu_pull(grad_hidden)[0].astype(bf16)
    expand_grad = jnp.einsum("rtd,rtf->df", normed_two, grad_pre, preferred_element_type=f32)
    grad_normed_two = jnp.einsum("rtf,df->rtd", grad_pre, expand_full, preferred_element_type=f32)
    grad_middle_norm, gain_two_grad = norm_back(middle, scale_two, gain_two_wide, grad_normed_two)
    grad_middle = cotangent.astype(f32) + grad_middle_norm
    grad_branch = grad_middle.astype(bf16)
    output_grad = jnp.einsum("rtd,rte->de", attended, grad_branch, preferred_element_type=f32)
    grad_attended = jnp.einsum(
        "rte,de->rtd", grad_branch, output_full, preferred_element_type=f32
    ).astype(bf16)
    grad_attended = grad_attended.reshape(row_count, local_len, head_count, head_size)
    grad_probs = jnp.einsum(
        "rihe,rjhe->rhij", grad_attended, value_heads, preferred_element_type=f32
    )
    row_delta = jnp.sum(probs * grad_probs, axis=-1)
    grad_scores = probs * (grad_probs - row_delta[..., None])
    bias_part = jnp.einsum(
        "hij,ijb->bh",
        jnp.sum(grad_scores, axis=0),
        onehot.astype(f32),
        precision=lax.Precision.HIGHEST,
    )
    scores_low = grad_scores.astype(bf16)
    grad_queries = jnp.einsum("rhij,rjhe->rihe", scores_low, key_heads, preferred_element_type=f32)
    grad_queries = grad_queries.reshape(row_count, local_len, model_width).astype(bf16)
    value_partial = jnp.einsum(
        "rhij,rihe->rjhe", probs_low, grad_attended, preferred_element_type=f32
    ).reshape(row_count, full_len, model_width)
    key_partial = jnp.einsum(
        "rhij,rihe->rjhe", scores_low, queries, preferred_element_type=f32
    ).reshape(row_count, full_len, model_width)
    key_summed, value_summed = (
        lax.psum_scatter(
            key_partial.astype(jnp.bfloat16), "seq", scatter_dimension=1, tiled=True
        ).astype(jnp.float32),
        lax.psum_scatter(
            value_partial.astype(jnp.bfloat16), "seq", scatter_dimension=1, tiled=True
        ).astype(jnp.float32),
    )
    grad_keys = key_summed.astype(bf16)
    grad_values = value_summed.astype(bf16)
    query_part = jnp.einsum("rtd,rte->de", normed_low, grad_queries, preferred_element_type=f32)
    key_part = jnp.einsum("rtd,rte->de", normed_low, grad_keys, preferred_element_type=f32)
    value_part = jnp.einsum("rtd,rte->de", normed_low, grad_values, preferred_element_type=f32)
    grad_normed_one = jnp.einsum(
        "rte,de->rtd", grad_queries, query_full, preferred_element_type=f32
    )
    grad_normed_one = grad_normed_one + jnp.einsum(
        "rte,de->rtd", grad_keys, key_full, preferred_element_type=f32
    )
    grad_normed_one = grad_normed_one + jnp.einsum(
        "rte,de->rtd", grad_values, value_full, preferred_element_type=f32
    )
    grad_input_norm, gain_one_grad = norm_back(
        input_wide, scale_one, gain_one_wide, grad_normed_one
    )
    input_grad = (grad_middle + grad_input_norm).astype(bf16)
    owned = (
        lax.psum_scatter(
            query_part.astype(jnp.bfloat16), "fsdp", scatter_dimension=0, tiled=True
        ).astype(jnp.float32),
        lax.psum_scatter(
            key_part.astype(jnp.bfloat16), "fsdp", scatter_dimension=0, tiled=True
        ).astype(jnp.float32),
        lax.psum_scatter(
            value_part.astype(jnp.bfloat16), "fsdp", scatter_dimension=0, tiled=True
        ).astype(jnp.float32),
        lax.psum_scatter(
            output_grad.astype(jnp.bfloat16), "fsdp", scatter_dimension=0, tiled=True
        ).astype(jnp.float32),
        lax.psum_scatter(
            expand_grad.astype(jnp.bfloat16), "fsdp", scatter_dimension=0, tiled=True
        ).astype(jnp.float32),
        lax.psum_scatter(
            contract_grad.astype(jnp.bfloat16), "fsdp", scatter_dimension=0, tiled=True
        ).astype(jnp.float32),
        lax.psum_scatter(
            gain_one_grad.astype(jnp.bfloat16), "fsdp", scatter_dimension=0, tiled=True
        ).astype(jnp.float32),
        lax.psum_scatter(
            gain_two_grad.astype(jnp.bfloat16), "fsdp", scatter_dimension=0, tiled=True
        ).astype(jnp.float32),
        lax.psum_scatter(
            bias_part.astype(jnp.bfloat16), "fsdp", scatter_dimension=0, tiled=True
        ).astype(jnp.float32),
    )
    summed = (
        lax.psum(owned[0].astype(jnp.bfloat16), "seq").astype(jnp.float32),
        lax.psum(owned[1].astype(jnp.bfloat16), "seq").astype(jnp.float32),
        lax.psum(owned[2].astype(jnp.bfloat16), "seq").astype(jnp.float32),
        lax.psum(owned[3].astype(jnp.bfloat16), "seq").astype(jnp.float32),
        lax.psum(owned[4].astype(jnp.bfloat16), "seq").astype(jnp.float32),
        lax.psum(owned[5].astype(jnp.bfloat16), "seq").astype(jnp.float32),
        lax.psum(owned[6].astype(jnp.bfloat16), "seq").astype(jnp.float32),
        lax.psum(owned[7].astype(jnp.bfloat16), "seq").astype(jnp.float32),
        lax.psum(owned[8].astype(jnp.bfloat16), "seq").astype(jnp.float32),
    )
    (
        query_grad,
        key_grad,
        value_grad,
        output_sum,
        expand_sum,
        contract_sum,
        gain_one_sum,
        gain_two_sum,
        bias_grad,
    ) = summed
    return (
        layer_output,
        input_grad,
        gain_one_sum,
        gain_two_sum,
        query_grad,
        key_grad,
        value_grad,
        output_sum,
        expand_sum,
        contract_sum,
        bias_grad,
    )


def solution(mesh):
    in_specs = (
        P("fsdp", "seq", None),
        P("fsdp", None),
        P("fsdp", None),
        P("fsdp", None),
        P("fsdp", None),
        P("fsdp", None),
        P("fsdp", None),
        P("fsdp"),
        P("fsdp"),
        P("fsdp", None),
        P("fsdp"),
        P("fsdp"),
        P("fsdp"),
        P("fsdp", "seq", None),
    )
    out_specs = (
        P("fsdp", "seq", None),
        P("fsdp", "seq", None),
        P("fsdp"),
        P("fsdp"),
        P("fsdp", None),
        P("fsdp", None),
        P("fsdp", None),
        P("fsdp", None),
        P("fsdp", None),
        P("fsdp", None),
        P("fsdp", None),
    )
    split = mesh.shape["fsdp"] == 16 and mesh.shape["seq"] == 2
    step = local_split if split else local
    return jax.shard_map(step, mesh=mesh, in_specs=in_specs, out_specs=out_specs, check_vma=False)
```

```python
import functools
import itertools
import math

import jax
import jax.numpy as jnp
from jax import lax
from jax.experimental import pallas as pl
from jax.experimental.pallas import tpu as pltpu
from jax.sharding import PartitionSpec as P

f32 = jnp.float32
bf16 = jnp.bfloat16
BUCKETS = 32
EPS = 1e-06
far_edges = (12, 16, 23, 32, 46, 64, 91)
HIDDEN = -(2.0**30)
VMEM = 56 * 1024 * 1024
ANY = pl.BlockSpec(memory_space=pl.ANY)
FULL = pl.BlockSpec(memory_space=pltpu.VMEM)
SCALARS = pl.BlockSpec(memory_space=pltpu.SMEM)


def dot(left, right, left_dim, right_dim):
    return lax.dot_general(
        left, right, (((left_dim,), (right_dim,)), ((), ())), preferred_element_type=f32
    )


def params():
    return pltpu.CompilerParams(vmem_limit_bytes=VMEM)


def cost(flops, byte_count, exps=0):
    return pl.CostEstimate(flops=flops // 1000, bytes_accessed=byte_count // 1000, transcendentals=exps // 1000)


def small_cost():
    return pl.CostEstimate(flops=1000, bytes_accessed=1000, transcendentals=0)


def bucket_of(offset):
    distance = jnp.abs(offset)
    beyond = jnp.zeros_like(distance)
    for far_edge in far_edges:
        beyond = beyond + (distance >= far_edge).astype(jnp.int32)
    nearby = jnp.where(distance < 8, distance, 8 + beyond)
    return nearby + 16 * (offset > 0).astype(jnp.int32)


def iota(shape, dim):
    return lax.broadcasted_iota(jnp.int32, shape, dim)


def narrow_kernel(place, q, k, v, gain_one, gain_two, table, out, side):
    column = pl.multiple_of(place[3] * 384, 128)
    pieces = [weight[:, pl.ds(column, 384)] for weight in (q, k, v)]
    for pair in range(3):
        parts = [piece[:, at : at + 64] for at in (pair * 128, pair * 128 + 64) for piece in pieces]
        out[:, pair * 384 : pair * 384 + 384] = jnp.concatenate(parts, axis=1)
    side[...] = jnp.zeros((8, 128), f32)
    side[0:1, 0:48] = gain_one[...].astype(f32)
    side[1:2, 0:48] = gain_two[...].astype(f32)
    side[2:3, 0:12] = table[0:1].astype(f32)
    side[2:3, 12:24] = table[1:2].astype(f32)
    wide = jnp.concatenate([side[...], jnp.zeros((120, 128), f32)], axis=0).T
    out[:, 1152:1280] = wide[0:48].astype(bf16)


def narrow_shard(place, q, k, v, gain_one, gain_two, table):
    return pl.pallas_call(
        narrow_kernel,
        out_shape=jax.ShapeDtypeStruct((48, 1280), bf16),
        in_specs=[SCALARS] + [FULL] * 6,
        out_specs=FULL,
        scratch_shapes=[pltpu.VMEM((8, 128), f32)],
        compiler_params=params(),
        cost_estimate=small_cost(),
        name="narrow_shard",
    )(place, q, k, v, gain_one.reshape(1, 48), gain_two.reshape(1, 48), table)


def wide_kernel(place, expand, output, contract, out, full, sems):
    x = place[3]
    pieces = [(expand.at[:, at * 768 : at * 768 + 768], out.at[at]) for at in range(4)]
    pieces.append((output, out.at[4]))
    for at in range(2):
        row = pl.multiple_of(x * 96 + at * 48, 16)
        pieces.append((contract.at[pl.ds(row, 48)], out.at[5 + at]))
        row = pl.multiple_of((1 - x) * 96 + at * 48, 16)
        pieces.append((contract.at[pl.ds(row, 48)], full.at[7 + at]))
    copies = [pltpu.make_async_copy(*piece, sems.at[at]) for at, piece in enumerate(pieces)]
    for copy in copies:
        copy.start()
    for copy in copies:
        copy.wait()
    full[0:7] = out[...]


def wide_shard(place, expand, output, contract):
    return pl.pallas_call(
        wide_kernel,
        out_shape=(
            jax.ShapeDtypeStruct((7, 48, 768), bf16), jax.ShapeDtypeStruct((9, 48, 768), bf16),
        ),
        in_specs=[SCALARS, ANY, ANY, ANY],
        out_specs=(FULL, FULL),
        scratch_shapes=[pltpu.SemaphoreType.DMA((9,))],
        compiler_params=params(),
        cost_estimate=small_cost(),
        name="wide_shard",
    )(place, expand, output, contract)


def narrow_blocks(refs):
    shard, b0, a1, a2, turned, b2, b3, four, three, last = refs
    near = [shard, b0, a1, turned.at[1], a2, b2, turned.at[0], b3]
    far = [four.at[0], four.at[1], four.at[2], three.at[1], four.at[3], three.at[2], three.at[0], last]
    return near, far


def place_blocks(place, near, far, dest, sems):
    z, y, c = place[0], place[1], place[2]
    copies = []
    for turn in range(4):
        for dy in range(2):
            owner = ((jnp.bitwise_xor(z, turn) * 2) + jnp.bitwise_xor(y, dy)) * 2
            for other, source in enumerate((near, far)):
                row = pl.multiple_of((owner + jnp.bitwise_xor(c, other)) * 48, 16)
                copy = pltpu.make_async_copy(
                    source[turn * 2 + dy], dest.at[pl.ds(row, 48)], sems.at[len(copies)]
                )
                copy.start()
                copies.append(copy)
    return copies


def place_tokens(x, near, far, dest, sems, count):
    copies = []
    for other, source in enumerate((near, far)):
        row = pl.multiple_of(jnp.bitwise_xor(x, other) * count, count)
        copy = pltpu.make_async_copy(source, dest.at[pl.ds(row, count)], sems.at[other])
        copy.start()
        copies.append(copy)
    return copies


def first_query(place, mine):
    return (place[3] if mine else 1 - place[3]) * 512


def project_kernel(place, x_near, x_far, *refs):
    (w_near, w_far), refs = narrow_blocks(refs[:10]), refs[10:]
    qkv, kept, sent, small, table, tiles, normed, xs, w, sems, xsems = refs
    tokens = place_tokens(place[3], x_near, x_far, xs, xsems, 512)
    blocks = place_blocks(place, w_near, w_far, w, sems)
    for copy in tokens + blocks:
        copy.wait()
    side = w[:, 1152:1280].astype(f32).T
    small[...] = side[:8]
    gain = side[0:1]
    row = iota((768, 128), 0)
    spot = row % 48
    bucket = (row // 48) * 2 + spot // 12
    match = (iota((768, 128), 1) == bucket) & (spot < 24)
    values = jnp.where(match, w[:, 1154:1155].astype(f32), 0.0).astype(bf16)
    head = iota((8, 768), 0)
    chosen = ((iota((8, 768), 1) % 48) % 12 == place[3] * 6 + head) & (head < 6)
    made = dot(chosen.astype(bf16), values, 1, 0)
    table[...] = made
    lane = iota((128, 512), 1)
    spread = (bucket_of(jnp.where(lane < 128, -128 - lane, 384 - lane)) == iota((128, 512), 0)).astype(bf16)
    turned = dot(made.astype(bf16), spread, 1, 0)
    for head in range(6):
        for block, (low, high) in enumerate(((384, 0), (256, 384), (128, 256))):
            parts = [turned[head : head + 1, at : at + 128] for at in (low, high)]
            wide = jnp.broadcast_to(jnp.concatenate(parts, axis=1), (128, 256))
            rolled = pltpu.roll(wide, 0, 1, stride=1, stride_axis=0)
            tiles[head, block * 128 : block * 128 + 128] = rolled[:, 128:256]
    for row in range(0, 1024, 256):
        wide = xs[row : row + 256].astype(f32)
        scale = lax.rsqrt(jnp.mean(wide * wide, axis=-1, keepdims=True) + EPS)
        normed[row : row + 256] = (wide * scale * gain).astype(bf16)
    for col in range(0, 1152, 384):
        made = dot(w[:, col : col + 384], normed[...], 0, 1)
        qkv[col : col + 384] = made.astype(bf16)
    turned = normed[...].T.reshape(8, 2, 48, 1024)
    kept[...] = jnp.where(place[2] == 0, turned[:, 0], turned[:, 1])
    sent[...] = jnp.where(place[2] == 0, turned[:, 1], turned[:, 0])


def project(place, x_near, x_far, blocks):
    return pl.pallas_call(
        project_kernel,
        out_shape=(
            jax.ShapeDtypeStruct((1152, 1024), bf16),
            jax.ShapeDtypeStruct((8, 48, 1024), bf16),
            jax.ShapeDtypeStruct((8, 48, 1024), bf16),
            jax.ShapeDtypeStruct((8, 768), f32),
            jax.ShapeDtypeStruct((8, 128), f32),
            jax.ShapeDtypeStruct((6, 384, 128), f32),
        ),
        in_specs=[SCALARS] + [ANY] * 12,
        out_specs=(FULL,) * 6,
        scratch_shapes=[
            pltpu.VMEM((1024, 768), bf16),
            pltpu.VMEM((1024, 768), bf16),
            pltpu.VMEM((768, 1280), bf16),
            pltpu.SemaphoreType.DMA((16,)),
            pltpu.SemaphoreType.DMA((2,)),
        ],
        compiler_params=params(),
        cost_estimate=small_cost(),
        name="project",
    )(place, x_near, x_far, *blocks)


def attend_kernel(mine, place, table, tile, q, k, v, out, kept, inverse, ka, kt, qt, vt, s):
    head = pl.program_id(0)
    first, valid, instr, pair = first_query(place, mine), place[4], place[5], place[6]

    @pl.when(head == 0)
    def _():
        kt[64:128] = jnp.zeros((64, 1024), bf16)
        qt[64:128] = jnp.zeros((64, 512), bf16)
        row = iota((16, 1024), 0)
        key = iota((16, 1024), 1)
        extra = jnp.where(row < 8, (key // 128 == row).astype(f32), 0.0)
        extra = jnp.where(row == 8, jnp.where(key >= valid, HIDDEN, 0.0), extra)
        extra = jnp.where(row == 9, (key >= instr).astype(f32), extra)
        kt[64:80] = extra.astype(bf16)
        vt[64:80] = jnp.where(row == 0, 1.0, 0.0).astype(bf16)

    row = iota((16, 512), 0)
    query = iota((16, 512), 1) + first
    block = query // 128
    extra = jnp.where(row <= block - 2, table[head, 15], 0.0)
    extra = jnp.where(row >= block + 2, table[head, 31], extra)
    extra = jnp.where(row == 8, 1.0, extra)
    guarded = (query < instr) & (pair == 1)
    extra = jnp.where(row == 9, jnp.where(guarded, HIDDEN, 0.0), extra)
    extra = jnp.where(row > 9, 0.0, extra)
    qt[64:80] = extra.astype(bf16)
    qt[0:64] = q[...]
    kt[0:64] = k[...]
    vt[0:64] = v[...]
    ka[...] = kt[...].T
    s[128:1152] = dot(ka[...], qt[...], 1, 0)
    for part in range(4):
        base = pl.multiple_of(first + part * 128, 128)
        cols = slice(part * 128, part * 128 + 128)
        s[pl.ds(base, 384), cols] = s[pl.ds(base, 384), cols] + tile[0]
    scores = s[128:1152]
    peak = jnp.max(scores, axis=0, keepdims=True)
    weights = jnp.exp(scores - peak).astype(bf16)
    kept[0] = weights
    summed = dot(vt[...], weights, 1, 0)
    share = 1.0 / summed[64:65]
    out[...] = (summed[0:64] * share).astype(bf16)
    inverse[0] = share


def attend(place, table, tiles, qkv, mine):
    half = (lambda s: s[3]) if mine else (lambda s: 1 - s[3])
    grid = pltpu.PrefetchScalarGridSpec(
        num_scalar_prefetch=1,
        grid=(6,),
        in_specs=[
            SCALARS,
            pl.BlockSpec((1, 384, 128), lambda h, s: (h, 0, 0)),
            pl.BlockSpec((64, 512), lambda h, s: (3 * h, half(s))),
            pl.BlockSpec((64, 1024), lambda h, s: (3 * h + 1, 0)),
            pl.BlockSpec((64, 1024), lambda h, s: (3 * h + 2, 0)),
        ],
        out_specs=(
            pl.BlockSpec((64, 512), lambda h, s: (h, 0)),
            pl.BlockSpec((1, 1024, 512), lambda h, s: (h, 0, 0)),
            pl.BlockSpec((1, 1, 512), lambda h, s: (h, 0, 0)),
        ),
        scratch_shapes=[
            pltpu.VMEM((1024, 128), bf16),
            pltpu.VMEM((128, 1024), bf16),
            pltpu.VMEM((128, 512), bf16),
            pltpu.VMEM((80, 1024), bf16),
            pltpu.VMEM((1280, 512), f32),
        ],
    )
    return pl.pallas_call(
        functools.partial(attend_kernel, mine),
        out_shape=(
            jax.ShapeDtypeStruct((384, 512), bf16),
            jax.ShapeDtypeStruct((6, 1024, 512), bf16),
            jax.ShapeDtypeStruct((6, 1, 512), f32),
        ),
        grid_spec=grid,
        compiler_params=params(),
        cost_estimate=small_cost(),
        name="attend_mine" if mine else "attend_theirs",
    )(place, table, tiles, qkv, qkv, qkv)


def diagonal_sums(band):
    flip = (iota((128, 128), 0) + iota((128, 128), 1) == 127).astype(f32)
    rows = []
    for block in range(3):
        here = lax.dot_general(
            flip, band[block * 128 : block * 128 + 128], (((1,), (0,)), ((), ())),
            precision=lax.Precision.HIGHEST, preferred_element_type=f32,
        )
        wide = jnp.concatenate([here, jnp.zeros((128, 128), f32)], axis=1)
        rolled = pltpu.roll(wide, 0, 1, stride=1, stride_axis=0)
        rows.append(jnp.sum(rolled, axis=0, keepdims=True))
    return rows


def bucket_sums(diagonals, sides):
    total = sides
    for block in range(3):
        offset = block * 128 - 1 - iota((256, 128), 0)
        spread = (bucket_of(offset) == iota((256, 128), 1)).astype(f32)
        total = total + lax.dot_general(
            diagonals[block], spread, (((1,), (0,)), ((), ())),
            precision=lax.Precision.HIGHEST, preferred_element_type=f32,
        )
    return total


def attend_back_kernel(carried, mine, place, grad, out, inverse, q, k, v, kept, *refs):
    if carried:
        dq_in, dk_in, dv_in, band_in, far_in, whole, diagonals, sides, *refs = refs
    else:
        dq, dk, dv, band, far, *refs = refs
    va, vt, kt, gt, ds = refs
    first = first_query(place, mine)

    @pl.when(pl.program_id(0) == 0)
    def _():
        row = iota((16, 1024), 0)
        key = iota((16, 1024), 1)
        vt[64:128] = jnp.zeros((64, 1024), bf16)
        vt[64:80] = jnp.where(row < 2, 1.0, 0.0).astype(bf16)
        if carried:
            diagonals[...] = jnp.zeros_like(diagonals)
            sides[...] = jnp.zeros_like(sides)
        kt[64:80] = jnp.where(row < 8, (key // 128 == row).astype(f32), 0.0).astype(bf16)
        gt[64:128] = jnp.zeros((64, 512), bf16)
        ds[0:128] = jnp.zeros((128, 512), bf16)
        ds[1152:1280] = jnp.zeros((128, 512), bf16)

    share = inverse[0]
    scaled = grad[...].astype(f32) * share
    delta = jnp.sum(scaled * out[...].astype(f32), axis=0, keepdims=True)
    high = delta.astype(bf16).astype(f32)
    row = iota((16, 512), 0)
    extra = jnp.where(row == 0, -high, jnp.where(row == 1, high - delta, 0.0))
    gt[64:80] = extra.astype(bf16)
    gt[0:64] = scaled.astype(bf16)
    vt[0:64] = v[...]
    kt[0:64] = k[...]
    va[...] = vt[...].T
    for row_at in range(0, 1024, 256):
        rows = slice(row_at, row_at + 256)
        pull = dot(va[rows], gt[...], 1, 0)
        ds[128 + row_at : 384 + row_at] = (kept[0, rows] * pull).astype(bf16)
    made = dot(kt[...], ds[128:1152], 1, 0)
    block = (iota((8, 512), 1) + first) // 128
    key_block = iota((8, 512), 0)
    totals = made[64:72]
    left = jnp.sum(jnp.where(key_block <= block - 2, totals, 0.0), axis=0, keepdims=True)
    right = jnp.sum(jnp.where(key_block >= block + 2, totals, 0.0), axis=0, keepdims=True)
    dv_made = dot(gt[0:64], kept[0], 1, 1)
    dk_made = dot(q[...], ds[128:1152], 1, 1)
    near = None
    for part in range(4):
        base = pl.multiple_of(first + part * 128, 128)
        window = ds[pl.ds(base, 384), part * 128 : part * 128 + 128].astype(f32)
        near = window if near is None else near + window
    if carried:
        whole[0, 0:64, pl.ds(pl.multiple_of(first, 512), 512)] = made[0:64].astype(bf16)
        whole[0, 0:64, pl.ds(pl.multiple_of(512 - first, 512), 512)] = dq_in[...]
        whole[0, 64:128] = (dk_made + dk_in[...]).astype(bf16)
        whole[0, 128:192] = (dv_made + dv_in[...]).astype(bf16)
        head = pl.program_id(0)
        for at, row in enumerate(diagonal_sums(near + band_in[0])):
            diagonals[at, pl.ds(head, 1)] = row
        lane = iota((1, 128), 1)
        left, right = (
            jnp.sum(side, axis=1, keepdims=True) for side in (left + far_in[0, 0:1], right + far_in[0, 1:2])
        )
        sides[pl.ds(head, 1)] = jnp.where(lane == 15, left, jnp.where(lane == 31, right, 0.0))
        whole[0, 192:208] = jnp.zeros((16, 1024), bf16)

        @pl.when(head == 5)
        def _():
            bias = bucket_sums([diagonals[at] for at in range(3)], sides[...])
            whole[0, 192:208, 0:128] = jnp.concatenate([bias, jnp.zeros((8, 128), f32)], axis=0).astype(bf16)

    else:
        dq[...] = made[0:64].astype(bf16)
        dk[...] = dk_made
        dv[...] = dv_made
        band[0] = near
        far[0] = jnp.concatenate([left, right, jnp.zeros((6, 512), f32)], axis=0)


def attend_back(place, grad, out, inverse, qkv, kept, carry, mine):
    count = 6
    half = (lambda s: s[3]) if mine else (lambda s: 1 - s[3])
    rows512 = pl.BlockSpec((64, 512), lambda h, s: (h, 0))
    rows1024 = pl.BlockSpec((64, 1024), lambda h, s: (h, 0))
    band_spec = pl.BlockSpec((1, 384, 128), lambda h, s: (h, 0, 0))
    far_spec = pl.BlockSpec((1, 8, 512), lambda h, s: (h, 0, 0))
    carry_specs = (rows512, rows1024, rows1024, band_spec, far_spec)
    in_specs = [
        rows512,
        rows512,
        pl.BlockSpec((1, 1, 512), lambda h, s: (h, 0, 0)),
        pl.BlockSpec((64, 512), lambda h, s: (3 * h, half(s))),
        pl.BlockSpec((64, 1024), lambda h, s: (3 * h + 1, 0)),
        pl.BlockSpec((64, 1024), lambda h, s: (3 * h + 2, 0)),
        pl.BlockSpec((1, 1024, 512), lambda h, s: (h, 0, 0)),
    ]
    if carry:
        out_shape = jax.ShapeDtypeStruct((count, 208, 1024), bf16)
        out_specs = pl.BlockSpec((1, 208, 1024), lambda h, s: (h, 0, 0))
        in_specs += carry_specs
    else:
        out_shape = (
            jax.ShapeDtypeStruct((64 * count, 512), bf16),
            jax.ShapeDtypeStruct((64 * count, 1024), f32),
            jax.ShapeDtypeStruct((64 * count, 1024), f32),
            jax.ShapeDtypeStruct((count, 384, 128), f32),
            jax.ShapeDtypeStruct((count, 8, 512), f32),
        )
        out_specs = carry_specs
    grid = pltpu.PrefetchScalarGridSpec(
        num_scalar_prefetch=1,
        grid=(count,),
        in_specs=in_specs,
        out_specs=out_specs,
        scratch_shapes=([pltpu.VMEM((3, 8, 256), f32), pltpu.VMEM((8, 128), f32)] if carry else [])
        + [
            pltpu.VMEM((1024, 128), bf16),
            pltpu.VMEM((128, 1024), bf16),
            pltpu.VMEM((80, 1024), bf16),
            pltpu.VMEM((128, 512), bf16),
            pltpu.VMEM((1280, 512), bf16),
        ],
    )
    return pl.pallas_call(
        functools.partial(attend_back_kernel, bool(carry), mine),
        out_shape=out_shape,
        grid_spec=grid,
        compiler_params=params(),
        cost_estimate=cost(count * 1024 * 512 * 1024, 6_000_000),
        name="attend_back_mine" if mine else "attend_back_theirs",
    )(place, grad, out, inverse, qkv, qkv, qkv, kept, *carry)


def gelu_both(wide):
    square = wide * wide
    inner = 0.7978845608 * wide * (1.0 + 0.044715 * square)
    bend = jnp.tanh(inner)
    half = 0.5 * (1.0 + bend)
    slope = 0.7978845608 * (1.0 + 3 * 0.044715 * square)
    return (wide * half, half + 0.5 * wide * (1.0 - bend * bend) * slope)


def all_blocks(full, three, two, y1, y3, side_a, side_b, side_c):
    blocks = [full, three[0], three[1], y1, three[2], two[1], two[0], y3]
    sides = [
        full.at[7:9], side_a.at[2], side_a.at[0], y1.at[7:9], side_a.at[1], side_b.at[1], side_b.at[0], side_c,
    ]
    return blocks, sides


def forward_kernel(
    place, att_near, att_far, x, cot, small, *refs
):
    full, y0, z1, z2, z3, y2, y1, y3, side_a, side_b, side_c = refs[:11]
    nears, near_sides = all_blocks(full, (y0, z1, z2), (z3, y2), y1, y3, side_a, side_b, side_c)
    full, three, two, y1, y3, side_a, side_b, side_c = refs[11:19]
    three, two = [three.at[at] for at in range(3)], [two.at[at] for at in range(2)]
    fars, far_sides = all_blocks(full, three, two, y1, y3, side_a, side_b, side_c)
    refs = refs[19:]
    (
        hid_keep_hbm, hid_send_hbm, pre_hbm, turned_keep, turned_send, result, middle_grad, near_grad, far_grad,
        w_out, w_up, w_down, hid_keep, hid_send, pre, normed_grad, pulled, middle, total, normed, att,
        sems, att_sems, out_sems,
    ) = refs
    z, y, c, xs = place[0], place[1], place[2], place[3]
    att_copies = []
    for other, source in enumerate((att_near, att_far)):
        row = pl.multiple_of(jnp.bitwise_xor(xs, other) * 384, 128)
        copy = pltpu.make_async_copy(source, att.at[pl.ds(row, 384)], att_sems.at[other])
        copy.start()
        att_copies.append(copy)
    groups = ([], [], [])
    for turn in range(4):
        for dy in range(2):
            owner = ((jnp.bitwise_xor(z, turn) * 2) + jnp.bitwise_xor(y, dy)) * 2
            for other in range(2):
                main = (nears, fars)[other][turn * 2 + dy]
                side = (near_sides, far_sides)[other][turn * 2 + dy]
                who = owner + jnp.bitwise_xor(c, other)
                row = pl.multiple_of(who * 48, 16)
                pieces = (
                    (0, main.at[4], w_out.at[pl.ds(row, 48)]),
                    (1, main.at[0:4], w_up.at[:, pl.ds(row, 48)]),
                    (2, main.at[5:7], w_down.at[pl.ds(who * 4 + xs * 2, 2)]),
                    (2, side, w_down.at[pl.ds(who * 4 + (1 - xs) * 2, 2)]),
                )
                for at, (group, source, dest) in enumerate(pieces):
                    sem = sems.at[at, turn * 4 + dy * 2 + other]
                    groups[group].append(pltpu.make_async_copy(source, dest, sem))
    for group in groups:
        for copy in group:
            copy.start()
    for copy in att_copies + groups[0]:
        copy.wait()
    gain = small[1:2]
    wide = x[...].astype(f32) + dot(att[...], w_out[...], 0, 0)
    middle[...] = wide
    scale = lax.rsqrt(jnp.mean(wide * wide, axis=-1, keepdims=True) + EPS)
    normed[...] = (wide * scale * gain).astype(bf16)
    for group in groups[1:]:
        for copy in group:
            copy.wait()
    total[...] = wide
    normed_grad[...] = jnp.zeros_like(normed_grad)

    def chunk(j, carry):
        down = w_down[pl.ds(j * 16, 16)].reshape(768, 768)
        pulled[...] = dot(cot[...], down, 1, 1)
        value, slope = gelu_both(dot(normed[...], w_up[j], 1, 0))
        value = value.astype(bf16)
        total[...] += dot(value, down, 1, 0)
        even = jnp.concatenate([value[:, 0:192], value[:, 384:576]], axis=1)
        odd = jnp.concatenate([value[:, 192:384], value[:, 576:768]], axis=1)
        hid_keep[j] = jnp.where(c == 0, even, odd)
        hid_send[j] = jnp.where(c == 0, odd, even)
        low = (pulled[...] * slope).astype(bf16)
        pre[j] = low
        normed_grad[...] += dot(low, w_up[j], 1, 1)
        return carry

    lax.fori_loop(0, 4, chunk, 0)
    outs = [
        pltpu.make_async_copy(hid_send, hid_send_hbm, out_sems.at[0]),
        pltpu.make_async_copy(hid_keep, hid_keep_hbm, out_sems.at[1]),
        pltpu.make_async_copy(pre.at[0:4], pre_hbm.at[0:4], out_sems.at[2]),
    ]
    for copy in outs:
        copy.start()
    for at, whole in enumerate((normed[...].T, att[...])):
        rows = whole.reshape(8, 2, 48, 512)
        turned_keep[at] = jnp.where(c == 0, rows[:, 0], rows[:, 1])
        turned_send[at] = jnp.where(c == 0, rows[:, 1], rows[:, 0])
    wide = middle[...]
    scale = lax.rsqrt(jnp.mean(wide * wide, axis=-1, keepdims=True) + EPS)
    unit = wide * scale
    incoming = normed_grad[...]
    direct = incoming * gain
    inward = scale * (direct - unit * jnp.mean(direct * unit, axis=-1, keepdims=True))
    grad = cot[...].astype(f32) + inward
    middle_grad[...] = grad
    low = grad.astype(bf16)
    pre[4] = low
    outs.append(pltpu.make_async_copy(pre.at[4], pre_hbm.at[4], out_sems.at[3]))
    outs[3].start()
    for other, dest in enumerate((near_grad, far_grad)):
        row = pl.multiple_of(jnp.bitwise_xor(xs, other) * 384, 128)
        dest[...] = dot(w_out[pl.ds(row, 384)], low, 1, 1).astype(bf16)
    result[...] = total[...].astype(bf16)
    for copy in outs:
        copy.wait()


def forward(place, att_near, att_far, x, cot, small, near, far):
    wide = jax.ShapeDtypeStruct((512, 768), f32)
    half = jax.ShapeDtypeStruct((384, 512), bf16)
    hidden = jax.ShapeDtypeStruct((4, 512, 384), bf16)
    turned = jax.ShapeDtypeStruct((2, 8, 48, 512), bf16)
    return pl.pallas_call(
        forward_kernel,
        out_shape=(
            hidden, hidden, jax.ShapeDtypeStruct((5, 512, 768), bf16), turned, turned,
            jax.ShapeDtypeStruct((512, 768), bf16), wide, half, half,
        ),
        in_specs=[SCALARS, ANY, ANY, FULL, FULL, FULL] + [ANY] * 19,
        out_specs=(ANY, ANY, ANY) + (FULL,) * 6,
        scratch_shapes=[
            pltpu.VMEM((768, 768), bf16),
            pltpu.VMEM((4, 768, 768), bf16),
            pltpu.VMEM((64, 48, 768), bf16),
            pltpu.VMEM((4, 512, 384), bf16),
            pltpu.VMEM((4, 512, 384), bf16),
            pltpu.VMEM((5, 512, 768), bf16),
            pltpu.VMEM((512, 768), f32),
            pltpu.VMEM((512, 768), f32),
            pltpu.VMEM((512, 768), f32),
            pltpu.VMEM((512, 768), f32),
            pltpu.VMEM((512, 768), bf16),
            pltpu.VMEM((768, 512), bf16),
            pltpu.SemaphoreType.DMA((4, 16)),
            pltpu.SemaphoreType.DMA((2,)),
            pltpu.SemaphoreType.DMA((4,)),
        ],
        compiler_params=params(),
        cost_estimate=cost(8_500_000_000, 20_000_000, 512 * 3072),
        name="forward",
    )(place, att_near, att_far, x, cot, small, *near, *far)


def contract_grad_kernel(place, hid, hid_far, cot, cot_far, send, keep):
    made = dot(hid[0], cot[...], 0, 0) + dot(hid_far[0], cot_far[...], 0, 0)
    made = made.astype(bf16).reshape(2, 2, 2, 48, 768)
    send[...] = jnp.where(place[3] == 0, made[:, 1], made[:, 0])
    keep[...] = jnp.where(place[3] == 0, made[:, 0], made[:, 1])


def contract_weight_grad(place, hid, hid_far, cot, cot_far):
    shape = jax.ShapeDtypeStruct((8, 2, 48, 768), bf16)
    spec = pl.BlockSpec((2, 2, 48, 768), lambda j: (j, 0, 0, 0))
    chunk = pl.BlockSpec((1, 512, 384), lambda j: (j, 0, 0))
    whole = pl.BlockSpec((512, 768), lambda j: (0, 0))
    return pl.pallas_call(
        contract_grad_kernel,
        out_shape=(shape, shape),
        grid=(4,),
        in_specs=[SCALARS, chunk, chunk, whole, whole],
        out_specs=(spec, spec),
        compiler_params=params(),
        cost_estimate=cost(2 * 512 * 3072 * 768, 9_000_000),
        name="contract_weight_grad",
    )(place, hid, hid_far, cot, cot_far)


def expand_grad_kernel(place, turned, turned_far, pre, pre_far, b_send, b_keep, c_send, c_keep):
    step = pl.program_id(0)

    def made(at):
        near = dot(turned[at].reshape(384, 512), pre[0], 1, 0)
        return (near + dot(turned_far[at].reshape(384, 512), pre_far[0], 1, 0)).astype(bf16)

    @pl.when(step < 3)
    def _():
        rows = made(0).reshape(4, 2, 48, 768)
        b_send[:, 0] = jnp.where(place[1] == 0, rows[:, 1], rows[:, 0])
        b_keep[:, 0] = jnp.where(place[1] == 0, rows[:, 0], rows[:, 1])

    def by_low(rows):
        rows = rows.reshape(2, 2, 2, 48, 768)
        low = place[0] % 2
        c_send[:, :, 0] = jnp.where(low == 0, rows[:, 1], rows[:, 0])
        c_keep[:, :, 0] = jnp.where(low == 0, rows[:, 0], rows[:, 1])

    @pl.when(step == 3)
    def _():
        by_low(made(0))

    @pl.when(step == 4)
    def _():
        by_low(made(1))


def expand_weight_grad(place, turned, turned_far, pre, pre_far):
    first = jax.ShapeDtypeStruct((4, 3, 48, 768), bf16)
    second = jax.ShapeDtypeStruct((2, 2, 2, 48, 768), bf16)
    first_spec = pl.BlockSpec((4, 1, 48, 768), lambda j: (0, jnp.minimum(j, 2), 0, 0))
    second_spec = pl.BlockSpec((2, 2, 1, 48, 768), lambda j: (0, 0, jnp.maximum(j - 3, 0), 0, 0))
    whole = pl.BlockSpec((2, 8, 48, 512), lambda j: (0, 0, 0, 0))
    chunk = pl.BlockSpec((1, 512, 768), lambda j: (j, 0, 0))
    return pl.pallas_call(
        expand_grad_kernel,
        out_shape=(first, first, second, second),
        grid=(5,),
        in_specs=[SCALARS, whole, whole, chunk, chunk],
        out_specs=(first_spec, first_spec, second_spec, second_spec),
        compiler_params=params(),
        cost_estimate=cost(2 * 512 * 768 * 3840, 12_000_000),
        name="expand_weight_grad",
    )(place, turned, turned_far, pre, pre_far)


def place_grads(whole, grad, sems):
    copies = []
    for head in range(6):
        dest = grad.at[head * 192 : head * 192 + 192]
        copies.append(pltpu.make_async_copy(whole.at[head, 0:192], dest, sems.at[head]))
        copies[-1].start()
    return copies


def weight_grad_kernel(place, mine, other, whole, near, far, grad, bias, sems, bias_sem):
    copies = place_grads(whole, grad, sems)
    copies.append(pltpu.make_async_copy(whole.at[5, 192:208, 0:128], bias, bias_sem))
    copies[-1].start()
    for copy in copies:
        copy.wait()
    for kind, rows, dest in ((place[2], mine, near), (1 - place[2], other, far)):
        spot = iota((384, 128), 0) % 48
        bucket = ((iota((384, 128), 0) // 48) * 2 + kind) * 2 + spot // 6
        chosen = jnp.where((iota((384, 128), 1) == bucket) & (spot < 12), 1.0, 0.0)
        per_head = dot(chosen.astype(bf16), bias[0:8], 1, 1)
        pattern = (iota((384, 8), 1) == (iota((384, 8), 0) % 48) % 6).astype(f32)
        column = jnp.sum(per_head * pattern, axis=1, keepdims=True)
        side = jnp.where(iota((384, 128), 1) == 0, column, 0.0)
        dest[:, :, 1152:1280] = side.astype(bf16).reshape(8, 48, 128)
        left = rows[...].reshape(384, 1024)
        for col in range(0, 1152, 384):
            made = dot(left, grad[col : col + 384], 1, 1)
            dest[:, :, col : col + 384] = made.astype(bf16).reshape(8, 48, 384)


def weight_grad(place, mine, other, whole):
    owned = jax.ShapeDtypeStruct((8, 48, 1280), bf16)
    return pl.pallas_call(
        weight_grad_kernel,
        out_shape=(owned, owned),
        in_specs=[SCALARS, FULL, FULL, ANY],
        out_specs=(FULL,) * 2,
        scratch_shapes=[
            pltpu.VMEM((1152, 1024), bf16),
            pltpu.VMEM((16, 128), bf16),
            pltpu.SemaphoreType.DMA((6,)),
            pltpu.SemaphoreType.DMA,
        ],
        compiler_params=params(),
        cost_estimate=cost(2 * 1024 * 768 * 1152, 6_000_000),
        name="weight_grad",
    )(place, mine, other, whole)


def project_back_kernel(place, *refs):
    (w_near, w_far), whole, refs = narrow_blocks(refs[:10]), refs[10], refs[11:]
    part_near, part_far, w, grad, sems, qsems = refs
    x = place[3]
    copies = place_blocks(place, w_near, w_far, w, sems) + place_grads(whole, grad, qsems)
    for copy in copies:
        copy.wait()
    for other, dest in ((1, part_far), (0, part_near)):
        start = pl.multiple_of(jnp.bitwise_xor(x, other) * 512, 512)
        dest[...] = dot(grad[:, pl.ds(start, 512)], w[:, 0:1152], 0, 1).astype(bf16)


def project_back(place, blocks, whole):
    part = jax.ShapeDtypeStruct((512, 768), bf16)
    return pl.pallas_call(
        project_back_kernel,
        out_shape=(part, part),
        in_specs=[SCALARS] + [ANY] * 11,
        out_specs=(FULL,) * 2,
        scratch_shapes=[
            pltpu.VMEM((768, 1280), bf16),
            pltpu.VMEM((1152, 1024), bf16),
            pltpu.SemaphoreType.DMA((16,)),
            pltpu.SemaphoreType.DMA((6,)),
        ],
        compiler_params=params(),
        cost_estimate=cost(2 * 1024 * 768 * 1152, 10_000_000),
        name="project_back",
    )(place, *blocks, whole)


def finish_kernel(place, a_near, a_far, g_near, g_far, qw, kw, vw, gain, contract, q, k, v, gain_grad, bias):
    swapped = place[3] == 1

    def ordered(near, far):
        near, far = near[...].astype(f32), far[...].astype(f32)
        return jnp.where(swapped, far, near), jnp.where(swapped, near, far)

    for half, wide in enumerate(ordered(a_near, a_far)):
        for at in range(2):
            row = half * 96 + at * 48
            contract[row : row + 48] = wide[at]
    first, second = ordered(g_near, g_far)
    for at, dest in enumerate((q, k, v)):
        for half, wide in enumerate((first, second)):
            for head in range(6):
                column = head * 192 + at * 64
                spot = half * 384 + head * 64
                dest[:, spot : spot + 64] = wide[:, column : column + 64]
    joint = q[...] * qw[...].astype(f32) + k[...] * kw[...].astype(f32) + v[...] * vw[...].astype(f32)
    summed = jnp.broadcast_to(jnp.sum(joint, axis=1, keepdims=True), (48, 128))
    blank = jnp.zeros((80, 128), f32)
    turned = jnp.concatenate([summed, blank], axis=0).T
    gain_grad[...] = turned[0:1, 0:48] / gain[...].astype(f32)
    first = jnp.concatenate([first[:, 1152:1280], blank], axis=0).T
    second = jnp.concatenate([second[:, 1152:1280], blank], axis=0).T
    for row in range(2):
        cols = slice(row * 6, row * 6 + 6)
        bias[row : row + 1, 0:6] = first[0:1, cols]
        bias[row : row + 1, 6:12] = second[0:1, cols]


def finish(place, a_near, a_far, g_near, g_far, qw, kw, vw, gain):
    full = jax.ShapeDtypeStruct((48, 768), f32)
    return pl.pallas_call(
        finish_kernel,
        out_shape=(
            jax.ShapeDtypeStruct((192, 768), f32),
            full, full, full, jax.ShapeDtypeStruct((1, 48), f32), jax.ShapeDtypeStruct((2, 12), f32),
        ),
        in_specs=[SCALARS] + [FULL] * 8,
        out_specs=(FULL,) * 6,
        compiler_params=params(),
        cost_estimate=cost(1000, 1_000_000),
        name="finish",
    )(place, a_near, a_far, g_near, g_far, qw, kw, vw, gain.reshape(1, 48))


def finish_wide_kernel(place, near, far, up, gain, expand, output, gain_grad):
    summed = near[...].astype(f32) + far[...].astype(f32)
    joint = jnp.zeros((48, 768), f32)
    for at in range(4):
        cols = slice(at * 768, at * 768 + 768)
        expand[:, cols] = summed[at]
        joint = joint + summed[at] * up[:, cols].astype(f32)
    output[...] = summed[4]
    column = jnp.broadcast_to(jnp.sum(joint, axis=1, keepdims=True), (48, 128))
    turned = jnp.concatenate([column, jnp.zeros((80, 128), f32)], axis=0).T
    gain_grad[...] = turned[0:1, 0:48] / gain[...].astype(f32)


def finish_wide(place, near, far, up, gain):
    return pl.pallas_call(
        finish_wide_kernel,
        out_shape=(
            jax.ShapeDtypeStruct((48, 3072), f32), jax.ShapeDtypeStruct((48, 768), f32), jax.ShapeDtypeStruct((1, 48), f32),
        ),
        in_specs=[SCALARS] + [FULL] * 4,
        out_specs=(FULL,) * 3,
        compiler_params=params(),
        cost_estimate=cost(1000, 2_000_000),
        name="finish_wide",
    )(place, near, far, up, gain.reshape(1, 48))


def input_grad_kernel(place, x, small, near, far, middle_grad, result):
    for row in range(0, 512, 256):
        rows = slice(row, row + 256)
        wide = x[rows].astype(f32)
        scale = lax.rsqrt(jnp.mean(wide * wide, axis=-1, keepdims=True) + EPS)
        unit = wide * scale
        direct = (near[rows].astype(f32) + far[rows].astype(f32)) * small[0:1]
        inward = scale * (direct - unit * jnp.mean(direct * unit, axis=-1, keepdims=True))
        result[rows] = (middle_grad[rows] + inward).astype(bf16)


def input_grad(place, x, small, near, far, middle_grad):
    return pl.pallas_call(
        input_grad_kernel,
        out_shape=jax.ShapeDtypeStruct((512, 768), bf16),
        in_specs=[SCALARS] + [FULL] * 5,
        out_specs=FULL,
        compiler_params=params(),
        cost_estimate=cost(512 * 768 * 20, 6_000_000),
        name="input_grad",
    )(place, x, small, near, far, middle_grad)


def swap(array, axis, bit):
    count = lax.axis_size(axis)
    return lax.ppermute(array, axis, [(i, i ^ bit) for i in range(count)])


def swap_both(array):
    pairs = [(i * 2 + j, (i ^ Y) * 2 + 1 - j) for i in range(lax.axis_size("fsdp")) for j in range(2)]
    return lax.ppermute(array, ("fsdp", "seq"), pairs)


CORE, Y, Z = 1, 2, 4


def after(value, *others):
    return lax.optimization_barrier((value, *others))[0]


class Line:
    def __init__(self, place):
        self.place = place

    def wait(self, *arrays):
        self.place = after(self.place, *arrays)

    def run(self, kernel, *args):
        made = kernel(self.place, *args)
        self.wait(jax.tree.leaves(made)[0])
        return made


def gather_part(array, part, own, now):
    _, dims, gone = part
    for axis in reversed(range(len(dims))):
        if dims[axis] == now:
            array = lax.dynamic_index_in_dim(array, 1 - own[now], axis, keepdims=False)
        elif dims[axis] in gone:
            array = lax.dynamic_index_in_dim(array, own[dims[axis]], axis, keepdims=False)
    return array.astype(f32)


def total(line, parts, own, now=None):
    arrays = after([part[0] for part in parts], line.place)
    made = None
    for array, part in zip(arrays, parts):
        term = gather_part(array, part, own, now)
        made = term if made is None else made + term
    made = lax.optimization_barrier(made.astype(bf16))
    line.wait(made)
    return made


def keep(parts, now, got):
    _, dims, gone = parts[0]
    left = tuple(dim for dim in dims if dim not in gone and dim != now)
    return [(a, d, g + (now,)) for a, d, g in parts] + [(got, left, ())]


def local_split(
    layer_input, query_weight, key_weight, value_weight, output_weight, expand_weight,
    contract_weight, attention_gain, feedforward_gain, bias_table, valid_len, instr_len, pair_flag,
    cotangent,
):
    owner, x = lax.axis_index("fsdp"), lax.axis_index("seq")
    z, y, c = owner // 4, (owner // 2) % 2, owner % 2
    where = jnp.stack([z, y, c, x]).astype(jnp.int32)
    line = Line(where)
    tokens, cot = layer_input[0], cotangent[0]

    def by_z(array):
        return swap(array, "fsdp", Z)

    def by_zz(array):
        return swap(array, "fsdp", 2 * Z)

    def by_y(array):
        return swap(array, "fsdp", Y)

    def by_core(array):
        return swap(array, "fsdp", CORE)

    def by_x(array):
        return swap(array, "seq", 1)

    shard = line.run(
        narrow_shard, query_weight, key_weight, value_weight, attention_gain, feedforward_gain, bias_table
    )
    a2, a1, b0 = by_zz(shard), by_z(shard), by_y(shard)
    x_far, cot_far = by_x(tokens), by_core(cot)
    rest, full = line.run(wide_shard, expand_weight, output_weight, contract_weight)
    a2, a1, b0, rest, cot_far = lax.optimization_barrier((a2, a1, b0, rest, cot_far))
    turned, b2 = by_z(jnp.stack([a2, b0])), by_y(a2)
    four = by_core(jnp.stack([shard, b0, a1, a2]))
    z2, z1 = by_zz(rest), by_z(rest)
    turned, b2, rest, x_far = lax.optimization_barrier((turned, b2, rest, x_far))
    b3 = by_y(turned[0])
    three = by_core(jnp.stack([turned[0], turned[1], b2]))
    b3, rest, three = lax.optimization_barrier((b3, rest, three))
    y0 = by_y(rest)
    narrow = [shard, b0, a1, a2, turned, b2, b3, four, three, by_core(b3)]

    lens = jnp.stack([valid_len[0], instr_len[0], pair_flag[0]])
    line.place = jnp.concatenate([line.place, lens])
    qkv, normed_kept, normed_sent, small, table, tiles = line.run(project, tokens, x_far, narrow)
    line.place, z1, z2, y0 = lax.optimization_barrier((line.place, z1, z2, y0))
    z3, y2 = by_z(z2), by_y(z2)
    sides, trio = jnp.stack([z1[5:], z2[5:], y0[5:]]), jnp.stack([y0, z1, z2])
    sides_a, far_full, far_three = by_x(sides), by_core(full), by_core(trio)
    line.wait(sides, trio)
    out_theirs, kept_theirs, inverse_theirs = line.run(attend, table, tiles, qkv, False)
    line.place, z3, y2, sides_a, out_theirs, far_full, far_three = lax.optimization_barrier(
        (line.place, z3, y2, sides_a, out_theirs, far_full, far_three)
    )
    out_got = by_x(out_theirs)
    y3 = by_y(z3)
    y1 = jnp.concatenate([y0, sides_a[2]], axis=0)
    sides, two = jnp.stack([z3[5:], y2[5:]]), jnp.stack([z3, y2])
    line.wait(y1, sides, two)
    y1, sides_b, far_two = by_z(y1), by_x(sides), by_core(two)
    out_mine, kept_mine, inverse_mine = line.run(attend, table, tiles, qkv, True)
    out_mine, out_got, sides_a, y3, sides_b, far_two, y1 = lax.optimization_barrier(
        (out_mine, out_got, sides_a, y3, sides_b, far_two, y1)
    )
    sides_c = by_x(y3[5:])
    near = [full, y0, z1, z2, z3, y2, y1, y3, sides_a, sides_b, sides_c]
    far = [far_full, far_three, far_two] + [by_core(block) for block in (y1, y3, sides_a, sides_b, sides_c)]
    hid, hid_sent, pre, turned, turned_sent, layer_output, middle_grad, grad_mine, grad_sent = line.run(
        forward, out_mine, out_got, tokens, cot, small, near, far
    )
    hid_far, grad_theirs, pre_far, turned_far = by_core(hid_sent), by_x(grad_sent), by_core(pre), by_core(turned_sent)

    own = {"high": z // 2, "low": z % 2, "y": y, "x": x}

    def parts(kept, got, *dims):
        lead = tuple({"high": 2, "low": 2, "y": 2}[dim] for dim in dims if dim != "n")
        shape = lead + kept.shape[-3:] if "n" in dims else lead + kept.shape[-2:]
        return [(array.reshape(shape), dims, ()) for array in (kept, got)]

    carry = line.run(
        lambda place: attend_back(place, grad_mine, out_mine, inverse_mine, qkv, kept_mine, (), True)
    )
    line.wait(grad_theirs)
    sent, kept = line.run(contract_weight_grad, hid, hid_far, cot, cot_far)
    a_parts = parts(kept, by_x(sent), "high", "low", "y", "n")
    b_sent, b_kept, c_sent, c_kept = line.run(expand_weight_grad, turned, turned_far, pre, pre_far)
    b_parts = parts(b_kept, by_y(b_sent), "high", "low", "n")
    c_got = by_z(c_sent)
    c_parts = parts(c_kept, c_got, "high", "y", "n")
    whole = line.run(
        lambda place: attend_back(
            place, grad_theirs, out_theirs, inverse_theirs, qkv, kept_theirs, carry, False
        )
    )
    line.wait(c_got)
    g_near, g_far = line.run(weight_grad, normed_kept, normed_sent, whole)
    g_parts = parts(g_near, by_core(g_far), "high", "low", "y")
    b_parts = keep(b_parts, "low", by_z(total(line, b_parts, own, "low")))
    c_parts = keep(c_parts, "y", by_y(total(line, c_parts, own, "y")))
    part_near, part_far = line.run(project_back, narrow, whole)
    part_got = by_x(part_far)
    a_parts = keep(a_parts, "y", by_y(total(line, a_parts, own, "y")))
    g_parts = keep(g_parts, "low", by_z(total(line, g_parts, own, "low")))
    b_parts = keep(b_parts, "high", by_zz(total(line, b_parts, own, "high")))
    c_parts = keep(c_parts, "high", by_zz(total(line, c_parts, own, "high")))
    g_parts = keep(g_parts, "y", by_y(total(line, g_parts, own, "y")))
    a_parts = keep(a_parts, "low", by_z(total(line, a_parts, own, "low")))
    b_low = jnp.concatenate([total(line, b_parts, own), total(line, c_parts, own)], axis=0)
    b_low = lax.optimization_barrier(b_low)
    b_other = by_x(b_low)
    line.wait(b_low)
    result = line.run(input_grad, tokens, small, part_near, part_got, middle_grad)
    g_parts = keep(g_parts, "high", by_zz(total(line, g_parts, own, "high")))
    a_parts = keep(a_parts, "high", by_zz(total(line, a_parts, own, "high")))
    expand_sum, output_sum, gain_two = line.run(finish_wide, b_low, b_other, expand_weight, feedforward_gain)
    g_low = total(line, g_parts, own)
    g_other = by_x(g_low)
    a_low = total(line, a_parts, own)
    a_other = by_x(a_low)
    contract_sum, *grads, gain_one, bias_grad = line.run(
        finish, a_low, a_other, g_low, g_other, query_weight, key_weight, value_weight, attention_gain
    )
    return (
        layer_output[None], result[None], gain_one[0], gain_two[0], *grads,
        output_sum, expand_sum, contract_sum, bias_grad,
    )


def bucket_table(query_pos, key_pos):
    offset = key_pos[None, :] - query_pos[:, None]
    distance = jnp.abs(offset)
    beyond = jnp.zeros_like(distance)
    for far_edge in far_edges:
        beyond = beyond + (distance >= far_edge).astype(jnp.int32)
    nearby = jnp.where(distance < 8, distance, 8 + beyond)
    return nearby + 16 * (offset > 0).astype(jnp.int32)


def visible_keys(query_pos, key_pos, valid_len, instr_len, pair_flag):
    in_valid = key_pos[None, None, :] < valid_len[:, None, None]
    guarded = (
        (pair_flag[:, None, None] == 1)
        & (query_pos[None, :, None] < instr_len[:, None, None])
        & (key_pos[None, None, :] >= instr_len[:, None, None])
    )
    return in_valid & jnp.logical_not(guarded)


def rms_scale(values):
    return lax.rsqrt(jnp.mean(values * values, axis=-1, keepdims=True) + EPS)


def norm_back(values, scale, gain, grad_out):
    normed = values * scale
    grad_normed = grad_out * gain
    grad_values = scale * (
        grad_normed - normed * jnp.mean(grad_normed * normed, axis=-1, keepdims=True)
    )
    return (grad_values, jnp.sum(grad_out * normed, axis=(0, 1)))


def gelu_tanh(values):
    return jax.nn.gelu(values, approximate=True)


def local(
    layer_input,
    query_weight,
    key_weight,
    value_weight,
    output_weight,
    expand_weight,
    contract_weight,
    attention_gain,
    feedforward_gain,
    bias_table,
    valid_len,
    instr_len,
    pair_flag,
    cotangent,
):
    f32 = jnp.float32
    bf16 = jnp.bfloat16
    row_count, local_len, model_width = layer_input.shape
    head_count = bias_table.shape[1]
    head_size = model_width // head_count
    full_len = local_len * lax.axis_size("seq")
    local_start = lax.axis_index("seq") * local_len
    query_pos = local_start + jnp.arange(local_len, dtype=jnp.int32)
    key_pos = jnp.arange(full_len, dtype=jnp.int32)
    buckets = bucket_table(query_pos, key_pos)
    onehot = buckets[:, :, None] == jnp.arange(BUCKETS, dtype=jnp.int32)[None, None, :]
    visible = visible_keys(query_pos, key_pos, valid_len, instr_len, pair_flag)
    input_wide = layer_input.astype(f32)

    def attend_probs(queries, key_heads, table_full):
        rel_bias = jnp.einsum(
            "ijb,bh->hij", onehot.astype(bf16), table_full, preferred_element_type=f32
        )
        raw_scores = jnp.einsum("rihe,rjhe->rhij", queries, key_heads, preferred_element_type=f32)
        scores = jnp.where(visible[:, None], raw_scores + rel_bias[None], -1000000000.0)
        row_peak = jnp.max(scores, axis=-1, keepdims=True)
        log_total = row_peak + jnp.log(jnp.sum(jnp.exp(scores - row_peak), axis=-1, keepdims=True))
        return (jnp.exp(scores - log_total), log_total[..., 0])

    def forward(weights):
        (
            query_full,
            key_full,
            value_full,
            output_full,
            expand_full,
            contract_full,
            gain_one,
            gain_two,
            table_full,
        ) = weights
        scale_one = rms_scale(input_wide)
        normed_low = (input_wide * scale_one * gain_one.astype(f32)).astype(bf16)

        def project(weight):
            return jnp.einsum("rtd,de->rte", normed_low, weight, preferred_element_type=f32).astype(
                bf16
            )

        query_low = project(query_full)
        key_low = project(key_full)
        value_low = project(value_full)
        key_all, value_all = (
            lax.all_gather(key_low, "seq", axis=1, tiled=True),
            lax.all_gather(value_low, "seq", axis=1, tiled=True),
        )
        queries = query_low.reshape(row_count, local_len, head_count, head_size)
        key_heads = key_all.reshape(row_count, full_len, head_count, head_size)
        value_heads = value_all.reshape(row_count, full_len, head_count, head_size)
        probs, log_total = attend_probs(queries, key_heads, table_full)
        probs_low = probs.astype(bf16)
        attended = jnp.einsum("rhij,rjhe->rihe", probs_low, value_heads, preferred_element_type=f32)
        attended = attended.reshape(row_count, local_len, model_width).astype(bf16)
        middle = input_wide + jnp.einsum(
            "rtd,de->rte", attended, output_full, preferred_element_type=f32
        )
        scale_two = rms_scale(middle)
        normed_two = (middle * scale_two * gain_two.astype(f32)).astype(bf16)
        hidden_pre = jnp.einsum("rtd,df->rtf", normed_two, expand_full, preferred_element_type=f32)
        hidden_low = gelu_tanh(hidden_pre).astype(bf16)
        result = middle + jnp.einsum(
            "rtf,fd->rtd", hidden_low, contract_full, preferred_element_type=f32
        )
        return (
            result,
            scale_one,
            normed_low,
            queries,
            key_heads,
            value_heads,
            probs,
            probs_low,
            log_total,
            attended,
            middle,
            scale_two,
            normed_two,
            hidden_pre,
            hidden_low,
        )

    stored = forward(
        (
            lax.all_gather(query_weight, "fsdp", axis=0, tiled=True),
            lax.all_gather(key_weight, "fsdp", axis=0, tiled=True),
            lax.all_gather(value_weight, "fsdp", axis=0, tiled=True),
            lax.all_gather(output_weight, "fsdp", axis=0, tiled=True),
            lax.all_gather(expand_weight, "fsdp", axis=0, tiled=True),
            lax.all_gather(contract_weight, "fsdp", axis=0, tiled=True),
            lax.all_gather(attention_gain, "fsdp", axis=0, tiled=True),
            lax.all_gather(feedforward_gain, "fsdp", axis=0, tiled=True),
            lax.all_gather(bias_table, "fsdp", axis=0, tiled=True),
        )
    )
    layer_output = stored[0].astype(bf16)
    gathered = (
        lax.all_gather(query_weight, "fsdp", axis=0, tiled=True),
        lax.all_gather(key_weight, "fsdp", axis=0, tiled=True),
        lax.all_gather(value_weight, "fsdp", axis=0, tiled=True),
        lax.all_gather(output_weight, "fsdp", axis=0, tiled=True),
        lax.all_gather(expand_weight, "fsdp", axis=0, tiled=True),
        lax.all_gather(contract_weight, "fsdp", axis=0, tiled=True),
        lax.all_gather(attention_gain, "fsdp", axis=0, tiled=True),
        lax.all_gather(feedforward_gain, "fsdp", axis=0, tiled=True),
        lax.all_gather(bias_table, "fsdp", axis=0, tiled=True),
    )
    kept = forward(gathered)
    (
        unused,
        scale_one,
        normed_low,
        queries,
        key_heads,
        value_heads,
        probs,
        probs_low,
        log_total,
        attended,
        middle,
        scale_two,
        normed_two,
        hidden_pre,
        hidden_low,
    ) = kept
    (
        query_full,
        key_full,
        value_full,
        output_full,
        expand_full,
        contract_full,
        gain_one,
        gain_two,
        table_full,
    ) = gathered
    gain_one_wide = gain_one.astype(f32)
    gain_two_wide = gain_two.astype(f32)
    contract_grad = jnp.einsum("rtf,rtd->fd", hidden_low, cotangent, preferred_element_type=f32)
    grad_hidden = jnp.einsum("rtd,fd->rtf", cotangent, contract_full, preferred_element_type=f32)
    gelu_pull = jax.vjp(gelu_tanh, hidden_pre)[1]
    grad_pre = gelu_pull(grad_hidden)[0].astype(bf16)
    expand_grad = jnp.einsum("rtd,rtf->df", normed_two, grad_pre, preferred_element_type=f32)
    grad_normed_two = jnp.einsum("rtf,df->rtd", grad_pre, expand_full, preferred_element_type=f32)
    grad_middle_norm, gain_two_grad = norm_back(middle, scale_two, gain_two_wide, grad_normed_two)
    grad_middle = cotangent.astype(f32) + grad_middle_norm
    grad_branch = grad_middle.astype(bf16)
    output_grad = jnp.einsum("rtd,rte->de", attended, grad_branch, preferred_element_type=f32)
    grad_attended = jnp.einsum(
        "rte,de->rtd", grad_branch, output_full, preferred_element_type=f32
    ).astype(bf16)
    grad_attended = grad_attended.reshape(row_count, local_len, head_count, head_size)
    grad_probs = jnp.einsum(
        "rihe,rjhe->rhij", grad_attended, value_heads, preferred_element_type=f32
    )
    row_delta = jnp.sum(probs * grad_probs, axis=-1)
    grad_scores = probs * (grad_probs - row_delta[..., None])
    bias_part = jnp.einsum(
        "hij,ijb->bh",
        jnp.sum(grad_scores, axis=0),
        onehot.astype(f32),
        precision=lax.Precision.HIGHEST,
    )
    scores_low = grad_scores.astype(bf16)
    grad_queries = jnp.einsum("rhij,rjhe->rihe", scores_low, key_heads, preferred_element_type=f32)
    grad_queries = grad_queries.reshape(row_count, local_len, model_width).astype(bf16)
    value_partial = jnp.einsum(
        "rhij,rihe->rjhe", probs_low, grad_attended, preferred_element_type=f32
    ).reshape(row_count, full_len, model_width)
    key_partial = jnp.einsum(
        "rhij,rihe->rjhe", scores_low, queries, preferred_element_type=f32
    ).reshape(row_count, full_len, model_width)
    key_summed, value_summed = (
        lax.psum_scatter(
            key_partial.astype(jnp.bfloat16), "seq", scatter_dimension=1, tiled=True
        ).astype(jnp.float32),
        lax.psum_scatter(
            value_partial.astype(jnp.bfloat16), "seq", scatter_dimension=1, tiled=True
        ).astype(jnp.float32),
    )
    grad_keys = key_summed.astype(bf16)
    grad_values = value_summed.astype(bf16)
    query_part = jnp.einsum("rtd,rte->de", normed_low, grad_queries, preferred_element_type=f32)
    key_part = jnp.einsum("rtd,rte->de", normed_low, grad_keys, preferred_element_type=f32)
    value_part = jnp.einsum("rtd,rte->de", normed_low, grad_values, preferred_element_type=f32)
    grad_normed_one = jnp.einsum(
        "rte,de->rtd", grad_queries, query_full, preferred_element_type=f32
    )
    grad_normed_one = grad_normed_one + jnp.einsum(
        "rte,de->rtd", grad_keys, key_full, preferred_element_type=f32
    )
    grad_normed_one = grad_normed_one + jnp.einsum(
        "rte,de->rtd", grad_values, value_full, preferred_element_type=f32
    )
    grad_input_norm, gain_one_grad = norm_back(
        input_wide, scale_one, gain_one_wide, grad_normed_one
    )
    input_grad = (grad_middle + grad_input_norm).astype(bf16)
    owned = (
        lax.psum_scatter(
            query_part.astype(jnp.bfloat16), "fsdp", scatter_dimension=0, tiled=True
        ).astype(jnp.float32),
        lax.psum_scatter(
            key_part.astype(jnp.bfloat16), "fsdp", scatter_dimension=0, tiled=True
        ).astype(jnp.float32),
        lax.psum_scatter(
            value_part.astype(jnp.bfloat16), "fsdp", scatter_dimension=0, tiled=True
        ).astype(jnp.float32),
        lax.psum_scatter(
            output_grad.astype(jnp.bfloat16), "fsdp", scatter_dimension=0, tiled=True
        ).astype(jnp.float32),
        lax.psum_scatter(
            expand_grad.astype(jnp.bfloat16), "fsdp", scatter_dimension=0, tiled=True
        ).astype(jnp.float32),
        lax.psum_scatter(
            contract_grad.astype(jnp.bfloat16), "fsdp", scatter_dimension=0, tiled=True
        ).astype(jnp.float32),
        lax.psum_scatter(
            gain_one_grad.astype(jnp.bfloat16), "fsdp", scatter_dimension=0, tiled=True
        ).astype(jnp.float32),
        lax.psum_scatter(
            gain_two_grad.astype(jnp.bfloat16), "fsdp", scatter_dimension=0, tiled=True
        ).astype(jnp.float32),
        lax.psum_scatter(
            bias_part.astype(jnp.bfloat16), "fsdp", scatter_dimension=0, tiled=True
        ).astype(jnp.float32),
    )
    summed = (
        lax.psum(owned[0].astype(jnp.bfloat16), "seq").astype(jnp.float32),
        lax.psum(owned[1].astype(jnp.bfloat16), "seq").astype(jnp.float32),
        lax.psum(owned[2].astype(jnp.bfloat16), "seq").astype(jnp.float32),
        lax.psum(owned[3].astype(jnp.bfloat16), "seq").astype(jnp.float32),
        lax.psum(owned[4].astype(jnp.bfloat16), "seq").astype(jnp.float32),
        lax.psum(owned[5].astype(jnp.bfloat16), "seq").astype(jnp.float32),
        lax.psum(owned[6].astype(jnp.bfloat16), "seq").astype(jnp.float32),
        lax.psum(owned[7].astype(jnp.bfloat16), "seq").astype(jnp.float32),
        lax.psum(owned[8].astype(jnp.bfloat16), "seq").astype(jnp.float32),
    )
    (
        query_grad,
        key_grad,
        value_grad,
        output_sum,
        expand_sum,
        contract_sum,
        gain_one_sum,
        gain_two_sum,
        bias_grad,
    ) = summed
    return (
        layer_output,
        input_grad,
        gain_one_sum,
        gain_two_sum,
        query_grad,
        key_grad,
        value_grad,
        output_sum,
        expand_sum,
        contract_sum,
        bias_grad,
    )


def solution(mesh):
    in_specs = (
        P("fsdp", "seq", None),
        P("fsdp", None),
        P("fsdp", None),
        P("fsdp", None),
        P("fsdp", None),
        P("fsdp", None),
        P("fsdp", None),
        P("fsdp"),
        P("fsdp"),
        P("fsdp", None),
        P("fsdp"),
        P("fsdp"),
        P("fsdp"),
        P("fsdp", "seq", None),
    )
    out_specs = (
        P("fsdp", "seq", None),
        P("fsdp", "seq", None),
        P("fsdp"),
        P("fsdp"),
        P("fsdp", None),
        P("fsdp", None),
        P("fsdp", None),
        P("fsdp", None),
        P("fsdp", None),
        P("fsdp", None),
        P("fsdp", None),
    )
    split = mesh.shape["fsdp"] == 16 and mesh.shape["seq"] == 2
    step = local_split if split else local
    return jax.shard_map(step, mesh=mesh, in_specs=in_specs, out_specs=out_specs, check_vma=False)
```

```python
import functools
import itertools
import math

import jax
import jax.numpy as jnp
from jax import lax
from jax.experimental import pallas as pl
from jax.experimental.pallas import tpu as pltpu
from jax.sharding import PartitionSpec as P

f32 = jnp.float32
bf16 = jnp.bfloat16
BUCKETS = 32
EPS = 1e-06
far_edges = (12, 16, 23, 32, 46, 64, 91)
HIDDEN = -(2.0**30)
VMEM = 56 * 1024 * 1024
ANY = pl.BlockSpec(memory_space=pl.ANY)
FULL = pl.BlockSpec(memory_space=pltpu.VMEM)
SCALARS = pl.BlockSpec(memory_space=pltpu.SMEM)


def dot(left, right, left_dim, right_dim):
    return lax.dot_general(
        left, right, (((left_dim,), (right_dim,)), ((), ())), preferred_element_type=f32
    )


def params():
    return pltpu.CompilerParams(vmem_limit_bytes=VMEM)


def cost(flops, byte_count, exps=0):
    return pl.CostEstimate(flops=flops // 1000, bytes_accessed=byte_count // 1000, transcendentals=exps // 1000)


def small_cost():
    return pl.CostEstimate(flops=1000, bytes_accessed=1000, transcendentals=0)


def bucket_of(offset):
    distance = jnp.abs(offset)
    beyond = jnp.zeros_like(distance)
    for far_edge in far_edges:
        beyond = beyond + (distance >= far_edge).astype(jnp.int32)
    nearby = jnp.where(distance < 8, distance, 8 + beyond)
    return nearby + 16 * (offset > 0).astype(jnp.int32)


def iota(shape, dim):
    return lax.broadcasted_iota(jnp.int32, shape, dim)


def narrow_kernel(place, q, k, v, gain_one, gain_two, table, out, side):
    column = pl.multiple_of(place[3] * 384, 128)
    pieces = [weight[:, pl.ds(column, 384)] for weight in (q, k, v)]
    for pair in range(3):
        parts = [piece[:, at : at + 64] for at in (pair * 128, pair * 128 + 64) for piece in pieces]
        out[:, pair * 384 : pair * 384 + 384] = jnp.concatenate(parts, axis=1)
    side[...] = jnp.zeros((8, 128), f32)
    side[0:1, 0:48] = gain_one[...].astype(f32)
    side[1:2, 0:48] = gain_two[...].astype(f32)
    side[2:3, 0:12] = table[0:1].astype(f32)
    side[2:3, 12:24] = table[1:2].astype(f32)
    wide = jnp.concatenate([side[...], jnp.zeros((120, 128), f32)], axis=0).T
    out[:, 1152:1280] = wide[0:48].astype(bf16)


def narrow_shard(place, q, k, v, gain_one, gain_two, table):
    return pl.pallas_call(
        narrow_kernel,
        out_shape=jax.ShapeDtypeStruct((48, 1280), bf16),
        in_specs=[SCALARS] + [FULL] * 6,
        out_specs=FULL,
        scratch_shapes=[pltpu.VMEM((8, 128), f32)],
        compiler_params=params(),
        cost_estimate=small_cost(),
        name="narrow_shard",
    )(place, q, k, v, gain_one.reshape(1, 48), gain_two.reshape(1, 48), table)


def wide_kernel(place, expand, output, contract, out, full, sems):
    x = place[3]
    pieces = [(expand.at[:, at * 768 : at * 768 + 768], out.at[at]) for at in range(4)]
    pieces.append((output, out.at[4]))
    for at in range(2):
        row = pl.multiple_of(x * 96 + at * 48, 16)
        pieces.append((contract.at[pl.ds(row, 48)], out.at[5 + at]))
        row = pl.multiple_of((1 - x) * 96 + at * 48, 16)
        pieces.append((contract.at[pl.ds(row, 48)], full.at[7 + at]))
    copies = [pltpu.make_async_copy(*piece, sems.at[at]) for at, piece in enumerate(pieces)]
    for copy in copies:
        copy.start()
    for copy in copies:
        copy.wait()
    full[0:7] = out[...]


def wide_shard(place, expand, output, contract):
    return pl.pallas_call(
        wide_kernel,
        out_shape=(
            jax.ShapeDtypeStruct((7, 48, 768), bf16), jax.ShapeDtypeStruct((9, 48, 768), bf16),
        ),
        in_specs=[SCALARS, ANY, ANY, ANY],
        out_specs=(FULL, FULL),
        scratch_shapes=[pltpu.SemaphoreType.DMA((9,))],
        compiler_params=params(),
        cost_estimate=small_cost(),
        name="wide_shard",
    )(place, expand, output, contract)


def narrow_blocks(refs):
    shard, b0, a1, a2, turned, b2, b3, four, three, last = refs
    near = [shard, b0, a1, turned.at[1], a2, b2, turned.at[0], b3]
    far = [four.at[0], four.at[1], four.at[2], three.at[1], four.at[3], three.at[2], three.at[0], last]
    return near, far


def place_blocks(place, near, far, dest, sems):
    z, y, c = place[0], place[1], place[2]
    copies = []
    for turn in range(4):
        for dy in range(2):
            owner = ((jnp.bitwise_xor(z, turn) * 2) + jnp.bitwise_xor(y, dy)) * 2
            for other, source in enumerate((near, far)):
                row = pl.multiple_of((owner + jnp.bitwise_xor(c, other)) * 48, 16)
                copy = pltpu.make_async_copy(
                    source[turn * 2 + dy], dest.at[pl.ds(row, 48)], sems.at[len(copies)]
                )
                copy.start()
                copies.append(copy)
    return copies


def place_tokens(x, near, far, dest, sems, count):
    copies = []
    for other, source in enumerate((near, far)):
        row = pl.multiple_of(jnp.bitwise_xor(x, other) * count, count)
        copy = pltpu.make_async_copy(source, dest.at[pl.ds(row, count)], sems.at[other])
        copy.start()
        copies.append(copy)
    return copies


def first_query(place, mine):
    return (place[3] if mine else 1 - place[3]) * 512


def project_kernel(place, x_near, x_far, *refs):
    (w_near, w_far), refs = narrow_blocks(refs[:10]), refs[10:]
    qkv, kept, sent, small, table, tiles, normed, xs, w, sems, xsems = refs
    tokens = place_tokens(place[3], x_near, x_far, xs, xsems, 512)
    blocks = place_blocks(place, w_near, w_far, w, sems)
    for copy in tokens + blocks:
        copy.wait()
    side = w[:, 1152:1280].astype(f32).T
    small[...] = side[:8]
    gain = side[0:1]
    row = iota((768, 128), 0)
    spot = row % 48
    bucket = (row // 48) * 2 + spot // 12
    match = (iota((768, 128), 1) == bucket) & (spot < 24)
    values = jnp.where(match, w[:, 1154:1155].astype(f32), 0.0).astype(bf16)
    head = iota((8, 768), 0)
    chosen = ((iota((8, 768), 1) % 48) % 12 == place[3] * 6 + head) & (head < 6)
    made = dot(chosen.astype(bf16), values, 1, 0)
    table[...] = made
    lane = iota((128, 512), 1)
    spread = (bucket_of(jnp.where(lane < 128, -128 - lane, 384 - lane)) == iota((128, 512), 0)).astype(bf16)
    turned = dot(made.astype(bf16), spread, 1, 0)
    for head in range(6):
        for block, (low, high) in enumerate(((384, 0), (256, 384), (128, 256))):
            parts = [turned[head : head + 1, at : at + 128] for at in (low, high)]
            wide = jnp.broadcast_to(jnp.concatenate(parts, axis=1), (128, 256))
            rolled = pltpu.roll(wide, 0, 1, stride=1, stride_axis=0)
            tiles[head, block * 128 : block * 128 + 128] = rolled[:, 128:256]
    for row in range(0, 1024, 256):
        wide = xs[row : row + 256].astype(f32)
        scale = lax.rsqrt(jnp.mean(wide * wide, axis=-1, keepdims=True) + EPS)
        normed[row : row + 256] = (wide * scale * gain).astype(bf16)
    for col in range(0, 1152, 384):
        made = dot(w[:, col : col + 384], normed[...], 0, 1)
        qkv[col : col + 384] = made.astype(bf16)
    turned = normed[...].T.reshape(8, 2, 48, 1024)
    kept[...] = jnp.where(place[2] == 0, turned[:, 0], turned[:, 1])
    sent[...] = jnp.where(place[2] == 0, turned[:, 1], turned[:, 0])


def project(place, x_near, x_far, blocks):
    return pl.pallas_call(
        project_kernel,
        out_shape=(
            jax.ShapeDtypeStruct((1152, 1024), bf16),
            jax.ShapeDtypeStruct((8, 48, 1024), bf16),
            jax.ShapeDtypeStruct((8, 48, 1024), bf16),
            jax.ShapeDtypeStruct((8, 768), f32),
            jax.ShapeDtypeStruct((8, 128), f32),
            jax.ShapeDtypeStruct((6, 384, 128), f32),
        ),
        in_specs=[SCALARS] + [ANY] * 12,
        out_specs=(FULL,) * 6,
        scratch_shapes=[
            pltpu.VMEM((1024, 768), bf16),
            pltpu.VMEM((1024, 768), bf16),
            pltpu.VMEM((768, 1280), bf16),
            pltpu.SemaphoreType.DMA((16,)),
            pltpu.SemaphoreType.DMA((2,)),
        ],
        compiler_params=params(),
        cost_estimate=small_cost(),
        name="project",
    )(place, x_near, x_far, *blocks)


def attend_kernel(mine, place, table, tile, q, k, v, out, kept, inverse, ka, kt, qt, vt, s):
    head = pl.program_id(0)
    first, valid, instr, pair = first_query(place, mine), place[4], place[5], place[6]

    @pl.when(head == 0)
    def _():
        kt[64:128] = jnp.zeros((64, 1024), bf16)
        qt[64:128] = jnp.zeros((64, 512), bf16)
        row = iota((16, 1024), 0)
        key = iota((16, 1024), 1)
        extra = jnp.where(row < 8, (key // 128 == row).astype(f32), 0.0)
        extra = jnp.where(row == 8, jnp.where(key >= valid, HIDDEN, 0.0), extra)
        extra = jnp.where(row == 9, (key >= instr).astype(f32), extra)
        kt[64:80] = extra.astype(bf16)
        vt[64:80] = jnp.where(row == 0, 1.0, 0.0).astype(bf16)

    row = iota((16, 512), 0)
    query = iota((16, 512), 1) + first
    block = query // 128
    extra = jnp.where(row <= block - 2, table[head, 15], 0.0)
    extra = jnp.where(row >= block + 2, table[head, 31], extra)
    extra = jnp.where(row == 8, 1.0, extra)
    guarded = (query < instr) & (pair == 1)
    extra = jnp.where(row == 9, jnp.where(guarded, HIDDEN, 0.0), extra)
    extra = jnp.where(row > 9, 0.0, extra)
    qt[64:80] = extra.astype(bf16)
    qt[0:64] = q[...]
    kt[0:64] = k[...]
    vt[0:64] = v[...]
    ka[...] = kt[...].T
    s[128:1152] = dot(ka[...], qt[...], 1, 0)
    for part in range(4):
        base = pl.multiple_of(first + part * 128, 128)
        cols = slice(part * 128, part * 128 + 128)
        s[pl.ds(base, 384), cols] = s[pl.ds(base, 384), cols] + tile[0]
    scores = s[128:1152]
    peak = jnp.max(scores, axis=0, keepdims=True)
    weights = jnp.exp(scores - peak).astype(bf16)
    kept[0] = weights
    summed = dot(vt[...], weights, 1, 0)
    share = 1.0 / summed[64:65]
    out[...] = (summed[0:64] * share).astype(bf16)
    inverse[0] = share


def attend(place, table, tiles, qkv, mine):
    half = (lambda s: s[3]) if mine else (lambda s: 1 - s[3])
    grid = pltpu.PrefetchScalarGridSpec(
        num_scalar_prefetch=1,
        grid=(6,),
        in_specs=[
            SCALARS,
            pl.BlockSpec((1, 384, 128), lambda h, s: (h, 0, 0)),
            pl.BlockSpec((64, 512), lambda h, s: (3 * h, half(s))),
            pl.BlockSpec((64, 1024), lambda h, s: (3 * h + 1, 0)),
            pl.BlockSpec((64, 1024), lambda h, s: (3 * h + 2, 0)),
        ],
        out_specs=(
            pl.BlockSpec((64, 512), lambda h, s: (h, 0)),
            pl.BlockSpec((1, 1024, 512), lambda h, s: (h, 0, 0)),
            pl.BlockSpec((1, 1, 512), lambda h, s: (h, 0, 0)),
        ),
        scratch_shapes=[
            pltpu.VMEM((1024, 128), bf16),
            pltpu.VMEM((128, 1024), bf16),
            pltpu.VMEM((128, 512), bf16),
            pltpu.VMEM((80, 1024), bf16),
            pltpu.VMEM((1280, 512), f32),
        ],
    )
    return pl.pallas_call(
        functools.partial(attend_kernel, mine),
        out_shape=(
            jax.ShapeDtypeStruct((384, 512), bf16),
            jax.ShapeDtypeStruct((6, 1024, 512), bf16),
            jax.ShapeDtypeStruct((6, 1, 512), f32),
        ),
        grid_spec=grid,
        compiler_params=params(),
        cost_estimate=small_cost(),
        name="attend_mine" if mine else "attend_theirs",
    )(place, table, tiles, qkv, qkv, qkv)


def diagonal_sums(band):
    flip = (iota((128, 128), 0) + iota((128, 128), 1) == 127).astype(f32)
    rows = []
    for block in range(3):
        here = lax.dot_general(
            flip, band[block * 128 : block * 128 + 128], (((1,), (0,)), ((), ())),
            precision=lax.Precision.HIGHEST, preferred_element_type=f32,
        )
        wide = jnp.concatenate([here, jnp.zeros((128, 128), f32)], axis=1)
        rolled = pltpu.roll(wide, 0, 1, stride=1, stride_axis=0)
        rows.append(jnp.sum(rolled, axis=0, keepdims=True))
    return rows


def bucket_sums(diagonals, sides):
    total = sides
    for block in range(3):
        offset = block * 128 - 1 - iota((256, 128), 0)
        spread = (bucket_of(offset) == iota((256, 128), 1)).astype(f32)
        total = total + lax.dot_general(
            diagonals[block], spread, (((1,), (0,)), ((), ())),
            precision=lax.Precision.HIGHEST, preferred_element_type=f32,
        )
    return total


def attend_back_kernel(carried, mine, place, grad, out, inverse, q, k, v, kept, *refs):
    if carried:
        dq_in, dk_in, dv_in, band_in, far_in, whole, diagonals, sides, *refs = refs
    else:
        dq, dk, dv, band, far, *refs = refs
    va, vt, kt, gt, ds = refs
    first = first_query(place, mine)

    @pl.when(pl.program_id(0) == 0)
    def _():
        row = iota((16, 1024), 0)
        key = iota((16, 1024), 1)
        vt[64:128] = jnp.zeros((64, 1024), bf16)
        vt[64:80] = jnp.where(row < 2, 1.0, 0.0).astype(bf16)
        if carried:
            diagonals[...] = jnp.zeros_like(diagonals)
            sides[...] = jnp.zeros_like(sides)
        kt[64:80] = jnp.where(row < 8, (key // 128 == row).astype(f32), 0.0).astype(bf16)
        gt[64:128] = jnp.zeros((64, 512), bf16)
        ds[0:128] = jnp.zeros((128, 512), bf16)
        ds[1152:1280] = jnp.zeros((128, 512), bf16)

    share = inverse[0]
    scaled = grad[...].astype(f32) * share
    delta = jnp.sum(scaled * out[...].astype(f32), axis=0, keepdims=True)
    high = delta.astype(bf16).astype(f32)
    row = iota((16, 512), 0)
    extra = jnp.where(row == 0, -high, jnp.where(row == 1, high - delta, 0.0))
    gt[64:80] = extra.astype(bf16)
    gt[0:64] = scaled.astype(bf16)
    vt[0:64] = v[...]
    kt[0:64] = k[...]
    va[...] = vt[...].T
    for row_at in range(0, 1024, 256):
        rows = slice(row_at, row_at + 256)
        pull = dot(va[rows], gt[...], 1, 0)
        ds[128 + row_at : 384 + row_at] = (kept[0, rows] * pull).astype(bf16)
    made = dot(kt[...], ds[128:1152], 1, 0)
    block = (iota((8, 512), 1) + first) // 128
    key_block = iota((8, 512), 0)
    totals = made[64:72]
    left = jnp.sum(jnp.where(key_block <= block - 2, totals, 0.0), axis=0, keepdims=True)
    right = jnp.sum(jnp.where(key_block >= block + 2, totals, 0.0), axis=0, keepdims=True)
    dv_made = dot(gt[0:64], kept[0], 1, 1)
    dk_made = dot(q[...], ds[128:1152], 1, 1)
    near = None
    for part in range(4):
        base = pl.multiple_of(first + part * 128, 128)
        window = ds[pl.ds(base, 384), part * 128 : part * 128 + 128].astype(f32)
        near = window if near is None else near + window
    if carried:
        whole[0, 0:64, pl.ds(pl.multiple_of(first, 512), 512)] = made[0:64].astype(bf16)
        whole[0, 0:64, pl.ds(pl.multiple_of(512 - first, 512), 512)] = dq_in[...]
        whole[0, 64:128] = (dk_made + dk_in[...]).astype(bf16)
        whole[0, 128:192] = (dv_made + dv_in[...]).astype(bf16)
        head = pl.program_id(0)
        for at, row in enumerate(diagonal_sums(near + band_in[0])):
            diagonals[at, pl.ds(head, 1)] = row
        lane = iota((1, 128), 1)
        left, right = (
            jnp.sum(side, axis=1, keepdims=True) for side in (left + far_in[0, 0:1], right + far_in[0, 1:2])
        )
        sides[pl.ds(head, 1)] = jnp.where(lane == 15, left, jnp.where(lane == 31, right, 0.0))
        whole[0, 192:208] = jnp.zeros((16, 1024), bf16)

        @pl.when(head == 5)
        def _():
            bias = bucket_sums([diagonals[at] for at in range(3)], sides[...])
            whole[0, 192:208, 0:128] = jnp.concatenate([bias, jnp.zeros((8, 128), f32)], axis=0).astype(bf16)

    else:
        dq[...] = made[0:64].astype(bf16)
        dk[...] = dk_made
        dv[...] = dv_made
        band[0] = near
        far[0] = jnp.concatenate([left, right, jnp.zeros((6, 512), f32)], axis=0)


def attend_back(place, grad, out, inverse, qkv, kept, carry, mine):
    count = 6
    half = (lambda s: s[3]) if mine else (lambda s: 1 - s[3])
    rows512 = pl.BlockSpec((64, 512), lambda h, s: (h, 0))
    rows1024 = pl.BlockSpec((64, 1024), lambda h, s: (h, 0))
    band_spec = pl.BlockSpec((1, 384, 128), lambda h, s: (h, 0, 0))
    far_spec = pl.BlockSpec((1, 8, 512), lambda h, s: (h, 0, 0))
    carry_specs = (rows512, rows1024, rows1024, band_spec, far_spec)
    in_specs = [
        rows512,
        rows512,
        pl.BlockSpec((1, 1, 512), lambda h, s: (h, 0, 0)),
        pl.BlockSpec((64, 512), lambda h, s: (3 * h, half(s))),
        pl.BlockSpec((64, 1024), lambda h, s: (3 * h + 1, 0)),
        pl.BlockSpec((64, 1024), lambda h, s: (3 * h + 2, 0)),
        pl.BlockSpec((1, 1024, 512), lambda h, s: (h, 0, 0)),
    ]
    if carry:
        out_shape = jax.ShapeDtypeStruct((count, 208, 1024), bf16)
        out_specs = pl.BlockSpec((1, 208, 1024), lambda h, s: (h, 0, 0))
        in_specs += carry_specs
    else:
        out_shape = (
            jax.ShapeDtypeStruct((64 * count, 512), bf16),
            jax.ShapeDtypeStruct((64 * count, 1024), f32),
            jax.ShapeDtypeStruct((64 * count, 1024), f32),
            jax.ShapeDtypeStruct((count, 384, 128), f32),
            jax.ShapeDtypeStruct((count, 8, 512), f32),
        )
        out_specs = carry_specs
    grid = pltpu.PrefetchScalarGridSpec(
        num_scalar_prefetch=1,
        grid=(count,),
        in_specs=in_specs,
        out_specs=out_specs,
        scratch_shapes=([pltpu.VMEM((3, 8, 256), f32), pltpu.VMEM((8, 128), f32)] if carry else [])
        + [
            pltpu.VMEM((1024, 128), bf16),
            pltpu.VMEM((128, 1024), bf16),
            pltpu.VMEM((80, 1024), bf16),
            pltpu.VMEM((128, 512), bf16),
            pltpu.VMEM((1280, 512), bf16),
        ],
    )
    return pl.pallas_call(
        functools.partial(attend_back_kernel, bool(carry), mine),
        out_shape=out_shape,
        grid_spec=grid,
        compiler_params=params(),
        cost_estimate=cost(count * 1024 * 512 * 1024, 6_000_000),
        name="attend_back_mine" if mine else "attend_back_theirs",
    )(place, grad, out, inverse, qkv, qkv, qkv, kept, *carry)


def gelu_both(wide):
    square = wide * wide
    inner = 0.7978845608 * wide * (1.0 + 0.044715 * square)
    bend = jnp.tanh(inner)
    half = 0.5 * (1.0 + bend)
    slope = 0.7978845608 * (1.0 + 3 * 0.044715 * square)
    return (wide * half, half + 0.5 * wide * (1.0 - bend * bend) * slope)


def all_blocks(full, three, two, y1, y3, side_a, side_b, side_c):
    blocks = [full, three[0], three[1], y1, three[2], two[1], two[0], y3]
    sides = [
        full.at[7:9], side_a.at[2], side_a.at[0], y1.at[7:9], side_a.at[1], side_b.at[1], side_b.at[0], side_c,
    ]
    return blocks, sides


def forward_kernel(
    place, att_near, att_far, x, cot, small, *refs
):
    full, y0, z1, z2, z3, y2, y1, y3, side_a, side_b, side_c = refs[:11]
    nears, near_sides = all_blocks(full, (y0, z1, z2), (z3, y2), y1, y3, side_a, side_b, side_c)
    full, three, two, y1, y3, side_a, side_b, side_c = refs[11:19]
    three, two = [three.at[at] for at in range(3)], [two.at[at] for at in range(2)]
    fars, far_sides = all_blocks(full, three, two, y1, y3, side_a, side_b, side_c)
    refs = refs[19:]
    (
        hid_keep_hbm, hid_send_hbm, pre_hbm, turned_keep, turned_send, result, middle_grad, near_grad, far_grad,
        w_out, w_up, w_down, hid_keep, hid_send, pre, normed_grad, pulled, middle, total, normed, att,
        sems, att_sems, out_sems,
    ) = refs
    z, y, c, xs = place[0], place[1], place[2], place[3]
    att_copies = []
    for other, source in enumerate((att_near, att_far)):
        row = pl.multiple_of(jnp.bitwise_xor(xs, other) * 384, 128)
        copy = pltpu.make_async_copy(source, att.at[pl.ds(row, 384)], att_sems.at[other])
        copy.start()
        att_copies.append(copy)
    groups = ([], [], [])
    for turn in range(4):
        for dy in range(2):
            owner = ((jnp.bitwise_xor(z, turn) * 2) + jnp.bitwise_xor(y, dy)) * 2
            for other in range(2):
                main = (nears, fars)[other][turn * 2 + dy]
                side = (near_sides, far_sides)[other][turn * 2 + dy]
                who = owner + jnp.bitwise_xor(c, other)
                row = pl.multiple_of(who * 48, 16)
                pieces = (
                    (0, main.at[4], w_out.at[pl.ds(row, 48)]),
                    (1, main.at[0:4], w_up.at[:, pl.ds(row, 48)]),
                    (2, main.at[5:7], w_down.at[pl.ds(who * 4 + xs * 2, 2)]),
                    (2, side, w_down.at[pl.ds(who * 4 + (1 - xs) * 2, 2)]),
                )
                for at, (group, source, dest) in enumerate(pieces):
                    sem = sems.at[at, turn * 4 + dy * 2 + other]
                    groups[group].append(pltpu.make_async_copy(source, dest, sem))
    for group in groups:
        for copy in group:
            copy.start()
    for copy in att_copies + groups[0]:
        copy.wait()
    gain = small[1:2]
    wide = x[...].astype(f32) + dot(att[...], w_out[...], 0, 0)
    middle[...] = wide
    scale = lax.rsqrt(jnp.mean(wide * wide, axis=-1, keepdims=True) + EPS)
    normed[...] = (wide * scale * gain).astype(bf16)
    for group in groups[1:]:
        for copy in group:
            copy.wait()
    total[...] = wide
    normed_grad[...] = jnp.zeros_like(normed_grad)

    def chunk(j, carry):
        down = w_down[pl.ds(j * 16, 16)].reshape(768, 768)
        pulled[...] = dot(cot[...], down, 1, 1)
        value, slope = gelu_both(dot(normed[...], w_up[j], 1, 0))
        value = value.astype(bf16)
        total[...] += dot(value, down, 1, 0)
        even = jnp.concatenate([value[:, 0:192], value[:, 384:576]], axis=1)
        odd = jnp.concatenate([value[:, 192:384], value[:, 576:768]], axis=1)
        hid_keep[j] = jnp.where(c == 0, even, odd)
        hid_send[j] = jnp.where(c == 0, odd, even)
        low = (pulled[...] * slope).astype(bf16)
        pre[j] = low
        normed_grad[...] += dot(low, w_up[j], 1, 1)
        return carry

    lax.fori_loop(0, 4, chunk, 0)
    outs = [
        pltpu.make_async_copy(hid_send, hid_send_hbm, out_sems.at[0]),
        pltpu.make_async_copy(hid_keep, hid_keep_hbm, out_sems.at[1]),
        pltpu.make_async_copy(pre.at[0:4], pre_hbm.at[0:4], out_sems.at[2]),
    ]
    for copy in outs:
        copy.start()
    for at, whole in enumerate((normed[...].T, att[...])):
        rows = whole.reshape(8, 2, 48, 512)
        turned_keep[at] = jnp.where(c == 0, rows[:, 0], rows[:, 1])
        turned_send[at] = jnp.where(c == 0, rows[:, 1], rows[:, 0])
    wide = middle[...]
    scale = lax.rsqrt(jnp.mean(wide * wide, axis=-1, keepdims=True) + EPS)
    unit = wide * scale
    incoming = normed_grad[...]
    direct = incoming * gain
    inward = scale * (direct - unit * jnp.mean(direct * unit, axis=-1, keepdims=True))
    grad = cot[...].astype(f32) + inward
    middle_grad[...] = grad
    low = grad.astype(bf16)
    pre[4] = low
    outs.append(pltpu.make_async_copy(pre.at[4], pre_hbm.at[4], out_sems.at[3]))
    outs[3].start()
    for other, dest in enumerate((near_grad, far_grad)):
        row = pl.multiple_of(jnp.bitwise_xor(xs, other) * 384, 128)
        dest[...] = dot(w_out[pl.ds(row, 384)], low, 1, 1).astype(bf16)
    result[...] = total[...].astype(bf16)
    for copy in outs:
        copy.wait()


def forward(place, att_near, att_far, x, cot, small, near, far):
    wide = jax.ShapeDtypeStruct((512, 768), f32)
    half = jax.ShapeDtypeStruct((384, 512), bf16)
    hidden = jax.ShapeDtypeStruct((4, 512, 384), bf16)
    turned = jax.ShapeDtypeStruct((2, 8, 48, 512), bf16)
    return pl.pallas_call(
        forward_kernel,
        out_shape=(
            hidden, hidden, jax.ShapeDtypeStruct((5, 512, 768), bf16), turned, turned,
            jax.ShapeDtypeStruct((512, 768), bf16), wide, half, half,
        ),
        in_specs=[SCALARS, ANY, ANY, FULL, FULL, FULL] + [ANY] * 19,
        out_specs=(ANY, ANY, ANY) + (FULL,) * 6,
        scratch_shapes=[
            pltpu.VMEM((768, 768), bf16),
            pltpu.VMEM((4, 768, 768), bf16),
            pltpu.VMEM((64, 48, 768), bf16),
            pltpu.VMEM((4, 512, 384), bf16),
            pltpu.VMEM((4, 512, 384), bf16),
            pltpu.VMEM((5, 512, 768), bf16),
            pltpu.VMEM((512, 768), f32),
            pltpu.VMEM((512, 768), f32),
            pltpu.VMEM((512, 768), f32),
            pltpu.VMEM((512, 768), f32),
            pltpu.VMEM((512, 768), bf16),
            pltpu.VMEM((768, 512), bf16),
            pltpu.SemaphoreType.DMA((4, 16)),
            pltpu.SemaphoreType.DMA((2,)),
            pltpu.SemaphoreType.DMA((4,)),
        ],
        compiler_params=params(),
        cost_estimate=cost(8_500_000_000, 20_000_000, 512 * 3072),
        name="forward",
    )(place, att_near, att_far, x, cot, small, *near, *far)


def contract_grad_kernel(place, hid, hid_far, cot, cot_far, send, keep):
    made = dot(hid[0], cot[...], 0, 0) + dot(hid_far[0], cot_far[...], 0, 0)
    made = made.astype(bf16).reshape(2, 2, 2, 48, 768)
    send[...] = jnp.where(place[3] == 0, made[:, 1], made[:, 0])
    keep[...] = jnp.where(place[3] == 0, made[:, 0], made[:, 1])


def contract_weight_grad(place, hid, hid_far, cot, cot_far):
    shape = jax.ShapeDtypeStruct((8, 2, 48, 768), bf16)
    spec = pl.BlockSpec((2, 2, 48, 768), lambda j: (j, 0, 0, 0))
    chunk = pl.BlockSpec((1, 512, 384), lambda j: (j, 0, 0))
    whole = pl.BlockSpec((512, 768), lambda j: (0, 0))
    return pl.pallas_call(
        contract_grad_kernel,
        out_shape=(shape, shape),
        grid=(4,),
        in_specs=[SCALARS, chunk, chunk, whole, whole],
        out_specs=(spec, spec),
        compiler_params=params(),
        cost_estimate=cost(2 * 512 * 3072 * 768, 9_000_000),
        name="contract_weight_grad",
    )(place, hid, hid_far, cot, cot_far)


def expand_grad_kernel(place, turned, turned_far, pre, pre_far, b_send, b_keep, c_send, c_keep):
    step = pl.program_id(0)

    def made(at):
        near = dot(turned[at].reshape(384, 512), pre[0], 1, 0)
        return (near + dot(turned_far[at].reshape(384, 512), pre_far[0], 1, 0)).astype(bf16)

    @pl.when(step < 3)
    def _():
        rows = made(0).reshape(4, 2, 48, 768)
        b_send[:, 0] = jnp.where(place[1] == 0, rows[:, 1], rows[:, 0])
        b_keep[:, 0] = jnp.where(place[1] == 0, rows[:, 0], rows[:, 1])

    def by_low(rows):
        rows = rows.reshape(2, 2, 2, 48, 768)
        low = place[0] % 2
        c_send[:, :, 0] = jnp.where(low == 0, rows[:, 1], rows[:, 0])
        c_keep[:, :, 0] = jnp.where(low == 0, rows[:, 0], rows[:, 1])

    @pl.when(step == 3)
    def _():
        by_low(made(0))

    @pl.when(step == 4)
    def _():
        by_low(made(1))


def expand_weight_grad(place, turned, turned_far, pre, pre_far):
    first = jax.ShapeDtypeStruct((4, 3, 48, 768), bf16)
    second = jax.ShapeDtypeStruct((2, 2, 2, 48, 768), bf16)
    first_spec = pl.BlockSpec((4, 1, 48, 768), lambda j: (0, jnp.minimum(j, 2), 0, 0))
    second_spec = pl.BlockSpec((2, 2, 1, 48, 768), lambda j: (0, 0, jnp.maximum(j - 3, 0), 0, 0))
    whole = pl.BlockSpec((2, 8, 48, 512), lambda j: (0, 0, 0, 0))
    chunk = pl.BlockSpec((1, 512, 768), lambda j: (j, 0, 0))
    return pl.pallas_call(
        expand_grad_kernel,
        out_shape=(first, first, second, second),
        grid=(5,),
        in_specs=[SCALARS, whole, whole, chunk, chunk],
        out_specs=(first_spec, first_spec, second_spec, second_spec),
        compiler_params=params(),
        cost_estimate=cost(2 * 512 * 768 * 3840, 12_000_000),
        name="expand_weight_grad",
    )(place, turned, turned_far, pre, pre_far)


def place_grads(whole, grad, sems):
    copies = []
    for head in range(6):
        dest = grad.at[head * 192 : head * 192 + 192]
        copies.append(pltpu.make_async_copy(whole.at[head, 0:192], dest, sems.at[head]))
        copies[-1].start()
    return copies


def weight_grad_kernel(place, mine, other, whole, near, far, grad, bias, sems, bias_sem):
    copies = place_grads(whole, grad, sems)
    copies.append(pltpu.make_async_copy(whole.at[5, 192:208, 0:128], bias, bias_sem))
    copies[-1].start()
    for copy in copies:
        copy.wait()
    for kind, rows, dest in ((place[2], mine, near), (1 - place[2], other, far)):
        spot = iota((384, 128), 0) % 48
        bucket = ((iota((384, 128), 0) // 48) * 2 + kind) * 2 + spot // 6
        chosen = jnp.where((iota((384, 128), 1) == bucket) & (spot < 12), 1.0, 0.0)
        per_head = dot(chosen.astype(bf16), bias[0:8], 1, 1)
        pattern = (iota((384, 8), 1) == (iota((384, 8), 0) % 48) % 6).astype(f32)
        column = jnp.sum(per_head * pattern, axis=1, keepdims=True)
        side = jnp.where(iota((384, 128), 1) == 0, column, 0.0)
        dest[:, :, 1152:1280] = side.astype(bf16).reshape(8, 48, 128)
        left = rows[...].reshape(384, 1024)
        for col in range(0, 1152, 384):
            made = dot(left, grad[col : col + 384], 1, 1)
            dest[:, :, col : col + 384] = made.astype(bf16).reshape(8, 48, 384)


def weight_grad(place, mine, other, whole):
    owned = jax.ShapeDtypeStruct((8, 48, 1280), bf16)
    return pl.pallas_call(
        weight_grad_kernel,
        out_shape=(owned, owned),
        in_specs=[SCALARS, FULL, FULL, ANY],
        out_specs=(FULL,) * 2,
        scratch_shapes=[
            pltpu.VMEM((1152, 1024), bf16),
            pltpu.VMEM((16, 128), bf16),
            pltpu.SemaphoreType.DMA((6,)),
            pltpu.SemaphoreType.DMA,
        ],
        compiler_params=params(),
        cost_estimate=cost(2 * 1024 * 768 * 1152, 6_000_000),
        name="weight_grad",
    )(place, mine, other, whole)


def project_back_kernel(place, *refs):
    (w_near, w_far), whole, refs = narrow_blocks(refs[:10]), refs[10], refs[11:]
    part_near, part_far, w, grad, sems, qsems = refs
    x = place[3]
    copies = place_blocks(place, w_near, w_far, w, sems) + place_grads(whole, grad, qsems)
    for copy in copies:
        copy.wait()
    for other, dest in ((1, part_far), (0, part_near)):
        start = pl.multiple_of(jnp.bitwise_xor(x, other) * 512, 512)
        dest[...] = dot(grad[:, pl.ds(start, 512)], w[:, 0:1152], 0, 1).astype(bf16)


def project_back(place, blocks, whole):
    part = jax.ShapeDtypeStruct((512, 768), bf16)
    return pl.pallas_call(
        project_back_kernel,
        out_shape=(part, part),
        in_specs=[SCALARS] + [ANY] * 11,
        out_specs=(FULL,) * 2,
        scratch_shapes=[
            pltpu.VMEM((768, 1280), bf16),
            pltpu.VMEM((1152, 1024), bf16),
            pltpu.SemaphoreType.DMA((16,)),
            pltpu.SemaphoreType.DMA((6,)),
        ],
        compiler_params=params(),
        cost_estimate=pl.CostEstimate(flops=20_000_000_000, bytes_accessed=10_000_000, transcendentals=0),
        name="project_back",
    )(place, *blocks, whole)


def finish_kernel(place, a_near, a_far, g_near, g_far, qw, kw, vw, gain, contract, q, k, v, gain_grad, bias):
    swapped = place[3] == 1

    def ordered(near, far):
        near, far = near[...].astype(f32), far[...].astype(f32)
        return jnp.where(swapped, far, near), jnp.where(swapped, near, far)

    for half, wide in enumerate(ordered(a_near, a_far)):
        for at in range(2):
            row = half * 96 + at * 48
            contract[row : row + 48] = wide[at]
    first, second = ordered(g_near, g_far)
    for at, dest in enumerate((q, k, v)):
        for half, wide in enumerate((first, second)):
            for head in range(6):
                column = head * 192 + at * 64
                spot = half * 384 + head * 64
                dest[:, spot : spot + 64] = wide[:, column : column + 64]
    joint = q[...] * qw[...].astype(f32) + k[...] * kw[...].astype(f32) + v[...] * vw[...].astype(f32)
    summed = jnp.broadcast_to(jnp.sum(joint, axis=1, keepdims=True), (48, 128))
    blank = jnp.zeros((80, 128), f32)
    turned = jnp.concatenate([summed, blank], axis=0).T
    gain_grad[...] = turned[0:1, 0:48] / gain[...].astype(f32)
    first = jnp.concatenate([first[:, 1152:1280], blank], axis=0).T
    second = jnp.concatenate([second[:, 1152:1280], blank], axis=0).T
    for row in range(2):
        cols = slice(row * 6, row * 6 + 6)
        bias[row : row + 1, 0:6] = first[0:1, cols]
        bias[row : row + 1, 6:12] = second[0:1, cols]


def finish(place, a_near, a_far, g_near, g_far, qw, kw, vw, gain):
    full = jax.ShapeDtypeStruct((48, 768), f32)
    return pl.pallas_call(
        finish_kernel,
        out_shape=(
            jax.ShapeDtypeStruct((192, 768), f32),
            full, full, full, jax.ShapeDtypeStruct((1, 48), f32), jax.ShapeDtypeStruct((2, 12), f32),
        ),
        in_specs=[SCALARS] + [FULL] * 8,
        out_specs=(FULL,) * 6,
        compiler_params=params(),
        cost_estimate=cost(1000, 1_000_000),
        name="finish",
    )(place, a_near, a_far, g_near, g_far, qw, kw, vw, gain.reshape(1, 48))


def finish_wide_kernel(
    place, x, small, near, far, middle_grad, b_near, b_far, up, gain, result, expand, output, gain_grad
):
    input_grad_kernel(place, x, small, near, far, middle_grad, result)
    summed = b_near[...].astype(f32) + b_far[...].astype(f32)
    joint = jnp.zeros((48, 768), f32)
    for at in range(4):
        cols = slice(at * 768, at * 768 + 768)
        expand[:, cols] = summed[at]
        joint = joint + summed[at] * up[:, cols].astype(f32)
    output[...] = summed[4]
    column = jnp.broadcast_to(jnp.sum(joint, axis=1, keepdims=True), (48, 128))
    turned = jnp.concatenate([column, jnp.zeros((80, 128), f32)], axis=0).T
    gain_grad[...] = turned[0:1, 0:48] / gain[...].astype(f32)


def finish_wide(place, x, small, near, far, middle_grad, b_near, b_far, up, gain):
    return pl.pallas_call(
        finish_wide_kernel,
        out_shape=(
            jax.ShapeDtypeStruct((512, 768), bf16), jax.ShapeDtypeStruct((48, 3072), f32),
            jax.ShapeDtypeStruct((48, 768), f32), jax.ShapeDtypeStruct((1, 48), f32),
        ),
        in_specs=[SCALARS] + [FULL] * 9,
        out_specs=(FULL,) * 4,
        compiler_params=params(),
        cost_estimate=cost(1000, 2_000_000),
        name="finish_wide",
    )(place, x, small, near, far, middle_grad, b_near, b_far, up, gain.reshape(1, 48))


def input_grad_kernel(place, x, small, near, far, middle_grad, result):
    for row in range(0, 512, 256):
        rows = slice(row, row + 256)
        wide = x[rows].astype(f32)
        scale = lax.rsqrt(jnp.mean(wide * wide, axis=-1, keepdims=True) + EPS)
        unit = wide * scale
        direct = (near[rows].astype(f32) + far[rows].astype(f32)) * small[0:1]
        inward = scale * (direct - unit * jnp.mean(direct * unit, axis=-1, keepdims=True))
        result[rows] = (middle_grad[rows] + inward).astype(bf16)


def swap(array, axis, bit):
    count = lax.axis_size(axis)
    return lax.ppermute(array, axis, [(i, i ^ bit) for i in range(count)])


def swap_both(array):
    pairs = [(i * 2 + j, (i ^ Y) * 2 + 1 - j) for i in range(lax.axis_size("fsdp")) for j in range(2)]
    return lax.ppermute(array, ("fsdp", "seq"), pairs)


CORE, Y, Z = 1, 2, 4


def after(value, *others):
    return lax.optimization_barrier((value, *others))[0]


class Line:
    def __init__(self, place):
        self.place = place

    def wait(self, *arrays):
        self.place = after(self.place, *arrays)

    def run(self, kernel, *args):
        made = kernel(self.place, *args)
        self.wait(jax.tree.leaves(made)[0])
        return made


def gather_part(array, part, own, now):
    _, dims, gone = part
    for axis in reversed(range(len(dims))):
        if dims[axis] == now:
            array = lax.dynamic_index_in_dim(array, 1 - own[now], axis, keepdims=False)
        elif dims[axis] in gone:
            array = lax.dynamic_index_in_dim(array, own[dims[axis]], axis, keepdims=False)
    return array.astype(f32)


def total(line, parts, own, now=None):
    arrays = after([part[0] for part in parts], line.place)
    made = None
    for array, part in zip(arrays, parts):
        term = gather_part(array, part, own, now)
        made = term if made is None else made + term
    made = lax.optimization_barrier(made.astype(bf16))
    line.wait(made)
    return made


def keep(parts, now, got):
    _, dims, gone = parts[0]
    left = tuple(dim for dim in dims if dim not in gone and dim != now)
    return [(a, d, g + (now,)) for a, d, g in parts] + [(got, left, ())]


def local_split(
    layer_input, query_weight, key_weight, value_weight, output_weight, expand_weight,
    contract_weight, attention_gain, feedforward_gain, bias_table, valid_len, instr_len, pair_flag,
    cotangent,
):
    owner, x = lax.axis_index("fsdp"), lax.axis_index("seq")
    z, y, c = owner // 4, (owner // 2) % 2, owner % 2
    where = jnp.stack([z, y, c, x]).astype(jnp.int32)
    line = Line(where)
    tokens, cot = layer_input[0], cotangent[0]

    def by_z(array):
        return swap(array, "fsdp", Z)

    def by_zz(array):
        return swap(array, "fsdp", 2 * Z)

    def by_y(array):
        return swap(array, "fsdp", Y)

    def by_core(array):
        return swap(array, "fsdp", CORE)

    def by_x(array):
        return swap(array, "seq", 1)

    shard = line.run(
        narrow_shard, query_weight, key_weight, value_weight, attention_gain, feedforward_gain, bias_table
    )
    a2, a1, b0 = by_zz(shard), by_z(shard), by_y(shard)
    x_far, cot_far = by_x(tokens), by_core(cot)
    rest, full = line.run(wide_shard, expand_weight, output_weight, contract_weight)
    a2, a1, b0, rest, cot_far = lax.optimization_barrier((a2, a1, b0, rest, cot_far))
    turned, b2 = by_z(jnp.stack([a2, b0])), by_y(a2)
    four = by_core(jnp.stack([shard, b0, a1, a2]))
    z2, z1, y0 = by_zz(rest), by_z(rest), by_y(rest)
    lens = jnp.stack([valid_len[0], instr_len[0], pair_flag[0]])
    place = jnp.concatenate([where, lens])
    turned, b2, x_far, line.place = lax.optimization_barrier((turned, b2, x_far, place))
    b3 = by_y(turned[0])
    three = by_core(jnp.stack([turned[0], turned[1], b2]))
    last = by_core(b3)
    z1, z2, y0, last, three = lax.optimization_barrier((z1, z2, y0, last, three))
    z3, y2 = by_z(z2), by_y(z2)
    sides = jnp.stack([z1[5:], z2[5:], y0[5:]])
    sides_a = by_x(sides)
    narrow = [shard, b0, a1, a2, turned, b2, b3, four, three, last]

    line.wait(sides)
    qkv, normed_kept, normed_sent, small, table, tiles = line.run(project, tokens, x_far, narrow)
    line.place, z3, y2, sides_a = lax.optimization_barrier((line.place, z3, y2, sides_a))
    y3 = by_y(z3)
    y1 = jnp.concatenate([y0, sides_a[2]], axis=0)
    sides, trio = jnp.stack([z3[5:], y2[5:]]), jnp.stack([y0, z1, z2])
    line.wait(y1, sides, trio)
    y1, sides_b, far_full, far_three = by_z(y1), by_x(sides), by_core(full), by_core(trio)
    out_theirs, kept_theirs, inverse_theirs = line.run(attend, table, tiles, qkv, False)
    line.place, y3, sides_b, far_full, far_three, out_theirs = lax.optimization_barrier(
        (line.place, y3, sides_b, far_full, far_three, out_theirs)
    )
    two = jnp.stack([z3, y2])
    line.wait(two)
    out_got, sides_c, far_two = by_x(out_theirs), by_x(y3[5:]), by_core(two)
    out_mine, kept_mine, inverse_mine = line.run(attend, table, tiles, qkv, True)
    out_mine, y1, out_got, sides_c, far_two, y3, sides_a, sides_b = lax.optimization_barrier(
        (out_mine, y1, out_got, sides_c, far_two, y3, sides_a, sides_b)
    )
    near = [full, y0, z1, z2, z3, y2, y1, y3, sides_a, sides_b, sides_c]
    far = [far_full, far_three, far_two] + [by_core(block) for block in (y1, y3, sides_a, sides_b, sides_c)]
    hid, hid_sent, pre, turned, turned_sent, layer_output, middle_grad, grad_mine, grad_sent = line.run(
        forward, out_mine, out_got, tokens, cot, small, near, far
    )
    hid_far, grad_theirs, pre_far, turned_far = by_core(hid_sent), by_x(grad_sent), by_core(pre), by_core(turned_sent)

    own = {"high": z // 2, "low": z % 2, "y": y, "x": x}

    def parts(kept, got, *dims):
        lead = tuple({"high": 2, "low": 2, "y": 2}[dim] for dim in dims if dim != "n")
        shape = lead + kept.shape[-3:] if "n" in dims else lead + kept.shape[-2:]
        return [(array.reshape(shape), dims, ()) for array in (kept, got)]

    carry = line.run(
        lambda place: attend_back(place, grad_mine, out_mine, inverse_mine, qkv, kept_mine, (), True)
    )
    line.wait(grad_theirs)
    b_sent, b_kept, c_sent, c_kept = line.run(expand_weight_grad, turned, turned_far, pre, pre_far)
    b_got, c_got = by_y(b_sent), by_z(c_sent)
    b_parts = parts(b_kept, b_got, "high", "low", "n")
    c_parts = parts(c_kept, c_got, "high", "y", "n")
    sent, kept = line.run(contract_weight_grad, hid, hid_far, cot, cot_far)
    a_got = by_x(sent)
    a_parts = parts(kept, a_got, "high", "low", "y", "n")
    whole = line.run(
        lambda place: attend_back(
            place, grad_theirs, out_theirs, inverse_theirs, qkv, kept_theirs, carry, False
        )
    )
    b_got = by_z(total(line, b_parts, own, "low"))
    b_parts = keep(b_parts, "low", b_got)
    c_got = by_y(total(line, c_parts, own, "y"))
    c_parts = keep(c_parts, "y", c_got)
    g_near, g_far = line.run(weight_grad, normed_kept, normed_sent, whole)
    g_parts = parts(g_near, by_core(g_far), "high", "low", "y")
    line.wait(a_got, b_got, c_got)
    part_near, part_far = line.run(project_back, narrow, whole)
    part_got = by_x(part_far)
    g_parts = keep(g_parts, "low", by_z(total(line, g_parts, own, "low")))
    a_parts = keep(a_parts, "y", by_y(total(line, a_parts, own, "y")))
    b_parts = keep(b_parts, "high", by_zz(total(line, b_parts, own, "high")))
    c_parts = keep(c_parts, "high", by_zz(total(line, c_parts, own, "high")))
    a_parts = keep(a_parts, "low", by_z(total(line, a_parts, own, "low")))
    g_parts = keep(g_parts, "y", by_y(total(line, g_parts, own, "y")))
    b_low = jnp.concatenate([total(line, b_parts, own), total(line, c_parts, own)], axis=0)
    b_low = lax.optimization_barrier(b_low)
    b_other = by_x(b_low)
    line.wait(b_low)
    a_parts = keep(a_parts, "high", by_zz(total(line, a_parts, own, "high")))
    g_parts = keep(g_parts, "high", by_zz(total(line, g_parts, own, "high")))
    result, expand_sum, output_sum, gain_two = line.run(
        finish_wide, tokens, small, part_near, part_got, middle_grad, b_low, b_other, expand_weight, feedforward_gain
    )
    a_low = total(line, a_parts, own)
    a_other = by_x(a_low)
    g_low = total(line, g_parts, own)
    g_other = by_x(g_low)
    contract_sum, *grads, gain_one, bias_grad = line.run(
        finish, a_low, a_other, g_low, g_other, query_weight, key_weight, value_weight, attention_gain
    )
    return (
        layer_output[None], result[None], gain_one[0], gain_two[0], *grads,
        output_sum, expand_sum, contract_sum, bias_grad,
    )


def bucket_table(query_pos, key_pos):
    offset = key_pos[None, :] - query_pos[:, None]
    distance = jnp.abs(offset)
    beyond = jnp.zeros_like(distance)
    for far_edge in far_edges:
        beyond = beyond + (distance >= far_edge).astype(jnp.int32)
    nearby = jnp.where(distance < 8, distance, 8 + beyond)
    return nearby + 16 * (offset > 0).astype(jnp.int32)


def visible_keys(query_pos, key_pos, valid_len, instr_len, pair_flag):
    in_valid = key_pos[None, None, :] < valid_len[:, None, None]
    guarded = (
        (pair_flag[:, None, None] == 1)
        & (query_pos[None, :, None] < instr_len[:, None, None])
        & (key_pos[None, None, :] >= instr_len[:, None, None])
    )
    return in_valid & jnp.logical_not(guarded)


def rms_scale(values):
    return lax.rsqrt(jnp.mean(values * values, axis=-1, keepdims=True) + EPS)


def norm_back(values, scale, gain, grad_out):
    normed = values * scale
    grad_normed = grad_out * gain
    grad_values = scale * (
        grad_normed - normed * jnp.mean(grad_normed * normed, axis=-1, keepdims=True)
    )
    return (grad_values, jnp.sum(grad_out * normed, axis=(0, 1)))


def gelu_tanh(values):
    return jax.nn.gelu(values, approximate=True)


def local(
    layer_input,
    query_weight,
    key_weight,
    value_weight,
    output_weight,
    expand_weight,
    contract_weight,
    attention_gain,
    feedforward_gain,
    bias_table,
    valid_len,
    instr_len,
    pair_flag,
    cotangent,
):
    f32 = jnp.float32
    bf16 = jnp.bfloat16
    row_count, local_len, model_width = layer_input.shape
    head_count = bias_table.shape[1]
    head_size = model_width // head_count
    full_len = local_len * lax.axis_size("seq")
    local_start = lax.axis_index("seq") * local_len
    query_pos = local_start + jnp.arange(local_len, dtype=jnp.int32)
    key_pos = jnp.arange(full_len, dtype=jnp.int32)
    buckets = bucket_table(query_pos, key_pos)
    onehot = buckets[:, :, None] == jnp.arange(BUCKETS, dtype=jnp.int32)[None, None, :]
    visible = visible_keys(query_pos, key_pos, valid_len, instr_len, pair_flag)
    input_wide = layer_input.astype(f32)

    def attend_probs(queries, key_heads, table_full):
        rel_bias = jnp.einsum(
            "ijb,bh->hij", onehot.astype(bf16), table_full, preferred_element_type=f32
        )
        raw_scores = jnp.einsum("rihe,rjhe->rhij", queries, key_heads, preferred_element_type=f32)
        scores = jnp.where(visible[:, None], raw_scores + rel_bias[None], -1000000000.0)
        row_peak = jnp.max(scores, axis=-1, keepdims=True)
        log_total = row_peak + jnp.log(jnp.sum(jnp.exp(scores - row_peak), axis=-1, keepdims=True))
        return (jnp.exp(scores - log_total), log_total[..., 0])

    def forward(weights):
        (
            query_full,
            key_full,
            value_full,
            output_full,
            expand_full,
            contract_full,
            gain_one,
            gain_two,
            table_full,
        ) = weights
        scale_one = rms_scale(input_wide)
        normed_low = (input_wide * scale_one * gain_one.astype(f32)).astype(bf16)

        def project(weight):
            return jnp.einsum("rtd,de->rte", normed_low, weight, preferred_element_type=f32).astype(
                bf16
            )

        query_low = project(query_full)
        key_low = project(key_full)
        value_low = project(value_full)
        key_all, value_all = (
            lax.all_gather(key_low, "seq", axis=1, tiled=True),
            lax.all_gather(value_low, "seq", axis=1, tiled=True),
        )
        queries = query_low.reshape(row_count, local_len, head_count, head_size)
        key_heads = key_all.reshape(row_count, full_len, head_count, head_size)
        value_heads = value_all.reshape(row_count, full_len, head_count, head_size)
        probs, log_total = attend_probs(queries, key_heads, table_full)
        probs_low = probs.astype(bf16)
        attended = jnp.einsum("rhij,rjhe->rihe", probs_low, value_heads, preferred_element_type=f32)
        attended = attended.reshape(row_count, local_len, model_width).astype(bf16)
        middle = input_wide + jnp.einsum(
            "rtd,de->rte", attended, output_full, preferred_element_type=f32
        )
        scale_two = rms_scale(middle)
        normed_two = (middle * scale_two * gain_two.astype(f32)).astype(bf16)
        hidden_pre = jnp.einsum("rtd,df->rtf", normed_two, expand_full, preferred_element_type=f32)
        hidden_low = gelu_tanh(hidden_pre).astype(bf16)
        result = middle + jnp.einsum(
            "rtf,fd->rtd", hidden_low, contract_full, preferred_element_type=f32
        )
        return (
            result,
            scale_one,
            normed_low,
            queries,
            key_heads,
            value_heads,
            probs,
            probs_low,
            log_total,
            attended,
            middle,
            scale_two,
            normed_two,
            hidden_pre,
            hidden_low,
        )

    stored = forward(
        (
            lax.all_gather(query_weight, "fsdp", axis=0, tiled=True),
            lax.all_gather(key_weight, "fsdp", axis=0, tiled=True),
            lax.all_gather(value_weight, "fsdp", axis=0, tiled=True),
            lax.all_gather(output_weight, "fsdp", axis=0, tiled=True),
            lax.all_gather(expand_weight, "fsdp", axis=0, tiled=True),
            lax.all_gather(contract_weight, "fsdp", axis=0, tiled=True),
            lax.all_gather(attention_gain, "fsdp", axis=0, tiled=True),
            lax.all_gather(feedforward_gain, "fsdp", axis=0, tiled=True),
            lax.all_gather(bias_table, "fsdp", axis=0, tiled=True),
        )
    )
    layer_output = stored[0].astype(bf16)
    gathered = (
        lax.all_gather(query_weight, "fsdp", axis=0, tiled=True),
        lax.all_gather(key_weight, "fsdp", axis=0, tiled=True),
        lax.all_gather(value_weight, "fsdp", axis=0, tiled=True),
        lax.all_gather(output_weight, "fsdp", axis=0, tiled=True),
        lax.all_gather(expand_weight, "fsdp", axis=0, tiled=True),
        lax.all_gather(contract_weight, "fsdp", axis=0, tiled=True),
        lax.all_gather(attention_gain, "fsdp", axis=0, tiled=True),
        lax.all_gather(feedforward_gain, "fsdp", axis=0, tiled=True),
        lax.all_gather(bias_table, "fsdp", axis=0, tiled=True),
    )
    kept = forward(gathered)
    (
        unused,
        scale_one,
        normed_low,
        queries,
        key_heads,
        value_heads,
        probs,
        probs_low,
        log_total,
        attended,
        middle,
        scale_two,
        normed_two,
        hidden_pre,
        hidden_low,
    ) = kept
    (
        query_full,
        key_full,
        value_full,
        output_full,
        expand_full,
        contract_full,
        gain_one,
        gain_two,
        table_full,
    ) = gathered
    gain_one_wide = gain_one.astype(f32)
    gain_two_wide = gain_two.astype(f32)
    contract_grad = jnp.einsum("rtf,rtd->fd", hidden_low, cotangent, preferred_element_type=f32)
    grad_hidden = jnp.einsum("rtd,fd->rtf", cotangent, contract_full, preferred_element_type=f32)
    gelu_pull = jax.vjp(gelu_tanh, hidden_pre)[1]
    grad_pre = gelu_pull(grad_hidden)[0].astype(bf16)
    expand_grad = jnp.einsum("rtd,rtf->df", normed_two, grad_pre, preferred_element_type=f32)
    grad_normed_two = jnp.einsum("rtf,df->rtd", grad_pre, expand_full, preferred_element_type=f32)
    grad_middle_norm, gain_two_grad = norm_back(middle, scale_two, gain_two_wide, grad_normed_two)
    grad_middle = cotangent.astype(f32) + grad_middle_norm
    grad_branch = grad_middle.astype(bf16)
    output_grad = jnp.einsum("rtd,rte->de", attended, grad_branch, preferred_element_type=f32)
    grad_attended = jnp.einsum(
        "rte,de->rtd", grad_branch, output_full, preferred_element_type=f32
    ).astype(bf16)
    grad_attended = grad_attended.reshape(row_count, local_len, head_count, head_size)
    grad_probs = jnp.einsum(
        "rihe,rjhe->rhij", grad_attended, value_heads, preferred_element_type=f32
    )
    row_delta = jnp.sum(probs * grad_probs, axis=-1)
    grad_scores = probs * (grad_probs - row_delta[..., None])
    bias_part = jnp.einsum(
        "hij,ijb->bh",
        jnp.sum(grad_scores, axis=0),
        onehot.astype(f32),
        precision=lax.Precision.HIGHEST,
    )
    scores_low = grad_scores.astype(bf16)
    grad_queries = jnp.einsum("rhij,rjhe->rihe", scores_low, key_heads, preferred_element_type=f32)
    grad_queries = grad_queries.reshape(row_count, local_len, model_width).astype(bf16)
    value_partial = jnp.einsum(
        "rhij,rihe->rjhe", probs_low, grad_attended, preferred_element_type=f32
    ).reshape(row_count, full_len, model_width)
    key_partial = jnp.einsum(
        "rhij,rihe->rjhe", scores_low, queries, preferred_element_type=f32
    ).reshape(row_count, full_len, model_width)
    key_summed, value_summed = (
        lax.psum_scatter(
            key_partial.astype(jnp.bfloat16), "seq", scatter_dimension=1, tiled=True
        ).astype(jnp.float32),
        lax.psum_scatter(
            value_partial.astype(jnp.bfloat16), "seq", scatter_dimension=1, tiled=True
        ).astype(jnp.float32),
    )
    grad_keys = key_summed.astype(bf16)
    grad_values = value_summed.astype(bf16)
    query_part = jnp.einsum("rtd,rte->de", normed_low, grad_queries, preferred_element_type=f32)
    key_part = jnp.einsum("rtd,rte->de", normed_low, grad_keys, preferred_element_type=f32)
    value_part = jnp.einsum("rtd,rte->de", normed_low, grad_values, preferred_element_type=f32)
    grad_normed_one = jnp.einsum(
        "rte,de->rtd", grad_queries, query_full, preferred_element_type=f32
    )
    grad_normed_one = grad_normed_one + jnp.einsum(
        "rte,de->rtd", grad_keys, key_full, preferred_element_type=f32
    )
    grad_normed_one = grad_normed_one + jnp.einsum(
        "rte,de->rtd", grad_values, value_full, preferred_element_type=f32
    )
    grad_input_norm, gain_one_grad = norm_back(
        input_wide, scale_one, gain_one_wide, grad_normed_one
    )
    input_grad = (grad_middle + grad_input_norm).astype(bf16)
    owned = (
        lax.psum_scatter(
            query_part.astype(jnp.bfloat16), "fsdp", scatter_dimension=0, tiled=True
        ).astype(jnp.float32),
        lax.psum_scatter(
            key_part.astype(jnp.bfloat16), "fsdp", scatter_dimension=0, tiled=True
        ).astype(jnp.float32),
        lax.psum_scatter(
            value_part.astype(jnp.bfloat16), "fsdp", scatter_dimension=0, tiled=True
        ).astype(jnp.float32),
        lax.psum_scatter(
            output_grad.astype(jnp.bfloat16), "fsdp", scatter_dimension=0, tiled=True
        ).astype(jnp.float32),
        lax.psum_scatter(
            expand_grad.astype(jnp.bfloat16), "fsdp", scatter_dimension=0, tiled=True
        ).astype(jnp.float32),
        lax.psum_scatter(
            contract_grad.astype(jnp.bfloat16), "fsdp", scatter_dimension=0, tiled=True
        ).astype(jnp.float32),
        lax.psum_scatter(
            gain_one_grad.astype(jnp.bfloat16), "fsdp", scatter_dimension=0, tiled=True
        ).astype(jnp.float32),
        lax.psum_scatter(
            gain_two_grad.astype(jnp.bfloat16), "fsdp", scatter_dimension=0, tiled=True
        ).astype(jnp.float32),
        lax.psum_scatter(
            bias_part.astype(jnp.bfloat16), "fsdp", scatter_dimension=0, tiled=True
        ).astype(jnp.float32),
    )
    summed = (
        lax.psum(owned[0].astype(jnp.bfloat16), "seq").astype(jnp.float32),
        lax.psum(owned[1].astype(jnp.bfloat16), "seq").astype(jnp.float32),
        lax.psum(owned[2].astype(jnp.bfloat16), "seq").astype(jnp.float32),
        lax.psum(owned[3].astype(jnp.bfloat16), "seq").astype(jnp.float32),
        lax.psum(owned[4].astype(jnp.bfloat16), "seq").astype(jnp.float32),
        lax.psum(owned[5].astype(jnp.bfloat16), "seq").astype(jnp.float32),
        lax.psum(owned[6].astype(jnp.bfloat16), "seq").astype(jnp.float32),
        lax.psum(owned[7].astype(jnp.bfloat16), "seq").astype(jnp.float32),
        lax.psum(owned[8].astype(jnp.bfloat16), "seq").astype(jnp.float32),
    )
    (
        query_grad,
        key_grad,
        value_grad,
        output_sum,
        expand_sum,
        contract_sum,
        gain_one_sum,
        gain_two_sum,
        bias_grad,
    ) = summed
    return (
        layer_output,
        input_grad,
        gain_one_sum,
        gain_two_sum,
        query_grad,
        key_grad,
        value_grad,
        output_sum,
        expand_sum,
        contract_sum,
        bias_grad,
    )


def solution(mesh):
    in_specs = (
        P("fsdp", "seq", None),
        P("fsdp", None),
        P("fsdp", None),
        P("fsdp", None),
        P("fsdp", None),
        P("fsdp", None),
        P("fsdp", None),
        P("fsdp"),
        P("fsdp"),
        P("fsdp", None),
        P("fsdp"),
        P("fsdp"),
        P("fsdp"),
        P("fsdp", "seq", None),
    )
    out_specs = (
        P("fsdp", "seq", None),
        P("fsdp", "seq", None),
        P("fsdp"),
        P("fsdp"),
        P("fsdp", None),
        P("fsdp", None),
        P("fsdp", None),
        P("fsdp", None),
        P("fsdp", None),
        P("fsdp", None),
        P("fsdp", None),
    )
    split = mesh.shape["fsdp"] == 16 and mesh.shape["seq"] == 2
    step = local_split if split else local
    return jax.shard_map(step, mesh=mesh, in_specs=in_specs, out_specs=out_specs, check_vma=False)
```

```python
import functools
import itertools
import math

import jax
import jax.numpy as jnp
from jax import lax
from jax.experimental import pallas as pl
from jax.experimental.pallas import tpu as pltpu
from jax.sharding import PartitionSpec as P

f32 = jnp.float32
bf16 = jnp.bfloat16
BUCKETS = 32
EPS = 1e-06
far_edges = (12, 16, 23, 32, 46, 64, 91)
HIDDEN = -(2.0**30)
VMEM = 56 * 1024 * 1024
ANY = pl.BlockSpec(memory_space=pl.ANY)
FULL = pl.BlockSpec(memory_space=pltpu.VMEM)
SCALARS = pl.BlockSpec(memory_space=pltpu.SMEM)


def dot(left, right, left_dim, right_dim):
    return lax.dot_general(
        left, right, (((left_dim,), (right_dim,)), ((), ())), preferred_element_type=f32
    )


def params(limit=VMEM):
    return pltpu.CompilerParams(vmem_limit_bytes=limit)


def cost(flops, byte_count, exps=0):
    return pl.CostEstimate(flops=flops // 1000, bytes_accessed=byte_count // 1000, transcendentals=exps // 1000)


def small_cost():
    return pl.CostEstimate(flops=1000, bytes_accessed=1000, transcendentals=0)


def bucket_of(offset):
    distance = jnp.abs(offset)
    beyond = jnp.zeros_like(distance)
    for far_edge in far_edges:
        beyond = beyond + (distance >= far_edge).astype(jnp.int32)
    nearby = jnp.where(distance < 8, distance, 8 + beyond)
    return nearby + 16 * (offset > 0).astype(jnp.int32)


def iota(shape, dim):
    return lax.broadcasted_iota(jnp.int32, shape, dim)


def narrow_kernel(place, q, k, v, gain_one, gain_two, table, out, side):
    column = pl.multiple_of(place[3] * 384, 128)
    pieces = [weight[:, pl.ds(column, 384)] for weight in (q, k, v)]
    for pair in range(3):
        parts = [piece[:, at : at + 64] for at in (pair * 128, pair * 128 + 64) for piece in pieces]
        out[:, pair * 384 : pair * 384 + 384] = jnp.concatenate(parts, axis=1)
    side[...] = jnp.zeros((8, 128), f32)
    side[0:1, 0:48] = gain_one[...].astype(f32)
    side[1:2, 0:48] = gain_two[...].astype(f32)
    side[2:3, 0:12] = table[0:1].astype(f32)
    side[2:3, 12:24] = table[1:2].astype(f32)
    wide = jnp.concatenate([side[...], jnp.zeros((120, 128), f32)], axis=0).T
    out[:, 1152:1280] = wide[0:48].astype(bf16)


def narrow_shard(place, q, k, v, gain_one, gain_two, table):
    return pl.pallas_call(
        narrow_kernel,
        out_shape=jax.ShapeDtypeStruct((48, 1280), bf16),
        in_specs=[SCALARS] + [FULL] * 6,
        out_specs=FULL,
        scratch_shapes=[pltpu.VMEM((8, 128), f32)],
        compiler_params=params(),
        cost_estimate=small_cost(),
        name="narrow_shard",
    )(place, q, k, v, gain_one.reshape(1, 48), gain_two.reshape(1, 48), table)


def wide_kernel(place, expand, output, contract, out, full, sems):
    x = place[3]
    pieces = [(expand.at[:, at * 768 : at * 768 + 768], out.at[at]) for at in range(4)]
    pieces.append((output, out.at[4]))
    for at in range(2):
        row = pl.multiple_of(x * 96 + at * 48, 16)
        pieces.append((contract.at[pl.ds(row, 48)], out.at[5 + at]))
        row = pl.multiple_of((1 - x) * 96 + at * 48, 16)
        pieces.append((contract.at[pl.ds(row, 48)], full.at[7 + at]))
    copies = [pltpu.make_async_copy(*piece, sems.at[at]) for at, piece in enumerate(pieces)]
    for copy in copies:
        copy.start()
    for copy in copies:
        copy.wait()
    full[0:7] = out[...]


def wide_shard(place, expand, output, contract):
    return pl.pallas_call(
        wide_kernel,
        out_shape=(
            jax.ShapeDtypeStruct((7, 48, 768), bf16), jax.ShapeDtypeStruct((9, 48, 768), bf16),
        ),
        in_specs=[SCALARS, ANY, ANY, ANY],
        out_specs=(FULL, FULL),
        scratch_shapes=[pltpu.SemaphoreType.DMA((9,))],
        compiler_params=params(),
        cost_estimate=small_cost(),
        name="wide_shard",
    )(place, expand, output, contract)


def narrow_blocks(refs):
    shard, b0, a1, a2, turned, b2, b3, four, three, last = refs
    near = [shard, b0, a1, turned.at[1], a2, b2, turned.at[0], b3]
    far = [four.at[0], four.at[1], four.at[2], three.at[1], four.at[3], three.at[2], three.at[0], last]
    return near, far


def place_blocks(place, near, far, dest, sems):
    z, y, c = place[0], place[1], place[2]
    copies = []
    for turn in range(4):
        for dy in range(2):
            owner = ((jnp.bitwise_xor(z, turn) * 2) + jnp.bitwise_xor(y, dy)) * 2
            for other, source in enumerate((near, far)):
                row = pl.multiple_of((owner + jnp.bitwise_xor(c, other)) * 48, 16)
                copy = pltpu.make_async_copy(
                    source[turn * 2 + dy], dest.at[pl.ds(row, 48)], sems.at[len(copies)]
                )
                copy.start()
                copies.append(copy)
    return copies


def place_tokens(x, near, far, dest, sems, count):
    copies = []
    for other, source in enumerate((near, far)):
        row = pl.multiple_of(jnp.bitwise_xor(x, other) * count, count)
        copy = pltpu.make_async_copy(source, dest.at[pl.ds(row, count)], sems.at[other])
        copy.start()
        copies.append(copy)
    return copies


def first_query(place, mine):
    return (place[3] if mine else 1 - place[3]) * 512


def project_kernel(place, x_near, x_far, *refs):
    (w_near, w_far), refs = narrow_blocks(refs[:10]), refs[10:]
    qkv, kept, sent, small, table, tiles, normed, xs, w, sems, xsems = refs
    tokens = place_tokens(place[3], x_near, x_far, xs, xsems, 512)
    blocks = place_blocks(place, w_near, w_far, w, sems)
    for copy in tokens + blocks:
        copy.wait()
    side = w[:, 1152:1280].astype(f32).T
    small[...] = side[:8]
    gain = side[0:1]
    row = iota((768, 128), 0)
    spot = row % 48
    bucket = (row // 48) * 2 + spot // 12
    match = (iota((768, 128), 1) == bucket) & (spot < 24)
    values = jnp.where(match, w[:, 1154:1155].astype(f32), 0.0).astype(bf16)
    head = iota((8, 768), 0)
    chosen = ((iota((8, 768), 1) % 48) % 12 == place[3] * 6 + head) & (head < 6)
    made = dot(chosen.astype(bf16), values, 1, 0)
    table[...] = made
    lane = iota((128, 512), 1)
    spread = (bucket_of(jnp.where(lane < 128, -128 - lane, 384 - lane)) == iota((128, 512), 0)).astype(bf16)
    turned = dot(made.astype(bf16), spread, 1, 0)
    for head in range(6):
        for block, (low, high) in enumerate(((384, 0), (256, 384), (128, 256))):
            parts = [turned[head : head + 1, at : at + 128] for at in (low, high)]
            wide = jnp.broadcast_to(jnp.concatenate(parts, axis=1), (128, 256))
            rolled = pltpu.roll(wide, 0, 1, stride=1, stride_axis=0)
            tiles[head, block * 128 : block * 128 + 128] = rolled[:, 128:256]
    for row in range(0, 1024, 256):
        wide = xs[row : row + 256].astype(f32)
        scale = lax.rsqrt(jnp.mean(wide * wide, axis=-1, keepdims=True) + EPS)
        normed[row : row + 256] = (wide * scale * gain).astype(bf16)
    for col in range(0, 1152, 384):
        made = dot(w[:, col : col + 384], normed[...], 0, 1)
        qkv[col : col + 384] = made.astype(bf16)
    turned = normed[...].T.reshape(8, 2, 48, 1024)
    kept[...] = jnp.where(place[2] == 0, turned[:, 0], turned[:, 1])
    sent[...] = jnp.where(place[2] == 0, turned[:, 1], turned[:, 0])


def project(place, x_near, x_far, blocks):
    return pl.pallas_call(
        project_kernel,
        out_shape=(
            jax.ShapeDtypeStruct((1152, 1024), bf16),
            jax.ShapeDtypeStruct((8, 48, 1024), bf16),
            jax.ShapeDtypeStruct((8, 48, 1024), bf16),
            jax.ShapeDtypeStruct((8, 768), f32),
            jax.ShapeDtypeStruct((8, 128), f32),
            jax.ShapeDtypeStruct((6, 384, 128), f32),
        ),
        in_specs=[SCALARS] + [ANY] * 12,
        out_specs=(FULL,) * 6,
        scratch_shapes=[
            pltpu.VMEM((1024, 768), bf16),
            pltpu.VMEM((1024, 768), bf16),
            pltpu.VMEM((768, 1280), bf16),
            pltpu.SemaphoreType.DMA((16,)),
            pltpu.SemaphoreType.DMA((2,)),
        ],
        compiler_params=params(),
        cost_estimate=small_cost(),
        name="project",
    )(place, x_near, x_far, *blocks)


def attend_kernel(mine, place, table, tile, q, k, v, out, kept, inverse, ka, kt, qt, vt, s):
    head = pl.program_id(0)
    first, valid, instr, pair = first_query(place, mine), place[4], place[5], place[6]

    @pl.when(head == 0)
    def _():
        kt[64:128] = jnp.zeros((64, 1024), bf16)
        qt[64:128] = jnp.zeros((64, 512), bf16)
        row = iota((16, 1024), 0)
        key = iota((16, 1024), 1)
        extra = jnp.where(row < 8, (key // 128 == row).astype(f32), 0.0)
        extra = jnp.where(row == 8, jnp.where(key >= valid, HIDDEN, 0.0), extra)
        extra = jnp.where(row == 9, (key >= instr).astype(f32), extra)
        kt[64:80] = extra.astype(bf16)
        vt[64:80] = jnp.where(row == 0, 1.0, 0.0).astype(bf16)

    row = iota((16, 512), 0)
    query = iota((16, 512), 1) + first
    block = query // 128
    extra = jnp.where(row <= block - 2, table[head, 15], 0.0)
    extra = jnp.where(row >= block + 2, table[head, 31], extra)
    extra = jnp.where(row == 8, 1.0, extra)
    guarded = (query < instr) & (pair == 1)
    extra = jnp.where(row == 9, jnp.where(guarded, HIDDEN, 0.0), extra)
    extra = jnp.where(row > 9, 0.0, extra)
    qt[64:80] = extra.astype(bf16)
    qt[0:64] = q[...]
    kt[0:64] = k[...]
    vt[0:64] = v[...]
    ka[...] = kt[...].T
    s[128:1152] = dot(ka[...], qt[...], 1, 0)
    for part in range(4):
        base = pl.multiple_of(first + part * 128, 128)
        cols = slice(part * 128, part * 128 + 128)
        s[pl.ds(base, 384), cols] = s[pl.ds(base, 384), cols] + tile[0]
    scores = s[128:1152]
    peak = jnp.max(scores, axis=0, keepdims=True)
    weights = jnp.exp(scores - peak).astype(bf16)
    kept[0] = weights
    summed = dot(vt[...], weights, 1, 0)
    share = 1.0 / summed[64:65]
    out[...] = (summed[0:64] * share).astype(bf16)
    inverse[0] = share


def attend(place, table, tiles, qkv, mine):
    half = (lambda s: s[3]) if mine else (lambda s: 1 - s[3])
    grid = pltpu.PrefetchScalarGridSpec(
        num_scalar_prefetch=1,
        grid=(6,),
        in_specs=[
            SCALARS,
            pl.BlockSpec((1, 384, 128), lambda h, s: (h, 0, 0)),
            pl.BlockSpec((64, 512), lambda h, s: (3 * h, half(s))),
            pl.BlockSpec((64, 1024), lambda h, s: (3 * h + 1, 0)),
            pl.BlockSpec((64, 1024), lambda h, s: (3 * h + 2, 0)),
        ],
        out_specs=(
            pl.BlockSpec((64, 512), lambda h, s: (h, 0)),
            pl.BlockSpec((1, 1024, 512), lambda h, s: (h, 0, 0)),
            pl.BlockSpec((1, 1, 512), lambda h, s: (h, 0, 0)),
        ),
        scratch_shapes=[
            pltpu.VMEM((1024, 128), bf16),
            pltpu.VMEM((128, 1024), bf16),
            pltpu.VMEM((128, 512), bf16),
            pltpu.VMEM((80, 1024), bf16),
            pltpu.VMEM((1280, 512), f32),
        ],
    )
    return pl.pallas_call(
        functools.partial(attend_kernel, mine),
        out_shape=(
            jax.ShapeDtypeStruct((384, 512), bf16),
            jax.ShapeDtypeStruct((6, 1024, 512), bf16),
            jax.ShapeDtypeStruct((6, 1, 512), f32),
        ),
        grid_spec=grid,
        compiler_params=params(),
        cost_estimate=small_cost(),
        name="attend_mine" if mine else "attend_theirs",
    )(place, table, tiles, qkv, qkv, qkv)


def diagonal_sums(band):
    flip = (iota((128, 128), 0) + iota((128, 128), 1) == 127).astype(f32)
    rows = []
    for block in range(3):
        here = lax.dot_general(
            flip, band[block * 128 : block * 128 + 128], (((1,), (0,)), ((), ())),
            precision=lax.Precision.HIGHEST, preferred_element_type=f32,
        )
        wide = jnp.concatenate([here, jnp.zeros((128, 128), f32)], axis=1)
        rolled = pltpu.roll(wide, 0, 1, stride=1, stride_axis=0)
        rows.append(jnp.sum(rolled, axis=0, keepdims=True))
    return rows


def bucket_sums(diagonals, sides):
    total = sides
    for block in range(3):
        offset = block * 128 - 1 - iota((256, 128), 0)
        spread = (bucket_of(offset) == iota((256, 128), 1)).astype(f32)
        total = total + lax.dot_general(
            diagonals[block], spread, (((1,), (0,)), ((), ())),
            precision=lax.Precision.HIGHEST, preferred_element_type=f32,
        )
    return total


def attend_back_kernel(carried, mine, place, grad, out, inverse, q, k, v, kept, *refs):
    if carried:
        dq_in, dk_in, dv_in, band_in, far_in, whole, diagonals, sides, *refs = refs
    else:
        dq, dk, dv, band, far, *refs = refs
    va, vt, kt, gt, ds = refs
    first = first_query(place, mine)

    @pl.when(pl.program_id(0) == 0)
    def _():
        row = iota((16, 1024), 0)
        key = iota((16, 1024), 1)
        vt[64:128] = jnp.zeros((64, 1024), bf16)
        vt[64:80] = jnp.where(row < 2, 1.0, 0.0).astype(bf16)
        if carried:
            diagonals[...] = jnp.zeros_like(diagonals)
            sides[...] = jnp.zeros_like(sides)
        kt[64:80] = jnp.where(row < 8, (key // 128 == row).astype(f32), 0.0).astype(bf16)
        gt[64:128] = jnp.zeros((64, 512), bf16)
        ds[0:128] = jnp.zeros((128, 512), bf16)
        ds[1152:1280] = jnp.zeros((128, 512), bf16)

    share = inverse[0]
    scaled = grad[...].astype(f32) * share
    delta = jnp.sum(scaled * out[...].astype(f32), axis=0, keepdims=True)
    high = delta.astype(bf16).astype(f32)
    row = iota((16, 512), 0)
    extra = jnp.where(row == 0, -high, jnp.where(row == 1, high - delta, 0.0))
    gt[64:80] = extra.astype(bf16)
    gt[0:64] = scaled.astype(bf16)
    vt[0:64] = v[...]
    kt[0:64] = k[...]
    va[...] = vt[...].T
    for row_at in range(0, 1024, 256):
        rows = slice(row_at, row_at + 256)
        pull = dot(va[rows], gt[...], 1, 0)
        ds[128 + row_at : 384 + row_at] = (kept[0, rows] * pull).astype(bf16)
    made = dot(kt[...], ds[128:1152], 1, 0)
    block = (iota((8, 512), 1) + first) // 128
    key_block = iota((8, 512), 0)
    totals = made[64:72]
    left = jnp.sum(jnp.where(key_block <= block - 2, totals, 0.0), axis=0, keepdims=True)
    right = jnp.sum(jnp.where(key_block >= block + 2, totals, 0.0), axis=0, keepdims=True)
    dv_made = dot(gt[0:64], kept[0], 1, 1)
    dk_made = dot(q[...], ds[128:1152], 1, 1)
    near = None
    for part in range(4):
        base = pl.multiple_of(first + part * 128, 128)
        window = ds[pl.ds(base, 384), part * 128 : part * 128 + 128].astype(f32)
        near = window if near is None else near + window
    if carried:
        whole[0, 0:64, pl.ds(pl.multiple_of(first, 512), 512)] = made[0:64].astype(bf16)
        whole[0, 0:64, pl.ds(pl.multiple_of(512 - first, 512), 512)] = dq_in[...]
        whole[0, 64:128] = (dk_made + dk_in[...]).astype(bf16)
        whole[0, 128:192] = (dv_made + dv_in[...]).astype(bf16)
        head = pl.program_id(0)
        for at, row in enumerate(diagonal_sums(near + band_in[0])):
            diagonals[at, pl.ds(head, 1)] = row
        lane = iota((1, 128), 1)
        left, right = (
            jnp.sum(side, axis=1, keepdims=True) for side in (left + far_in[0, 0:1], right + far_in[0, 1:2])
        )
        sides[pl.ds(head, 1)] = jnp.where(lane == 15, left, jnp.where(lane == 31, right, 0.0))
        whole[0, 192:208] = jnp.zeros((16, 1024), bf16)

        @pl.when(head == 5)
        def _():
            bias = bucket_sums([diagonals[at] for at in range(3)], sides[...])
            whole[0, 192:208, 0:128] = jnp.concatenate([bias, jnp.zeros((8, 128), f32)], axis=0).astype(bf16)

    else:
        dq[...] = made[0:64].astype(bf16)
        dk[...] = dk_made
        dv[...] = dv_made
        band[0] = near
        far[0] = jnp.concatenate([left, right, jnp.zeros((6, 512), f32)], axis=0)


def attend_back(place, grad, out, inverse, qkv, kept, carry, mine):
    count = 6
    half = (lambda s: s[3]) if mine else (lambda s: 1 - s[3])
    rows512 = pl.BlockSpec((64, 512), lambda h, s: (h, 0))
    rows1024 = pl.BlockSpec((64, 1024), lambda h, s: (h, 0))
    band_spec = pl.BlockSpec((1, 384, 128), lambda h, s: (h, 0, 0))
    far_spec = pl.BlockSpec((1, 8, 512), lambda h, s: (h, 0, 0))
    carry_specs = (rows512, rows1024, rows1024, band_spec, far_spec)
    in_specs = [
        rows512,
        rows512,
        pl.BlockSpec((1, 1, 512), lambda h, s: (h, 0, 0)),
        pl.BlockSpec((64, 512), lambda h, s: (3 * h, half(s))),
        pl.BlockSpec((64, 1024), lambda h, s: (3 * h + 1, 0)),
        pl.BlockSpec((64, 1024), lambda h, s: (3 * h + 2, 0)),
        pl.BlockSpec((1, 1024, 512), lambda h, s: (h, 0, 0)),
    ]
    if carry:
        out_shape = jax.ShapeDtypeStruct((count, 208, 1024), bf16)
        out_specs = pl.BlockSpec((1, 208, 1024), lambda h, s: (h, 0, 0))
        in_specs += carry_specs
    else:
        out_shape = (
            jax.ShapeDtypeStruct((64 * count, 512), bf16),
            jax.ShapeDtypeStruct((64 * count, 1024), f32),
            jax.ShapeDtypeStruct((64 * count, 1024), f32),
            jax.ShapeDtypeStruct((count, 384, 128), f32),
            jax.ShapeDtypeStruct((count, 8, 512), f32),
        )
        out_specs = carry_specs
    grid = pltpu.PrefetchScalarGridSpec(
        num_scalar_prefetch=1,
        grid=(count,),
        in_specs=in_specs,
        out_specs=out_specs,
        scratch_shapes=([pltpu.VMEM((3, 8, 256), f32), pltpu.VMEM((8, 128), f32)] if carry else [])
        + [
            pltpu.VMEM((1024, 128), bf16),
            pltpu.VMEM((128, 1024), bf16),
            pltpu.VMEM((80, 1024), bf16),
            pltpu.VMEM((128, 512), bf16),
            pltpu.VMEM((1280, 512), bf16),
        ],
    )
    return pl.pallas_call(
        functools.partial(attend_back_kernel, bool(carry), mine),
        out_shape=out_shape,
        grid_spec=grid,
        compiler_params=params(VMEM if carry else 66_000_000),
        cost_estimate=cost(count * 1024 * 512 * 1024, 6_000_000),
        name="attend_back_mine" if mine else "attend_back_theirs",
    )(place, grad, out, inverse, qkv, qkv, qkv, kept, *carry)


def gelu_both(wide):
    square = wide * wide
    inner = 0.7978845608 * wide * (1.0 + 0.044715 * square)
    bend = jnp.tanh(inner)
    half = 0.5 * (1.0 + bend)
    slope = 0.7978845608 * (1.0 + 3 * 0.044715 * square)
    return (wide * half, half + 0.5 * wide * (1.0 - bend * bend) * slope)


def all_blocks(full, three, two, y1, y3, side_a, side_b, side_c):
    blocks = [full, three[0], three[1], y1, three[2], two[1], two[0], y3]
    sides = [
        full.at[7:9], side_a.at[2], side_a.at[0], y1.at[7:9], side_a.at[1], side_b.at[1], side_b.at[0], side_c,
    ]
    return blocks, sides


def forward_kernel(
    place, att_near, att_far, x, cot, small, *refs
):
    full, y0, z1, z2, z3, y2, y1, y3, side_a, side_b, side_c = refs[:11]
    nears, near_sides = all_blocks(full, (y0, z1, z2), (z3, y2), y1, y3, side_a, side_b, side_c)
    full, three, two, y1, y3, side_a, side_b, side_c = refs[11:19]
    three, two = [three.at[at] for at in range(3)], [two.at[at] for at in range(2)]
    fars, far_sides = all_blocks(full, three, two, y1, y3, side_a, side_b, side_c)
    refs = refs[19:]
    (
        hid_keep_hbm, hid_send_hbm, pre_hbm, turned_keep, turned_send, result, middle_grad, near_grad, far_grad,
        w_out, w_up, w_down, hid_keep, hid_send, pre, normed_grad, pulled, middle, total, normed, att,
        sems, att_sems, out_sems,
    ) = refs
    z, y, c, xs = place[0], place[1], place[2], place[3]
    att_copies = []
    for other, source in enumerate((att_near, att_far)):
        row = pl.multiple_of(jnp.bitwise_xor(xs, other) * 384, 128)
        copy = pltpu.make_async_copy(source, att.at[pl.ds(row, 384)], att_sems.at[other])
        copy.start()
        att_copies.append(copy)
    groups = ([], [], [])
    for turn in range(4):
        for dy in range(2):
            owner = ((jnp.bitwise_xor(z, turn) * 2) + jnp.bitwise_xor(y, dy)) * 2
            for other in range(2):
                main = (nears, fars)[other][turn * 2 + dy]
                side = (near_sides, far_sides)[other][turn * 2 + dy]
                who = owner + jnp.bitwise_xor(c, other)
                row = pl.multiple_of(who * 48, 16)
                pieces = (
                    (0, main.at[4], w_out.at[pl.ds(row, 48)]),
                    (1, main.at[0:4], w_up.at[:, pl.ds(row, 48)]),
                    (2, main.at[5:7], w_down.at[pl.ds(who * 4 + xs * 2, 2)]),
                    (2, side, w_down.at[pl.ds(who * 4 + (1 - xs) * 2, 2)]),
                )
                for at, (group, source, dest) in enumerate(pieces):
                    sem = sems.at[at, turn * 4 + dy * 2 + other]
                    groups[group].append(pltpu.make_async_copy(source, dest, sem))
    for group in groups:
        for copy in group:
            copy.start()
    for copy in att_copies + groups[0]:
        copy.wait()
    gain = small[1:2]
    wide = x[...].astype(f32) + dot(att[...], w_out[...], 0, 0)
    middle[...] = wide
    scale = lax.rsqrt(jnp.mean(wide * wide, axis=-1, keepdims=True) + EPS)
    normed[...] = (wide * scale * gain).astype(bf16)
    for group in groups[1:]:
        for copy in group:
            copy.wait()
    total[...] = wide
    normed_grad[...] = jnp.zeros_like(normed_grad)

    def chunk(j, carry):
        down = w_down[pl.ds(j * 16, 16)].reshape(768, 768)
        pulled[...] = dot(cot[...], down, 1, 1)
        value, slope = gelu_both(dot(normed[...], w_up[j], 1, 0))
        value = value.astype(bf16)
        total[...] += dot(value, down, 1, 0)
        even = jnp.concatenate([value[:, 0:192], value[:, 384:576]], axis=1)
        odd = jnp.concatenate([value[:, 192:384], value[:, 576:768]], axis=1)
        hid_keep[j] = jnp.where(c == 0, even, odd)
        hid_send[j] = jnp.where(c == 0, odd, even)
        low = (pulled[...] * slope).astype(bf16)
        pre[j] = low
        normed_grad[...] += dot(low, w_up[j], 1, 1)
        return carry

    lax.fori_loop(0, 4, chunk, 0)
    outs = [
        pltpu.make_async_copy(hid_send, hid_send_hbm, out_sems.at[0]),
        pltpu.make_async_copy(hid_keep, hid_keep_hbm, out_sems.at[1]),
        pltpu.make_async_copy(pre.at[0:4], pre_hbm.at[0:4], out_sems.at[2]),
    ]
    for copy in outs:
        copy.start()
    for at, whole in enumerate((normed[...].T, att[...])):
        rows = whole.reshape(8, 2, 48, 512)
        turned_keep[at] = jnp.where(c == 0, rows[:, 0], rows[:, 1])
        turned_send[at] = jnp.where(c == 0, rows[:, 1], rows[:, 0])
    wide = middle[...]
    scale = lax.rsqrt(jnp.mean(wide * wide, axis=-1, keepdims=True) + EPS)
    unit = wide * scale
    incoming = normed_grad[...]
    direct = incoming * gain
    inward = scale * (direct - unit * jnp.mean(direct * unit, axis=-1, keepdims=True))
    grad = cot[...].astype(f32) + inward
    middle_grad[...] = grad
    low = grad.astype(bf16)
    pre[4] = low
    outs.append(pltpu.make_async_copy(pre.at[4], pre_hbm.at[4], out_sems.at[3]))
    outs[3].start()
    for other, dest in enumerate((near_grad, far_grad)):
        row = pl.multiple_of(jnp.bitwise_xor(xs, other) * 384, 128)
        dest[...] = dot(w_out[pl.ds(row, 384)], low, 1, 1).astype(bf16)
    result[...] = total[...].astype(bf16)
    for copy in outs:
        copy.wait()


def forward(place, att_near, att_far, x, cot, small, near, far):
    wide = jax.ShapeDtypeStruct((512, 768), f32)
    half = jax.ShapeDtypeStruct((384, 512), bf16)
    hidden = jax.ShapeDtypeStruct((4, 512, 384), bf16)
    turned = jax.ShapeDtypeStruct((2, 8, 48, 512), bf16)
    return pl.pallas_call(
        forward_kernel,
        out_shape=(
            hidden, hidden, jax.ShapeDtypeStruct((5, 512, 768), bf16), turned, turned,
            jax.ShapeDtypeStruct((512, 768), bf16), wide, half, half,
        ),
        in_specs=[SCALARS, ANY, ANY, FULL, FULL, FULL] + [ANY] * 19,
        out_specs=(ANY, ANY, ANY) + (FULL,) * 6,
        scratch_shapes=[
            pltpu.VMEM((768, 768), bf16),
            pltpu.VMEM((4, 768, 768), bf16),
            pltpu.VMEM((64, 48, 768), bf16),
            pltpu.VMEM((4, 512, 384), bf16),
            pltpu.VMEM((4, 512, 384), bf16),
            pltpu.VMEM((5, 512, 768), bf16),
            pltpu.VMEM((512, 768), f32),
            pltpu.VMEM((512, 768), f32),
            pltpu.VMEM((512, 768), f32),
            pltpu.VMEM((512, 768), f32),
            pltpu.VMEM((512, 768), bf16),
            pltpu.VMEM((768, 512), bf16),
            pltpu.SemaphoreType.DMA((4, 16)),
            pltpu.SemaphoreType.DMA((2,)),
            pltpu.SemaphoreType.DMA((4,)),
        ],
        compiler_params=params(),
        cost_estimate=cost(8_500_000_000, 20_000_000, 512 * 3072),
        name="forward",
    )(place, att_near, att_far, x, cot, small, *near, *far)


def contract_grad_kernel(place, hid, hid_far, cot, cot_far, send, keep):
    made = dot(hid[0], cot[...], 0, 0) + dot(hid_far[0], cot_far[...], 0, 0)
    made = made.astype(bf16).reshape(2, 2, 2, 48, 768)
    send[...] = jnp.where(place[3] == 0, made[:, 1], made[:, 0])
    keep[...] = jnp.where(place[3] == 0, made[:, 0], made[:, 1])


def contract_weight_grad(place, hid, hid_far, cot, cot_far):
    shape = jax.ShapeDtypeStruct((8, 2, 48, 768), bf16)
    spec = pl.BlockSpec((2, 2, 48, 768), lambda j: (j, 0, 0, 0))
    chunk = pl.BlockSpec((1, 512, 384), lambda j: (j, 0, 0))
    whole = pl.BlockSpec((512, 768), lambda j: (0, 0))
    return pl.pallas_call(
        contract_grad_kernel,
        out_shape=(shape, shape),
        grid=(4,),
        in_specs=[SCALARS, chunk, chunk, whole, whole],
        out_specs=(spec, spec),
        compiler_params=params(),
        cost_estimate=cost(2 * 512 * 3072 * 768, 9_000_000),
        name="contract_weight_grad",
    )(place, hid, hid_far, cot, cot_far)


def expand_grad_kernel(place, turned, turned_far, pre, pre_far, b_send, b_keep, c_send, c_keep):
    step = pl.program_id(0)

    def made(at):
        near = dot(turned[at].reshape(384, 512), pre[0], 1, 0)
        return (near + dot(turned_far[at].reshape(384, 512), pre_far[0], 1, 0)).astype(bf16)

    @pl.when(step < 3)
    def _():
        rows = made(0).reshape(4, 2, 48, 768)
        b_send[:, 0] = jnp.where(place[1] == 0, rows[:, 1], rows[:, 0])
        b_keep[:, 0] = jnp.where(place[1] == 0, rows[:, 0], rows[:, 1])

    def by_low(rows):
        rows = rows.reshape(2, 2, 2, 48, 768)
        low = place[0] % 2
        c_send[:, :, 0] = jnp.where(low == 0, rows[:, 1], rows[:, 0])
        c_keep[:, :, 0] = jnp.where(low == 0, rows[:, 0], rows[:, 1])

    @pl.when(step == 3)
    def _():
        by_low(made(0))

    @pl.when(step == 4)
    def _():
        by_low(made(1))


def expand_weight_grad(place, turned, turned_far, pre, pre_far):
    first = jax.ShapeDtypeStruct((4, 3, 48, 768), bf16)
    second = jax.ShapeDtypeStruct((2, 2, 2, 48, 768), bf16)
    first_spec = pl.BlockSpec((4, 1, 48, 768), lambda j: (0, jnp.minimum(j, 2), 0, 0))
    second_spec = pl.BlockSpec((2, 2, 1, 48, 768), lambda j: (0, 0, jnp.maximum(j - 3, 0), 0, 0))
    whole = pl.BlockSpec((2, 8, 48, 512), lambda j: (0, 0, 0, 0))
    chunk = pl.BlockSpec((1, 512, 768), lambda j: (j, 0, 0))
    return pl.pallas_call(
        expand_grad_kernel,
        out_shape=(first, first, second, second),
        grid=(5,),
        in_specs=[SCALARS, whole, whole, chunk, chunk],
        out_specs=(first_spec, first_spec, second_spec, second_spec),
        compiler_params=params(),
        cost_estimate=cost(2 * 512 * 768 * 3840, 12_000_000),
        name="expand_weight_grad",
    )(place, turned, turned_far, pre, pre_far)


def place_grads(whole, grad, sems):
    copies = []
    for head in range(6):
        dest = grad.at[head * 192 : head * 192 + 192]
        copies.append(pltpu.make_async_copy(whole.at[head, 0:192], dest, sems.at[head]))
        copies[-1].start()
    return copies


def weight_grad_kernel(place, mine, other, whole, near, far, grad, bias, sems, bias_sem):
    copies = place_grads(whole, grad, sems)
    copies.append(pltpu.make_async_copy(whole.at[5, 192:208, 0:128], bias, bias_sem))
    copies[-1].start()
    for copy in copies:
        copy.wait()
    for kind, rows, dest in ((place[2], mine, near), (1 - place[2], other, far)):
        spot = iota((384, 128), 0) % 48
        bucket = ((iota((384, 128), 0) // 48) * 2 + kind) * 2 + spot // 6
        chosen = jnp.where((iota((384, 128), 1) == bucket) & (spot < 12), 1.0, 0.0)
        per_head = dot(chosen.astype(bf16), bias[0:8], 1, 1)
        pattern = (iota((384, 8), 1) == (iota((384, 8), 0) % 48) % 6).astype(f32)
        column = jnp.sum(per_head * pattern, axis=1, keepdims=True)
        side = jnp.where(iota((384, 128), 1) == 0, column, 0.0)
        dest[:, :, 1152:1280] = side.astype(bf16).reshape(8, 48, 128)
        left = rows[...].reshape(384, 1024)
        for col in range(0, 1152, 384):
            made = dot(left, grad[col : col + 384], 1, 1)
            dest[:, :, col : col + 384] = made.astype(bf16).reshape(8, 48, 384)


def weight_grad(place, mine, other, whole):
    owned = jax.ShapeDtypeStruct((8, 48, 1280), bf16)
    return pl.pallas_call(
        weight_grad_kernel,
        out_shape=(owned, owned),
        in_specs=[SCALARS, FULL, FULL, ANY],
        out_specs=(FULL,) * 2,
        scratch_shapes=[
            pltpu.VMEM((1152, 1024), bf16),
            pltpu.VMEM((16, 128), bf16),
            pltpu.SemaphoreType.DMA((6,)),
            pltpu.SemaphoreType.DMA,
        ],
        compiler_params=params(),
        cost_estimate=cost(2 * 1024 * 768 * 1152, 6_000_000),
        name="weight_grad",
    )(place, mine, other, whole)


def project_back_kernel(place, *refs):
    (w_near, w_far), whole, refs = narrow_blocks(refs[:10]), refs[10], refs[11:]
    part_near, part_far, w, grad, sems, qsems = refs
    x = place[3]
    copies = place_blocks(place, w_near, w_far, w, sems) + place_grads(whole, grad, qsems)
    for copy in copies:
        copy.wait()
    for other, dest in ((1, part_far), (0, part_near)):
        start = pl.multiple_of(jnp.bitwise_xor(x, other) * 512, 512)
        dest[...] = dot(grad[:, pl.ds(start, 512)], w[:, 0:1152], 0, 1).astype(bf16)


def project_back(place, blocks, whole):
    part = jax.ShapeDtypeStruct((512, 768), bf16)
    return pl.pallas_call(
        project_back_kernel,
        out_shape=(part, part),
        in_specs=[SCALARS] + [ANY] * 11,
        out_specs=(FULL,) * 2,
        scratch_shapes=[
            pltpu.VMEM((768, 1280), bf16),
            pltpu.VMEM((1152, 1024), bf16),
            pltpu.SemaphoreType.DMA((16,)),
            pltpu.SemaphoreType.DMA((6,)),
        ],
        compiler_params=params(),
        cost_estimate=cost(2 * 1024 * 768 * 1152, 10_000_000),
        name="project_back",
    )(place, *blocks, whole)


def pass_kernel(place, result):
    for at in range(7):
        result[at] = place[at]


def hand_on(place):
    return pl.pallas_call(
        pass_kernel,
        out_shape=jax.ShapeDtypeStruct((7,), jnp.int32),
        in_specs=[SCALARS],
        out_specs=SCALARS,
        cost_estimate=pl.CostEstimate(flops=20_000_000_000, bytes_accessed=1000, transcendentals=0),
        name="hand_on",
    )(place)


def finish_kernel(place, a_near, a_far, g_near, g_far, qw, kw, vw, gain, contract, q, k, v, gain_grad, bias):
    swapped = place[3] == 1

    def ordered(near, far):
        near, far = near[...].astype(f32), far[...].astype(f32)
        return jnp.where(swapped, far, near), jnp.where(swapped, near, far)

    for half, wide in enumerate(ordered(a_near, a_far)):
        for at in range(2):
            row = half * 96 + at * 48
            contract[row : row + 48] = wide[at]
    first, second = ordered(g_near, g_far)
    for at, dest in enumerate((q, k, v)):
        for half, wide in enumerate((first, second)):
            for head in range(6):
                column = head * 192 + at * 64
                spot = half * 384 + head * 64
                dest[:, spot : spot + 64] = wide[:, column : column + 64]
    joint = q[...] * qw[...].astype(f32) + k[...] * kw[...].astype(f32) + v[...] * vw[...].astype(f32)
    summed = jnp.broadcast_to(jnp.sum(joint, axis=1, keepdims=True), (48, 128))
    blank = jnp.zeros((80, 128), f32)
    turned = jnp.concatenate([summed, blank], axis=0).T
    gain_grad[...] = turned[0:1, 0:48] / gain[...].astype(f32)
    first = jnp.concatenate([first[:, 1152:1280], blank], axis=0).T
    second = jnp.concatenate([second[:, 1152:1280], blank], axis=0).T
    for row in range(2):
        cols = slice(row * 6, row * 6 + 6)
        bias[row : row + 1, 0:6] = first[0:1, cols]
        bias[row : row + 1, 6:12] = second[0:1, cols]


def finish(place, a_near, a_far, g_near, g_far, qw, kw, vw, gain):
    full = jax.ShapeDtypeStruct((48, 768), f32)
    return pl.pallas_call(
        finish_kernel,
        out_shape=(
            jax.ShapeDtypeStruct((192, 768), f32),
            full, full, full, jax.ShapeDtypeStruct((1, 48), f32), jax.ShapeDtypeStruct((2, 12), f32),
        ),
        in_specs=[SCALARS] + [FULL] * 8,
        out_specs=(FULL,) * 6,
        compiler_params=params(),
        cost_estimate=cost(1000, 1_000_000),
        name="finish",
    )(place, a_near, a_far, g_near, g_far, qw, kw, vw, gain.reshape(1, 48))


def finish_wide_kernel(
    place, x, small, near, far, middle_grad, b_near, b_far, up, gain, result, expand, output, gain_grad
):
    input_grad_kernel(place, x, small, near, far, middle_grad, result)
    summed = b_near[...].astype(f32) + b_far[...].astype(f32)
    joint = jnp.zeros((48, 768), f32)
    for at in range(4):
        cols = slice(at * 768, at * 768 + 768)
        expand[:, cols] = summed[at]
        joint = joint + summed[at] * up[:, cols].astype(f32)
    output[...] = summed[4]
    column = jnp.broadcast_to(jnp.sum(joint, axis=1, keepdims=True), (48, 128))
    turned = jnp.concatenate([column, jnp.zeros((80, 128), f32)], axis=0).T
    gain_grad[...] = turned[0:1, 0:48] / gain[...].astype(f32)


def finish_wide(place, x, small, near, far, middle_grad, b_near, b_far, up, gain):
    return pl.pallas_call(
        finish_wide_kernel,
        out_shape=(
            jax.ShapeDtypeStruct((512, 768), bf16), jax.ShapeDtypeStruct((48, 3072), f32),
            jax.ShapeDtypeStruct((48, 768), f32), jax.ShapeDtypeStruct((1, 48), f32),
        ),
        in_specs=[SCALARS] + [FULL] * 9,
        out_specs=(FULL,) * 4,
        compiler_params=params(),
        cost_estimate=cost(1000, 2_000_000),
        name="finish_wide",
    )(place, x, small, near, far, middle_grad, b_near, b_far, up, gain.reshape(1, 48))


def input_grad_kernel(place, x, small, near, far, middle_grad, result):
    for row in range(0, 512, 256):
        rows = slice(row, row + 256)
        wide = x[rows].astype(f32)
        scale = lax.rsqrt(jnp.mean(wide * wide, axis=-1, keepdims=True) + EPS)
        unit = wide * scale
        direct = (near[rows].astype(f32) + far[rows].astype(f32)) * small[0:1]
        inward = scale * (direct - unit * jnp.mean(direct * unit, axis=-1, keepdims=True))
        result[rows] = (middle_grad[rows] + inward).astype(bf16)


def swap(array, axis, bit):
    count = lax.axis_size(axis)
    return lax.ppermute(array, axis, [(i, i ^ bit) for i in range(count)])


def swap_both(array):
    pairs = [(i * 2 + j, (i ^ Y) * 2 + 1 - j) for i in range(lax.axis_size("fsdp")) for j in range(2)]
    return lax.ppermute(array, ("fsdp", "seq"), pairs)


CORE, Y, Z = 1, 2, 4


def after(value, *others):
    return lax.optimization_barrier((value, *others))[0]


class Line:
    def __init__(self, place):
        self.place = place

    def wait(self, *arrays):
        self.place = after(self.place, *arrays)

    def run(self, kernel, *args):
        made = kernel(self.place, *args)
        self.wait(jax.tree.leaves(made)[0])
        return made


def gather_part(array, part, own, now):
    _, dims, gone = part
    for axis in reversed(range(len(dims))):
        if dims[axis] == now:
            array = lax.dynamic_index_in_dim(array, 1 - own[now], axis, keepdims=False)
        elif dims[axis] in gone:
            array = lax.dynamic_index_in_dim(array, own[dims[axis]], axis, keepdims=False)
    return array.astype(f32)


def total(line, parts, own, now=None):
    arrays = after([part[0] for part in parts], line.place)
    made = None
    for array, part in zip(arrays, parts):
        term = gather_part(array, part, own, now)
        made = term if made is None else made + term
    made = lax.optimization_barrier(made.astype(bf16))
    line.wait(made)
    return made


def keep(parts, now, got):
    _, dims, gone = parts[0]
    left = tuple(dim for dim in dims if dim not in gone and dim != now)
    return [(a, d, g + (now,)) for a, d, g in parts] + [(got, left, ())]


def local_split(
    layer_input, query_weight, key_weight, value_weight, output_weight, expand_weight,
    contract_weight, attention_gain, feedforward_gain, bias_table, valid_len, instr_len, pair_flag,
    cotangent,
):
    owner, x = lax.axis_index("fsdp"), lax.axis_index("seq")
    z, y, c = owner // 4, (owner // 2) % 2, owner % 2
    where = jnp.stack([z, y, c, x]).astype(jnp.int32)
    line = Line(where)
    tokens, cot = layer_input[0], cotangent[0]

    def by_z(array):
        return swap(array, "fsdp", Z)

    def by_zz(array):
        return swap(array, "fsdp", 2 * Z)

    def by_y(array):
        return swap(array, "fsdp", Y)

    def by_core(array):
        return swap(array, "fsdp", CORE)

    def by_x(array):
        return swap(array, "seq", 1)

    shard = line.run(
        narrow_shard, query_weight, key_weight, value_weight, attention_gain, feedforward_gain, bias_table
    )
    a2, a1, b0 = by_zz(shard), by_z(shard), by_y(shard)
    x_far, cot_far = by_x(tokens), by_core(cot)
    rest, full = line.run(wide_shard, expand_weight, output_weight, contract_weight)
    a2, a1, b0, rest, cot_far = lax.optimization_barrier((a2, a1, b0, rest, cot_far))
    turned, b2 = by_z(jnp.stack([a2, b0])), by_y(a2)
    four = by_core(jnp.stack([shard, b0, a1, a2]))
    z2, z1, y0 = by_zz(rest), by_z(rest), by_y(rest)
    lens = jnp.stack([valid_len[0], instr_len[0], pair_flag[0]])
    place = jnp.concatenate([where, lens])
    turned, b2, x_far, line.place = lax.optimization_barrier((turned, b2, x_far, place))
    b3 = by_y(turned[0])
    three = by_core(jnp.stack([turned[0], turned[1], b2]))
    last = by_core(b3)
    z1, z2, y0, last, three = lax.optimization_barrier((z1, z2, y0, last, three))
    z3, y2 = by_z(z2), by_y(z2)
    sides = jnp.stack([z1[5:], z2[5:], y0[5:]])
    sides_a = by_x(sides)
    narrow = [shard, b0, a1, a2, turned, b2, b3, four, three, last]

    line.wait(sides)
    qkv, normed_kept, normed_sent, small, table, tiles = line.run(project, tokens, x_far, narrow)
    line.place, z3, y2, sides_a = lax.optimization_barrier((line.place, z3, y2, sides_a))
    y3 = by_y(z3)
    y1 = jnp.concatenate([y0, sides_a[2]], axis=0)
    sides, trio = jnp.stack([z3[5:], y2[5:]]), jnp.stack([y0, z1, z2])
    line.wait(y1, sides, trio)
    y1, sides_b, far_full, far_three = by_z(y1), by_x(sides), by_core(full), by_core(trio)
    out_theirs, kept_theirs, inverse_theirs = line.run(attend, table, tiles, qkv, False)
    line.place, y3, sides_b, far_full, far_three, out_theirs = lax.optimization_barrier(
        (line.place, y3, sides_b, far_full, far_three, out_theirs)
    )
    two = jnp.stack([z3, y2])
    line.wait(two)
    out_got, sides_c, far_two = by_x(out_theirs), by_x(y3[5:]), by_core(two)
    out_mine, kept_mine, inverse_mine = line.run(attend, table, tiles, qkv, True)
    out_mine, y1, out_got, sides_c, far_two, y3, sides_a, sides_b = lax.optimization_barrier(
        (out_mine, y1, out_got, sides_c, far_two, y3, sides_a, sides_b)
    )
    near = [full, y0, z1, z2, z3, y2, y1, y3, sides_a, sides_b, sides_c]
    far = [far_full, far_three, far_two] + [by_core(block) for block in (y1, y3, sides_a, sides_b, sides_c)]
    hid, hid_sent, pre, turned, turned_sent, layer_output, middle_grad, grad_mine, grad_sent = line.run(
        forward, out_mine, out_got, tokens, cot, small, near, far
    )
    hid_far, grad_theirs, pre_far, turned_far = by_core(hid_sent), by_x(grad_sent), by_core(pre), by_core(turned_sent)

    own = {"high": z // 2, "low": z % 2, "y": y, "x": x}

    def parts(kept, got, *dims):
        lead = tuple({"high": 2, "low": 2, "y": 2}[dim] for dim in dims if dim != "n")
        shape = lead + kept.shape[-3:] if "n" in dims else lead + kept.shape[-2:]
        return [(array.reshape(shape), dims, ()) for array in (kept, got)]

    carry = line.run(
        lambda place: attend_back(place, grad_mine, out_mine, inverse_mine, qkv, kept_mine, (), True)
    )
    line.wait(grad_theirs)
    b_sent, b_kept, c_sent, c_kept = line.run(expand_weight_grad, turned, turned_far, pre, pre_far)
    b_got, c_got = by_y(b_sent), by_z(c_sent)
    b_parts = parts(b_kept, b_got, "high", "low", "n")
    c_parts = parts(c_kept, c_got, "high", "y", "n")
    sent, kept = line.run(contract_weight_grad, hid, hid_far, cot, cot_far)
    a_got = by_x(sent)
    a_parts = parts(kept, a_got, "high", "low", "y", "n")
    whole = line.run(
        lambda place: attend_back(
            place, grad_theirs, out_theirs, inverse_theirs, qkv, kept_theirs, carry, False
        )
    )
    b_got = by_z(total(line, b_parts, own, "low"))
    b_parts = keep(b_parts, "low", b_got)
    c_got = by_y(total(line, c_parts, own, "y"))
    c_parts = keep(c_parts, "y", c_got)
    g_near, g_far = line.run(weight_grad, normed_kept, normed_sent, whole)
    g_parts = parts(g_near, by_core(g_far), "high", "low", "y")
    line.wait(a_got, b_got, c_got)
    line.place = hand_on(line.place)
    g_parts = keep(g_parts, "low", by_z(total(line, g_parts, own, "low")))
    a_parts = keep(a_parts, "y", by_y(total(line, a_parts, own, "y")))
    b_parts = keep(b_parts, "high", by_zz(total(line, b_parts, own, "high")))
    c_parts = keep(c_parts, "high", by_zz(total(line, c_parts, own, "high")))
    part_near, part_far = line.run(project_back, narrow, whole)
    part_got = by_x(part_far)
    a_parts = keep(a_parts, "low", by_z(total(line, a_parts, own, "low")))
    g_parts = keep(g_parts, "y", by_y(total(line, g_parts, own, "y")))
    b_low = jnp.concatenate([total(line, b_parts, own), total(line, c_parts, own)], axis=0)
    b_low = lax.optimization_barrier(b_low)
    b_other = by_x(b_low)
    line.wait(b_low)
    a_parts = keep(a_parts, "high", by_zz(total(line, a_parts, own, "high")))
    g_parts = keep(g_parts, "high", by_zz(total(line, g_parts, own, "high")))
    a_low = total(line, a_parts, own)
    a_other = by_x(a_low)
    g_low = total(line, g_parts, own)
    g_other = by_x(g_low)
    result, expand_sum, output_sum, gain_two = line.run(
        finish_wide, tokens, small, part_near, part_got, middle_grad, b_low, b_other, expand_weight, feedforward_gain
    )
    contract_sum, *grads, gain_one, bias_grad = line.run(
        finish, a_low, a_other, g_low, g_other, query_weight, key_weight, value_weight, attention_gain
    )
    return (
        layer_output[None], result[None], gain_one[0], gain_two[0], *grads,
        output_sum, expand_sum, contract_sum, bias_grad,
    )


def bucket_table(query_pos, key_pos):
    offset = key_pos[None, :] - query_pos[:, None]
    distance = jnp.abs(offset)
    beyond = jnp.zeros_like(distance)
    for far_edge in far_edges:
        beyond = beyond + (distance >= far_edge).astype(jnp.int32)
    nearby = jnp.where(distance < 8, distance, 8 + beyond)
    return nearby + 16 * (offset > 0).astype(jnp.int32)


def visible_keys(query_pos, key_pos, valid_len, instr_len, pair_flag):
    in_valid = key_pos[None, None, :] < valid_len[:, None, None]
    guarded = (
        (pair_flag[:, None, None] == 1)
        & (query_pos[None, :, None] < instr_len[:, None, None])
        & (key_pos[None, None, :] >= instr_len[:, None, None])
    )
    return in_valid & jnp.logical_not(guarded)


def rms_scale(values):
    return lax.rsqrt(jnp.mean(values * values, axis=-1, keepdims=True) + EPS)


def norm_back(values, scale, gain, grad_out):
    normed = values * scale
    grad_normed = grad_out * gain
    grad_values = scale * (
        grad_normed - normed * jnp.mean(grad_normed * normed, axis=-1, keepdims=True)
    )
    return (grad_values, jnp.sum(grad_out * normed, axis=(0, 1)))


def gelu_tanh(values):
    return jax.nn.gelu(values, approximate=True)


def local(
    layer_input,
    query_weight,
    key_weight,
    value_weight,
    output_weight,
    expand_weight,
    contract_weight,
    attention_gain,
    feedforward_gain,
    bias_table,
    valid_len,
    instr_len,
    pair_flag,
    cotangent,
):
    f32 = jnp.float32
    bf16 = jnp.bfloat16
    row_count, local_len, model_width = layer_input.shape
    head_count = bias_table.shape[1]
    head_size = model_width // head_count
    full_len = local_len * lax.axis_size("seq")
    local_start = lax.axis_index("seq") * local_len
    query_pos = local_start + jnp.arange(local_len, dtype=jnp.int32)
    key_pos = jnp.arange(full_len, dtype=jnp.int32)
    buckets = bucket_table(query_pos, key_pos)
    onehot = buckets[:, :, None] == jnp.arange(BUCKETS, dtype=jnp.int32)[None, None, :]
    visible = visible_keys(query_pos, key_pos, valid_len, instr_len, pair_flag)
    input_wide = layer_input.astype(f32)

    def attend_probs(queries, key_heads, table_full):
        rel_bias = jnp.einsum(
            "ijb,bh->hij", onehot.astype(bf16), table_full, preferred_element_type=f32
        )
        raw_scores = jnp.einsum("rihe,rjhe->rhij", queries, key_heads, preferred_element_type=f32)
        scores = jnp.where(visible[:, None], raw_scores + rel_bias[None], -1000000000.0)
        row_peak = jnp.max(scores, axis=-1, keepdims=True)
        log_total = row_peak + jnp.log(jnp.sum(jnp.exp(scores - row_peak), axis=-1, keepdims=True))
        return (jnp.exp(scores - log_total), log_total[..., 0])

    def forward(weights):
        (
            query_full,
            key_full,
            value_full,
            output_full,
            expand_full,
            contract_full,
            gain_one,
            gain_two,
            table_full,
        ) = weights
        scale_one = rms_scale(input_wide)
        normed_low = (input_wide * scale_one * gain_one.astype(f32)).astype(bf16)

        def project(weight):
            return jnp.einsum("rtd,de->rte", normed_low, weight, preferred_element_type=f32).astype(
                bf16
            )

        query_low = project(query_full)
        key_low = project(key_full)
        value_low = project(value_full)
        key_all, value_all = (
            lax.all_gather(key_low, "seq", axis=1, tiled=True),
            lax.all_gather(value_low, "seq", axis=1, tiled=True),
        )
        queries = query_low.reshape(row_count, local_len, head_count, head_size)
        key_heads = key_all.reshape(row_count, full_len, head_count, head_size)
        value_heads = value_all.reshape(row_count, full_len, head_count, head_size)
        probs, log_total = attend_probs(queries, key_heads, table_full)
        probs_low = probs.astype(bf16)
        attended = jnp.einsum("rhij,rjhe->rihe", probs_low, value_heads, preferred_element_type=f32)
        attended = attended.reshape(row_count, local_len, model_width).astype(bf16)
        middle = input_wide + jnp.einsum(
            "rtd,de->rte", attended, output_full, preferred_element_type=f32
        )
        scale_two = rms_scale(middle)
        normed_two = (middle * scale_two * gain_two.astype(f32)).astype(bf16)
        hidden_pre = jnp.einsum("rtd,df->rtf", normed_two, expand_full, preferred_element_type=f32)
        hidden_low = gelu_tanh(hidden_pre).astype(bf16)
        result = middle + jnp.einsum(
            "rtf,fd->rtd", hidden_low, contract_full, preferred_element_type=f32
        )
        return (
            result,
            scale_one,
            normed_low,
            queries,
            key_heads,
            value_heads,
            probs,
            probs_low,
            log_total,
            attended,
            middle,
            scale_two,
            normed_two,
            hidden_pre,
            hidden_low,
        )

    stored = forward(
        (
            lax.all_gather(query_weight, "fsdp", axis=0, tiled=True),
            lax.all_gather(key_weight, "fsdp", axis=0, tiled=True),
            lax.all_gather(value_weight, "fsdp", axis=0, tiled=True),
            lax.all_gather(output_weight, "fsdp", axis=0, tiled=True),
            lax.all_gather(expand_weight, "fsdp", axis=0, tiled=True),
            lax.all_gather(contract_weight, "fsdp", axis=0, tiled=True),
            lax.all_gather(attention_gain, "fsdp", axis=0, tiled=True),
            lax.all_gather(feedforward_gain, "fsdp", axis=0, tiled=True),
            lax.all_gather(bias_table, "fsdp", axis=0, tiled=True),
        )
    )
    layer_output = stored[0].astype(bf16)
    gathered = (
        lax.all_gather(query_weight, "fsdp", axis=0, tiled=True),
        lax.all_gather(key_weight, "fsdp", axis=0, tiled=True),
        lax.all_gather(value_weight, "fsdp", axis=0, tiled=True),
        lax.all_gather(output_weight, "fsdp", axis=0, tiled=True),
        lax.all_gather(expand_weight, "fsdp", axis=0, tiled=True),
        lax.all_gather(contract_weight, "fsdp", axis=0, tiled=True),
        lax.all_gather(attention_gain, "fsdp", axis=0, tiled=True),
        lax.all_gather(feedforward_gain, "fsdp", axis=0, tiled=True),
        lax.all_gather(bias_table, "fsdp", axis=0, tiled=True),
    )
    kept = forward(gathered)
    (
        unused,
        scale_one,
        normed_low,
        queries,
        key_heads,
        value_heads,
        probs,
        probs_low,
        log_total,
        attended,
        middle,
        scale_two,
        normed_two,
        hidden_pre,
        hidden_low,
    ) = kept
    (
        query_full,
        key_full,
        value_full,
        output_full,
        expand_full,
        contract_full,
        gain_one,
        gain_two,
        table_full,
    ) = gathered
    gain_one_wide = gain_one.astype(f32)
    gain_two_wide = gain_two.astype(f32)
    contract_grad = jnp.einsum("rtf,rtd->fd", hidden_low, cotangent, preferred_element_type=f32)
    grad_hidden = jnp.einsum("rtd,fd->rtf", cotangent, contract_full, preferred_element_type=f32)
    gelu_pull = jax.vjp(gelu_tanh, hidden_pre)[1]
    grad_pre = gelu_pull(grad_hidden)[0].astype(bf16)
    expand_grad = jnp.einsum("rtd,rtf->df", normed_two, grad_pre, preferred_element_type=f32)
    grad_normed_two = jnp.einsum("rtf,df->rtd", grad_pre, expand_full, preferred_element_type=f32)
    grad_middle_norm, gain_two_grad = norm_back(middle, scale_two, gain_two_wide, grad_normed_two)
    grad_middle = cotangent.astype(f32) + grad_middle_norm
    grad_branch = grad_middle.astype(bf16)
    output_grad = jnp.einsum("rtd,rte->de", attended, grad_branch, preferred_element_type=f32)
    grad_attended = jnp.einsum(
        "rte,de->rtd", grad_branch, output_full, preferred_element_type=f32
    ).astype(bf16)
    grad_attended = grad_attended.reshape(row_count, local_len, head_count, head_size)
    grad_probs = jnp.einsum(
        "rihe,rjhe->rhij", grad_attended, value_heads, preferred_element_type=f32
    )
    row_delta = jnp.sum(probs * grad_probs, axis=-1)
    grad_scores = probs * (grad_probs - row_delta[..., None])
    bias_part = jnp.einsum(
        "hij,ijb->bh",
        jnp.sum(grad_scores, axis=0),
        onehot.astype(f32),
        precision=lax.Precision.HIGHEST,
    )
    scores_low = grad_scores.astype(bf16)
    grad_queries = jnp.einsum("rhij,rjhe->rihe", scores_low, key_heads, preferred_element_type=f32)
    grad_queries = grad_queries.reshape(row_count, local_len, model_width).astype(bf16)
    value_partial = jnp.einsum(
        "rhij,rihe->rjhe", probs_low, grad_attended, preferred_element_type=f32
    ).reshape(row_count, full_len, model_width)
    key_partial = jnp.einsum(
        "rhij,rihe->rjhe", scores_low, queries, preferred_element_type=f32
    ).reshape(row_count, full_len, model_width)
    key_summed, value_summed = (
        lax.psum_scatter(
            key_partial.astype(jnp.bfloat16), "seq", scatter_dimension=1, tiled=True
        ).astype(jnp.float32),
        lax.psum_scatter(
            value_partial.astype(jnp.bfloat16), "seq", scatter_dimension=1, tiled=True
        ).astype(jnp.float32),
    )
    grad_keys = key_summed.astype(bf16)
    grad_values = value_summed.astype(bf16)
    query_part = jnp.einsum("rtd,rte->de", normed_low, grad_queries, preferred_element_type=f32)
    key_part = jnp.einsum("rtd,rte->de", normed_low, grad_keys, preferred_element_type=f32)
    value_part = jnp.einsum("rtd,rte->de", normed_low, grad_values, preferred_element_type=f32)
    grad_normed_one = jnp.einsum(
        "rte,de->rtd", grad_queries, query_full, preferred_element_type=f32
    )
    grad_normed_one = grad_normed_one + jnp.einsum(
        "rte,de->rtd", grad_keys, key_full, preferred_element_type=f32
    )
    grad_normed_one = grad_normed_one + jnp.einsum(
        "rte,de->rtd", grad_values, value_full, preferred_element_type=f32
    )
    grad_input_norm, gain_one_grad = norm_back(
        input_wide, scale_one, gain_one_wide, grad_normed_one
    )
    input_grad = (grad_middle + grad_input_norm).astype(bf16)
    owned = (
        lax.psum_scatter(
            query_part.astype(jnp.bfloat16), "fsdp", scatter_dimension=0, tiled=True
        ).astype(jnp.float32),
        lax.psum_scatter(
            key_part.astype(jnp.bfloat16), "fsdp", scatter_dimension=0, tiled=True
        ).astype(jnp.float32),
        lax.psum_scatter(
            value_part.astype(jnp.bfloat16), "fsdp", scatter_dimension=0, tiled=True
        ).astype(jnp.float32),
        lax.psum_scatter(
            output_grad.astype(jnp.bfloat16), "fsdp", scatter_dimension=0, tiled=True
        ).astype(jnp.float32),
        lax.psum_scatter(
            expand_grad.astype(jnp.bfloat16), "fsdp", scatter_dimension=0, tiled=True
        ).astype(jnp.float32),
        lax.psum_scatter(
            contract_grad.astype(jnp.bfloat16), "fsdp", scatter_dimension=0, tiled=True
        ).astype(jnp.float32),
        lax.psum_scatter(
            gain_one_grad.astype(jnp.bfloat16), "fsdp", scatter_dimension=0, tiled=True
        ).astype(jnp.float32),
        lax.psum_scatter(
            gain_two_grad.astype(jnp.bfloat16), "fsdp", scatter_dimension=0, tiled=True
        ).astype(jnp.float32),
        lax.psum_scatter(
            bias_part.astype(jnp.bfloat16), "fsdp", scatter_dimension=0, tiled=True
        ).astype(jnp.float32),
    )
    summed = (
        lax.psum(owned[0].astype(jnp.bfloat16), "seq").astype(jnp.float32),
        lax.psum(owned[1].astype(jnp.bfloat16), "seq").astype(jnp.float32),
        lax.psum(owned[2].astype(jnp.bfloat16), "seq").astype(jnp.float32),
        lax.psum(owned[3].astype(jnp.bfloat16), "seq").astype(jnp.float32),
        lax.psum(owned[4].astype(jnp.bfloat16), "seq").astype(jnp.float32),
        lax.psum(owned[5].astype(jnp.bfloat16), "seq").astype(jnp.float32),
        lax.psum(owned[6].astype(jnp.bfloat16), "seq").astype(jnp.float32),
        lax.psum(owned[7].astype(jnp.bfloat16), "seq").astype(jnp.float32),
        lax.psum(owned[8].astype(jnp.bfloat16), "seq").astype(jnp.float32),
    )
    (
        query_grad,
        key_grad,
        value_grad,
        output_sum,
        expand_sum,
        contract_sum,
        gain_one_sum,
        gain_two_sum,
        bias_grad,
    ) = summed
    return (
        layer_output,
        input_grad,
        gain_one_sum,
        gain_two_sum,
        query_grad,
        key_grad,
        value_grad,
        output_sum,
        expand_sum,
        contract_sum,
        bias_grad,
    )


def solution(mesh):
    in_specs = (
        P("fsdp", "seq", None),
        P("fsdp", None),
        P("fsdp", None),
        P("fsdp", None),
        P("fsdp", None),
        P("fsdp", None),
        P("fsdp", None),
        P("fsdp"),
        P("fsdp"),
        P("fsdp", None),
        P("fsdp"),
        P("fsdp"),
        P("fsdp"),
        P("fsdp", "seq", None),
    )
    out_specs = (
        P("fsdp", "seq", None),
        P("fsdp", "seq", None),
        P("fsdp"),
        P("fsdp"),
        P("fsdp", None),
        P("fsdp", None),
        P("fsdp", None),
        P("fsdp", None),
        P("fsdp", None),
        P("fsdp", None),
        P("fsdp", None),
    )
    split = mesh.shape["fsdp"] == 16 and mesh.shape["seq"] == 2
    step = local_split if split else local
    return jax.shard_map(step, mesh=mesh, in_specs=in_specs, out_specs=out_specs, check_vma=False)
```

```python
import functools
import itertools
import math

import jax
import jax.numpy as jnp
from jax import lax
from jax.experimental import pallas as pl
from jax.experimental.pallas import tpu as pltpu
from jax.sharding import PartitionSpec as P

f32 = jnp.float32
bf16 = jnp.bfloat16
BUCKETS = 32
EPS = 1e-06
far_edges = (12, 16, 23, 32, 46, 64, 91)
HIDDEN = -(2.0**30)
VMEM = 56 * 1024 * 1024
ANY = pl.BlockSpec(memory_space=pl.ANY)
FULL = pl.BlockSpec(memory_space=pltpu.VMEM)
SCALARS = pl.BlockSpec(memory_space=pltpu.SMEM)


def dot(left, right, left_dim, right_dim):
    return lax.dot_general(
        left, right, (((left_dim,), (right_dim,)), ((), ())), preferred_element_type=f32
    )


def params(limit=VMEM):
    return pltpu.CompilerParams(vmem_limit_bytes=limit)


def cost(flops, byte_count, exps=0):
    return pl.CostEstimate(flops=flops // 1000, bytes_accessed=byte_count // 1000, transcendentals=exps // 1000)


def small_cost():
    return pl.CostEstimate(flops=1000, bytes_accessed=1000, transcendentals=0)


def bucket_of(offset):
    distance = jnp.abs(offset)
    beyond = jnp.zeros_like(distance)
    for far_edge in far_edges:
        beyond = beyond + (distance >= far_edge).astype(jnp.int32)
    nearby = jnp.where(distance < 8, distance, 8 + beyond)
    return nearby + 16 * (offset > 0).astype(jnp.int32)


def iota(shape, dim):
    return lax.broadcasted_iota(jnp.int32, shape, dim)


def narrow_kernel(place, q, k, v, gain_one, gain_two, table, out, side):
    column = pl.multiple_of(place[3] * 384, 128)
    pieces = [weight[:, pl.ds(column, 384)] for weight in (q, k, v)]
    for pair in range(3):
        parts = [piece[:, at : at + 64] for at in (pair * 128, pair * 128 + 64) for piece in pieces]
        out[:, pair * 384 : pair * 384 + 384] = jnp.concatenate(parts, axis=1)
    side[...] = jnp.zeros((8, 128), f32)
    side[0:1, 0:48] = gain_one[...].astype(f32)
    side[1:2, 0:48] = gain_two[...].astype(f32)
    side[2:3, 0:12] = table[0:1].astype(f32)
    side[2:3, 12:24] = table[1:2].astype(f32)
    wide = jnp.concatenate([side[...], jnp.zeros((120, 128), f32)], axis=0).T
    out[:, 1152:1280] = wide[0:48].astype(bf16)


def narrow_shard(place, q, k, v, gain_one, gain_two, table):
    return pl.pallas_call(
        narrow_kernel,
        out_shape=jax.ShapeDtypeStruct((48, 1280), bf16),
        in_specs=[SCALARS] + [FULL] * 6,
        out_specs=FULL,
        scratch_shapes=[pltpu.VMEM((8, 128), f32)],
        compiler_params=params(),
        cost_estimate=small_cost(),
        name="narrow_shard",
    )(place, q, k, v, gain_one.reshape(1, 48), gain_two.reshape(1, 48), table)


def wide_kernel(place, expand, output, contract, out, full, sems):
    x = place[3]
    pieces = [(expand.at[:, at * 768 : at * 768 + 768], out.at[at]) for at in range(4)]
    pieces.append((output, out.at[4]))
    for at in range(2):
        row = pl.multiple_of(x * 96 + at * 48, 16)
        pieces.append((contract.at[pl.ds(row, 48)], out.at[5 + at]))
        row = pl.multiple_of((1 - x) * 96 + at * 48, 16)
        pieces.append((contract.at[pl.ds(row, 48)], full.at[7 + at]))
    copies = [pltpu.make_async_copy(*piece, sems.at[at]) for at, piece in enumerate(pieces)]
    for copy in copies:
        copy.start()
    for copy in copies:
        copy.wait()
    full[0:7] = out[...]


def wide_shard(place, expand, output, contract):
    return pl.pallas_call(
        wide_kernel,
        out_shape=(
            jax.ShapeDtypeStruct((7, 48, 768), bf16), jax.ShapeDtypeStruct((9, 48, 768), bf16),
        ),
        in_specs=[SCALARS, ANY, ANY, ANY],
        out_specs=(FULL, FULL),
        scratch_shapes=[pltpu.SemaphoreType.DMA((9,))],
        compiler_params=params(),
        cost_estimate=small_cost(),
        name="wide_shard",
    )(place, expand, output, contract)


def narrow_blocks(refs):
    shard, b0, a1, a2, turned, b2, b3, four, three, last = refs
    near = [shard, b0, a1, turned.at[1], a2, b2, turned.at[0], b3]
    far = [four.at[0], four.at[1], four.at[2], three.at[1], four.at[3], three.at[2], three.at[0], last]
    return near, far


def place_blocks(place, near, far, dest, sems):
    z, y, c = place[0], place[1], place[2]
    copies = []
    for turn in range(4):
        for dy in range(2):
            owner = ((jnp.bitwise_xor(z, turn) * 2) + jnp.bitwise_xor(y, dy)) * 2
            for other, source in enumerate((near, far)):
                row = pl.multiple_of((owner + jnp.bitwise_xor(c, other)) * 48, 16)
                copy = pltpu.make_async_copy(
                    source[turn * 2 + dy], dest.at[pl.ds(row, 48)], sems.at[len(copies)]
                )
                copy.start()
                copies.append(copy)
    return copies


def place_tokens(x, near, far, dest, sems, count):
    copies = []
    for other, source in enumerate((near, far)):
        row = pl.multiple_of(jnp.bitwise_xor(x, other) * count, count)
        copy = pltpu.make_async_copy(source, dest.at[pl.ds(row, count)], sems.at[other])
        copy.start()
        copies.append(copy)
    return copies


def first_query(place, mine):
    return (place[3] if mine else 1 - place[3]) * 512


def project_kernel(place, x_near, x_far, *refs):
    (w_near, w_far), refs = narrow_blocks(refs[:10]), refs[10:]
    qkv, kept, sent, small, table, tiles, normed, xs, w, sems, xsems = refs
    tokens = place_tokens(place[3], x_near, x_far, xs, xsems, 512)
    blocks = place_blocks(place, w_near, w_far, w, sems)
    for copy in tokens + blocks:
        copy.wait()
    side = w[:, 1152:1280].astype(f32).T
    small[...] = side[:8]
    gain = side[0:1]
    row = iota((768, 128), 0)
    spot = row % 48
    bucket = (row // 48) * 2 + spot // 12
    match = (iota((768, 128), 1) == bucket) & (spot < 24)
    values = jnp.where(match, w[:, 1154:1155].astype(f32), 0.0).astype(bf16)
    head = iota((8, 768), 0)
    chosen = ((iota((8, 768), 1) % 48) % 12 == place[3] * 6 + head) & (head < 6)
    made = dot(chosen.astype(bf16), values, 1, 0)
    table[...] = made
    lane = iota((128, 512), 1)
    spread = (bucket_of(jnp.where(lane < 128, -128 - lane, 384 - lane)) == iota((128, 512), 0)).astype(bf16)
    turned = dot(made.astype(bf16), spread, 1, 0)
    for head in range(6):
        for block, (low, high) in enumerate(((384, 0), (256, 384), (128, 256))):
            parts = [turned[head : head + 1, at : at + 128] for at in (low, high)]
            wide = jnp.broadcast_to(jnp.concatenate(parts, axis=1), (128, 256))
            rolled = pltpu.roll(wide, 0, 1, stride=1, stride_axis=0)
            tiles[head, block * 128 : block * 128 + 128] = rolled[:, 128:256]
    for row in range(0, 1024, 256):
        wide = xs[row : row + 256].astype(f32)
        scale = lax.rsqrt(jnp.mean(wide * wide, axis=-1, keepdims=True) + EPS)
        normed[row : row + 256] = (wide * scale * gain).astype(bf16)
    for col in range(0, 1152, 384):
        made = dot(w[:, col : col + 384], normed[...], 0, 1)
        qkv[col : col + 384] = made.astype(bf16)
    turned = normed[...].T.reshape(8, 2, 48, 1024)
    kept[...] = jnp.where(place[2] == 0, turned[:, 0], turned[:, 1])
    sent[...] = jnp.where(place[2] == 0, turned[:, 1], turned[:, 0])


def project(place, x_near, x_far, blocks):
    return pl.pallas_call(
        project_kernel,
        out_shape=(
            jax.ShapeDtypeStruct((1152, 1024), bf16),
            jax.ShapeDtypeStruct((8, 48, 1024), bf16),
            jax.ShapeDtypeStruct((8, 48, 1024), bf16),
            jax.ShapeDtypeStruct((8, 768), f32),
            jax.ShapeDtypeStruct((8, 128), f32),
            jax.ShapeDtypeStruct((6, 384, 128), f32),
        ),
        in_specs=[SCALARS] + [ANY] * 12,
        out_specs=(FULL,) * 6,
        scratch_shapes=[
            pltpu.VMEM((1024, 768), bf16),
            pltpu.VMEM((1024, 768), bf16),
            pltpu.VMEM((768, 1280), bf16),
            pltpu.SemaphoreType.DMA((16,)),
            pltpu.SemaphoreType.DMA((2,)),
        ],
        compiler_params=params(),
        cost_estimate=small_cost(),
        name="project",
    )(place, x_near, x_far, *blocks)


def attend_kernel(mine, place, table, tile, q, k, v, out, kept, inverse, ka, kt, qt, vt, s):
    head = pl.program_id(0)
    first, valid, instr, pair = first_query(place, mine), place[4], place[5], place[6]

    @pl.when(head == 0)
    def _():
        kt[64:128] = jnp.zeros((64, 1024), bf16)
        qt[64:128] = jnp.zeros((64, 512), bf16)
        row = iota((16, 1024), 0)
        key = iota((16, 1024), 1)
        extra = jnp.where(row < 8, (key // 128 == row).astype(f32), 0.0)
        extra = jnp.where(row == 8, jnp.where(key >= valid, HIDDEN, 0.0), extra)
        extra = jnp.where(row == 9, (key >= instr).astype(f32), extra)
        kt[64:80] = extra.astype(bf16)
        vt[64:80] = jnp.where(row == 0, 1.0, 0.0).astype(bf16)

    row = iota((16, 512), 0)
    query = iota((16, 512), 1) + first
    block = query // 128
    extra = jnp.where(row <= block - 2, table[head, 15], 0.0)
    extra = jnp.where(row >= block + 2, table[head, 31], extra)
    extra = jnp.where(row == 8, 1.0, extra)
    guarded = (query < instr) & (pair == 1)
    extra = jnp.where(row == 9, jnp.where(guarded, HIDDEN, 0.0), extra)
    extra = jnp.where(row > 9, 0.0, extra)
    qt[64:80] = extra.astype(bf16)
    qt[0:64] = q[...]
    kt[0:64] = k[...]
    vt[0:64] = v[...]
    ka[...] = kt[...].T
    s[128:1152] = dot(ka[...], qt[...], 1, 0)
    for part in range(4):
        base = pl.multiple_of(first + part * 128, 128)
        cols = slice(part * 128, part * 128 + 128)
        s[pl.ds(base, 384), cols] = s[pl.ds(base, 384), cols] + tile[0]
    scores = s[128:1152]
    peak = jnp.max(scores, axis=0, keepdims=True)
    weights = jnp.exp(scores - peak).astype(bf16)
    kept[0] = weights
    summed = dot(vt[...], weights, 1, 0)
    share = 1.0 / summed[64:65]
    out[...] = (summed[0:64] * share).astype(bf16)
    inverse[0] = share


def attend(place, table, tiles, qkv, mine):
    half = (lambda s: s[3]) if mine else (lambda s: 1 - s[3])
    grid = pltpu.PrefetchScalarGridSpec(
        num_scalar_prefetch=1,
        grid=(6,),
        in_specs=[
            SCALARS,
            pl.BlockSpec((1, 384, 128), lambda h, s: (h, 0, 0)),
            pl.BlockSpec((64, 512), lambda h, s: (3 * h, half(s))),
            pl.BlockSpec((64, 1024), lambda h, s: (3 * h + 1, 0)),
            pl.BlockSpec((64, 1024), lambda h, s: (3 * h + 2, 0)),
        ],
        out_specs=(
            pl.BlockSpec((64, 512), lambda h, s: (h, 0)),
            pl.BlockSpec((1, 1024, 512), lambda h, s: (h, 0, 0)),
            pl.BlockSpec((1, 1, 512), lambda h, s: (h, 0, 0)),
        ),
        scratch_shapes=[
            pltpu.VMEM((1024, 128), bf16),
            pltpu.VMEM((128, 1024), bf16),
            pltpu.VMEM((128, 512), bf16),
            pltpu.VMEM((80, 1024), bf16),
            pltpu.VMEM((1280, 512), f32),
        ],
    )
    return pl.pallas_call(
        functools.partial(attend_kernel, mine),
        out_shape=(
            jax.ShapeDtypeStruct((384, 512), bf16),
            jax.ShapeDtypeStruct((6, 1024, 512), bf16),
            jax.ShapeDtypeStruct((6, 1, 512), f32),
        ),
        grid_spec=grid,
        compiler_params=params(),
        cost_estimate=small_cost(),
        name="attend_mine" if mine else "attend_theirs",
    )(place, table, tiles, qkv, qkv, qkv)


def diagonal_sums(band):
    flip = (iota((128, 128), 0) + iota((128, 128), 1) == 127).astype(f32)
    rows = []
    for block in range(3):
        here = lax.dot_general(
            flip, band[block * 128 : block * 128 + 128], (((1,), (0,)), ((), ())),
            precision=lax.Precision.HIGHEST, preferred_element_type=f32,
        )
        wide = jnp.concatenate([here, jnp.zeros((128, 128), f32)], axis=1)
        rolled = pltpu.roll(wide, 0, 1, stride=1, stride_axis=0)
        rows.append(jnp.sum(rolled, axis=0, keepdims=True))
    return rows


def bucket_sums(diagonals, sides):
    total = sides
    for block in range(3):
        offset = block * 128 - 1 - iota((256, 128), 0)
        spread = (bucket_of(offset) == iota((256, 128), 1)).astype(f32)
        total = total + lax.dot_general(
            diagonals[block], spread, (((1,), (0,)), ((), ())),
            precision=lax.Precision.HIGHEST, preferred_element_type=f32,
        )
    return total


def attend_back_kernel(carried, mine, place, grad, out, inverse, q, k, v, kept, *refs):
    if carried:
        dq_in, dk_in, dv_in, band_in, far_in, whole, diagonals, sides, *refs = refs
    else:
        dq, dk, dv, band, far, *refs = refs
    va, vt, kt, gt, ds = refs
    first = first_query(place, mine)

    @pl.when(pl.program_id(0) == 0)
    def _():
        row = iota((16, 1024), 0)
        key = iota((16, 1024), 1)
        vt[64:128] = jnp.zeros((64, 1024), bf16)
        vt[64:80] = jnp.where(row < 2, 1.0, 0.0).astype(bf16)
        if carried:
            diagonals[...] = jnp.zeros_like(diagonals)
            sides[...] = jnp.zeros_like(sides)
        kt[64:80] = jnp.where(row < 8, (key // 128 == row).astype(f32), 0.0).astype(bf16)
        gt[64:128] = jnp.zeros((64, 512), bf16)
        ds[0:128] = jnp.zeros((128, 512), bf16)
        ds[1152:1280] = jnp.zeros((128, 512), bf16)

    share = inverse[0]
    scaled = grad[...].astype(f32) * share
    delta = jnp.sum(scaled * out[...].astype(f32), axis=0, keepdims=True)
    high = delta.astype(bf16).astype(f32)
    row = iota((16, 512), 0)
    extra = jnp.where(row == 0, -high, jnp.where(row == 1, high - delta, 0.0))
    gt[64:80] = extra.astype(bf16)
    gt[0:64] = scaled.astype(bf16)
    vt[0:64] = v[...]
    kt[0:64] = k[...]
    va[...] = vt[...].T
    for row_at in range(0, 1024, 256):
        rows = slice(row_at, row_at + 256)
        pull = dot(va[rows], gt[...], 1, 0)
        ds[128 + row_at : 384 + row_at] = (kept[0, rows] * pull).astype(bf16)
    made = dot(kt[...], ds[128:1152], 1, 0)
    block = (iota((8, 512), 1) + first) // 128
    key_block = iota((8, 512), 0)
    totals = made[64:72]
    left = jnp.sum(jnp.where(key_block <= block - 2, totals, 0.0), axis=0, keepdims=True)
    right = jnp.sum(jnp.where(key_block >= block + 2, totals, 0.0), axis=0, keepdims=True)
    dv_made = dot(gt[0:64], kept[0], 1, 1)
    dk_made = dot(q[...], ds[128:1152], 1, 1)
    near = None
    for part in range(4):
        base = pl.multiple_of(first + part * 128, 128)
        window = ds[pl.ds(base, 384), part * 128 : part * 128 + 128].astype(f32)
        near = window if near is None else near + window
    if carried:
        whole[0, 0:64, pl.ds(pl.multiple_of(first, 512), 512)] = made[0:64].astype(bf16)
        whole[0, 0:64, pl.ds(pl.multiple_of(512 - first, 512), 512)] = dq_in[...]
        whole[0, 64:128] = (dk_made + dk_in[...]).astype(bf16)
        whole[0, 128:192] = (dv_made + dv_in[...]).astype(bf16)
        head = pl.program_id(0)
        for at, row in enumerate(diagonal_sums(near + band_in[0])):
            diagonals[at, pl.ds(head, 1)] = row
        lane = iota((1, 128), 1)
        left, right = (
            jnp.sum(side, axis=1, keepdims=True) for side in (left + far_in[0, 0:1], right + far_in[0, 1:2])
        )
        sides[pl.ds(head, 1)] = jnp.where(lane == 15, left, jnp.where(lane == 31, right, 0.0))
        whole[0, 192:208] = jnp.zeros((16, 1024), bf16)

        @pl.when(head == 5)
        def _():
            bias = bucket_sums([diagonals[at] for at in range(3)], sides[...])
            whole[0, 192:208, 0:128] = jnp.concatenate([bias, jnp.zeros((8, 128), f32)], axis=0).astype(bf16)

    else:
        dq[...] = made[0:64].astype(bf16)
        dk[...] = dk_made
        dv[...] = dv_made
        band[0] = near
        far[0] = jnp.concatenate([left, right, jnp.zeros((6, 512), f32)], axis=0)


def attend_back(place, grad, out, inverse, qkv, kept, carry, mine):
    count = 6
    half = (lambda s: s[3]) if mine else (lambda s: 1 - s[3])
    rows512 = pl.BlockSpec((64, 512), lambda h, s: (h, 0))
    rows1024 = pl.BlockSpec((64, 1024), lambda h, s: (h, 0))
    band_spec = pl.BlockSpec((1, 384, 128), lambda h, s: (h, 0, 0))
    far_spec = pl.BlockSpec((1, 8, 512), lambda h, s: (h, 0, 0))
    carry_specs = (rows512, rows1024, rows1024, band_spec, far_spec)
    in_specs = [
        rows512,
        rows512,
        pl.BlockSpec((1, 1, 512), lambda h, s: (h, 0, 0)),
        pl.BlockSpec((64, 512), lambda h, s: (3 * h, half(s))),
        pl.BlockSpec((64, 1024), lambda h, s: (3 * h + 1, 0)),
        pl.BlockSpec((64, 1024), lambda h, s: (3 * h + 2, 0)),
        pl.BlockSpec((1, 1024, 512), lambda h, s: (h, 0, 0)),
    ]
    if carry:
        out_shape = jax.ShapeDtypeStruct((count, 208, 1024), bf16)
        out_specs = pl.BlockSpec((1, 208, 1024), lambda h, s: (h, 0, 0))
        in_specs += carry_specs
    else:
        out_shape = (
            jax.ShapeDtypeStruct((64 * count, 512), bf16),
            jax.ShapeDtypeStruct((64 * count, 1024), f32),
            jax.ShapeDtypeStruct((64 * count, 1024), f32),
            jax.ShapeDtypeStruct((count, 384, 128), f32),
            jax.ShapeDtypeStruct((count, 8, 512), f32),
        )
        out_specs = carry_specs
    grid = pltpu.PrefetchScalarGridSpec(
        num_scalar_prefetch=1,
        grid=(count,),
        in_specs=in_specs,
        out_specs=out_specs,
        scratch_shapes=([pltpu.VMEM((3, 8, 256), f32), pltpu.VMEM((8, 128), f32)] if carry else [])
        + [
            pltpu.VMEM((1024, 128), bf16),
            pltpu.VMEM((128, 1024), bf16),
            pltpu.VMEM((80, 1024), bf16),
            pltpu.VMEM((128, 512), bf16),
            pltpu.VMEM((1280, 512), bf16),
        ],
    )
    return pl.pallas_call(
        functools.partial(attend_back_kernel, bool(carry), mine),
        out_shape=out_shape,
        grid_spec=grid,
        compiler_params=params(VMEM if carry else 66_000_000),
        cost_estimate=cost(count * 1024 * 512 * 1024, 6_000_000),
        name="attend_back_mine" if mine else "attend_back_theirs",
    )(place, grad, out, inverse, qkv, qkv, qkv, kept, *carry)


def gelu_both(wide):
    square = wide * wide
    inner = 0.7978845608 * wide * (1.0 + 0.044715 * square)
    bend = jnp.tanh(inner)
    half = 0.5 * (1.0 + bend)
    slope = 0.7978845608 * (1.0 + 3 * 0.044715 * square)
    return (wide * half, half + 0.5 * wide * (1.0 - bend * bend) * slope)


def all_blocks(full, three, two, y1, y3, side_a, side_b, side_c):
    blocks = [full, three[0], three[1], y1, three[2], two[1], two[0], y3]
    sides = [
        full.at[7:9], side_a.at[2], side_a.at[0], y1.at[7:9], side_a.at[1], side_b.at[1], side_b.at[0], side_c,
    ]
    return blocks, sides


def forward_kernel(
    place, att_near, att_far, x, cot, small, *refs
):
    full, y0, z1, z2, z3, y2, y1, y3, side_a, side_b, side_c = refs[:11]
    nears, near_sides = all_blocks(full, (y0, z1, z2), (z3, y2), y1, y3, side_a, side_b, side_c)
    full, three, two, y1, y3, side_a, side_b, side_c = refs[11:19]
    three, two = [three.at[at] for at in range(3)], [two.at[at] for at in range(2)]
    fars, far_sides = all_blocks(full, three, two, y1, y3, side_a, side_b, side_c)
    refs = refs[19:]
    (
        hid_keep_hbm, hid_send_hbm, pre_hbm, turned_keep, turned_send, result, middle_grad, near_grad, far_grad,
        w_out, w_up, w_down, hid_keep, hid_send, pre, normed_grad, pulled, middle, total, normed, att,
        sems, att_sems, out_sems,
    ) = refs
    z, y, c, xs = place[0], place[1], place[2], place[3]
    att_copies = []
    for other, source in enumerate((att_near, att_far)):
        row = pl.multiple_of(jnp.bitwise_xor(xs, other) * 384, 128)
        copy = pltpu.make_async_copy(source, att.at[pl.ds(row, 384)], att_sems.at[other])
        copy.start()
        att_copies.append(copy)
    groups = ([], [], [])
    for turn in range(4):
        for dy in range(2):
            owner = ((jnp.bitwise_xor(z, turn) * 2) + jnp.bitwise_xor(y, dy)) * 2
            for other in range(2):
                main = (nears, fars)[other][turn * 2 + dy]
                side = (near_sides, far_sides)[other][turn * 2 + dy]
                who = owner + jnp.bitwise_xor(c, other)
                row = pl.multiple_of(who * 48, 16)
                pieces = (
                    (0, main.at[4], w_out.at[pl.ds(row, 48)]),
                    (1, main.at[0:4], w_up.at[:, pl.ds(row, 48)]),
                    (2, main.at[5:7], w_down.at[pl.ds(who * 4 + xs * 2, 2)]),
                    (2, side, w_down.at[pl.ds(who * 4 + (1 - xs) * 2, 2)]),
                )
                for at, (group, source, dest) in enumerate(pieces):
                    sem = sems.at[at, turn * 4 + dy * 2 + other]
                    groups[group].append(pltpu.make_async_copy(source, dest, sem))
    for group in groups:
        for copy in group:
            copy.start()
    for copy in att_copies + groups[0]:
        copy.wait()
    gain = small[1:2]
    wide = x[...].astype(f32) + dot(att[...], w_out[...], 0, 0)
    middle[...] = wide
    scale = lax.rsqrt(jnp.mean(wide * wide, axis=-1, keepdims=True) + EPS)
    normed[...] = (wide * scale * gain).astype(bf16)
    for group in groups[1:]:
        for copy in group:
            copy.wait()
    total[...] = wide
    normed_grad[...] = jnp.zeros_like(normed_grad)

    def chunk(j, carry):
        down = w_down[pl.ds(j * 16, 16)].reshape(768, 768)
        pulled[...] = dot(cot[...], down, 1, 1)
        value, slope = gelu_both(dot(normed[...], w_up[j], 1, 0))
        value = value.astype(bf16)
        total[...] += dot(value, down, 1, 0)
        even = jnp.concatenate([value[:, 0:192], value[:, 384:576]], axis=1)
        odd = jnp.concatenate([value[:, 192:384], value[:, 576:768]], axis=1)
        hid_keep[j] = jnp.where(c == 0, even, odd)
        hid_send[j] = jnp.where(c == 0, odd, even)
        low = (pulled[...] * slope).astype(bf16)
        pre[j] = low
        normed_grad[...] += dot(low, w_up[j], 1, 1)
        return carry

    lax.fori_loop(0, 4, chunk, 0)
    outs = [
        pltpu.make_async_copy(hid_send, hid_send_hbm, out_sems.at[0]),
        pltpu.make_async_copy(hid_keep, hid_keep_hbm, out_sems.at[1]),
        pltpu.make_async_copy(pre.at[0:4], pre_hbm.at[0:4], out_sems.at[2]),
    ]
    for copy in outs:
        copy.start()
    for at, whole in enumerate((normed[...].T, att[...])):
        rows = whole.reshape(8, 2, 48, 512)
        turned_keep[at] = jnp.where(c == 0, rows[:, 0], rows[:, 1])
        turned_send[at] = jnp.where(c == 0, rows[:, 1], rows[:, 0])
    wide = middle[...]
    scale = lax.rsqrt(jnp.mean(wide * wide, axis=-1, keepdims=True) + EPS)
    unit = wide * scale
    incoming = normed_grad[...]
    direct = incoming * gain
    inward = scale * (direct - unit * jnp.mean(direct * unit, axis=-1, keepdims=True))
    grad = cot[...].astype(f32) + inward
    middle_grad[...] = grad
    low = grad.astype(bf16)
    pre[4] = low
    outs.append(pltpu.make_async_copy(pre.at[4], pre_hbm.at[4], out_sems.at[3]))
    outs[3].start()
    for other, dest in enumerate((near_grad, far_grad)):
        row = pl.multiple_of(jnp.bitwise_xor(xs, other) * 384, 128)
        dest[...] = dot(w_out[pl.ds(row, 384)], low, 1, 1).astype(bf16)
    result[...] = total[...].astype(bf16)
    for copy in outs:
        copy.wait()


def forward(place, att_near, att_far, x, cot, small, near, far):
    wide = jax.ShapeDtypeStruct((512, 768), f32)
    half = jax.ShapeDtypeStruct((384, 512), bf16)
    hidden = jax.ShapeDtypeStruct((4, 512, 384), bf16)
    turned = jax.ShapeDtypeStruct((2, 8, 48, 512), bf16)
    return pl.pallas_call(
        forward_kernel,
        out_shape=(
            hidden, hidden, jax.ShapeDtypeStruct((5, 512, 768), bf16), turned, turned,
            jax.ShapeDtypeStruct((512, 768), bf16), wide, half, half,
        ),
        in_specs=[SCALARS, ANY, ANY, FULL, FULL, FULL] + [ANY] * 19,
        out_specs=(ANY, ANY, ANY) + (FULL,) * 6,
        scratch_shapes=[
            pltpu.VMEM((768, 768), bf16),
            pltpu.VMEM((4, 768, 768), bf16),
            pltpu.VMEM((64, 48, 768), bf16),
            pltpu.VMEM((4, 512, 384), bf16),
            pltpu.VMEM((4, 512, 384), bf16),
            pltpu.VMEM((5, 512, 768), bf16),
            pltpu.VMEM((512, 768), f32),
            pltpu.VMEM((512, 768), f32),
            pltpu.VMEM((512, 768), f32),
            pltpu.VMEM((512, 768), f32),
            pltpu.VMEM((512, 768), bf16),
            pltpu.VMEM((768, 512), bf16),
            pltpu.SemaphoreType.DMA((4, 16)),
            pltpu.SemaphoreType.DMA((2,)),
            pltpu.SemaphoreType.DMA((4,)),
        ],
        compiler_params=params(),
        cost_estimate=cost(8_500_000_000, 20_000_000, 512 * 3072),
        name="forward",
    )(place, att_near, att_far, x, cot, small, *near, *far)


def contract_grad_kernel(place, hid, hid_far, cot, cot_far, send, keep):
    made = dot(hid[0], cot[...], 0, 0) + dot(hid_far[0], cot_far[...], 0, 0)
    made = made.astype(bf16).reshape(2, 2, 2, 48, 768)
    send[...] = jnp.where(place[3] == 0, made[:, 1], made[:, 0])
    keep[...] = jnp.where(place[3] == 0, made[:, 0], made[:, 1])


def contract_weight_grad(place, hid, hid_far, cot, cot_far):
    shape = jax.ShapeDtypeStruct((8, 2, 48, 768), bf16)
    spec = pl.BlockSpec((2, 2, 48, 768), lambda j: (j, 0, 0, 0))
    chunk = pl.BlockSpec((1, 512, 384), lambda j: (j, 0, 0))
    whole = pl.BlockSpec((512, 768), lambda j: (0, 0))
    return pl.pallas_call(
        contract_grad_kernel,
        out_shape=(shape, shape),
        grid=(4,),
        in_specs=[SCALARS, chunk, chunk, whole, whole],
        out_specs=(spec, spec),
        compiler_params=params(),
        cost_estimate=cost(2 * 512 * 3072 * 768, 9_000_000),
        name="contract_weight_grad",
    )(place, hid, hid_far, cot, cot_far)


def expand_grad_kernel(place, turned, turned_far, pre, pre_far, b_send, b_keep, c_send, c_keep):
    step = pl.program_id(0)

    def made(at):
        near = dot(turned[at].reshape(384, 512), pre[0], 1, 0)
        return (near + dot(turned_far[at].reshape(384, 512), pre_far[0], 1, 0)).astype(bf16)

    @pl.when(step < 3)
    def _():
        rows = made(0).reshape(4, 2, 48, 768)
        b_send[:, 0] = jnp.where(place[1] == 0, rows[:, 1], rows[:, 0])
        b_keep[:, 0] = jnp.where(place[1] == 0, rows[:, 0], rows[:, 1])

    def by_low(rows):
        rows = rows.reshape(2, 2, 2, 48, 768)
        low = place[0] % 2
        c_send[:, :, 0] = jnp.where(low == 0, rows[:, 1], rows[:, 0])
        c_keep[:, :, 0] = jnp.where(low == 0, rows[:, 0], rows[:, 1])

    @pl.when(step == 3)
    def _():
        by_low(made(0))

    @pl.when(step == 4)
    def _():
        by_low(made(1))


def expand_weight_grad(place, turned, turned_far, pre, pre_far):
    first = jax.ShapeDtypeStruct((4, 3, 48, 768), bf16)
    second = jax.ShapeDtypeStruct((2, 2, 2, 48, 768), bf16)
    first_spec = pl.BlockSpec((4, 1, 48, 768), lambda j: (0, jnp.minimum(j, 2), 0, 0))
    second_spec = pl.BlockSpec((2, 2, 1, 48, 768), lambda j: (0, 0, jnp.maximum(j - 3, 0), 0, 0))
    whole = pl.BlockSpec((2, 8, 48, 512), lambda j: (0, 0, 0, 0))
    chunk = pl.BlockSpec((1, 512, 768), lambda j: (j, 0, 0))
    return pl.pallas_call(
        expand_grad_kernel,
        out_shape=(first, first, second, second),
        grid=(5,),
        in_specs=[SCALARS, whole, whole, chunk, chunk],
        out_specs=(first_spec, first_spec, second_spec, second_spec),
        compiler_params=params(),
        cost_estimate=cost(2 * 512 * 768 * 3840, 12_000_000),
        name="expand_weight_grad",
    )(place, turned, turned_far, pre, pre_far)


def place_grads(whole, grad, sems):
    copies = []
    for head in range(6):
        dest = grad.at[head * 192 : head * 192 + 192]
        copies.append(pltpu.make_async_copy(whole.at[head, 0:192], dest, sems.at[head]))
        copies[-1].start()
    return copies


def weight_grad_kernel(place, mine, other, whole, near, far, grad, bias, sems, bias_sem):
    copies = place_grads(whole, grad, sems)
    copies.append(pltpu.make_async_copy(whole.at[5, 192:208, 0:128], bias, bias_sem))
    copies[-1].start()
    for copy in copies:
        copy.wait()
    for kind, rows, dest in ((place[2], mine, near), (1 - place[2], other, far)):
        spot = iota((384, 128), 0) % 48
        bucket = ((iota((384, 128), 0) // 48) * 2 + kind) * 2 + spot // 6
        chosen = jnp.where((iota((384, 128), 1) == bucket) & (spot < 12), 1.0, 0.0)
        per_head = dot(chosen.astype(bf16), bias[0:8], 1, 1)
        pattern = (iota((384, 8), 1) == (iota((384, 8), 0) % 48) % 6).astype(f32)
        column = jnp.sum(per_head * pattern, axis=1, keepdims=True)
        side = jnp.where(iota((384, 128), 1) == 0, column, 0.0)
        dest[:, :, 1152:1280] = side.astype(bf16).reshape(8, 48, 128)
        left = rows[...].reshape(384, 1024)
        for col in range(0, 1152, 384):
            made = dot(left, grad[col : col + 384], 1, 1)
            dest[:, :, col : col + 384] = made.astype(bf16).reshape(8, 48, 384)


def weight_grad(place, mine, other, whole):
    owned = jax.ShapeDtypeStruct((8, 48, 1280), bf16)
    return pl.pallas_call(
        weight_grad_kernel,
        out_shape=(owned, owned),
        in_specs=[SCALARS, FULL, FULL, ANY],
        out_specs=(FULL,) * 2,
        scratch_shapes=[
            pltpu.VMEM((1152, 1024), bf16),
            pltpu.VMEM((16, 128), bf16),
            pltpu.SemaphoreType.DMA((6,)),
            pltpu.SemaphoreType.DMA,
        ],
        compiler_params=params(),
        cost_estimate=cost(2 * 1024 * 768 * 1152, 6_000_000),
        name="weight_grad",
    )(place, mine, other, whole)


def project_back_kernel(place, *refs):
    (w_near, w_far), whole, refs = narrow_blocks(refs[:10]), refs[10], refs[11:]
    part_near, part_far, w, grad, sems, qsems = refs
    x = place[3]
    copies = place_blocks(place, w_near, w_far, w, sems) + place_grads(whole, grad, qsems)
    for copy in copies:
        copy.wait()
    for other, dest in ((1, part_far), (0, part_near)):
        start = pl.multiple_of(jnp.bitwise_xor(x, other) * 512, 512)
        dest[...] = dot(grad[:, pl.ds(start, 512)], w[:, 0:1152], 0, 1).astype(bf16)


def project_back(place, blocks, whole):
    part = jax.ShapeDtypeStruct((512, 768), bf16)
    return pl.pallas_call(
        project_back_kernel,
        out_shape=(part, part),
        in_specs=[SCALARS] + [ANY] * 11,
        out_specs=(FULL,) * 2,
        scratch_shapes=[
            pltpu.VMEM((768, 1280), bf16),
            pltpu.VMEM((1152, 1024), bf16),
            pltpu.SemaphoreType.DMA((16,)),
            pltpu.SemaphoreType.DMA((6,)),
        ],
        compiler_params=params(),
        cost_estimate=cost(2 * 1024 * 768 * 1152, 10_000_000),
        name="project_back",
    )(place, *blocks, whole)


def pass_kernel(place, result):
    for at in range(7):
        result[at] = place[at]


def hand_on(place):
    return pl.pallas_call(
        pass_kernel,
        out_shape=jax.ShapeDtypeStruct((7,), jnp.int32),
        in_specs=[SCALARS],
        out_specs=SCALARS,
        cost_estimate=pl.CostEstimate(flops=20_000_000_000, bytes_accessed=1000, transcendentals=0),
        name="hand_on",
    )(place)


def finish_kernel(place, a_near, a_far, g_near, g_far, qw, kw, vw, gain, contract, q, k, v, gain_grad, bias):
    swapped = place[3] == 1

    def ordered(near, far):
        near, far = near[...].astype(f32), far[...].astype(f32)
        return jnp.where(swapped, far, near), jnp.where(swapped, near, far)

    for half, wide in enumerate(ordered(a_near, a_far)):
        for at in range(2):
            row = half * 96 + at * 48
            contract[row : row + 48] = wide[at]
    first, second = ordered(g_near, g_far)
    for at, dest in enumerate((q, k, v)):
        for half, wide in enumerate((first, second)):
            for head in range(6):
                column = head * 192 + at * 64
                spot = half * 384 + head * 64
                dest[:, spot : spot + 64] = wide[:, column : column + 64]
    joint = q[...] * qw[...].astype(f32) + k[...] * kw[...].astype(f32) + v[...] * vw[...].astype(f32)
    summed = jnp.broadcast_to(jnp.sum(joint, axis=1, keepdims=True), (48, 128))
    blank = jnp.zeros((80, 128), f32)
    turned = jnp.concatenate([summed, blank], axis=0).T
    gain_grad[...] = turned[0:1, 0:48] / gain[...].astype(f32)
    first = jnp.concatenate([first[:, 1152:1280], blank], axis=0).T
    second = jnp.concatenate([second[:, 1152:1280], blank], axis=0).T
    for row in range(2):
        cols = slice(row * 6, row * 6 + 6)
        bias[row : row + 1, 0:6] = first[0:1, cols]
        bias[row : row + 1, 6:12] = second[0:1, cols]


def finish(place, a_near, a_far, g_near, g_far, qw, kw, vw, gain):
    full = jax.ShapeDtypeStruct((48, 768), f32)
    return pl.pallas_call(
        finish_kernel,
        out_shape=(
            jax.ShapeDtypeStruct((192, 768), f32),
            full, full, full, jax.ShapeDtypeStruct((1, 48), f32), jax.ShapeDtypeStruct((2, 12), f32),
        ),
        in_specs=[SCALARS] + [FULL] * 8,
        out_specs=(FULL,) * 6,
        compiler_params=params(),
        cost_estimate=cost(1000, 1_000_000),
        name="finish",
    )(place, a_near, a_far, g_near, g_far, qw, kw, vw, gain.reshape(1, 48))


def finish_wide_kernel(place, b_near, b_far, up, gain, expand, output, gain_grad):
    near, far = b_near[...].astype(f32), b_far[...].astype(f32)
    sides = (jnp.where(place[3] == 0, near, far), jnp.where(place[3] == 0, far, near))
    joint = jnp.zeros((48, 384), f32)
    for half, side in enumerate(sides):
        for at in range(4):
            cols = slice(at * 768 + half * 384, at * 768 + half * 384 + 384)
            expand[:, cols] = side[at]
            joint = joint + side[at] * up[:, cols].astype(f32)
        output[:, half * 384 : half * 384 + 384] = side[4]
    column = jnp.broadcast_to(jnp.sum(joint, axis=1, keepdims=True), (48, 128))
    turned = jnp.concatenate([column, jnp.zeros((80, 128), f32)], axis=0).T
    gain_grad[...] = turned[0:1, 0:48] / gain[...].astype(f32)


def finish_wide(place, b_near, b_far, up, gain):
    return pl.pallas_call(
        finish_wide_kernel,
        out_shape=(
            jax.ShapeDtypeStruct((48, 3072), f32),
            jax.ShapeDtypeStruct((48, 768), f32), jax.ShapeDtypeStruct((1, 48), f32),
        ),
        in_specs=[SCALARS] + [FULL] * 4,
        out_specs=(FULL,) * 3,
        compiler_params=params(),
        cost_estimate=cost(1000, 2_000_000),
        name="finish_wide",
    )(place, b_near, b_far, up, gain.reshape(1, 48))


def input_grad_kernel(place, x, small, near, far, middle_grad, result):
    for row in range(0, 512, 256):
        rows = slice(row, row + 256)
        wide = x[rows].astype(f32)
        scale = lax.rsqrt(jnp.mean(wide * wide, axis=-1, keepdims=True) + EPS)
        unit = wide * scale
        direct = (near[rows].astype(f32) + far[rows].astype(f32)) * small[0:1]
        inward = scale * (direct - unit * jnp.mean(direct * unit, axis=-1, keepdims=True))
        result[rows] = (middle_grad[rows] + inward).astype(bf16)


def input_grad(place, x, small, near, far, middle_grad):
    return pl.pallas_call(
        input_grad_kernel,
        out_shape=jax.ShapeDtypeStruct((512, 768), bf16),
        in_specs=[SCALARS] + [FULL] * 5,
        out_specs=FULL,
        compiler_params=params(),
        cost_estimate=cost(512 * 768 * 20, 6_000_000),
        name="input_grad",
    )(place, x, small, near, far, middle_grad)


def swap(array, axis, bit):
    count = lax.axis_size(axis)
    return lax.ppermute(array, axis, [(i, i ^ bit) for i in range(count)])


def swap_both(array):
    pairs = [(i * 2 + j, (i ^ Y) * 2 + 1 - j) for i in range(lax.axis_size("fsdp")) for j in range(2)]
    return lax.ppermute(array, ("fsdp", "seq"), pairs)


CORE, Y, Z = 1, 2, 4


def after(value, *others):
    return lax.optimization_barrier((value, *others))[0]


class Line:
    def __init__(self, place):
        self.place = place

    def wait(self, *arrays):
        self.place = after(self.place, *arrays)

    def run(self, kernel, *args):
        made = kernel(self.place, *args)
        self.wait(jax.tree.leaves(made)[0])
        return made


def gather_part(array, part, own, now):
    _, dims, gone = part
    for axis in reversed(range(len(dims))):
        if dims[axis] == now:
            array = lax.dynamic_index_in_dim(array, 1 - own[now], axis, keepdims=False)
        elif dims[axis] in gone:
            array = lax.dynamic_index_in_dim(array, own[dims[axis]], axis, keepdims=False)
    return array.astype(f32)


def total(line, parts, own, now=None):
    arrays = after([part[0] for part in parts], line.place)
    made = None
    for array, part in zip(arrays, parts):
        term = gather_part(array, part, own, now)
        made = term if made is None else made + term
    made = lax.optimization_barrier(made.astype(bf16))
    line.wait(made)
    return made


def sum_parts(parts, own, now=None):
    made = None
    for part in parts:
        term = gather_part(part[0], part, own, now)
        made = term if made is None else made + term
    return made


def keep(parts, now, got):
    _, dims, gone = parts[0]
    left = tuple(dim for dim in dims if dim not in gone and dim != now)
    return [(a, d, g + (now,)) for a, d, g in parts] + [(got, left, ())]


def local_split(
    layer_input, query_weight, key_weight, value_weight, output_weight, expand_weight,
    contract_weight, attention_gain, feedforward_gain, bias_table, valid_len, instr_len, pair_flag,
    cotangent,
):
    owner, x = lax.axis_index("fsdp"), lax.axis_index("seq")
    z, y, c = owner // 4, (owner // 2) % 2, owner % 2
    where = jnp.stack([z, y, c, x]).astype(jnp.int32)
    line = Line(where)
    tokens, cot = layer_input[0], cotangent[0]

    def by_z(array):
        return swap(array, "fsdp", Z)

    def by_zz(array):
        return swap(array, "fsdp", 2 * Z)

    def by_y(array):
        return swap(array, "fsdp", Y)

    def by_core(array):
        return swap(array, "fsdp", CORE)

    def by_x(array):
        return swap(array, "seq", 1)

    shard = line.run(
        narrow_shard, query_weight, key_weight, value_weight, attention_gain, feedforward_gain, bias_table
    )
    a2, a1, b0 = by_zz(shard), by_z(shard), by_y(shard)
    x_far, cot_far = by_x(tokens), by_core(cot)
    rest, full = line.run(wide_shard, expand_weight, output_weight, contract_weight)
    a2, a1, b0, rest, cot_far = lax.optimization_barrier((a2, a1, b0, rest, cot_far))
    turned, b2 = by_z(jnp.stack([a2, b0])), by_y(a2)
    four = by_core(jnp.stack([shard, b0, a1, a2]))
    z2, z1, y0 = by_zz(rest), by_z(rest), by_y(rest)
    lens = jnp.stack([valid_len[0], instr_len[0], pair_flag[0]])
    place = jnp.concatenate([where, lens])
    turned, b2, x_far, line.place = lax.optimization_barrier((turned, b2, x_far, place))
    b3 = by_y(turned[0])
    three = by_core(jnp.stack([turned[0], turned[1], b2]))
    last = by_core(b3)
    z1, z2, y0, last, three = lax.optimization_barrier((z1, z2, y0, last, three))
    z3, y2 = by_z(z2), by_y(z2)
    sides = jnp.stack([z1[5:], z2[5:], y0[5:]])
    sides_a = by_x(sides)
    narrow = [shard, b0, a1, a2, turned, b2, b3, four, three, last]

    line.wait(sides)
    qkv, normed_kept, normed_sent, small, table, tiles = line.run(project, tokens, x_far, narrow)
    line.place, z3, y2, sides_a = lax.optimization_barrier((line.place, z3, y2, sides_a))
    y3 = by_y(z3)
    y1 = jnp.concatenate([y0, sides_a[2]], axis=0)
    sides, trio = jnp.stack([z3[5:], y2[5:]]), jnp.stack([y0, z1, z2])
    line.wait(y1, sides, trio)
    y1, sides_b, far_full, far_three = by_z(y1), by_x(sides), by_core(full), by_core(trio)
    out_theirs, kept_theirs, inverse_theirs = line.run(attend, table, tiles, qkv, False)
    line.place, y3, sides_b, far_full, far_three, out_theirs = lax.optimization_barrier(
        (line.place, y3, sides_b, far_full, far_three, out_theirs)
    )
    two = jnp.stack([z3, y2])
    line.wait(two)
    out_got, sides_c, far_two = by_x(out_theirs), by_x(y3[5:]), by_core(two)
    out_mine, kept_mine, inverse_mine = line.run(attend, table, tiles, qkv, True)
    out_mine, y1, out_got, sides_c, far_two, y3, sides_a, sides_b = lax.optimization_barrier(
        (out_mine, y1, out_got, sides_c, far_two, y3, sides_a, sides_b)
    )
    near = [full, y0, z1, z2, z3, y2, y1, y3, sides_a, sides_b, sides_c]
    far = [far_full, far_three, far_two] + [by_core(block) for block in (y1, y3, sides_a, sides_b, sides_c)]
    hid, hid_sent, pre, turned, turned_sent, layer_output, middle_grad, grad_mine, grad_sent = line.run(
        forward, out_mine, out_got, tokens, cot, small, near, far
    )
    hid_far, grad_theirs, pre_far, turned_far = by_core(hid_sent), by_x(grad_sent), by_core(pre), by_core(turned_sent)

    own = {"high": z // 2, "low": z % 2, "y": y, "x": x}

    def parts(kept, got, *dims):
        lead = tuple({"high": 2, "low": 2, "y": 2}[dim] for dim in dims if dim != "n")
        shape = lead + kept.shape[-3:] if "n" in dims else lead + kept.shape[-2:]
        return [(array.reshape(shape), dims, ()) for array in (kept, got)]

    carry = line.run(
        lambda place: attend_back(place, grad_mine, out_mine, inverse_mine, qkv, kept_mine, (), True)
    )
    line.wait(grad_theirs)
    b_sent, b_kept, c_sent, c_kept = line.run(expand_weight_grad, turned, turned_far, pre, pre_far)
    b_got, c_got = by_y(b_sent), by_z(c_sent)
    b_parts = parts(b_kept, b_got, "high", "low", "n")
    c_parts = parts(c_kept, c_got, "high", "y", "n")
    sent, kept = line.run(contract_weight_grad, hid, hid_far, cot, cot_far)
    a_got = by_x(sent)
    a_parts = parts(kept, a_got, "high", "low", "y", "n")
    whole = line.run(
        lambda place: attend_back(
            place, grad_theirs, out_theirs, inverse_theirs, qkv, kept_theirs, carry, False
        )
    )
    b_got = by_z(total(line, b_parts, own, "low"))
    b_parts = keep(b_parts, "low", b_got)
    c_got = by_y(total(line, c_parts, own, "y"))
    c_parts = keep(c_parts, "y", c_got)
    g_near, g_far = line.run(weight_grad, normed_kept, normed_sent, whole)
    g_parts = parts(g_near, by_core(g_far), "high", "low", "y")
    line.wait(a_got, b_got, c_got)
    line.place = hand_on(line.place)
    g_parts = keep(g_parts, "low", by_z(total(line, g_parts, own, "low")))
    a_parts = keep(a_parts, "y", by_y(total(line, a_parts, own, "y")))
    arrays = after([part[0] for part in b_parts + c_parts], line.place)
    held = [(array, *part[1:]) for array, part in zip(arrays, b_parts + c_parts)]
    joint = jnp.concatenate([sum_parts(held[:3], own), sum_parts(held[3:], own)], axis=1).astype(bf16)
    sent = lax.dynamic_slice_in_dim(joint, (1 - x) * 384, 384, axis=3)
    kept = lax.dynamic_slice_in_dim(joint, x * 384, 384, axis=3)
    sent, kept = lax.optimization_barrier((sent, kept))
    line.wait(sent, kept)
    bc_parts = [(kept, ("high", "n"), ()), (by_x(sent), ("high", "n"), ())]
    part_near, part_far = line.run(project_back, narrow, whole)
    part_got = by_x(part_far)
    a_parts = keep(a_parts, "low", by_z(total(line, a_parts, own, "low")))
    bc_parts = keep(bc_parts, "high", by_zz(total(line, bc_parts, own, "high")))
    g_parts = keep(g_parts, "y", by_y(total(line, g_parts, own, "y")))
    a_parts = keep(a_parts, "high", by_zz(total(line, a_parts, own, "high")))
    b_low = total(line, bc_parts, own)
    b_other = by_x(b_low)
    g_parts = keep(g_parts, "high", by_zz(total(line, g_parts, own, "high")))
    result = line.run(input_grad, tokens, small, part_near, part_got, middle_grad)
    a_low = total(line, a_parts, own)
    a_other = by_x(a_low)
    g_low = total(line, g_parts, own)
    g_other = by_x(g_low)
    expand_sum, output_sum, gain_two = line.run(finish_wide, b_low, b_other, expand_weight, feedforward_gain)
    contract_sum, *grads, gain_one, bias_grad = line.run(
        finish, a_low, a_other, g_low, g_other, query_weight, key_weight, value_weight, attention_gain
    )
    return (
        layer_output[None], result[None], gain_one[0], gain_two[0], *grads,
        output_sum, expand_sum, contract_sum, bias_grad,
    )


def bucket_table(query_pos, key_pos):
    offset = key_pos[None, :] - query_pos[:, None]
    distance = jnp.abs(offset)
    beyond = jnp.zeros_like(distance)
    for far_edge in far_edges:
        beyond = beyond + (distance >= far_edge).astype(jnp.int32)
    nearby = jnp.where(distance < 8, distance, 8 + beyond)
    return nearby + 16 * (offset > 0).astype(jnp.int32)


def visible_keys(query_pos, key_pos, valid_len, instr_len, pair_flag):
    in_valid = key_pos[None, None, :] < valid_len[:, None, None]
    guarded = (
        (pair_flag[:, None, None] == 1)
        & (query_pos[None, :, None] < instr_len[:, None, None])
        & (key_pos[None, None, :] >= instr_len[:, None, None])
    )
    return in_valid & jnp.logical_not(guarded)


def rms_scale(values):
    return lax.rsqrt(jnp.mean(values * values, axis=-1, keepdims=True) + EPS)


def norm_back(values, scale, gain, grad_out):
    normed = values * scale
    grad_normed = grad_out * gain
    grad_values = scale * (
        grad_normed - normed * jnp.mean(grad_normed * normed, axis=-1, keepdims=True)
    )
    return (grad_values, jnp.sum(grad_out * normed, axis=(0, 1)))


def gelu_tanh(values):
    return jax.nn.gelu(values, approximate=True)


def local(
    layer_input,
    query_weight,
    key_weight,
    value_weight,
    output_weight,
    expand_weight,
    contract_weight,
    attention_gain,
    feedforward_gain,
    bias_table,
    valid_len,
    instr_len,
    pair_flag,
    cotangent,
):
    f32 = jnp.float32
    bf16 = jnp.bfloat16
    row_count, local_len, model_width = layer_input.shape
    head_count = bias_table.shape[1]
    head_size = model_width // head_count
    full_len = local_len * lax.axis_size("seq")
    local_start = lax.axis_index("seq") * local_len
    query_pos = local_start + jnp.arange(local_len, dtype=jnp.int32)
    key_pos = jnp.arange(full_len, dtype=jnp.int32)
    buckets = bucket_table(query_pos, key_pos)
    onehot = buckets[:, :, None] == jnp.arange(BUCKETS, dtype=jnp.int32)[None, None, :]
    visible = visible_keys(query_pos, key_pos, valid_len, instr_len, pair_flag)
    input_wide = layer_input.astype(f32)

    def attend_probs(queries, key_heads, table_full):
        rel_bias = jnp.einsum(
            "ijb,bh->hij", onehot.astype(bf16), table_full, preferred_element_type=f32
        )
        raw_scores = jnp.einsum("rihe,rjhe->rhij", queries, key_heads, preferred_element_type=f32)
        scores = jnp.where(visible[:, None], raw_scores + rel_bias[None], -1000000000.0)
        row_peak = jnp.max(scores, axis=-1, keepdims=True)
        log_total = row_peak + jnp.log(jnp.sum(jnp.exp(scores - row_peak), axis=-1, keepdims=True))
        return (jnp.exp(scores - log_total), log_total[..., 0])

    def forward(weights):
        (
            query_full,
            key_full,
            value_full,
            output_full,
            expand_full,
            contract_full,
            gain_one,
            gain_two,
            table_full,
        ) = weights
        scale_one = rms_scale(input_wide)
        normed_low = (input_wide * scale_one * gain_one.astype(f32)).astype(bf16)

        def project(weight):
            return jnp.einsum("rtd,de->rte", normed_low, weight, preferred_element_type=f32).astype(
                bf16
            )

        query_low = project(query_full)
        key_low = project(key_full)
        value_low = project(value_full)
        key_all, value_all = (
            lax.all_gather(key_low, "seq", axis=1, tiled=True),
            lax.all_gather(value_low, "seq", axis=1, tiled=True),
        )
        queries = query_low.reshape(row_count, local_len, head_count, head_size)
        key_heads = key_all.reshape(row_count, full_len, head_count, head_size)
        value_heads = value_all.reshape(row_count, full_len, head_count, head_size)
        probs, log_total = attend_probs(queries, key_heads, table_full)
        probs_low = probs.astype(bf16)
        attended = jnp.einsum("rhij,rjhe->rihe", probs_low, value_heads, preferred_element_type=f32)
        attended = attended.reshape(row_count, local_len, model_width).astype(bf16)
        middle = input_wide + jnp.einsum(
            "rtd,de->rte", attended, output_full, preferred_element_type=f32
        )
        scale_two = rms_scale(middle)
        normed_two = (middle * scale_two * gain_two.astype(f32)).astype(bf16)
        hidden_pre = jnp.einsum("rtd,df->rtf", normed_two, expand_full, preferred_element_type=f32)
        hidden_low = gelu_tanh(hidden_pre).astype(bf16)
        result = middle + jnp.einsum(
            "rtf,fd->rtd", hidden_low, contract_full, preferred_element_type=f32
        )
        return (
            result,
            scale_one,
            normed_low,
            queries,
            key_heads,
            value_heads,
            probs,
            probs_low,
            log_total,
            attended,
            middle,
            scale_two,
            normed_two,
            hidden_pre,
            hidden_low,
        )

    stored = forward(
        (
            lax.all_gather(query_weight, "fsdp", axis=0, tiled=True),
            lax.all_gather(key_weight, "fsdp", axis=0, tiled=True),
            lax.all_gather(value_weight, "fsdp", axis=0, tiled=True),
            lax.all_gather(output_weight, "fsdp", axis=0, tiled=True),
            lax.all_gather(expand_weight, "fsdp", axis=0, tiled=True),
            lax.all_gather(contract_weight, "fsdp", axis=0, tiled=True),
            lax.all_gather(attention_gain, "fsdp", axis=0, tiled=True),
            lax.all_gather(feedforward_gain, "fsdp", axis=0, tiled=True),
            lax.all_gather(bias_table, "fsdp", axis=0, tiled=True),
        )
    )
    layer_output = stored[0].astype(bf16)
    gathered = (
        lax.all_gather(query_weight, "fsdp", axis=0, tiled=True),
        lax.all_gather(key_weight, "fsdp", axis=0, tiled=True),
        lax.all_gather(value_weight, "fsdp", axis=0, tiled=True),
        lax.all_gather(output_weight, "fsdp", axis=0, tiled=True),
        lax.all_gather(expand_weight, "fsdp", axis=0, tiled=True),
        lax.all_gather(contract_weight, "fsdp", axis=0, tiled=True),
        lax.all_gather(attention_gain, "fsdp", axis=0, tiled=True),
        lax.all_gather(feedforward_gain, "fsdp", axis=0, tiled=True),
        lax.all_gather(bias_table, "fsdp", axis=0, tiled=True),
    )
    kept = forward(gathered)
    (
        unused,
        scale_one,
        normed_low,
        queries,
        key_heads,
        value_heads,
        probs,
        probs_low,
        log_total,
        attended,
        middle,
        scale_two,
        normed_two,
        hidden_pre,
        hidden_low,
    ) = kept
    (
        query_full,
        key_full,
        value_full,
        output_full,
        expand_full,
        contract_full,
        gain_one,
        gain_two,
        table_full,
    ) = gathered
    gain_one_wide = gain_one.astype(f32)
    gain_two_wide = gain_two.astype(f32)
    contract_grad = jnp.einsum("rtf,rtd->fd", hidden_low, cotangent, preferred_element_type=f32)
    grad_hidden = jnp.einsum("rtd,fd->rtf", cotangent, contract_full, preferred_element_type=f32)
    gelu_pull = jax.vjp(gelu_tanh, hidden_pre)[1]
    grad_pre = gelu_pull(grad_hidden)[0].astype(bf16)
    expand_grad = jnp.einsum("rtd,rtf->df", normed_two, grad_pre, preferred_element_type=f32)
    grad_normed_two = jnp.einsum("rtf,df->rtd", grad_pre, expand_full, preferred_element_type=f32)
    grad_middle_norm, gain_two_grad = norm_back(middle, scale_two, gain_two_wide, grad_normed_two)
    grad_middle = cotangent.astype(f32) + grad_middle_norm
    grad_branch = grad_middle.astype(bf16)
    output_grad = jnp.einsum("rtd,rte->de", attended, grad_branch, preferred_element_type=f32)
    grad_attended = jnp.einsum(
        "rte,de->rtd", grad_branch, output_full, preferred_element_type=f32
    ).astype(bf16)
    grad_attended = grad_attended.reshape(row_count, local_len, head_count, head_size)
    grad_probs = jnp.einsum(
        "rihe,rjhe->rhij", grad_attended, value_heads, preferred_element_type=f32
    )
    row_delta = jnp.sum(probs * grad_probs, axis=-1)
    grad_scores = probs * (grad_probs - row_delta[..., None])
    bias_part = jnp.einsum(
        "hij,ijb->bh",
        jnp.sum(grad_scores, axis=0),
        onehot.astype(f32),
        precision=lax.Precision.HIGHEST,
    )
    scores_low = grad_scores.astype(bf16)
    grad_queries = jnp.einsum("rhij,rjhe->rihe", scores_low, key_heads, preferred_element_type=f32)
    grad_queries = grad_queries.reshape(row_count, local_len, model_width).astype(bf16)
    value_partial = jnp.einsum(
        "rhij,rihe->rjhe", probs_low, grad_attended, preferred_element_type=f32
    ).reshape(row_count, full_len, model_width)
    key_partial = jnp.einsum(
        "rhij,rihe->rjhe", scores_low, queries, preferred_element_type=f32
    ).reshape(row_count, full_len, model_width)
    key_summed, value_summed = (
        lax.psum_scatter(
            key_partial.astype(jnp.bfloat16), "seq", scatter_dimension=1, tiled=True
        ).astype(jnp.float32),
        lax.psum_scatter(
            value_partial.astype(jnp.bfloat16), "seq", scatter_dimension=1, tiled=True
        ).astype(jnp.float32),
    )
    grad_keys = key_summed.astype(bf16)
    grad_values = value_summed.astype(bf16)
    query_part = jnp.einsum("rtd,rte->de", normed_low, grad_queries, preferred_element_type=f32)
    key_part = jnp.einsum("rtd,rte->de", normed_low, grad_keys, preferred_element_type=f32)
    value_part = jnp.einsum("rtd,rte->de", normed_low, grad_values, preferred_element_type=f32)
    grad_normed_one = jnp.einsum(
        "rte,de->rtd", grad_queries, query_full, preferred_element_type=f32
    )
    grad_normed_one = grad_normed_one + jnp.einsum(
        "rte,de->rtd", grad_keys, key_full, preferred_element_type=f32
    )
    grad_normed_one = grad_normed_one + jnp.einsum(
        "rte,de->rtd", grad_values, value_full, preferred_element_type=f32
    )
    grad_input_norm, gain_one_grad = norm_back(
        input_wide, scale_one, gain_one_wide, grad_normed_one
    )
    input_grad = (grad_middle + grad_input_norm).astype(bf16)
    owned = (
        lax.psum_scatter(
            query_part.astype(jnp.bfloat16), "fsdp", scatter_dimension=0, tiled=True
        ).astype(jnp.float32),
        lax.psum_scatter(
            key_part.astype(jnp.bfloat16), "fsdp", scatter_dimension=0, tiled=True
        ).astype(jnp.float32),
        lax.psum_scatter(
            value_part.astype(jnp.bfloat16), "fsdp", scatter_dimension=0, tiled=True
        ).astype(jnp.float32),
        lax.psum_scatter(
            output_grad.astype(jnp.bfloat16), "fsdp", scatter_dimension=0, tiled=True
        ).astype(jnp.float32),
        lax.psum_scatter(
            expand_grad.astype(jnp.bfloat16), "fsdp", scatter_dimension=0, tiled=True
        ).astype(jnp.float32),
        lax.psum_scatter(
            contract_grad.astype(jnp.bfloat16), "fsdp", scatter_dimension=0, tiled=True
        ).astype(jnp.float32),
        lax.psum_scatter(
            gain_one_grad.astype(jnp.bfloat16), "fsdp", scatter_dimension=0, tiled=True
        ).astype(jnp.float32),
        lax.psum_scatter(
            gain_two_grad.astype(jnp.bfloat16), "fsdp", scatter_dimension=0, tiled=True
        ).astype(jnp.float32),
        lax.psum_scatter(
            bias_part.astype(jnp.bfloat16), "fsdp", scatter_dimension=0, tiled=True
        ).astype(jnp.float32),
    )
    summed = (
        lax.psum(owned[0].astype(jnp.bfloat16), "seq").astype(jnp.float32),
        lax.psum(owned[1].astype(jnp.bfloat16), "seq").astype(jnp.float32),
        lax.psum(owned[2].astype(jnp.bfloat16), "seq").astype(jnp.float32),
        lax.psum(owned[3].astype(jnp.bfloat16), "seq").astype(jnp.float32),
        lax.psum(owned[4].astype(jnp.bfloat16), "seq").astype(jnp.float32),
        lax.psum(owned[5].astype(jnp.bfloat16), "seq").astype(jnp.float32),
        lax.psum(owned[6].astype(jnp.bfloat16), "seq").astype(jnp.float32),
        lax.psum(owned[7].astype(jnp.bfloat16), "seq").astype(jnp.float32),
        lax.psum(owned[8].astype(jnp.bfloat16), "seq").astype(jnp.float32),
    )
    (
        query_grad,
        key_grad,
        value_grad,
        output_sum,
        expand_sum,
        contract_sum,
        gain_one_sum,
        gain_two_sum,
        bias_grad,
    ) = summed
    return (
        layer_output,
        input_grad,
        gain_one_sum,
        gain_two_sum,
        query_grad,
        key_grad,
        value_grad,
        output_sum,
        expand_sum,
        contract_sum,
        bias_grad,
    )


def solution(mesh):
    in_specs = (
        P("fsdp", "seq", None),
        P("fsdp", None),
        P("fsdp", None),
        P("fsdp", None),
        P("fsdp", None),
        P("fsdp", None),
        P("fsdp", None),
        P("fsdp"),
        P("fsdp"),
        P("fsdp", None),
        P("fsdp"),
        P("fsdp"),
        P("fsdp"),
        P("fsdp", "seq", None),
    )
    out_specs = (
        P("fsdp", "seq", None),
        P("fsdp", "seq", None),
        P("fsdp"),
        P("fsdp"),
        P("fsdp", None),
        P("fsdp", None),
        P("fsdp", None),
        P("fsdp", None),
        P("fsdp", None),
        P("fsdp", None),
        P("fsdp", None),
    )
    split = mesh.shape["fsdp"] == 16 and mesh.shape["seq"] == 2
    step = local_split if split else local
    return jax.shard_map(step, mesh=mesh, in_specs=in_specs, out_specs=out_specs, check_vma=False)
```

```python
import functools
import itertools
import math

import jax
import jax.numpy as jnp
from jax import lax
from jax.experimental import pallas as pl
from jax.experimental.pallas import tpu as pltpu
from jax.sharding import PartitionSpec as P

f32 = jnp.float32
bf16 = jnp.bfloat16
BUCKETS = 32
EPS = 1e-06
far_edges = (12, 16, 23, 32, 46, 64, 91)
HIDDEN = -(2.0**30)
VMEM = 56 * 1024 * 1024
MOST = 66_900_000
ANY = pl.BlockSpec(memory_space=pl.ANY)
FULL = pl.BlockSpec(memory_space=pltpu.VMEM)
SCALARS = pl.BlockSpec(memory_space=pltpu.SMEM)


def dot(left, right, left_dim, right_dim):
    return lax.dot_general(
        left, right, (((left_dim,), (right_dim,)), ((), ())), preferred_element_type=f32
    )


def params(limit=VMEM):
    return pltpu.CompilerParams(vmem_limit_bytes=limit)


def cost(flops, byte_count, exps=0):
    return pl.CostEstimate(flops=flops // 1000, bytes_accessed=byte_count // 1000, transcendentals=exps // 1000)


def small_cost():
    return pl.CostEstimate(flops=1000, bytes_accessed=1000, transcendentals=0)


def bucket_of(offset):
    distance = jnp.abs(offset)
    beyond = jnp.zeros_like(distance)
    for far_edge in far_edges:
        beyond = beyond + (distance >= far_edge).astype(jnp.int32)
    nearby = jnp.where(distance < 8, distance, 8 + beyond)
    return nearby + 16 * (offset > 0).astype(jnp.int32)


def iota(shape, dim):
    return lax.broadcasted_iota(jnp.int32, shape, dim)


def narrow_kernel(place, q, k, v, gain_one, gain_two, table, out, side):
    column = pl.multiple_of(place[3] * 384, 128)
    pieces = [weight[:, pl.ds(column, 384)] for weight in (q, k, v)]
    for pair in range(3):
        parts = [piece[:, at : at + 64] for at in (pair * 128, pair * 128 + 64) for piece in pieces]
        out[:, pair * 384 : pair * 384 + 384] = jnp.concatenate(parts, axis=1)
    side[...] = jnp.zeros((8, 128), f32)
    side[0:1, 0:48] = gain_one[...].astype(f32)
    side[1:2, 0:48] = gain_two[...].astype(f32)
    side[2:3, 0:12] = table[0:1].astype(f32)
    side[2:3, 12:24] = table[1:2].astype(f32)
    wide = jnp.concatenate([side[...], jnp.zeros((120, 128), f32)], axis=0).T
    out[:, 1152:1280] = wide[0:48].astype(bf16)


def narrow_shard(place, q, k, v, gain_one, gain_two, table):
    return pl.pallas_call(
        narrow_kernel,
        out_shape=jax.ShapeDtypeStruct((48, 1280), bf16),
        in_specs=[SCALARS] + [FULL] * 6,
        out_specs=FULL,
        scratch_shapes=[pltpu.VMEM((8, 128), f32)],
        compiler_params=params(),
        cost_estimate=small_cost(),
        name="narrow_shard",
    )(place, q, k, v, gain_one.reshape(1, 48), gain_two.reshape(1, 48), table)


def wide_kernel(place, expand, output, contract, out, full, sems):
    x = place[3]
    pieces = [(expand.at[:, at * 768 : at * 768 + 768], out.at[at]) for at in range(4)]
    pieces.append((output, out.at[4]))
    for at in range(2):
        row = pl.multiple_of(x * 96 + at * 48, 16)
        pieces.append((contract.at[pl.ds(row, 48)], out.at[5 + at]))
        row = pl.multiple_of((1 - x) * 96 + at * 48, 16)
        pieces.append((contract.at[pl.ds(row, 48)], full.at[7 + at]))
    copies = [pltpu.make_async_copy(*piece, sems.at[at]) for at, piece in enumerate(pieces)]
    for copy in copies:
        copy.start()
    for copy in copies:
        copy.wait()
    full[0:7] = out[...]


def wide_shard(place, expand, output, contract):
    return pl.pallas_call(
        wide_kernel,
        out_shape=(
            jax.ShapeDtypeStruct((7, 48, 768), bf16), jax.ShapeDtypeStruct((9, 48, 768), bf16),
        ),
        in_specs=[SCALARS, ANY, ANY, ANY],
        out_specs=(FULL, FULL),
        scratch_shapes=[pltpu.SemaphoreType.DMA((9,))],
        compiler_params=params(),
        cost_estimate=small_cost(),
        name="wide_shard",
    )(place, expand, output, contract)


def narrow_blocks(refs):
    shard, b0, a1, a2, turned, b2, b3, four, three, last = refs
    near = [shard, b0, a1, turned.at[1], a2, b2, turned.at[0], b3]
    far = [four.at[0], four.at[1], four.at[2], three.at[1], four.at[3], three.at[2], three.at[0], last]
    return near, far


def place_blocks(place, near, far, dest, sems):
    z, y, c = place[0], place[1], place[2]
    copies = []
    for turn in range(4):
        for dy in range(2):
            owner = ((jnp.bitwise_xor(z, turn) * 2) + jnp.bitwise_xor(y, dy)) * 2
            for other, source in enumerate((near, far)):
                row = pl.multiple_of((owner + jnp.bitwise_xor(c, other)) * 48, 16)
                copy = pltpu.make_async_copy(
                    source[turn * 2 + dy], dest.at[pl.ds(row, 48)], sems.at[len(copies)]
                )
                copy.start()
                copies.append(copy)
    return copies


def place_tokens(x, near, far, dest, sems, count):
    copies = []
    for other, source in enumerate((near, far)):
        row = pl.multiple_of(jnp.bitwise_xor(x, other) * count, count)
        copy = pltpu.make_async_copy(source, dest.at[pl.ds(row, count)], sems.at[other])
        copy.start()
        copies.append(copy)
    return copies


def first_query(place, mine):
    return (place[3] if mine else 1 - place[3]) * 512


def project_kernel(place, x_near, x_far, *refs):
    (w_near, w_far), refs = narrow_blocks(refs[:10]), refs[10:]
    qkv, kept, sent, small, table, tiles, normed, xs, w, sems, xsems = refs
    tokens = place_tokens(place[3], x_near, x_far, xs, xsems, 512)
    blocks = place_blocks(place, w_near, w_far, w, sems)
    for copy in tokens + blocks:
        copy.wait()
    side = w[:, 1152:1280].astype(f32).T
    small[...] = side[:8]
    gain = side[0:1]
    row = iota((768, 128), 0)
    spot = row % 48
    bucket = (row // 48) * 2 + spot // 12
    match = (iota((768, 128), 1) == bucket) & (spot < 24)
    values = jnp.where(match, w[:, 1154:1155].astype(f32), 0.0).astype(bf16)
    head = iota((8, 768), 0)
    chosen = ((iota((8, 768), 1) % 48) % 12 == place[3] * 6 + head) & (head < 6)
    made = dot(chosen.astype(bf16), values, 1, 0)
    table[...] = made
    lane = iota((128, 512), 1)
    spread = (bucket_of(jnp.where(lane < 128, -128 - lane, 384 - lane)) == iota((128, 512), 0)).astype(bf16)
    turned = dot(made.astype(bf16), spread, 1, 0)
    for head in range(6):
        for block, (low, high) in enumerate(((384, 0), (256, 384), (128, 256))):
            parts = [turned[head : head + 1, at : at + 128] for at in (low, high)]
            wide = jnp.broadcast_to(jnp.concatenate(parts, axis=1), (128, 256))
            rolled = pltpu.roll(wide, 0, 1, stride=1, stride_axis=0)
            tiles[head, block * 128 : block * 128 + 128] = rolled[:, 128:256]
    for row in range(0, 1024, 256):
        wide = xs[row : row + 256].astype(f32)
        scale = lax.rsqrt(jnp.mean(wide * wide, axis=-1, keepdims=True) + EPS)
        normed[row : row + 256] = (wide * scale * gain).astype(bf16)
    for col in range(0, 1152, 384):
        made = dot(w[:, col : col + 384], normed[...], 0, 1)
        qkv[col : col + 384] = made.astype(bf16)
    turned = normed[...].T.reshape(8, 2, 48, 1024)
    kept[...] = jnp.where(place[2] == 0, turned[:, 0], turned[:, 1])
    sent[...] = jnp.where(place[2] == 0, turned[:, 1], turned[:, 0])


def project(place, x_near, x_far, blocks):
    return pl.pallas_call(
        project_kernel,
        out_shape=(
            jax.ShapeDtypeStruct((1152, 1024), bf16),
            jax.ShapeDtypeStruct((8, 48, 1024), bf16),
            jax.ShapeDtypeStruct((8, 48, 1024), bf16),
            jax.ShapeDtypeStruct((8, 768), f32),
            jax.ShapeDtypeStruct((8, 128), f32),
            jax.ShapeDtypeStruct((6, 384, 128), f32),
        ),
        in_specs=[SCALARS] + [ANY] * 12,
        out_specs=(FULL,) * 6,
        scratch_shapes=[
            pltpu.VMEM((1024, 768), bf16),
            pltpu.VMEM((1024, 768), bf16),
            pltpu.VMEM((768, 1280), bf16),
            pltpu.SemaphoreType.DMA((16,)),
            pltpu.SemaphoreType.DMA((2,)),
        ],
        compiler_params=params(),
        cost_estimate=small_cost(),
        name="project",
    )(place, x_near, x_far, *blocks)


def attend_kernel(mine, place, table, tile, q, k, v, out, kept, inverse, ka, kt, qt, vt, s):
    head = pl.program_id(0)
    first, valid, instr, pair = first_query(place, mine), place[4], place[5], place[6]

    @pl.when(head == 0)
    def _():
        kt[64:128] = jnp.zeros((64, 1024), bf16)
        qt[64:128] = jnp.zeros((64, 512), bf16)
        row = iota((16, 1024), 0)
        key = iota((16, 1024), 1)
        extra = jnp.where(row < 8, (key // 128 == row).astype(f32), 0.0)
        extra = jnp.where(row == 8, jnp.where(key >= valid, HIDDEN, 0.0), extra)
        extra = jnp.where(row == 9, (key >= instr).astype(f32), extra)
        kt[64:80] = extra.astype(bf16)
        vt[64:80] = jnp.where(row == 0, 1.0, 0.0).astype(bf16)

    row = iota((16, 512), 0)
    query = iota((16, 512), 1) + first
    block = query // 128
    extra = jnp.where(row <= block - 2, table[head, 15], 0.0)
    extra = jnp.where(row >= block + 2, table[head, 31], extra)
    extra = jnp.where(row == 8, 1.0, extra)
    guarded = (query < instr) & (pair == 1)
    extra = jnp.where(row == 9, jnp.where(guarded, HIDDEN, 0.0), extra)
    extra = jnp.where(row > 9, 0.0, extra)
    qt[64:80] = extra.astype(bf16)
    qt[0:64] = q[...]
    kt[0:64] = k[...]
    vt[0:64] = v[...]
    ka[...] = kt[...].T
    s[128:1152] = dot(ka[...], qt[...], 1, 0)
    for part in range(4):
        base = pl.multiple_of(first + part * 128, 128)
        cols = slice(part * 128, part * 128 + 128)
        s[pl.ds(base, 384), cols] = s[pl.ds(base, 384), cols] + tile[0]
    scores = s[128:1152]
    peak = jnp.max(scores, axis=0, keepdims=True)
    weights = jnp.exp(scores - peak).astype(bf16)
    kept[0] = weights
    summed = dot(vt[...], weights, 1, 0)
    share = 1.0 / summed[64:65]
    out[...] = (summed[0:64] * share).astype(bf16)
    inverse[0] = share


def attend(place, table, tiles, qkv, mine):
    half = (lambda s: s[3]) if mine else (lambda s: 1 - s[3])
    grid = pltpu.PrefetchScalarGridSpec(
        num_scalar_prefetch=1,
        grid=(6,),
        in_specs=[
            SCALARS,
            pl.BlockSpec((1, 384, 128), lambda h, s: (h, 0, 0)),
            pl.BlockSpec((64, 512), lambda h, s: (3 * h, half(s))),
            pl.BlockSpec((64, 1024), lambda h, s: (3 * h + 1, 0)),
            pl.BlockSpec((64, 1024), lambda h, s: (3 * h + 2, 0)),
        ],
        out_specs=(
            pl.BlockSpec((64, 512), lambda h, s: (h, 0)),
            pl.BlockSpec((1, 1024, 512), lambda h, s: (h, 0, 0)),
            pl.BlockSpec((1, 1, 512), lambda h, s: (h, 0, 0)),
        ),
        scratch_shapes=[
            pltpu.VMEM((1024, 128), bf16),
            pltpu.VMEM((128, 1024), bf16),
            pltpu.VMEM((128, 512), bf16),
            pltpu.VMEM((80, 1024), bf16),
            pltpu.VMEM((1280, 512), f32),
        ],
    )
    return pl.pallas_call(
        functools.partial(attend_kernel, mine),
        out_shape=(
            jax.ShapeDtypeStruct((384, 512), bf16),
            jax.ShapeDtypeStruct((6, 1024, 512), bf16),
            jax.ShapeDtypeStruct((6, 1, 512), f32),
        ),
        grid_spec=grid,
        compiler_params=params(),
        cost_estimate=small_cost(),
        name="attend_mine" if mine else "attend_theirs",
    )(place, table, tiles, qkv, qkv, qkv)


def diagonal_sums(band):
    flip = (iota((128, 128), 0) + iota((128, 128), 1) == 127).astype(f32)
    rows = []
    for block in range(3):
        here = lax.dot_general(
            flip, band[block * 128 : block * 128 + 128], (((1,), (0,)), ((), ())),
            precision=lax.Precision.HIGHEST, preferred_element_type=f32,
        )
        wide = jnp.concatenate([here, jnp.zeros((128, 128), f32)], axis=1)
        rolled = pltpu.roll(wide, 0, 1, stride=1, stride_axis=0)
        rows.append(jnp.sum(rolled, axis=0, keepdims=True))
    return rows


def bucket_sums(diagonals, sides):
    total = sides
    for block in range(3):
        offset = block * 128 - 1 - iota((256, 128), 0)
        spread = (bucket_of(offset) == iota((256, 128), 1)).astype(f32)
        total = total + lax.dot_general(
            diagonals[block], spread, (((1,), (0,)), ((), ())),
            precision=lax.Precision.HIGHEST, preferred_element_type=f32,
        )
    return total


def attend_back_kernel(carried, mine, place, grad, out, inverse, q, k, v, kept, *refs):
    if carried:
        dq_in, dk_in, dv_in, band_in, far_in, whole, diagonals, sides, *refs = refs
    else:
        dq, dk, dv, band, far, *refs = refs
    va, vt, kt, gt, ds = refs
    first = first_query(place, mine)

    @pl.when(pl.program_id(0) == 0)
    def _():
        row = iota((16, 1024), 0)
        key = iota((16, 1024), 1)
        vt[64:128] = jnp.zeros((64, 1024), bf16)
        vt[64:80] = jnp.where(row < 2, 1.0, 0.0).astype(bf16)
        if carried:
            diagonals[...] = jnp.zeros_like(diagonals)
            sides[...] = jnp.zeros_like(sides)
        kt[64:80] = jnp.where(row < 8, (key // 128 == row).astype(f32), 0.0).astype(bf16)
        gt[64:128] = jnp.zeros((64, 512), bf16)
        ds[0:128] = jnp.zeros((128, 512), bf16)
        ds[1152:1280] = jnp.zeros((128, 512), bf16)

    share = inverse[0]
    scaled = grad[...].astype(f32) * share
    delta = jnp.sum(scaled * out[...].astype(f32), axis=0, keepdims=True)
    high = delta.astype(bf16).astype(f32)
    row = iota((16, 512), 0)
    extra = jnp.where(row == 0, -high, jnp.where(row == 1, high - delta, 0.0))
    gt[64:80] = extra.astype(bf16)
    gt[0:64] = scaled.astype(bf16)
    vt[0:64] = v[...]
    kt[0:64] = k[...]
    va[...] = vt[...].T
    for row_at in range(0, 1024, 256):
        rows = slice(row_at, row_at + 256)
        pull = dot(va[rows], gt[...], 1, 0)
        ds[128 + row_at : 384 + row_at] = (kept[0, rows] * pull).astype(bf16)
    made = dot(kt[...], ds[128:1152], 1, 0)
    block = (iota((8, 512), 1) + first) // 128
    key_block = iota((8, 512), 0)
    totals = made[64:72]
    left = jnp.sum(jnp.where(key_block <= block - 2, totals, 0.0), axis=0, keepdims=True)
    right = jnp.sum(jnp.where(key_block >= block + 2, totals, 0.0), axis=0, keepdims=True)
    dv_made = dot(gt[0:64], kept[0], 1, 1)
    dk_made = dot(q[...], ds[128:1152], 1, 1)
    near = None
    for part in range(4):
        base = pl.multiple_of(first + part * 128, 128)
        window = ds[pl.ds(base, 384), part * 128 : part * 128 + 128].astype(f32)
        near = window if near is None else near + window
    if carried:
        whole[0, 0:64, pl.ds(pl.multiple_of(first, 512), 512)] = made[0:64].astype(bf16)
        whole[0, 0:64, pl.ds(pl.multiple_of(512 - first, 512), 512)] = dq_in[...]
        whole[0, 64:128] = (dk_made + dk_in[...]).astype(bf16)
        whole[0, 128:192] = (dv_made + dv_in[...]).astype(bf16)
        head = pl.program_id(0)
        for at, row in enumerate(diagonal_sums(near + band_in[0])):
            diagonals[at, pl.ds(head, 1)] = row
        lane = iota((1, 128), 1)
        left, right = (
            jnp.sum(side, axis=1, keepdims=True) for side in (left + far_in[0, 0:1], right + far_in[0, 1:2])
        )
        sides[pl.ds(head, 1)] = jnp.where(lane == 15, left, jnp.where(lane == 31, right, 0.0))
        whole[0, 192:208] = jnp.zeros((16, 1024), bf16)

        @pl.when(head == 5)
        def _():
            bias = bucket_sums([diagonals[at] for at in range(3)], sides[...])
            whole[0, 192:208, 0:128] = jnp.concatenate([bias, jnp.zeros((8, 128), f32)], axis=0).astype(bf16)

    else:
        dq[...] = made[0:64].astype(bf16)
        dk[...] = dk_made
        dv[...] = dv_made
        band[0] = near
        far[0] = jnp.concatenate([left, right, jnp.zeros((6, 512), f32)], axis=0)


def attend_back(place, grad, out, inverse, qkv, kept, carry, mine):
    count = 6
    half = (lambda s: s[3]) if mine else (lambda s: 1 - s[3])
    rows512 = pl.BlockSpec((64, 512), lambda h, s: (h, 0))
    rows1024 = pl.BlockSpec((64, 1024), lambda h, s: (h, 0))
    band_spec = pl.BlockSpec((1, 384, 128), lambda h, s: (h, 0, 0))
    far_spec = pl.BlockSpec((1, 8, 512), lambda h, s: (h, 0, 0))
    carry_specs = (rows512, rows1024, rows1024, band_spec, far_spec)
    in_specs = [
        rows512,
        rows512,
        pl.BlockSpec((1, 1, 512), lambda h, s: (h, 0, 0)),
        pl.BlockSpec((64, 512), lambda h, s: (3 * h, half(s))),
        pl.BlockSpec((64, 1024), lambda h, s: (3 * h + 1, 0)),
        pl.BlockSpec((64, 1024), lambda h, s: (3 * h + 2, 0)),
        pl.BlockSpec((1, 1024, 512), lambda h, s: (h, 0, 0)),
    ]
    if carry:
        out_shape = jax.ShapeDtypeStruct((count, 208, 1024), bf16)
        out_specs = pl.BlockSpec((1, 208, 1024), lambda h, s: (h, 0, 0))
        in_specs += carry_specs
    else:
        out_shape = (
            jax.ShapeDtypeStruct((64 * count, 512), bf16),
            jax.ShapeDtypeStruct((64 * count, 1024), f32),
            jax.ShapeDtypeStruct((64 * count, 1024), f32),
            jax.ShapeDtypeStruct((count, 384, 128), f32),
            jax.ShapeDtypeStruct((count, 8, 512), f32),
        )
        out_specs = carry_specs
    grid = pltpu.PrefetchScalarGridSpec(
        num_scalar_prefetch=1,
        grid=(count,),
        in_specs=in_specs,
        out_specs=out_specs,
        scratch_shapes=([pltpu.VMEM((3, 8, 256), f32), pltpu.VMEM((8, 128), f32)] if carry else [])
        + [
            pltpu.VMEM((1024, 128), bf16),
            pltpu.VMEM((128, 1024), bf16),
            pltpu.VMEM((80, 1024), bf16),
            pltpu.VMEM((128, 512), bf16),
            pltpu.VMEM((1280, 512), bf16),
        ],
    )
    return pl.pallas_call(
        functools.partial(attend_back_kernel, bool(carry), mine),
        out_shape=out_shape,
        grid_spec=grid,
        compiler_params=params(VMEM if carry else MOST),
        cost_estimate=cost(count * 1024 * 512 * 1024, 6_000_000),
        name="attend_back_mine" if mine else "attend_back_theirs",
    )(place, grad, out, inverse, qkv, qkv, qkv, kept, *carry)


def gelu_both(wide):
    square = wide * wide
    inner = 0.7978845608 * wide * (1.0 + 0.044715 * square)
    bend = jnp.tanh(inner)
    half = 0.5 * (1.0 + bend)
    slope = 0.7978845608 * (1.0 + 3 * 0.044715 * square)
    return (wide * half, half + 0.5 * wide * (1.0 - bend * bend) * slope)


def all_blocks(full, three, two, y1, y3, side_a, side_b, side_c):
    blocks = [full, three[0], three[1], y1, three[2], two[1], two[0], y3]
    sides = [
        full.at[7:9], side_a.at[2], side_a.at[0], y1.at[7:9], side_a.at[1], side_b.at[1], side_b.at[0], side_c,
    ]
    return blocks, sides


def forward_kernel(
    place, att_near, att_far, x, cot, small, *refs
):
    full, y0, z1, z2, z3, y2, y1, y3, side_a, side_b, side_c = refs[:11]
    nears, near_sides = all_blocks(full, (y0, z1, z2), (z3, y2), y1, y3, side_a, side_b, side_c)
    full, three, two, y1, y3, side_a, side_b, side_c = refs[11:19]
    three, two = [three.at[at] for at in range(3)], [two.at[at] for at in range(2)]
    fars, far_sides = all_blocks(full, three, two, y1, y3, side_a, side_b, side_c)
    refs = refs[19:]
    (
        hid_keep_hbm, hid_send_hbm, pre_hbm, turned_keep, turned_send, result, middle_grad, near_grad, far_grad,
        w_out, w_up, w_down, hid_keep, hid_send, pre, normed_grad, pulled, middle, total, normed, att,
        sems, att_sems, out_sems,
    ) = refs
    z, y, c, xs = place[0], place[1], place[2], place[3]
    att_copies = []
    for other, source in enumerate((att_near, att_far)):
        row = pl.multiple_of(jnp.bitwise_xor(xs, other) * 384, 128)
        copy = pltpu.make_async_copy(source, att.at[pl.ds(row, 384)], att_sems.at[other])
        copy.start()
        att_copies.append(copy)
    groups = ([], [], [])
    for turn in range(4):
        for dy in range(2):
            owner = ((jnp.bitwise_xor(z, turn) * 2) + jnp.bitwise_xor(y, dy)) * 2
            for other in range(2):
                main = (nears, fars)[other][turn * 2 + dy]
                side = (near_sides, far_sides)[other][turn * 2 + dy]
                who = owner + jnp.bitwise_xor(c, other)
                row = pl.multiple_of(who * 48, 16)
                pieces = (
                    (0, main.at[4], w_out.at[pl.ds(row, 48)]),
                    (1, main.at[0:4], w_up.at[:, pl.ds(row, 48)]),
                    (2, main.at[5:7], w_down.at[pl.ds(who * 4 + xs * 2, 2)]),
                    (2, side, w_down.at[pl.ds(who * 4 + (1 - xs) * 2, 2)]),
                )
                for at, (group, source, dest) in enumerate(pieces):
                    sem = sems.at[at, turn * 4 + dy * 2 + other]
                    groups[group].append(pltpu.make_async_copy(source, dest, sem))
    for group in groups:
        for copy in group:
            copy.start()
    for copy in att_copies + groups[0]:
        copy.wait()
    gain = small[1:2]
    wide = x[...].astype(f32) + dot(att[...], w_out[...], 0, 0)
    middle[...] = wide
    scale = lax.rsqrt(jnp.mean(wide * wide, axis=-1, keepdims=True) + EPS)
    normed[...] = (wide * scale * gain).astype(bf16)
    for group in groups[1:]:
        for copy in group:
            copy.wait()
    total[...] = wide
    normed_grad[...] = jnp.zeros_like(normed_grad)

    def chunk(j, carry):
        down = w_down[pl.ds(j * 16, 16)].reshape(768, 768)
        pulled[...] = dot(cot[...], down, 1, 1)
        value, slope = gelu_both(dot(normed[...], w_up[j], 1, 0))
        value = value.astype(bf16)
        total[...] += dot(value, down, 1, 0)
        even = jnp.concatenate([value[:, 0:192], value[:, 384:576]], axis=1)
        odd = jnp.concatenate([value[:, 192:384], value[:, 576:768]], axis=1)
        hid_keep[j] = jnp.where(c == 0, even, odd)
        hid_send[j] = jnp.where(c == 0, odd, even)
        low = (pulled[...] * slope).astype(bf16)
        pre[j] = low
        normed_grad[...] += dot(low, w_up[j], 1, 1)
        return carry

    lax.fori_loop(0, 4, chunk, 0)
    outs = [
        pltpu.make_async_copy(hid_send, hid_send_hbm, out_sems.at[0]),
        pltpu.make_async_copy(hid_keep, hid_keep_hbm, out_sems.at[1]),
        pltpu.make_async_copy(pre.at[0:4], pre_hbm.at[0:4], out_sems.at[2]),
    ]
    for copy in outs:
        copy.start()
    for at, whole in enumerate((normed[...].T, att[...])):
        rows = whole.reshape(8, 2, 48, 512)
        turned_keep[at] = jnp.where(c == 0, rows[:, 0], rows[:, 1])
        turned_send[at] = jnp.where(c == 0, rows[:, 1], rows[:, 0])
    wide = middle[...]
    scale = lax.rsqrt(jnp.mean(wide * wide, axis=-1, keepdims=True) + EPS)
    unit = wide * scale
    incoming = normed_grad[...]
    direct = incoming * gain
    inward = scale * (direct - unit * jnp.mean(direct * unit, axis=-1, keepdims=True))
    grad = cot[...].astype(f32) + inward
    middle_grad[...] = grad
    low = grad.astype(bf16)
    pre[4] = low
    outs.append(pltpu.make_async_copy(pre.at[4], pre_hbm.at[4], out_sems.at[3]))
    outs[3].start()
    for other, dest in enumerate((near_grad, far_grad)):
        row = pl.multiple_of(jnp.bitwise_xor(xs, other) * 384, 128)
        dest[...] = dot(w_out[pl.ds(row, 384)], low, 1, 1).astype(bf16)
    result[...] = total[...].astype(bf16)
    for copy in outs:
        copy.wait()


def forward(place, att_near, att_far, x, cot, small, near, far):
    wide = jax.ShapeDtypeStruct((512, 768), f32)
    half = jax.ShapeDtypeStruct((384, 512), bf16)
    hidden = jax.ShapeDtypeStruct((4, 512, 384), bf16)
    turned = jax.ShapeDtypeStruct((2, 8, 48, 512), bf16)
    return pl.pallas_call(
        forward_kernel,
        out_shape=(
            hidden, hidden, jax.ShapeDtypeStruct((5, 512, 768), bf16), turned, turned,
            jax.ShapeDtypeStruct((512, 768), bf16), wide, half, half,
        ),
        in_specs=[SCALARS, ANY, ANY, FULL, FULL, FULL] + [ANY] * 19,
        out_specs=(ANY, ANY, ANY) + (FULL,) * 6,
        scratch_shapes=[
            pltpu.VMEM((768, 768), bf16),
            pltpu.VMEM((4, 768, 768), bf16),
            pltpu.VMEM((64, 48, 768), bf16),
            pltpu.VMEM((4, 512, 384), bf16),
            pltpu.VMEM((4, 512, 384), bf16),
            pltpu.VMEM((5, 512, 768), bf16),
            pltpu.VMEM((512, 768), f32),
            pltpu.VMEM((512, 768), f32),
            pltpu.VMEM((512, 768), f32),
            pltpu.VMEM((512, 768), f32),
            pltpu.VMEM((512, 768), bf16),
            pltpu.VMEM((768, 512), bf16),
            pltpu.SemaphoreType.DMA((4, 16)),
            pltpu.SemaphoreType.DMA((2,)),
            pltpu.SemaphoreType.DMA((4,)),
        ],
        compiler_params=params(),
        cost_estimate=cost(8_500_000_000, 20_000_000, 512 * 3072),
        name="forward",
    )(place, att_near, att_far, x, cot, small, *near, *far)


def contract_grad_kernel(place, hid, hid_far, cot, cot_far, send, keep):
    made = dot(hid[0], cot[...], 0, 0) + dot(hid_far[0], cot_far[...], 0, 0)
    made = made.astype(bf16).reshape(2, 2, 2, 48, 768)
    send[...] = jnp.where(place[3] == 0, made[:, 1], made[:, 0])
    keep[...] = jnp.where(place[3] == 0, made[:, 0], made[:, 1])


def contract_weight_grad(place, hid, hid_far, cot, cot_far):
    shape = jax.ShapeDtypeStruct((8, 2, 48, 768), bf16)
    spec = pl.BlockSpec((2, 2, 48, 768), lambda j: (j, 0, 0, 0))
    chunk = pl.BlockSpec((1, 512, 384), lambda j: (j, 0, 0))
    whole = pl.BlockSpec((512, 768), lambda j: (0, 0))
    return pl.pallas_call(
        contract_grad_kernel,
        out_shape=(shape, shape),
        grid=(4,),
        in_specs=[SCALARS, chunk, chunk, whole, whole],
        out_specs=(spec, spec),
        compiler_params=params(),
        cost_estimate=cost(2 * 512 * 3072 * 768, 9_000_000),
        name="contract_weight_grad",
    )(place, hid, hid_far, cot, cot_far)


def expand_grad_kernel(place, turned, turned_far, pre, pre_far, b_send, b_keep, c_send, c_keep):
    step = pl.program_id(0)

    def made(at):
        near = dot(turned[at].reshape(384, 512), pre[0], 1, 0)
        return (near + dot(turned_far[at].reshape(384, 512), pre_far[0], 1, 0)).astype(bf16)

    @pl.when(step < 3)
    def _():
        rows = made(0).reshape(4, 2, 48, 768)
        b_send[:, 0] = jnp.where(place[1] == 0, rows[:, 1], rows[:, 0])
        b_keep[:, 0] = jnp.where(place[1] == 0, rows[:, 0], rows[:, 1])

    def by_low(rows):
        rows = rows.reshape(2, 2, 2, 48, 768)
        low = place[0] % 2
        c_send[:, :, 0] = jnp.where(low == 0, rows[:, 1], rows[:, 0])
        c_keep[:, :, 0] = jnp.where(low == 0, rows[:, 0], rows[:, 1])

    @pl.when(step == 3)
    def _():
        by_low(made(0))

    @pl.when(step == 4)
    def _():
        by_low(made(1))


def expand_weight_grad(place, turned, turned_far, pre, pre_far):
    first = jax.ShapeDtypeStruct((4, 3, 48, 768), bf16)
    second = jax.ShapeDtypeStruct((2, 2, 2, 48, 768), bf16)
    first_spec = pl.BlockSpec((4, 1, 48, 768), lambda j: (0, jnp.minimum(j, 2), 0, 0))
    second_spec = pl.BlockSpec((2, 2, 1, 48, 768), lambda j: (0, 0, jnp.maximum(j - 3, 0), 0, 0))
    whole = pl.BlockSpec((2, 8, 48, 512), lambda j: (0, 0, 0, 0))
    chunk = pl.BlockSpec((1, 512, 768), lambda j: (j, 0, 0))
    return pl.pallas_call(
        expand_grad_kernel,
        out_shape=(first, first, second, second),
        grid=(5,),
        in_specs=[SCALARS, whole, whole, chunk, chunk],
        out_specs=(first_spec, first_spec, second_spec, second_spec),
        compiler_params=params(),
        cost_estimate=cost(2 * 512 * 768 * 3840, 12_000_000),
        name="expand_weight_grad",
    )(place, turned, turned_far, pre, pre_far)


def place_grads(whole, grad, sems):
    copies = []
    for head in range(6):
        dest = grad.at[head * 192 : head * 192 + 192]
        copies.append(pltpu.make_async_copy(whole.at[head, 0:192], dest, sems.at[head]))
        copies[-1].start()
    return copies


def weight_grad_kernel(place, mine, other, whole, near, far, grad, bias, sems, bias_sem):
    copies = place_grads(whole, grad, sems)
    copies.append(pltpu.make_async_copy(whole.at[5, 192:208, 0:128], bias, bias_sem))
    copies[-1].start()
    for copy in copies:
        copy.wait()
    for kind, rows, dest in ((place[2], mine, near), (1 - place[2], other, far)):
        spot = iota((384, 128), 0) % 48
        bucket = ((iota((384, 128), 0) // 48) * 2 + kind) * 2 + spot // 6
        chosen = jnp.where((iota((384, 128), 1) == bucket) & (spot < 12), 1.0, 0.0)
        per_head = dot(chosen.astype(bf16), bias[0:8], 1, 1)
        pattern = (iota((384, 8), 1) == (iota((384, 8), 0) % 48) % 6).astype(f32)
        column = jnp.sum(per_head * pattern, axis=1, keepdims=True)
        side = jnp.where(iota((384, 128), 1) == 0, column, 0.0)
        dest[:, :, 1152:1280] = side.astype(bf16).reshape(8, 48, 128)
        left = rows[...].reshape(384, 1024)
        for col in range(0, 1152, 384):
            made = dot(left, grad[col : col + 384], 1, 1)
            dest[:, :, col : col + 384] = made.astype(bf16).reshape(8, 48, 384)


def weight_grad(place, mine, other, whole):
    owned = jax.ShapeDtypeStruct((8, 48, 1280), bf16)
    return pl.pallas_call(
        weight_grad_kernel,
        out_shape=(owned, owned),
        in_specs=[SCALARS, FULL, FULL, ANY],
        out_specs=(FULL,) * 2,
        scratch_shapes=[
            pltpu.VMEM((1152, 1024), bf16),
            pltpu.VMEM((16, 128), bf16),
            pltpu.SemaphoreType.DMA((6,)),
            pltpu.SemaphoreType.DMA,
        ],
        compiler_params=params(),
        cost_estimate=cost(2 * 1024 * 768 * 1152, 6_000_000),
        name="weight_grad",
    )(place, mine, other, whole)


def project_back_kernel(place, *refs):
    (w_near, w_far), whole, refs = narrow_blocks(refs[:10]), refs[10], refs[11:]
    part_near, part_far, w, grad, sems, qsems = refs
    x = place[3]
    copies = place_blocks(place, w_near, w_far, w, sems) + place_grads(whole, grad, qsems)
    for copy in copies:
        copy.wait()
    for other, dest in ((1, part_far), (0, part_near)):
        start = pl.multiple_of(jnp.bitwise_xor(x, other) * 512, 512)
        dest[...] = dot(grad[:, pl.ds(start, 512)], w[:, 0:1152], 0, 1).astype(bf16)


def project_back(place, blocks, whole):
    part = jax.ShapeDtypeStruct((512, 768), bf16)
    return pl.pallas_call(
        project_back_kernel,
        out_shape=(part, part),
        in_specs=[SCALARS] + [ANY] * 11,
        out_specs=(FULL,) * 2,
        scratch_shapes=[
            pltpu.VMEM((768, 1280), bf16),
            pltpu.VMEM((1152, 1024), bf16),
            pltpu.SemaphoreType.DMA((16,)),
            pltpu.SemaphoreType.DMA((6,)),
        ],
        compiler_params=params(),
        cost_estimate=cost(2 * 1024 * 768 * 1152, 10_000_000),
        name="project_back",
    )(place, *blocks, whole)


def pass_kernel(place, result):
    for at in range(7):
        result[at] = place[at]


def hand_on(place):
    return pl.pallas_call(
        pass_kernel,
        out_shape=jax.ShapeDtypeStruct((7,), jnp.int32),
        in_specs=[SCALARS],
        out_specs=SCALARS,
        cost_estimate=pl.CostEstimate(flops=20_000_000_000, bytes_accessed=1000, transcendentals=0),
        name="hand_on",
    )(place)


def finish_kernel(place, a_near, a_far, g_near, g_far, qw, kw, vw, gain, contract, q, k, v, gain_grad, bias):
    swapped = place[3] == 1

    def ordered(near, far):
        near, far = near[...].astype(f32), far[...].astype(f32)
        return jnp.where(swapped, far, near), jnp.where(swapped, near, far)

    for half, wide in enumerate(ordered(a_near, a_far)):
        for at in range(2):
            row = half * 96 + at * 48
            contract[row : row + 48] = wide[at]
    first, second = ordered(g_near, g_far)
    for at, dest in enumerate((q, k, v)):
        for half, wide in enumerate((first, second)):
            for head in range(6):
                column = head * 192 + at * 64
                spot = half * 384 + head * 64
                dest[:, spot : spot + 64] = wide[:, column : column + 64]
    joint = q[...] * qw[...].astype(f32) + k[...] * kw[...].astype(f32) + v[...] * vw[...].astype(f32)
    summed = jnp.broadcast_to(jnp.sum(joint, axis=1, keepdims=True), (48, 128))
    blank = jnp.zeros((80, 128), f32)
    turned = jnp.concatenate([summed, blank], axis=0).T
    gain_grad[...] = turned[0:1, 0:48] / gain[...].astype(f32)
    first = jnp.concatenate([first[:, 1152:1280], blank], axis=0).T
    second = jnp.concatenate([second[:, 1152:1280], blank], axis=0).T
    for row in range(2):
        cols = slice(row * 6, row * 6 + 6)
        bias[row : row + 1, 0:6] = first[0:1, cols]
        bias[row : row + 1, 6:12] = second[0:1, cols]


def finish(place, a_near, a_far, g_near, g_far, qw, kw, vw, gain):
    full = jax.ShapeDtypeStruct((48, 768), f32)
    return pl.pallas_call(
        finish_kernel,
        out_shape=(
            jax.ShapeDtypeStruct((192, 768), f32),
            full, full, full, jax.ShapeDtypeStruct((1, 48), f32), jax.ShapeDtypeStruct((2, 12), f32),
        ),
        in_specs=[SCALARS] + [FULL] * 8,
        out_specs=(FULL,) * 6,
        compiler_params=params(),
        cost_estimate=cost(1000, 1_000_000),
        name="finish",
    )(place, a_near, a_far, g_near, g_far, qw, kw, vw, gain.reshape(1, 48))


def finish_wide_kernel(place, b_near, b_far, up, gain, expand, output, gain_grad):
    near, far = b_near[...].astype(f32), b_far[...].astype(f32)
    sides = (jnp.where(place[3] == 0, near, far), jnp.where(place[3] == 0, far, near))
    joint = jnp.zeros((48, 384), f32)
    for half, side in enumerate(sides):
        for at in range(4):
            cols = slice(at * 768 + half * 384, at * 768 + half * 384 + 384)
            expand[:, cols] = side[at]
            joint = joint + side[at] * up[:, cols].astype(f32)
        output[:, half * 384 : half * 384 + 384] = side[4]
    column = jnp.broadcast_to(jnp.sum(joint, axis=1, keepdims=True), (48, 128))
    turned = jnp.concatenate([column, jnp.zeros((80, 128), f32)], axis=0).T
    gain_grad[...] = turned[0:1, 0:48] / gain[...].astype(f32)


def finish_wide(place, b_near, b_far, up, gain):
    return pl.pallas_call(
        finish_wide_kernel,
        out_shape=(
            jax.ShapeDtypeStruct((48, 3072), f32),
            jax.ShapeDtypeStruct((48, 768), f32), jax.ShapeDtypeStruct((1, 48), f32),
        ),
        in_specs=[SCALARS] + [FULL] * 4,
        out_specs=(FULL,) * 3,
        compiler_params=params(MOST),
        cost_estimate=cost(1000, 2_000_000),
        name="finish_wide",
    )(place, b_near, b_far, up, gain.reshape(1, 48))


def input_grad_kernel(place, x, small, near, far, middle_grad, result):
    for row in range(0, 512, 256):
        rows = slice(row, row + 256)
        wide = x[rows].astype(f32)
        scale = lax.rsqrt(jnp.mean(wide * wide, axis=-1, keepdims=True) + EPS)
        unit = wide * scale
        direct = (near[rows].astype(f32) + far[rows].astype(f32)) * small[0:1]
        inward = scale * (direct - unit * jnp.mean(direct * unit, axis=-1, keepdims=True))
        result[rows] = (middle_grad[rows] + inward).astype(bf16)


def input_grad(place, x, small, near, far, middle_grad):
    return pl.pallas_call(
        input_grad_kernel,
        out_shape=jax.ShapeDtypeStruct((512, 768), bf16),
        in_specs=[SCALARS] + [FULL] * 5,
        out_specs=FULL,
        compiler_params=params(),
        cost_estimate=cost(512 * 768 * 20, 6_000_000),
        name="input_grad",
    )(place, x, small, near, far, middle_grad)


def swap(array, axis, bit):
    count = lax.axis_size(axis)
    return lax.ppermute(array, axis, [(i, i ^ bit) for i in range(count)])


def swap_both(array):
    pairs = [(i * 2 + j, (i ^ Y) * 2 + 1 - j) for i in range(lax.axis_size("fsdp")) for j in range(2)]
    return lax.ppermute(array, ("fsdp", "seq"), pairs)


CORE, Y, Z = 1, 2, 4


def after(value, *others):
    return lax.optimization_barrier((value, *others))[0]


class Line:
    def __init__(self, place):
        self.place = place

    def wait(self, *arrays):
        self.place = after(self.place, *arrays)

    def run(self, kernel, *args):
        made = kernel(self.place, *args)
        self.wait(jax.tree.leaves(made)[0])
        return made


def gather_part(array, part, own, now):
    _, dims, gone = part
    for axis in reversed(range(len(dims))):
        if dims[axis] == now:
            array = lax.dynamic_index_in_dim(array, 1 - own[now], axis, keepdims=False)
        elif dims[axis] in gone:
            array = lax.dynamic_index_in_dim(array, own[dims[axis]], axis, keepdims=False)
    return array.astype(f32)


def total(line, parts, own, now=None):
    arrays = after([part[0] for part in parts], line.place)
    made = None
    for array, part in zip(arrays, parts):
        term = gather_part(array, part, own, now)
        made = term if made is None else made + term
    made = lax.optimization_barrier(made.astype(bf16))
    line.wait(made)
    return made


def sum_parts(parts, own, now=None):
    made = None
    for part in parts:
        term = gather_part(part[0], part, own, now)
        made = term if made is None else made + term
    return made


def keep(parts, now, got):
    _, dims, gone = parts[0]
    left = tuple(dim for dim in dims if dim not in gone and dim != now)
    return [(a, d, g + (now,)) for a, d, g in parts] + [(got, left, ())]


def local_split(
    layer_input, query_weight, key_weight, value_weight, output_weight, expand_weight,
    contract_weight, attention_gain, feedforward_gain, bias_table, valid_len, instr_len, pair_flag,
    cotangent,
):
    owner, x = lax.axis_index("fsdp"), lax.axis_index("seq")
    z, y, c = owner // 4, (owner // 2) % 2, owner % 2
    where = jnp.stack([z, y, c, x]).astype(jnp.int32)
    line = Line(where)
    tokens, cot = layer_input[0], cotangent[0]

    def by_z(array):
        return swap(array, "fsdp", Z)

    def by_zz(array):
        return swap(array, "fsdp", 2 * Z)

    def by_y(array):
        return swap(array, "fsdp", Y)

    def by_core(array):
        return swap(array, "fsdp", CORE)

    def by_x(array):
        return swap(array, "seq", 1)

    shard = line.run(
        narrow_shard, query_weight, key_weight, value_weight, attention_gain, feedforward_gain, bias_table
    )
    a2, a1, b0 = by_zz(shard), by_z(shard), by_y(shard)
    x_far, cot_far = by_x(tokens), by_core(cot)
    rest, full = line.run(wide_shard, expand_weight, output_weight, contract_weight)
    a2, a1, b0, rest, cot_far = lax.optimization_barrier((a2, a1, b0, rest, cot_far))
    turned, b2 = by_z(jnp.stack([a2, b0])), by_y(a2)
    four = by_core(jnp.stack([shard, b0, a1, a2]))
    z2, z1, y0 = by_zz(rest), by_z(rest), by_y(rest)
    lens = jnp.stack([valid_len[0], instr_len[0], pair_flag[0]])
    place = jnp.concatenate([where, lens])
    turned, b2, x_far, line.place = lax.optimization_barrier((turned, b2, x_far, place))
    b3 = by_y(turned[0])
    three = by_core(jnp.stack([turned[0], turned[1], b2]))
    last = by_core(b3)
    z1, z2, y0, last, three = lax.optimization_barrier((z1, z2, y0, last, three))
    z3, y2 = by_z(z2), by_y(z2)
    sides = jnp.stack([z1[5:], z2[5:], y0[5:]])
    sides_a = by_x(sides)
    narrow = [shard, b0, a1, a2, turned, b2, b3, four, three, last]

    line.wait(sides)
    qkv, normed_kept, normed_sent, small, table, tiles = line.run(project, tokens, x_far, narrow)
    line.place, z3, y2, sides_a = lax.optimization_barrier((line.place, z3, y2, sides_a))
    y3 = by_y(z3)
    y1 = jnp.concatenate([y0, sides_a[2]], axis=0)
    sides, trio = jnp.stack([z3[5:], y2[5:]]), jnp.stack([y0, z1, z2])
    line.wait(y1, sides, trio)
    y1, sides_b, far_full, far_three = by_z(y1), by_x(sides), by_core(full), by_core(trio)
    out_theirs, kept_theirs, inverse_theirs = line.run(attend, table, tiles, qkv, False)
    line.place, y3, sides_b, far_full, far_three, out_theirs = lax.optimization_barrier(
        (line.place, y3, sides_b, far_full, far_three, out_theirs)
    )
    two = jnp.stack([z3, y2])
    line.wait(two)
    out_got, sides_c, far_two = by_x(out_theirs), by_x(y3[5:]), by_core(two)
    out_mine, kept_mine, inverse_mine = line.run(attend, table, tiles, qkv, True)
    out_mine, y1, out_got, sides_c, far_two, y3, sides_a, sides_b = lax.optimization_barrier(
        (out_mine, y1, out_got, sides_c, far_two, y3, sides_a, sides_b)
    )
    near = [full, y0, z1, z2, z3, y2, y1, y3, sides_a, sides_b, sides_c]
    far = [far_full, far_three, far_two] + [by_core(block) for block in (y1, y3, sides_a, sides_b, sides_c)]
    hid, hid_sent, pre, turned, turned_sent, layer_output, middle_grad, grad_mine, grad_sent = line.run(
        forward, out_mine, out_got, tokens, cot, small, near, far
    )
    hid_far, grad_theirs, pre_far, turned_far = by_core(hid_sent), by_x(grad_sent), by_core(pre), by_core(turned_sent)

    own = {"high": z // 2, "low": z % 2, "y": y, "x": x}

    def parts(kept, got, *dims):
        lead = tuple({"high": 2, "low": 2, "y": 2}[dim] for dim in dims if dim != "n")
        shape = lead + kept.shape[-3:] if "n" in dims else lead + kept.shape[-2:]
        return [(array.reshape(shape), dims, ()) for array in (kept, got)]

    carry = line.run(
        lambda place: attend_back(place, grad_mine, out_mine, inverse_mine, qkv, kept_mine, (), True)
    )
    line.wait(grad_theirs)
    b_sent, b_kept, c_sent, c_kept = line.run(expand_weight_grad, turned, turned_far, pre, pre_far)
    b_got, c_got = by_y(b_sent), by_z(c_sent)
    b_parts = parts(b_kept, b_got, "high", "low", "n")
    c_parts = parts(c_kept, c_got, "high", "y", "n")
    sent, kept = line.run(contract_weight_grad, hid, hid_far, cot, cot_far)
    a_got = by_x(sent)
    a_parts = parts(kept, a_got, "high", "low", "y", "n")
    whole = line.run(
        lambda place: attend_back(
            place, grad_theirs, out_theirs, inverse_theirs, qkv, kept_theirs, carry, False
        )
    )
    b_got = by_z(total(line, b_parts, own, "low"))
    b_parts = keep(b_parts, "low", b_got)
    c_got = by_y(total(line, c_parts, own, "y"))
    c_parts = keep(c_parts, "y", c_got)
    g_near, g_far = line.run(weight_grad, normed_kept, normed_sent, whole)
    g_parts = parts(g_near, by_core(g_far), "high", "low", "y")
    line.wait(a_got, b_got, c_got)
    line.place = hand_on(line.place)
    g_parts = keep(g_parts, "low", by_z(total(line, g_parts, own, "low")))
    a_parts = keep(a_parts, "y", by_y(total(line, a_parts, own, "y")))
    arrays = after([part[0] for part in b_parts + c_parts], line.place)
    held = [(array, *part[1:]) for array, part in zip(arrays, b_parts + c_parts)]
    joint = jnp.concatenate([sum_parts(held[:3], own), sum_parts(held[3:], own)], axis=1).astype(bf16)
    sent = lax.dynamic_slice_in_dim(joint, (1 - x) * 384, 384, axis=3)
    kept = lax.dynamic_slice_in_dim(joint, x * 384, 384, axis=3)
    sent, kept = lax.optimization_barrier((sent, kept))
    line.wait(sent, kept)
    bc_parts = [(kept, ("high", "n"), ()), (by_x(sent), ("high", "n"), ())]
    part_near, part_far = line.run(project_back, narrow, whole)
    part_got = by_x(part_far)
    a_parts = keep(a_parts, "low", by_z(total(line, a_parts, own, "low")))
    bc_parts = keep(bc_parts, "high", by_zz(total(line, bc_parts, own, "high")))
    g_parts = keep(g_parts, "y", by_y(total(line, g_parts, own, "y")))
    a_parts = keep(a_parts, "high", by_zz(total(line, a_parts, own, "high")))
    b_low = total(line, bc_parts, own)
    b_other = by_x(b_low)
    g_parts = keep(g_parts, "high", by_zz(total(line, g_parts, own, "high")))
    result = line.run(input_grad, tokens, small, part_near, part_got, middle_grad)
    a_low = total(line, a_parts, own)
    a_other = by_x(a_low)
    g_low = total(line, g_parts, own)
    g_other = by_x(g_low)
    expand_sum, output_sum, gain_two = line.run(finish_wide, b_low, b_other, expand_weight, feedforward_gain)
    contract_sum, *grads, gain_one, bias_grad = line.run(
        finish, a_low, a_other, g_low, g_other, query_weight, key_weight, value_weight, attention_gain
    )
    return (
        layer_output[None], result[None], gain_one[0], gain_two[0], *grads,
        output_sum, expand_sum, contract_sum, bias_grad,
    )


def bucket_table(query_pos, key_pos):
    offset = key_pos[None, :] - query_pos[:, None]
    distance = jnp.abs(offset)
    beyond = jnp.zeros_like(distance)
    for far_edge in far_edges:
        beyond = beyond + (distance >= far_edge).astype(jnp.int32)
    nearby = jnp.where(distance < 8, distance, 8 + beyond)
    return nearby + 16 * (offset > 0).astype(jnp.int32)


def visible_keys(query_pos, key_pos, valid_len, instr_len, pair_flag):
    in_valid = key_pos[None, None, :] < valid_len[:, None, None]
    guarded = (
        (pair_flag[:, None, None] == 1)
        & (query_pos[None, :, None] < instr_len[:, None, None])
        & (key_pos[None, None, :] >= instr_len[:, None, None])
    )
    return in_valid & jnp.logical_not(guarded)


def rms_scale(values):
    return lax.rsqrt(jnp.mean(values * values, axis=-1, keepdims=True) + EPS)


def norm_back(values, scale, gain, grad_out):
    normed = values * scale
    grad_normed = grad_out * gain
    grad_values = scale * (
        grad_normed - normed * jnp.mean(grad_normed * normed, axis=-1, keepdims=True)
    )
    return (grad_values, jnp.sum(grad_out * normed, axis=(0, 1)))


def gelu_tanh(values):
    return jax.nn.gelu(values, approximate=True)


def local(
    layer_input,
    query_weight,
    key_weight,
    value_weight,
    output_weight,
    expand_weight,
    contract_weight,
    attention_gain,
    feedforward_gain,
    bias_table,
    valid_len,
    instr_len,
    pair_flag,
    cotangent,
):
    f32 = jnp.float32
    bf16 = jnp.bfloat16
    row_count, local_len, model_width = layer_input.shape
    head_count = bias_table.shape[1]
    head_size = model_width // head_count
    full_len = local_len * lax.axis_size("seq")
    local_start = lax.axis_index("seq") * local_len
    query_pos = local_start + jnp.arange(local_len, dtype=jnp.int32)
    key_pos = jnp.arange(full_len, dtype=jnp.int32)
    buckets = bucket_table(query_pos, key_pos)
    onehot = buckets[:, :, None] == jnp.arange(BUCKETS, dtype=jnp.int32)[None, None, :]
    visible = visible_keys(query_pos, key_pos, valid_len, instr_len, pair_flag)
    input_wide = layer_input.astype(f32)

    def attend_probs(queries, key_heads, table_full):
        rel_bias = jnp.einsum(
            "ijb,bh->hij", onehot.astype(bf16), table_full, preferred_element_type=f32
        )
        raw_scores = jnp.einsum("rihe,rjhe->rhij", queries, key_heads, preferred_element_type=f32)
        scores = jnp.where(visible[:, None], raw_scores + rel_bias[None], -1000000000.0)
        row_peak = jnp.max(scores, axis=-1, keepdims=True)
        log_total = row_peak + jnp.log(jnp.sum(jnp.exp(scores - row_peak), axis=-1, keepdims=True))
        return (jnp.exp(scores - log_total), log_total[..., 0])

    def forward(weights):
        (
            query_full,
            key_full,
            value_full,
            output_full,
            expand_full,
            contract_full,
            gain_one,
            gain_two,
            table_full,
        ) = weights
        scale_one = rms_scale(input_wide)
        normed_low = (input_wide * scale_one * gain_one.astype(f32)).astype(bf16)

        def project(weight):
            return jnp.einsum("rtd,de->rte", normed_low, weight, preferred_element_type=f32).astype(
                bf16
            )

        query_low = project(query_full)
        key_low = project(key_full)
        value_low = project(value_full)
        key_all, value_all = (
            lax.all_gather(key_low, "seq", axis=1, tiled=True),
            lax.all_gather(value_low, "seq", axis=1, tiled=True),
        )
        queries = query_low.reshape(row_count, local_len, head_count, head_size)
        key_heads = key_all.reshape(row_count, full_len, head_count, head_size)
        value_heads = value_all.reshape(row_count, full_len, head_count, head_size)
        probs, log_total = attend_probs(queries, key_heads, table_full)
        probs_low = probs.astype(bf16)
        attended = jnp.einsum("rhij,rjhe->rihe", probs_low, value_heads, preferred_element_type=f32)
        attended = attended.reshape(row_count, local_len, model_width).astype(bf16)
        middle = input_wide + jnp.einsum(
            "rtd,de->rte", attended, output_full, preferred_element_type=f32
        )
        scale_two = rms_scale(middle)
        normed_two = (middle * scale_two * gain_two.astype(f32)).astype(bf16)
        hidden_pre = jnp.einsum("rtd,df->rtf", normed_two, expand_full, preferred_element_type=f32)
        hidden_low = gelu_tanh(hidden_pre).astype(bf16)
        result = middle + jnp.einsum(
            "rtf,fd->rtd", hidden_low, contract_full, preferred_element_type=f32
        )
        return (
            result,
            scale_one,
            normed_low,
            queries,
            key_heads,
            value_heads,
            probs,
            probs_low,
            log_total,
            attended,
            middle,
            scale_two,
            normed_two,
            hidden_pre,
            hidden_low,
        )

    stored = forward(
        (
            lax.all_gather(query_weight, "fsdp", axis=0, tiled=True),
            lax.all_gather(key_weight, "fsdp", axis=0, tiled=True),
            lax.all_gather(value_weight, "fsdp", axis=0, tiled=True),
            lax.all_gather(output_weight, "fsdp", axis=0, tiled=True),
            lax.all_gather(expand_weight, "fsdp", axis=0, tiled=True),
            lax.all_gather(contract_weight, "fsdp", axis=0, tiled=True),
            lax.all_gather(attention_gain, "fsdp", axis=0, tiled=True),
            lax.all_gather(feedforward_gain, "fsdp", axis=0, tiled=True),
            lax.all_gather(bias_table, "fsdp", axis=0, tiled=True),
        )
    )
    layer_output = stored[0].astype(bf16)
    gathered = (
        lax.all_gather(query_weight, "fsdp", axis=0, tiled=True),
        lax.all_gather(key_weight, "fsdp", axis=0, tiled=True),
        lax.all_gather(value_weight, "fsdp", axis=0, tiled=True),
        lax.all_gather(output_weight, "fsdp", axis=0, tiled=True),
        lax.all_gather(expand_weight, "fsdp", axis=0, tiled=True),
        lax.all_gather(contract_weight, "fsdp", axis=0, tiled=True),
        lax.all_gather(attention_gain, "fsdp", axis=0, tiled=True),
        lax.all_gather(feedforward_gain, "fsdp", axis=0, tiled=True),
        lax.all_gather(bias_table, "fsdp", axis=0, tiled=True),
    )
    kept = forward(gathered)
    (
        unused,
        scale_one,
        normed_low,
        queries,
        key_heads,
        value_heads,
        probs,
        probs_low,
        log_total,
        attended,
        middle,
        scale_two,
        normed_two,
        hidden_pre,
        hidden_low,
    ) = kept
    (
        query_full,
        key_full,
        value_full,
        output_full,
        expand_full,
        contract_full,
        gain_one,
        gain_two,
        table_full,
    ) = gathered
    gain_one_wide = gain_one.astype(f32)
    gain_two_wide = gain_two.astype(f32)
    contract_grad = jnp.einsum("rtf,rtd->fd", hidden_low, cotangent, preferred_element_type=f32)
    grad_hidden = jnp.einsum("rtd,fd->rtf", cotangent, contract_full, preferred_element_type=f32)
    gelu_pull = jax.vjp(gelu_tanh, hidden_pre)[1]
    grad_pre = gelu_pull(grad_hidden)[0].astype(bf16)
    expand_grad = jnp.einsum("rtd,rtf->df", normed_two, grad_pre, preferred_element_type=f32)
    grad_normed_two = jnp.einsum("rtf,df->rtd", grad_pre, expand_full, preferred_element_type=f32)
    grad_middle_norm, gain_two_grad = norm_back(middle, scale_two, gain_two_wide, grad_normed_two)
    grad_middle = cotangent.astype(f32) + grad_middle_norm
    grad_branch = grad_middle.astype(bf16)
    output_grad = jnp.einsum("rtd,rte->de", attended, grad_branch, preferred_element_type=f32)
    grad_attended = jnp.einsum(
        "rte,de->rtd", grad_branch, output_full, preferred_element_type=f32
    ).astype(bf16)
    grad_attended = grad_attended.reshape(row_count, local_len, head_count, head_size)
    grad_probs = jnp.einsum(
        "rihe,rjhe->rhij", grad_attended, value_heads, preferred_element_type=f32
    )
    row_delta = jnp.sum(probs * grad_probs, axis=-1)
    grad_scores = probs * (grad_probs - row_delta[..., None])
    bias_part = jnp.einsum(
        "hij,ijb->bh",
        jnp.sum(grad_scores, axis=0),
        onehot.astype(f32),
        precision=lax.Precision.HIGHEST,
    )
    scores_low = grad_scores.astype(bf16)
    grad_queries = jnp.einsum("rhij,rjhe->rihe", scores_low, key_heads, preferred_element_type=f32)
    grad_queries = grad_queries.reshape(row_count, local_len, model_width).astype(bf16)
    value_partial = jnp.einsum(
        "rhij,rihe->rjhe", probs_low, grad_attended, preferred_element_type=f32
    ).reshape(row_count, full_len, model_width)
    key_partial = jnp.einsum(
        "rhij,rihe->rjhe", scores_low, queries, preferred_element_type=f32
    ).reshape(row_count, full_len, model_width)
    key_summed, value_summed = (
        lax.psum_scatter(
            key_partial.astype(jnp.bfloat16), "seq", scatter_dimension=1, tiled=True
        ).astype(jnp.float32),
        lax.psum_scatter(
            value_partial.astype(jnp.bfloat16), "seq", scatter_dimension=1, tiled=True
        ).astype(jnp.float32),
    )
    grad_keys = key_summed.astype(bf16)
    grad_values = value_summed.astype(bf16)
    query_part = jnp.einsum("rtd,rte->de", normed_low, grad_queries, preferred_element_type=f32)
    key_part = jnp.einsum("rtd,rte->de", normed_low, grad_keys, preferred_element_type=f32)
    value_part = jnp.einsum("rtd,rte->de", normed_low, grad_values, preferred_element_type=f32)
    grad_normed_one = jnp.einsum(
        "rte,de->rtd", grad_queries, query_full, preferred_element_type=f32
    )
    grad_normed_one = grad_normed_one + jnp.einsum(
        "rte,de->rtd", grad_keys, key_full, preferred_element_type=f32
    )
    grad_normed_one = grad_normed_one + jnp.einsum(
        "rte,de->rtd", grad_values, value_full, preferred_element_type=f32
    )
    grad_input_norm, gain_one_grad = norm_back(
        input_wide, scale_one, gain_one_wide, grad_normed_one
    )
    input_grad = (grad_middle + grad_input_norm).astype(bf16)
    owned = (
        lax.psum_scatter(
            query_part.astype(jnp.bfloat16), "fsdp", scatter_dimension=0, tiled=True
        ).astype(jnp.float32),
        lax.psum_scatter(
            key_part.astype(jnp.bfloat16), "fsdp", scatter_dimension=0, tiled=True
        ).astype(jnp.float32),
        lax.psum_scatter(
            value_part.astype(jnp.bfloat16), "fsdp", scatter_dimension=0, tiled=True
        ).astype(jnp.float32),
        lax.psum_scatter(
            output_grad.astype(jnp.bfloat16), "fsdp", scatter_dimension=0, tiled=True
        ).astype(jnp.float32),
        lax.psum_scatter(
            expand_grad.astype(jnp.bfloat16), "fsdp", scatter_dimension=0, tiled=True
        ).astype(jnp.float32),
        lax.psum_scatter(
            contract_grad.astype(jnp.bfloat16), "fsdp", scatter_dimension=0, tiled=True
        ).astype(jnp.float32),
        lax.psum_scatter(
            gain_one_grad.astype(jnp.bfloat16), "fsdp", scatter_dimension=0, tiled=True
        ).astype(jnp.float32),
        lax.psum_scatter(
            gain_two_grad.astype(jnp.bfloat16), "fsdp", scatter_dimension=0, tiled=True
        ).astype(jnp.float32),
        lax.psum_scatter(
            bias_part.astype(jnp.bfloat16), "fsdp", scatter_dimension=0, tiled=True
        ).astype(jnp.float32),
    )
    summed = (
        lax.psum(owned[0].astype(jnp.bfloat16), "seq").astype(jnp.float32),
        lax.psum(owned[1].astype(jnp.bfloat16), "seq").astype(jnp.float32),
        lax.psum(owned[2].astype(jnp.bfloat16), "seq").astype(jnp.float32),
        lax.psum(owned[3].astype(jnp.bfloat16), "seq").astype(jnp.float32),
        lax.psum(owned[4].astype(jnp.bfloat16), "seq").astype(jnp.float32),
        lax.psum(owned[5].astype(jnp.bfloat16), "seq").astype(jnp.float32),
        lax.psum(owned[6].astype(jnp.bfloat16), "seq").astype(jnp.float32),
        lax.psum(owned[7].astype(jnp.bfloat16), "seq").astype(jnp.float32),
        lax.psum(owned[8].astype(jnp.bfloat16), "seq").astype(jnp.float32),
    )
    (
        query_grad,
        key_grad,
        value_grad,
        output_sum,
        expand_sum,
        contract_sum,
        gain_one_sum,
        gain_two_sum,
        bias_grad,
    ) = summed
    return (
        layer_output,
        input_grad,
        gain_one_sum,
        gain_two_sum,
        query_grad,
        key_grad,
        value_grad,
        output_sum,
        expand_sum,
        contract_sum,
        bias_grad,
    )


def solution(mesh):
    in_specs = (
        P("fsdp", "seq", None),
        P("fsdp", None),
        P("fsdp", None),
        P("fsdp", None),
        P("fsdp", None),
        P("fsdp", None),
        P("fsdp", None),
        P("fsdp"),
        P("fsdp"),
        P("fsdp", None),
        P("fsdp"),
        P("fsdp"),
        P("fsdp"),
        P("fsdp", "seq", None),
    )
    out_specs = (
        P("fsdp", "seq", None),
        P("fsdp", "seq", None),
        P("fsdp"),
        P("fsdp"),
        P("fsdp", None),
        P("fsdp", None),
        P("fsdp", None),
        P("fsdp", None),
        P("fsdp", None),
        P("fsdp", None),
        P("fsdp", None),
    )
    split = mesh.shape["fsdp"] == 16 and mesh.shape["seq"] == 2
    step = local_split if split else local
    return jax.shard_map(step, mesh=mesh, in_specs=in_specs, out_specs=out_specs, check_vma=False)
```

```python
import functools
import itertools
import math

import jax
import jax.numpy as jnp
from jax import lax
from jax.experimental import pallas as pl
from jax.experimental.pallas import tpu as pltpu
from jax.sharding import PartitionSpec as P

f32 = jnp.float32
bf16 = jnp.bfloat16
BUCKETS = 32
EPS = 1e-06
far_edges = (12, 16, 23, 32, 46, 64, 91)
HIDDEN = -(2.0**30)
VMEM = 56 * 1024 * 1024
MOST = 66_900_000
ANY = pl.BlockSpec(memory_space=pl.ANY)
FULL = pl.BlockSpec(memory_space=pltpu.VMEM)
SCALARS = pl.BlockSpec(memory_space=pltpu.SMEM)


def dot(left, right, left_dim, right_dim):
    return lax.dot_general(
        left, right, (((left_dim,), (right_dim,)), ((), ())), preferred_element_type=f32
    )


def params(limit=VMEM):
    return pltpu.CompilerParams(vmem_limit_bytes=limit)


def cost(flops, byte_count, exps=0):
    return pl.CostEstimate(flops=flops // 1000, bytes_accessed=byte_count // 1000, transcendentals=exps // 1000)


def small_cost():
    return pl.CostEstimate(flops=1000, bytes_accessed=1000, transcendentals=0)


def bucket_of(offset):
    distance = jnp.abs(offset)
    beyond = jnp.zeros_like(distance)
    for far_edge in far_edges:
        beyond = beyond + (distance >= far_edge).astype(jnp.int32)
    nearby = jnp.where(distance < 8, distance, 8 + beyond)
    return nearby + 16 * (offset > 0).astype(jnp.int32)


def iota(shape, dim):
    return lax.broadcasted_iota(jnp.int32, shape, dim)


def narrow_kernel(place, q, k, v, gain_one, gain_two, table, out, side):
    column = pl.multiple_of(place[3] * 384, 128)
    pieces = [weight[:, pl.ds(column, 384)] for weight in (q, k, v)]
    for pair in range(3):
        parts = [piece[:, at : at + 64] for at in (pair * 128, pair * 128 + 64) for piece in pieces]
        out[:, pair * 384 : pair * 384 + 384] = jnp.concatenate(parts, axis=1)
    side[...] = jnp.zeros((8, 128), f32)
    side[0:1, 0:48] = gain_one[...].astype(f32)
    side[1:2, 0:48] = gain_two[...].astype(f32)
    rows = table[...].astype(f32)
    side[2:3, 0:12] = rows[0:1]
    side[2:3, 12:24] = rows[1:2]
    wide = jnp.concatenate([side[...], jnp.zeros((120, 128), f32)], axis=0).T
    out[:, 1152:1280] = wide[0:48].astype(bf16)


def narrow_shard(place, q, k, v, gain_one, gain_two, table):
    return pl.pallas_call(
        narrow_kernel,
        out_shape=jax.ShapeDtypeStruct((48, 1280), bf16),
        in_specs=[SCALARS] + [FULL] * 6,
        out_specs=FULL,
        scratch_shapes=[pltpu.VMEM((8, 128), f32)],
        compiler_params=params(),
        cost_estimate=small_cost(),
        name="narrow_shard",
    )(place, q, k, v, gain_one.reshape(1, 48), gain_two.reshape(1, 48), table)


def wide_kernel(place, expand, output, contract, out, full, sems):
    x = place[3]
    pieces = [(expand.at[:, at * 768 : at * 768 + 768], out.at[at]) for at in range(4)]
    pieces.append((output, out.at[4]))
    for at in range(2):
        row = pl.multiple_of(x * 96 + at * 48, 16)
        pieces.append((contract.at[pl.ds(row, 48)], out.at[5 + at]))
        row = pl.multiple_of((1 - x) * 96 + at * 48, 16)
        pieces.append((contract.at[pl.ds(row, 48)], full.at[7 + at]))
    copies = [pltpu.make_async_copy(*piece, sems.at[at]) for at, piece in enumerate(pieces)]
    for copy in copies:
        copy.start()
    for copy in copies:
        copy.wait()
    full[0:7] = out[...]


def wide_shard(place, expand, output, contract):
    return pl.pallas_call(
        wide_kernel,
        out_shape=(
            jax.ShapeDtypeStruct((7, 48, 768), bf16), jax.ShapeDtypeStruct((9, 48, 768), bf16),
        ),
        in_specs=[SCALARS, ANY, ANY, ANY],
        out_specs=(FULL, FULL),
        scratch_shapes=[pltpu.SemaphoreType.DMA((9,))],
        compiler_params=params(),
        cost_estimate=small_cost(),
        name="wide_shard",
    )(place, expand, output, contract)


def narrow_blocks(refs):
    shard, b0, a1, a2, turned, b2, b3, four, three, last = refs
    near = [shard, b0, a1, turned.at[1], a2, b2, turned.at[0], b3]
    far = [four.at[0], four.at[1], four.at[2], three.at[1], four.at[3], three.at[2], three.at[0], last]
    return near, far


def place_blocks(place, near, far, dest, sems):
    z, y, c = place[0], place[1], place[2]
    copies = []
    for turn in range(4):
        for dy in range(2):
            owner = ((jnp.bitwise_xor(z, turn) * 2) + jnp.bitwise_xor(y, dy)) * 2
            for other, source in enumerate((near, far)):
                row = pl.multiple_of((owner + jnp.bitwise_xor(c, other)) * 48, 16)
                copy = pltpu.make_async_copy(
                    source[turn * 2 + dy], dest.at[pl.ds(row, 48)], sems.at[len(copies)]
                )
                copy.start()
                copies.append(copy)
    return copies


def place_tokens(x, near, far, dest, sems, count):
    copies = []
    for other, source in enumerate((near, far)):
        row = pl.multiple_of(jnp.bitwise_xor(x, other) * count, count)
        copy = pltpu.make_async_copy(source, dest.at[pl.ds(row, count)], sems.at[other])
        copy.start()
        copies.append(copy)
    return copies


def first_query(place, mine):
    return (place[3] if mine else 1 - place[3]) * 512


def project_kernel(place, x_near, x_far, *refs):
    (w_near, w_far), refs = narrow_blocks(refs[:10]), refs[10:]
    qkv, kept, sent, small, table, tiles, normed, xs, w, sems, xsems = refs
    tokens = place_tokens(place[3], x_near, x_far, xs, xsems, 512)
    blocks = place_blocks(place, w_near, w_far, w, sems)
    for copy in tokens + blocks:
        copy.wait()
    side = w[:, 1152:1280].astype(f32).T
    small[...] = side[:8]
    gain = side[0:1]
    row = iota((768, 128), 0)
    spot = row % 48
    bucket = (row // 48) * 2 + spot // 12
    match = (iota((768, 128), 1) == bucket) & (spot < 24)
    values = jnp.where(match, w[:, 1154:1155].astype(f32), 0.0).astype(bf16)
    head = iota((8, 768), 0)
    chosen = ((iota((8, 768), 1) % 48) % 12 == place[3] * 6 + head) & (head < 6)
    made = dot(chosen.astype(bf16), values, 1, 0)
    table[...] = made
    lane = iota((128, 512), 1)
    spread = (bucket_of(jnp.where(lane < 128, -128 - lane, 384 - lane)) == iota((128, 512), 0)).astype(bf16)
    turned = dot(made.astype(bf16), spread, 1, 0)
    for head in range(6):
        for block, (low, high) in enumerate(((384, 0), (256, 384), (128, 256))):
            parts = [turned[head : head + 1, at : at + 128] for at in (low, high)]
            wide = jnp.broadcast_to(jnp.concatenate(parts, axis=1), (128, 256))
            rolled = pltpu.roll(wide, 0, 1, stride=1, stride_axis=0)
            tiles[head, block * 128 : block * 128 + 128] = rolled[:, 128:256]
    for row in range(0, 1024, 256):
        wide = xs[row : row + 256].astype(f32)
        scale = lax.rsqrt(jnp.mean(wide * wide, axis=-1, keepdims=True) + EPS)
        normed[row : row + 256] = (wide * scale * gain).astype(bf16)
    for col in range(0, 1152, 384):
        made = dot(w[:, col : col + 384], normed[...], 0, 1)
        qkv[col : col + 384] = made.astype(bf16)
    turned = normed[...].T.reshape(8, 2, 48, 1024)
    kept[...] = jnp.where(place[2] == 0, turned[:, 0], turned[:, 1])
    sent[...] = jnp.where(place[2] == 0, turned[:, 1], turned[:, 0])


def project(place, x_near, x_far, blocks):
    return pl.pallas_call(
        project_kernel,
        out_shape=(
            jax.ShapeDtypeStruct((1152, 1024), bf16),
            jax.ShapeDtypeStruct((8, 48, 1024), bf16),
            jax.ShapeDtypeStruct((8, 48, 1024), bf16),
            jax.ShapeDtypeStruct((8, 768), f32),
            jax.ShapeDtypeStruct((8, 128), f32),
            jax.ShapeDtypeStruct((6, 384, 128), f32),
        ),
        in_specs=[SCALARS] + [ANY] * 12,
        out_specs=(FULL,) * 6,
        scratch_shapes=[
            pltpu.VMEM((1024, 768), bf16),
            pltpu.VMEM((1024, 768), bf16),
            pltpu.VMEM((768, 1280), bf16),
            pltpu.SemaphoreType.DMA((16,)),
            pltpu.SemaphoreType.DMA((2,)),
        ],
        compiler_params=params(),
        cost_estimate=small_cost(),
        name="project",
    )(place, x_near, x_far, *blocks)


def attend_kernel(mine, place, table, tile, q, k, v, out, kept, inverse, ka, kt, qt, vt, s):
    head = pl.program_id(0)
    first, valid, instr, pair = first_query(place, mine), place[4], place[5], place[6]

    @pl.when(head == 0)
    def _():
        kt[64:128] = jnp.zeros((64, 1024), bf16)
        qt[64:128] = jnp.zeros((64, 512), bf16)
        row = iota((16, 1024), 0)
        key = iota((16, 1024), 1)
        extra = jnp.where(row < 8, (key // 128 == row).astype(f32), 0.0)
        extra = jnp.where(row == 8, jnp.where(key >= valid, HIDDEN, 0.0), extra)
        extra = jnp.where(row == 9, (key >= instr).astype(f32), extra)
        kt[64:80] = extra.astype(bf16)
        vt[64:80] = jnp.where(row == 0, 1.0, 0.0).astype(bf16)

    row = iota((16, 512), 0)
    query = iota((16, 512), 1) + first
    block = query // 128
    extra = jnp.where(row <= block - 2, table[head, 15], 0.0)
    extra = jnp.where(row >= block + 2, table[head, 31], extra)
    extra = jnp.where(row == 8, 1.0, extra)
    guarded = (query < instr) & (pair == 1)
    extra = jnp.where(row == 9, jnp.where(guarded, HIDDEN, 0.0), extra)
    extra = jnp.where(row > 9, 0.0, extra)
    qt[64:80] = extra.astype(bf16)
    qt[0:64] = q[...]
    kt[0:64] = k[...]
    vt[0:64] = v[...]
    ka[...] = kt[...].T
    s[128:1152] = dot(ka[...], qt[...], 1, 0)
    for part in range(4):
        base = pl.multiple_of(first + part * 128, 128)
        cols = slice(part * 128, part * 128 + 128)
        s[pl.ds(base, 384), cols] = s[pl.ds(base, 384), cols] + tile[0]
    scores = s[128:1152]
    peak = jnp.max(scores, axis=0, keepdims=True)
    weights = jnp.exp(scores - peak).astype(bf16)
    kept[0] = weights
    summed = dot(vt[...], weights, 1, 0)
    share = 1.0 / summed[64:65]
    out[...] = (summed[0:64] * share).astype(bf16)
    inverse[0] = share


def attend(place, table, tiles, qkv, mine):
    half = (lambda s: s[3]) if mine else (lambda s: 1 - s[3])
    grid = pltpu.PrefetchScalarGridSpec(
        num_scalar_prefetch=1,
        grid=(6,),
        in_specs=[
            SCALARS,
            pl.BlockSpec((1, 384, 128), lambda h, s: (h, 0, 0)),
            pl.BlockSpec((64, 512), lambda h, s: (3 * h, half(s))),
            pl.BlockSpec((64, 1024), lambda h, s: (3 * h + 1, 0)),
            pl.BlockSpec((64, 1024), lambda h, s: (3 * h + 2, 0)),
        ],
        out_specs=(
            pl.BlockSpec((64, 512), lambda h, s: (h, 0)),
            pl.BlockSpec((1, 1024, 512), lambda h, s: (h, 0, 0)),
            pl.BlockSpec((1, 1, 512), lambda h, s: (h, 0, 0)),
        ),
        scratch_shapes=[
            pltpu.VMEM((1024, 128), bf16),
            pltpu.VMEM((128, 1024), bf16),
            pltpu.VMEM((128, 512), bf16),
            pltpu.VMEM((80, 1024), bf16),
            pltpu.VMEM((1280, 512), f32),
        ],
    )
    return pl.pallas_call(
        functools.partial(attend_kernel, mine),
        out_shape=(
            jax.ShapeDtypeStruct((384, 512), bf16),
            jax.ShapeDtypeStruct((6, 1024, 512), bf16),
            jax.ShapeDtypeStruct((6, 1, 512), f32),
        ),
        grid_spec=grid,
        compiler_params=params(),
        cost_estimate=small_cost(),
        name="attend_mine" if mine else "attend_theirs",
    )(place, table, tiles, qkv, qkv, qkv)


def diagonal_sums(band):
    flip = (iota((128, 128), 0) + iota((128, 128), 1) == 127).astype(f32)
    rows = []
    for block in range(3):
        here = lax.dot_general(
            flip, band[block * 128 : block * 128 + 128], (((1,), (0,)), ((), ())),
            precision=lax.Precision.HIGHEST, preferred_element_type=f32,
        )
        wide = jnp.concatenate([here, jnp.zeros((128, 128), f32)], axis=1)
        rolled = pltpu.roll(wide, 0, 1, stride=1, stride_axis=0)
        rows.append(jnp.sum(rolled, axis=0, keepdims=True))
    return rows


def bucket_sums(diagonals, sides):
    total = sides
    for block in range(3):
        offset = block * 128 - 1 - iota((256, 128), 0)
        spread = (bucket_of(offset) == iota((256, 128), 1)).astype(f32)
        total = total + lax.dot_general(
            diagonals[block], spread, (((1,), (0,)), ((), ())),
            precision=lax.Precision.HIGHEST, preferred_element_type=f32,
        )
    return total


def attend_back_kernel(carried, mine, place, grad, out, inverse, q, k, v, kept, *refs):
    if carried:
        dq_in, dk_in, dv_in, band_in, far_in, whole, diagonals, sides, *refs = refs
    else:
        dq, dk, dv, band, far, *refs = refs
    va, vt, kt, gt, ds = refs
    first = first_query(place, mine)

    @pl.when(pl.program_id(0) == 0)
    def _():
        row = iota((16, 1024), 0)
        key = iota((16, 1024), 1)
        vt[64:128] = jnp.zeros((64, 1024), bf16)
        vt[64:80] = jnp.where(row < 2, 1.0, 0.0).astype(bf16)
        if carried:
            diagonals[...] = jnp.zeros_like(diagonals)
            sides[...] = jnp.zeros_like(sides)
        kt[64:80] = jnp.where(row < 8, (key // 128 == row).astype(f32), 0.0).astype(bf16)
        gt[64:128] = jnp.zeros((64, 512), bf16)
        ds[0:128] = jnp.zeros((128, 512), bf16)
        ds[1152:1280] = jnp.zeros((128, 512), bf16)

    share = inverse[0]
    scaled = grad[...].astype(f32) * share
    delta = jnp.sum(scaled * out[...].astype(f32), axis=0, keepdims=True)
    high = delta.astype(bf16).astype(f32)
    row = iota((16, 512), 0)
    extra = jnp.where(row == 0, -high, jnp.where(row == 1, high - delta, 0.0))
    gt[64:80] = extra.astype(bf16)
    gt[0:64] = scaled.astype(bf16)
    vt[0:64] = v[...]
    kt[0:64] = k[...]
    va[...] = vt[...].T
    for row_at in range(0, 1024, 256):
        rows = slice(row_at, row_at + 256)
        pull = dot(va[rows], gt[...], 1, 0)
        ds[128 + row_at : 384 + row_at] = (kept[0, rows] * pull).astype(bf16)
    made = dot(kt[...], ds[128:1152], 1, 0)
    block = (iota((8, 512), 1) + first) // 128
    key_block = iota((8, 512), 0)
    totals = made[64:72]
    left = jnp.sum(jnp.where(key_block <= block - 2, totals, 0.0), axis=0, keepdims=True)
    right = jnp.sum(jnp.where(key_block >= block + 2, totals, 0.0), axis=0, keepdims=True)
    dv_made = dot(gt[0:64], kept[0], 1, 1)
    dk_made = dot(q[...], ds[128:1152], 1, 1)
    near = None
    for part in range(4):
        base = pl.multiple_of(first + part * 128, 128)
        window = ds[pl.ds(base, 384), part * 128 : part * 128 + 128].astype(f32)
        near = window if near is None else near + window
    if carried:
        whole[0, 0:64, pl.ds(pl.multiple_of(first, 512), 512)] = made[0:64].astype(bf16)
        whole[0, 0:64, pl.ds(pl.multiple_of(512 - first, 512), 512)] = dq_in[...]
        whole[0, 64:128] = (dk_made + dk_in[...]).astype(bf16)
        whole[0, 128:192] = (dv_made + dv_in[...]).astype(bf16)
        head = pl.program_id(0)
        for at, row in enumerate(diagonal_sums(near + band_in[0])):
            diagonals[at, pl.ds(head, 1)] = row
        lane = iota((1, 128), 1)
        left, right = (
            jnp.sum(side, axis=1, keepdims=True) for side in (left + far_in[0, 0:1], right + far_in[0, 1:2])
        )
        sides[pl.ds(head, 1)] = jnp.where(lane == 15, left, jnp.where(lane == 31, right, 0.0))
        whole[0, 192:208] = jnp.zeros((16, 1024), bf16)

        @pl.when(head == 5)
        def _():
            bias = bucket_sums([diagonals[at] for at in range(3)], sides[...])
            whole[0, 192:208, 0:128] = jnp.concatenate([bias, jnp.zeros((8, 128), f32)], axis=0).astype(bf16)

    else:
        dq[...] = made[0:64].astype(bf16)
        dk[...] = dk_made
        dv[...] = dv_made
        band[0] = near
        far[0] = jnp.concatenate([left, right, jnp.zeros((6, 512), f32)], axis=0)


def attend_back(place, grad, out, inverse, qkv, kept, carry, mine):
    count = 6
    half = (lambda s: s[3]) if mine else (lambda s: 1 - s[3])
    rows512 = pl.BlockSpec((64, 512), lambda h, s: (h, 0))
    rows1024 = pl.BlockSpec((64, 1024), lambda h, s: (h, 0))
    band_spec = pl.BlockSpec((1, 384, 128), lambda h, s: (h, 0, 0))
    far_spec = pl.BlockSpec((1, 8, 512), lambda h, s: (h, 0, 0))
    carry_specs = (rows512, rows1024, rows1024, band_spec, far_spec)
    in_specs = [
        rows512,
        rows512,
        pl.BlockSpec((1, 1, 512), lambda h, s: (h, 0, 0)),
        pl.BlockSpec((64, 512), lambda h, s: (3 * h, half(s))),
        pl.BlockSpec((64, 1024), lambda h, s: (3 * h + 1, 0)),
        pl.BlockSpec((64, 1024), lambda h, s: (3 * h + 2, 0)),
        pl.BlockSpec((1, 1024, 512), lambda h, s: (h, 0, 0)),
    ]
    if carry:
        out_shape = jax.ShapeDtypeStruct((count, 208, 1024), bf16)
        out_specs = pl.BlockSpec((1, 208, 1024), lambda h, s: (h, 0, 0))
        in_specs += carry_specs
    else:
        out_shape = (
            jax.ShapeDtypeStruct((64 * count, 512), bf16),
            jax.ShapeDtypeStruct((64 * count, 1024), f32),
            jax.ShapeDtypeStruct((64 * count, 1024), f32),
            jax.ShapeDtypeStruct((count, 384, 128), f32),
            jax.ShapeDtypeStruct((count, 8, 512), f32),
        )
        out_specs = carry_specs
    grid = pltpu.PrefetchScalarGridSpec(
        num_scalar_prefetch=1,
        grid=(count,),
        in_specs=in_specs,
        out_specs=out_specs,
        scratch_shapes=([pltpu.VMEM((3, 8, 256), f32), pltpu.VMEM((8, 128), f32)] if carry else [])
        + [
            pltpu.VMEM((1024, 128), bf16),
            pltpu.VMEM((128, 1024), bf16),
            pltpu.VMEM((80, 1024), bf16),
            pltpu.VMEM((128, 512), bf16),
            pltpu.VMEM((1280, 512), bf16),
        ],
    )
    return pl.pallas_call(
        functools.partial(attend_back_kernel, bool(carry), mine),
        out_shape=out_shape,
        grid_spec=grid,
        compiler_params=params(VMEM if carry else MOST),
        cost_estimate=cost(count * 1024 * 512 * 1024, 6_000_000),
        name="attend_back_mine" if mine else "attend_back_theirs",
    )(place, grad, out, inverse, qkv, qkv, qkv, kept, *carry)


def gelu_both(wide):
    square = wide * wide
    inner = 0.7978845608 * wide * (1.0 + 0.044715 * square)
    bend = jnp.tanh(inner)
    half = 0.5 * (1.0 + bend)
    slope = 0.7978845608 * (1.0 + 3 * 0.044715 * square)
    return (wide * half, half + 0.5 * wide * (1.0 - bend * bend) * slope)


def all_blocks(full, three, two, y1, y3, side_a, side_b, side_c):
    blocks = [full, three[0], three[1], y1, three[2], two[1], two[0], y3]
    sides = [
        full.at[7:9], side_a.at[2], side_a.at[0], y1.at[7:9], side_a.at[1], side_b.at[1], side_b.at[0], side_c,
    ]
    return blocks, sides


def forward_kernel(
    place, att_near, att_far, x, cot, small, *refs
):
    full, y0, z1, z2, z3, y2, y1, y3, side_a, side_b, side_c = refs[:11]
    nears, near_sides = all_blocks(full, (y0, z1, z2), (z3, y2), y1, y3, side_a, side_b, side_c)
    full, three, two, y1, y3, side_a, side_b, side_c = refs[11:19]
    three, two = [three.at[at] for at in range(3)], [two.at[at] for at in range(2)]
    fars, far_sides = all_blocks(full, three, two, y1, y3, side_a, side_b, side_c)
    refs = refs[19:]
    (
        hid_keep_hbm, hid_send_hbm, pre_hbm, turned_keep, turned_send, result, middle_grad, near_grad, far_grad,
        w_out, w_up, w_down, hid_keep, hid_send, pre, normed_grad, pulled, middle, total, normed, att,
        sems, att_sems, out_sems,
    ) = refs
    z, y, c, xs = place[0], place[1], place[2], place[3]
    att_copies = []
    for other, source in enumerate((att_near, att_far)):
        row = pl.multiple_of(jnp.bitwise_xor(xs, other) * 384, 128)
        copy = pltpu.make_async_copy(source, att.at[pl.ds(row, 384)], att_sems.at[other])
        copy.start()
        att_copies.append(copy)
    groups = ([], [], [])
    for turn in range(4):
        for dy in range(2):
            owner = ((jnp.bitwise_xor(z, turn) * 2) + jnp.bitwise_xor(y, dy)) * 2
            for other in range(2):
                main = (nears, fars)[other][turn * 2 + dy]
                side = (near_sides, far_sides)[other][turn * 2 + dy]
                who = owner + jnp.bitwise_xor(c, other)
                row = pl.multiple_of(who * 48, 16)
                pieces = (
                    (0, main.at[4], w_out.at[pl.ds(row, 48)]),
                    (1, main.at[0:4], w_up.at[:, pl.ds(row, 48)]),
                    (2, main.at[5:7], w_down.at[pl.ds(who * 4 + xs * 2, 2)]),
                    (2, side, w_down.at[pl.ds(who * 4 + (1 - xs) * 2, 2)]),
                )
                for at, (group, source, dest) in enumerate(pieces):
                    sem = sems.at[at, turn * 4 + dy * 2 + other]
                    groups[group].append(pltpu.make_async_copy(source, dest, sem))
    for group in groups:
        for copy in group:
            copy.start()
    for copy in att_copies + groups[0]:
        copy.wait()
    gain = small[1:2]
    wide = x[...].astype(f32) + dot(att[...], w_out[...], 0, 0)
    middle[...] = wide
    scale = lax.rsqrt(jnp.mean(wide * wide, axis=-1, keepdims=True) + EPS)
    normed[...] = (wide * scale * gain).astype(bf16)
    for group in groups[1:]:
        for copy in group:
            copy.wait()
    total[...] = wide
    normed_grad[...] = jnp.zeros_like(normed_grad)

    def chunk(j, carry):
        down = w_down[pl.ds(j * 16, 16)].reshape(768, 768)
        pulled[...] = dot(cot[...], down, 1, 1)
        value, slope = gelu_both(dot(normed[...], w_up[j], 1, 0))
        value = value.astype(bf16)
        total[...] += dot(value, down, 1, 0)
        even = jnp.concatenate([value[:, 0:192], value[:, 384:576]], axis=1)
        odd = jnp.concatenate([value[:, 192:384], value[:, 576:768]], axis=1)
        hid_keep[j] = jnp.where(c == 0, even, odd)
        hid_send[j] = jnp.where(c == 0, odd, even)
        low = (pulled[...] * slope).astype(bf16)
        pre[j] = low
        normed_grad[...] += dot(low, w_up[j], 1, 1)
        return carry

    lax.fori_loop(0, 4, chunk, 0)
    outs = [
        pltpu.make_async_copy(hid_send, hid_send_hbm, out_sems.at[0]),
        pltpu.make_async_copy(hid_keep, hid_keep_hbm, out_sems.at[1]),
        pltpu.make_async_copy(pre.at[0:4], pre_hbm.at[0:4], out_sems.at[2]),
    ]
    for copy in outs:
        copy.start()
    for at, whole in enumerate((normed[...].T, att[...])):
        rows = whole.reshape(8, 2, 48, 512)
        turned_keep[at] = jnp.where(c == 0, rows[:, 0], rows[:, 1])
        turned_send[at] = jnp.where(c == 0, rows[:, 1], rows[:, 0])
    wide = middle[...]
    scale = lax.rsqrt(jnp.mean(wide * wide, axis=-1, keepdims=True) + EPS)
    unit = wide * scale
    incoming = normed_grad[...]
    direct = incoming * gain
    inward = scale * (direct - unit * jnp.mean(direct * unit, axis=-1, keepdims=True))
    grad = cot[...].astype(f32) + inward
    middle_grad[...] = grad
    low = grad.astype(bf16)
    pre[4] = low
    outs.append(pltpu.make_async_copy(pre.at[4], pre_hbm.at[4], out_sems.at[3]))
    outs[3].start()
    for other, dest in enumerate((near_grad, far_grad)):
        row = pl.multiple_of(jnp.bitwise_xor(xs, other) * 384, 128)
        dest[...] = dot(w_out[pl.ds(row, 384)], low, 1, 1).astype(bf16)
    result[...] = total[...].astype(bf16)
    for copy in outs:
        copy.wait()


def forward(place, att_near, att_far, x, cot, small, near, far):
    wide = jax.ShapeDtypeStruct((512, 768), f32)
    half = jax.ShapeDtypeStruct((384, 512), bf16)
    hidden = jax.ShapeDtypeStruct((4, 512, 384), bf16)
    turned = jax.ShapeDtypeStruct((2, 8, 48, 512), bf16)
    return pl.pallas_call(
        forward_kernel,
        out_shape=(
            hidden, hidden, jax.ShapeDtypeStruct((5, 512, 768), bf16), turned, turned,
            jax.ShapeDtypeStruct((512, 768), bf16), wide, half, half,
        ),
        in_specs=[SCALARS, ANY, ANY, FULL, FULL, FULL] + [ANY] * 19,
        out_specs=(ANY, ANY, ANY) + (FULL,) * 6,
        scratch_shapes=[
            pltpu.VMEM((768, 768), bf16),
            pltpu.VMEM((4, 768, 768), bf16),
            pltpu.VMEM((64, 48, 768), bf16),
            pltpu.VMEM((4, 512, 384), bf16),
            pltpu.VMEM((4, 512, 384), bf16),
            pltpu.VMEM((5, 512, 768), bf16),
            pltpu.VMEM((512, 768), f32),
            pltpu.VMEM((512, 768), f32),
            pltpu.VMEM((512, 768), f32),
            pltpu.VMEM((512, 768), f32),
            pltpu.VMEM((512, 768), bf16),
            pltpu.VMEM((768, 512), bf16),
            pltpu.SemaphoreType.DMA((4, 16)),
            pltpu.SemaphoreType.DMA((2,)),
            pltpu.SemaphoreType.DMA((4,)),
        ],
        compiler_params=params(),
        cost_estimate=cost(8_500_000_000, 20_000_000, 512 * 3072),
        name="forward",
    )(place, att_near, att_far, x, cot, small, *near, *far)


def contract_grad_kernel(place, hid, hid_far, cot, cot_far, send, keep):
    made = dot(hid[0], cot[...], 0, 0) + dot(hid_far[0], cot_far[...], 0, 0)
    made = made.astype(bf16).reshape(2, 2, 2, 48, 768)
    send[...] = jnp.where(place[3] == 0, made[:, 1], made[:, 0])
    keep[...] = jnp.where(place[3] == 0, made[:, 0], made[:, 1])


def contract_weight_grad(place, hid, hid_far, cot, cot_far):
    shape = jax.ShapeDtypeStruct((8, 2, 48, 768), bf16)
    spec = pl.BlockSpec((2, 2, 48, 768), lambda j: (j, 0, 0, 0))
    chunk = pl.BlockSpec((1, 512, 384), lambda j: (j, 0, 0))
    whole = pl.BlockSpec((512, 768), lambda j: (0, 0))
    return pl.pallas_call(
        contract_grad_kernel,
        out_shape=(shape, shape),
        grid=(4,),
        in_specs=[SCALARS, chunk, chunk, whole, whole],
        out_specs=(spec, spec),
        compiler_params=params(),
        cost_estimate=cost(2 * 512 * 3072 * 768, 9_000_000),
        name="contract_weight_grad",
    )(place, hid, hid_far, cot, cot_far)


def expand_grad_kernel(place, turned, turned_far, pre, pre_far, b_send, b_keep, c_send, c_keep):
    step = pl.program_id(0)

    def made(at):
        near = dot(turned[at].reshape(384, 512), pre[0], 1, 0)
        return (near + dot(turned_far[at].reshape(384, 512), pre_far[0], 1, 0)).astype(bf16)

    @pl.when(step < 3)
    def _():
        rows = made(0).reshape(4, 2, 48, 768)
        b_send[:, 0] = jnp.where(place[1] == 0, rows[:, 1], rows[:, 0])
        b_keep[:, 0] = jnp.where(place[1] == 0, rows[:, 0], rows[:, 1])

    def by_low(rows):
        rows = rows.reshape(2, 2, 2, 48, 768)
        low = place[0] % 2
        c_send[:, :, 0] = jnp.where(low == 0, rows[:, 1], rows[:, 0])
        c_keep[:, :, 0] = jnp.where(low == 0, rows[:, 0], rows[:, 1])

    @pl.when(step == 3)
    def _():
        by_low(made(0))

    @pl.when(step == 4)
    def _():
        by_low(made(1))


def expand_weight_grad(place, turned, turned_far, pre, pre_far):
    first = jax.ShapeDtypeStruct((4, 3, 48, 768), bf16)
    second = jax.ShapeDtypeStruct((2, 2, 2, 48, 768), bf16)
    first_spec = pl.BlockSpec((4, 1, 48, 768), lambda j: (0, jnp.minimum(j, 2), 0, 0))
    second_spec = pl.BlockSpec((2, 2, 1, 48, 768), lambda j: (0, 0, jnp.maximum(j - 3, 0), 0, 0))
    whole = pl.BlockSpec((2, 8, 48, 512), lambda j: (0, 0, 0, 0))
    chunk = pl.BlockSpec((1, 512, 768), lambda j: (j, 0, 0))
    return pl.pallas_call(
        expand_grad_kernel,
        out_shape=(first, first, second, second),
        grid=(5,),
        in_specs=[SCALARS, whole, whole, chunk, chunk],
        out_specs=(first_spec, first_spec, second_spec, second_spec),
        compiler_params=params(),
        cost_estimate=cost(2 * 512 * 768 * 3840, 12_000_000),
        name="expand_weight_grad",
    )(place, turned, turned_far, pre, pre_far)


def place_grads(whole, grad, sems):
    copies = []
    for head in range(6):
        dest = grad.at[head * 192 : head * 192 + 192]
        copies.append(pltpu.make_async_copy(whole.at[head, 0:192], dest, sems.at[head]))
        copies[-1].start()
    return copies


def weight_grad_kernel(place, mine, other, whole, near, far, grad, bias, sems, bias_sem):
    copies = place_grads(whole, grad, sems)
    copies.append(pltpu.make_async_copy(whole.at[5, 192:208, 0:128], bias, bias_sem))
    copies[-1].start()
    for copy in copies:
        copy.wait()
    for kind, rows, dest in ((place[2], mine, near), (1 - place[2], other, far)):
        spot = iota((384, 128), 0) % 48
        bucket = ((iota((384, 128), 0) // 48) * 2 + kind) * 2 + spot // 6
        chosen = jnp.where((iota((384, 128), 1) == bucket) & (spot < 12), 1.0, 0.0)
        per_head = dot(chosen.astype(bf16), bias[...], 1, 1)
        pattern = (iota((384, 16), 1) == (iota((384, 16), 0) % 48) % 6).astype(f32)
        column = jnp.sum(per_head * pattern, axis=1, keepdims=True)
        side = jnp.where(iota((384, 128), 1) == 0, column, 0.0)
        dest[:, :, 1152:1280] = side.astype(bf16).reshape(8, 48, 128)
        left = rows[...].reshape(384, 1024)
        for col in range(0, 1152, 384):
            made = dot(left, grad[col : col + 384], 1, 1)
            dest[:, :, col : col + 384] = made.astype(bf16).reshape(8, 48, 384)


def weight_grad(place, mine, other, whole):
    owned = jax.ShapeDtypeStruct((8, 48, 1280), bf16)
    return pl.pallas_call(
        weight_grad_kernel,
        out_shape=(owned, owned),
        in_specs=[SCALARS, FULL, FULL, ANY],
        out_specs=(FULL,) * 2,
        scratch_shapes=[
            pltpu.VMEM((1152, 1024), bf16),
            pltpu.VMEM((16, 128), bf16),
            pltpu.SemaphoreType.DMA((6,)),
            pltpu.SemaphoreType.DMA,
        ],
        compiler_params=params(),
        cost_estimate=cost(2 * 1024 * 768 * 1152, 6_000_000),
        name="weight_grad",
    )(place, mine, other, whole)


def project_back_kernel(place, *refs):
    (w_near, w_far), whole, refs = narrow_blocks(refs[:10]), refs[10], refs[11:]
    part_near, part_far, w, grad, sems, qsems = refs
    x = place[3]
    copies = place_blocks(place, w_near, w_far, w, sems) + place_grads(whole, grad, qsems)
    for copy in copies:
        copy.wait()
    for other, dest in ((1, part_far), (0, part_near)):
        start = pl.multiple_of(jnp.bitwise_xor(x, other) * 512, 512)
        dest[...] = dot(grad[:, pl.ds(start, 512)], w[:, 0:1152], 0, 1).astype(bf16)


def project_back(place, blocks, whole):
    part = jax.ShapeDtypeStruct((512, 768), bf16)
    return pl.pallas_call(
        project_back_kernel,
        out_shape=(part, part),
        in_specs=[SCALARS] + [ANY] * 11,
        out_specs=(FULL,) * 2,
        scratch_shapes=[
            pltpu.VMEM((768, 1280), bf16),
            pltpu.VMEM((1152, 1024), bf16),
            pltpu.SemaphoreType.DMA((16,)),
            pltpu.SemaphoreType.DMA((6,)),
        ],
        compiler_params=params(),
        cost_estimate=cost(2 * 1024 * 768 * 1152, 10_000_000),
        name="project_back",
    )(place, *blocks, whole)


def pass_kernel(place, result):
    for at in range(7):
        result[at] = place[at]


def hand_on(place):
    return pl.pallas_call(
        pass_kernel,
        out_shape=jax.ShapeDtypeStruct((7,), jnp.int32),
        in_specs=[SCALARS],
        out_specs=SCALARS,
        cost_estimate=pl.CostEstimate(flops=20_000_000_000, bytes_accessed=1000, transcendentals=0),
        name="hand_on",
    )(place)


def finish_kernel(place, a_near, a_far, g_near, g_far, qw, kw, vw, gain, contract, q, k, v, gain_grad, bias):
    swapped = place[3] == 1

    def ordered(near, far):
        near, far = near[...].astype(f32), far[...].astype(f32)
        return jnp.where(swapped, far, near), jnp.where(swapped, near, far)

    for half, wide in enumerate(ordered(a_near, a_far)):
        for at in range(2):
            row = half * 96 + at * 48
            contract[row : row + 48] = wide[at]
    first, second = ordered(g_near, g_far)
    for at, dest in enumerate((q, k, v)):
        for half, wide in enumerate((first, second)):
            for head in range(6):
                column = head * 192 + at * 64
                spot = half * 384 + head * 64
                dest[:, spot : spot + 64] = wide[:, column : column + 64]
    joint = q[...] * qw[...].astype(f32) + k[...] * kw[...].astype(f32) + v[...] * vw[...].astype(f32)
    summed = jnp.broadcast_to(jnp.sum(joint, axis=1, keepdims=True), (48, 128))
    blank = jnp.zeros((80, 128), f32)
    turned = jnp.concatenate([summed, blank], axis=0).T
    gain_grad[...] = turned[0:1, 0:48] / gain[...].astype(f32)
    first = jnp.concatenate([first[:, 1152:1280], blank], axis=0).T
    second = jnp.concatenate([second[:, 1152:1280], blank], axis=0).T
    for row in range(2):
        cols = slice(row * 6, row * 6 + 6)
        bias[row : row + 1, 0:6] = first[0:1, cols]
        bias[row : row + 1, 6:12] = second[0:1, cols]


def finish(place, a_near, a_far, g_near, g_far, qw, kw, vw, gain):
    full = jax.ShapeDtypeStruct((48, 768), f32)
    return pl.pallas_call(
        finish_kernel,
        out_shape=(
            jax.ShapeDtypeStruct((192, 768), f32),
            full, full, full, jax.ShapeDtypeStruct((1, 48), f32), jax.ShapeDtypeStruct((2, 12), f32),
        ),
        in_specs=[SCALARS] + [FULL] * 8,
        out_specs=(FULL,) * 6,
        compiler_params=params(),
        cost_estimate=cost(1000, 1_000_000),
        name="finish",
    )(place, a_near, a_far, g_near, g_far, qw, kw, vw, gain.reshape(1, 48))


def finish_wide_kernel(place, b_near, b_far, up, gain, expand, output, gain_grad):
    near, far = b_near[...].astype(f32), b_far[...].astype(f32)
    sides = (jnp.where(place[3] == 0, near, far), jnp.where(place[3] == 0, far, near))
    joint = jnp.zeros((48, 384), f32)
    for half, side in enumerate(sides):
        for at in range(4):
            cols = slice(at * 768 + half * 384, at * 768 + half * 384 + 384)
            expand[:, cols] = side[at]
            joint = joint + side[at] * up[:, cols].astype(f32)
        output[:, half * 384 : half * 384 + 384] = side[4]
    column = jnp.broadcast_to(jnp.sum(joint, axis=1, keepdims=True), (48, 128))
    turned = jnp.concatenate([column, jnp.zeros((80, 128), f32)], axis=0).T
    gain_grad[...] = turned[0:1, 0:48] / gain[...].astype(f32)


def finish_wide(place, b_near, b_far, up, gain):
    return pl.pallas_call(
        finish_wide_kernel,
        out_shape=(
            jax.ShapeDtypeStruct((48, 3072), f32),
            jax.ShapeDtypeStruct((48, 768), f32), jax.ShapeDtypeStruct((1, 48), f32),
        ),
        in_specs=[SCALARS] + [FULL] * 4,
        out_specs=(FULL,) * 3,
        compiler_params=params(MOST),
        cost_estimate=cost(1000, 2_000_000),
        name="finish_wide",
    )(place, b_near, b_far, up, gain.reshape(1, 48))


def input_grad_kernel(place, x, small, near, far, middle_grad, result):
    for row in range(0, 512, 256):
        rows = slice(row, row + 256)
        wide = x[rows].astype(f32)
        scale = lax.rsqrt(jnp.mean(wide * wide, axis=-1, keepdims=True) + EPS)
        unit = wide * scale
        direct = (near[rows].astype(f32) + far[rows].astype(f32)) * small[0:1]
        inward = scale * (direct - unit * jnp.mean(direct * unit, axis=-1, keepdims=True))
        result[rows] = (middle_grad[rows] + inward).astype(bf16)


def input_grad(place, x, small, near, far, middle_grad):
    return pl.pallas_call(
        input_grad_kernel,
        out_shape=jax.ShapeDtypeStruct((512, 768), bf16),
        in_specs=[SCALARS] + [FULL] * 5,
        out_specs=FULL,
        compiler_params=params(),
        cost_estimate=cost(512 * 768 * 20, 6_000_000),
        name="input_grad",
    )(place, x, small, near, far, middle_grad)


def swap(array, axis, bit):
    count = lax.axis_size(axis)
    return lax.ppermute(array, axis, [(i, i ^ bit) for i in range(count)])


def swap_both(array):
    pairs = [(i * 2 + j, (i ^ Y) * 2 + 1 - j) for i in range(lax.axis_size("fsdp")) for j in range(2)]
    return lax.ppermute(array, ("fsdp", "seq"), pairs)


CORE, Y, Z = 1, 2, 4


def after(value, *others):
    return lax.optimization_barrier((value, *others))[0]


class Line:
    def __init__(self, place):
        self.place = place

    def wait(self, *arrays):
        self.place = after(self.place, *arrays)

    def run(self, kernel, *args):
        made = kernel(self.place, *args)
        self.wait(jax.tree.leaves(made)[0])
        return made


def gather_part(array, part, own, now):
    _, dims, gone = part
    for axis in reversed(range(len(dims))):
        if dims[axis] == now:
            array = lax.dynamic_index_in_dim(array, 1 - own[now], axis, keepdims=False)
        elif dims[axis] in gone:
            array = lax.dynamic_index_in_dim(array, own[dims[axis]], axis, keepdims=False)
    return array.astype(f32)


def total(line, parts, own, now=None):
    arrays = after([part[0] for part in parts], line.place)
    made = None
    for array, part in zip(arrays, parts):
        term = gather_part(array, part, own, now)
        made = term if made is None else made + term
    made = lax.optimization_barrier(made.astype(bf16))
    line.wait(made)
    return made


def sum_parts(parts, own, now=None):
    made = None
    for part in parts:
        term = gather_part(part[0], part, own, now)
        made = term if made is None else made + term
    return made


def keep(parts, now, got):
    _, dims, gone = parts[0]
    left = tuple(dim for dim in dims if dim not in gone and dim != now)
    return [(a, d, g + (now,)) for a, d, g in parts] + [(got, left, ())]


def local_split(
    layer_input, query_weight, key_weight, value_weight, output_weight, expand_weight,
    contract_weight, attention_gain, feedforward_gain, bias_table, valid_len, instr_len, pair_flag,
    cotangent,
):
    owner, x = lax.axis_index("fsdp"), lax.axis_index("seq")
    z, y, c = owner // 4, (owner // 2) % 2, owner % 2
    where = jnp.stack([z, y, c, x]).astype(jnp.int32)
    line = Line(where)
    tokens, cot = layer_input[0], cotangent[0]

    def by_z(array):
        return swap(array, "fsdp", Z)

    def by_zz(array):
        return swap(array, "fsdp", 2 * Z)

    def by_y(array):
        return swap(array, "fsdp", Y)

    def by_core(array):
        return swap(array, "fsdp", CORE)

    def by_x(array):
        return swap(array, "seq", 1)

    shard = line.run(
        narrow_shard, query_weight, key_weight, value_weight, attention_gain, feedforward_gain, bias_table
    )
    a2, a1, b0 = by_zz(shard), by_z(shard), by_y(shard)
    x_far, cot_far = by_x(tokens), by_core(cot)
    rest, full = line.run(wide_shard, expand_weight, output_weight, contract_weight)
    a2, a1, b0, rest, cot_far = lax.optimization_barrier((a2, a1, b0, rest, cot_far))
    turned, b2 = by_z(jnp.stack([a2, b0])), by_y(a2)
    four = by_core(jnp.stack([shard, b0, a1, a2]))
    z2, z1, y0 = by_zz(rest), by_z(rest), by_y(rest)
    lens = jnp.stack([valid_len[0], instr_len[0], pair_flag[0]])
    place = jnp.concatenate([where, lens])
    turned, b2, x_far, line.place = lax.optimization_barrier((turned, b2, x_far, place))
    b3 = by_y(turned[0])
    three = by_core(jnp.stack([turned[0], turned[1], b2]))
    last = by_core(b3)
    z1, z2, y0, last, three = lax.optimization_barrier((z1, z2, y0, last, three))
    z3, y2 = by_z(z2), by_y(z2)
    sides = jnp.stack([z1[5:], z2[5:], y0[5:]])
    sides_a = by_x(sides)
    narrow = [shard, b0, a1, a2, turned, b2, b3, four, three, last]

    line.wait(sides)
    qkv, normed_kept, normed_sent, small, table, tiles = line.run(project, tokens, x_far, narrow)
    line.place, z3, y2, sides_a = lax.optimization_barrier((line.place, z3, y2, sides_a))
    y3 = by_y(z3)
    y1 = jnp.concatenate([y0, sides_a[2]], axis=0)
    sides, trio = jnp.stack([z3[5:], y2[5:]]), jnp.stack([y0, z1, z2])
    line.wait(y1, sides, trio)
    y1, sides_b, far_full, far_three = by_z(y1), by_x(sides), by_core(full), by_core(trio)
    out_theirs, kept_theirs, inverse_theirs = line.run(attend, table, tiles, qkv, False)
    line.place, y3, sides_b, far_full, far_three, out_theirs = lax.optimization_barrier(
        (line.place, y3, sides_b, far_full, far_three, out_theirs)
    )
    two = jnp.stack([z3, y2])
    line.wait(two)
    out_got, sides_c, far_two = by_x(out_theirs), by_x(y3[5:]), by_core(two)
    out_mine, kept_mine, inverse_mine = line.run(attend, table, tiles, qkv, True)
    out_mine, y1, out_got, sides_c, far_two, y3, sides_a, sides_b = lax.optimization_barrier(
        (out_mine, y1, out_got, sides_c, far_two, y3, sides_a, sides_b)
    )
    near = [full, y0, z1, z2, z3, y2, y1, y3, sides_a, sides_b, sides_c]
    far = [far_full, far_three, far_two] + [by_core(block) for block in (y1, y3, sides_a, sides_b, sides_c)]
    hid, hid_sent, pre, turned, turned_sent, layer_output, middle_grad, grad_mine, grad_sent = line.run(
        forward, out_mine, out_got, tokens, cot, small, near, far
    )
    hid_far, grad_theirs, pre_far, turned_far = by_core(hid_sent), by_x(grad_sent), by_core(pre), by_core(turned_sent)

    own = {"high": z // 2, "low": z % 2, "y": y, "x": x}

    def parts(kept, got, *dims):
        lead = tuple({"high": 2, "low": 2, "y": 2}[dim] for dim in dims if dim != "n")
        shape = lead + kept.shape[-3:] if "n" in dims else lead + kept.shape[-2:]
        return [(array.reshape(shape), dims, ()) for array in (kept, got)]

    carry = line.run(
        lambda place: attend_back(place, grad_mine, out_mine, inverse_mine, qkv, kept_mine, (), True)
    )
    line.wait(grad_theirs)
    b_sent, b_kept, c_sent, c_kept = line.run(expand_weight_grad, turned, turned_far, pre, pre_far)
    b_got, c_got = by_y(b_sent), by_z(c_sent)
    b_parts = parts(b_kept, b_got, "high", "low", "n")
    c_parts = parts(c_kept, c_got, "high", "y", "n")
    sent, kept = line.run(contract_weight_grad, hid, hid_far, cot, cot_far)
    a_got = by_x(sent)
    a_parts = parts(kept, a_got, "high", "low", "y", "n")
    whole = line.run(
        lambda place: attend_back(
            place, grad_theirs, out_theirs, inverse_theirs, qkv, kept_theirs, carry, False
        )
    )
    b_got = by_z(total(line, b_parts, own, "low"))
    b_parts = keep(b_parts, "low", b_got)
    c_got = by_y(total(line, c_parts, own, "y"))
    c_parts = keep(c_parts, "y", c_got)
    g_near, g_far = line.run(weight_grad, normed_kept, normed_sent, whole)
    g_parts = parts(g_near, by_core(g_far), "high", "low", "y")
    line.wait(a_got, b_got, c_got)
    line.place = hand_on(line.place)
    g_parts = keep(g_parts, "low", by_z(total(line, g_parts, own, "low")))
    a_parts = keep(a_parts, "y", by_y(total(line, a_parts, own, "y")))
    arrays = after([part[0] for part in b_parts + c_parts], line.place)
    held = [(array, *part[1:]) for array, part in zip(arrays, b_parts + c_parts)]
    joint = jnp.concatenate([sum_parts(held[:3], own), sum_parts(held[3:], own)], axis=1).astype(bf16)
    sent = lax.dynamic_slice_in_dim(joint, (1 - x) * 384, 384, axis=3)
    kept = lax.dynamic_slice_in_dim(joint, x * 384, 384, axis=3)
    sent, kept = lax.optimization_barrier((sent, kept))
    line.wait(sent, kept)
    bc_parts = [(kept, ("high", "n"), ()), (by_x(sent), ("high", "n"), ())]
    part_near, part_far = line.run(project_back, narrow, whole)
    part_got = by_x(part_far)
    a_parts = keep(a_parts, "low", by_z(total(line, a_parts, own, "low")))
    bc_parts = keep(bc_parts, "high", by_zz(total(line, bc_parts, own, "high")))
    g_parts = keep(g_parts, "y", by_y(total(line, g_parts, own, "y")))
    a_parts = keep(a_parts, "high", by_zz(total(line, a_parts, own, "high")))
    b_low = total(line, bc_parts, own)
    b_other = by_x(b_low)
    g_parts = keep(g_parts, "high", by_zz(total(line, g_parts, own, "high")))
    result = line.run(input_grad, tokens, small, part_near, part_got, middle_grad)
    a_low = total(line, a_parts, own)
    a_other = by_x(a_low)
    g_low = total(line, g_parts, own)
    g_other = by_x(g_low)
    expand_sum, output_sum, gain_two = line.run(finish_wide, b_low, b_other, expand_weight, feedforward_gain)
    contract_sum, *grads, gain_one, bias_grad = line.run(
        finish, a_low, a_other, g_low, g_other, query_weight, key_weight, value_weight, attention_gain
    )
    return (
        layer_output[None], result[None], gain_one[0], gain_two[0], *grads,
        output_sum, expand_sum, contract_sum, bias_grad,
    )


def bucket_table(query_pos, key_pos):
    offset = key_pos[None, :] - query_pos[:, None]
    distance = jnp.abs(offset)
    beyond = jnp.zeros_like(distance)
    for far_edge in far_edges:
        beyond = beyond + (distance >= far_edge).astype(jnp.int32)
    nearby = jnp.where(distance < 8, distance, 8 + beyond)
    return nearby + 16 * (offset > 0).astype(jnp.int32)


def visible_keys(query_pos, key_pos, valid_len, instr_len, pair_flag):
    in_valid = key_pos[None, None, :] < valid_len[:, None, None]
    guarded = (
        (pair_flag[:, None, None] == 1)
        & (query_pos[None, :, None] < instr_len[:, None, None])
        & (key_pos[None, None, :] >= instr_len[:, None, None])
    )
    return in_valid & jnp.logical_not(guarded)


def rms_scale(values):
    return lax.rsqrt(jnp.mean(values * values, axis=-1, keepdims=True) + EPS)


def norm_back(values, scale, gain, grad_out):
    normed = values * scale
    grad_normed = grad_out * gain
    grad_values = scale * (
        grad_normed - normed * jnp.mean(grad_normed * normed, axis=-1, keepdims=True)
    )
    return (grad_values, jnp.sum(grad_out * normed, axis=(0, 1)))


def gelu_tanh(values):
    return jax.nn.gelu(values, approximate=True)


def local(
    layer_input,
    query_weight,
    key_weight,
    value_weight,
    output_weight,
    expand_weight,
    contract_weight,
    attention_gain,
    feedforward_gain,
    bias_table,
    valid_len,
    instr_len,
    pair_flag,
    cotangent,
):
    f32 = jnp.float32
    bf16 = jnp.bfloat16
    row_count, local_len, model_width = layer_input.shape
    head_count = bias_table.shape[1]
    head_size = model_width // head_count
    full_len = local_len * lax.axis_size("seq")
    local_start = lax.axis_index("seq") * local_len
    query_pos = local_start + jnp.arange(local_len, dtype=jnp.int32)
    key_pos = jnp.arange(full_len, dtype=jnp.int32)
    buckets = bucket_table(query_pos, key_pos)
    onehot = buckets[:, :, None] == jnp.arange(BUCKETS, dtype=jnp.int32)[None, None, :]
    visible = visible_keys(query_pos, key_pos, valid_len, instr_len, pair_flag)
    input_wide = layer_input.astype(f32)

    def attend_probs(queries, key_heads, table_full):
        rel_bias = jnp.einsum(
            "ijb,bh->hij", onehot.astype(bf16), table_full, preferred_element_type=f32
        )
        raw_scores = jnp.einsum("rihe,rjhe->rhij", queries, key_heads, preferred_element_type=f32)
        scores = jnp.where(visible[:, None], raw_scores + rel_bias[None], -1000000000.0)
        row_peak = jnp.max(scores, axis=-1, keepdims=True)
        log_total = row_peak + jnp.log(jnp.sum(jnp.exp(scores - row_peak), axis=-1, keepdims=True))
        return (jnp.exp(scores - log_total), log_total[..., 0])

    def forward(weights):
        (
            query_full,
            key_full,
            value_full,
            output_full,
            expand_full,
            contract_full,
            gain_one,
            gain_two,
            table_full,
        ) = weights
        scale_one = rms_scale(input_wide)
        normed_low = (input_wide * scale_one * gain_one.astype(f32)).astype(bf16)

        def project(weight):
            return jnp.einsum("rtd,de->rte", normed_low, weight, preferred_element_type=f32).astype(
                bf16
            )

        query_low = project(query_full)
        key_low = project(key_full)
        value_low = project(value_full)
        key_all, value_all = (
            lax.all_gather(key_low, "seq", axis=1, tiled=True),
            lax.all_gather(value_low, "seq", axis=1, tiled=True),
        )
        queries = query_low.reshape(row_count, local_len, head_count, head_size)
        key_heads = key_all.reshape(row_count, full_len, head_count, head_size)
        value_heads = value_all.reshape(row_count, full_len, head_count, head_size)
        probs, log_total = attend_probs(queries, key_heads, table_full)
        probs_low = probs.astype(bf16)
        attended = jnp.einsum("rhij,rjhe->rihe", probs_low, value_heads, preferred_element_type=f32)
        attended = attended.reshape(row_count, local_len, model_width).astype(bf16)
        middle = input_wide + jnp.einsum(
            "rtd,de->rte", attended, output_full, preferred_element_type=f32
        )
        scale_two = rms_scale(middle)
        normed_two = (middle * scale_two * gain_two.astype(f32)).astype(bf16)
        hidden_pre = jnp.einsum("rtd,df->rtf", normed_two, expand_full, preferred_element_type=f32)
        hidden_low = gelu_tanh(hidden_pre).astype(bf16)
        result = middle + jnp.einsum(
            "rtf,fd->rtd", hidden_low, contract_full, preferred_element_type=f32
        )
        return (
            result,
            scale_one,
            normed_low,
            queries,
            key_heads,
            value_heads,
            probs,
            probs_low,
            log_total,
            attended,
            middle,
            scale_two,
            normed_two,
            hidden_pre,
            hidden_low,
        )

    stored = forward(
        (
            lax.all_gather(query_weight, "fsdp", axis=0, tiled=True),
            lax.all_gather(key_weight, "fsdp", axis=0, tiled=True),
            lax.all_gather(value_weight, "fsdp", axis=0, tiled=True),
            lax.all_gather(output_weight, "fsdp", axis=0, tiled=True),
            lax.all_gather(expand_weight, "fsdp", axis=0, tiled=True),
            lax.all_gather(contract_weight, "fsdp", axis=0, tiled=True),
            lax.all_gather(attention_gain, "fsdp", axis=0, tiled=True),
            lax.all_gather(feedforward_gain, "fsdp", axis=0, tiled=True),
            lax.all_gather(bias_table, "fsdp", axis=0, tiled=True),
        )
    )
    layer_output = stored[0].astype(bf16)
    gathered = (
        lax.all_gather(query_weight, "fsdp", axis=0, tiled=True),
        lax.all_gather(key_weight, "fsdp", axis=0, tiled=True),
        lax.all_gather(value_weight, "fsdp", axis=0, tiled=True),
        lax.all_gather(output_weight, "fsdp", axis=0, tiled=True),
        lax.all_gather(expand_weight, "fsdp", axis=0, tiled=True),
        lax.all_gather(contract_weight, "fsdp", axis=0, tiled=True),
        lax.all_gather(attention_gain, "fsdp", axis=0, tiled=True),
        lax.all_gather(feedforward_gain, "fsdp", axis=0, tiled=True),
        lax.all_gather(bias_table, "fsdp", axis=0, tiled=True),
    )
    kept = forward(gathered)
    (
        unused,
        scale_one,
        normed_low,
        queries,
        key_heads,
        value_heads,
        probs,
        probs_low,
        log_total,
        attended,
        middle,
        scale_two,
        normed_two,
        hidden_pre,
        hidden_low,
    ) = kept
    (
        query_full,
        key_full,
        value_full,
        output_full,
        expand_full,
        contract_full,
        gain_one,
        gain_two,
        table_full,
    ) = gathered
    gain_one_wide = gain_one.astype(f32)
    gain_two_wide = gain_two.astype(f32)
    contract_grad = jnp.einsum("rtf,rtd->fd", hidden_low, cotangent, preferred_element_type=f32)
    grad_hidden = jnp.einsum("rtd,fd->rtf", cotangent, contract_full, preferred_element_type=f32)
    gelu_pull = jax.vjp(gelu_tanh, hidden_pre)[1]
    grad_pre = gelu_pull(grad_hidden)[0].astype(bf16)
    expand_grad = jnp.einsum("rtd,rtf->df", normed_two, grad_pre, preferred_element_type=f32)
    grad_normed_two = jnp.einsum("rtf,df->rtd", grad_pre, expand_full, preferred_element_type=f32)
    grad_middle_norm, gain_two_grad = norm_back(middle, scale_two, gain_two_wide, grad_normed_two)
    grad_middle = cotangent.astype(f32) + grad_middle_norm
    grad_branch = grad_middle.astype(bf16)
    output_grad = jnp.einsum("rtd,rte->de", attended, grad_branch, preferred_element_type=f32)
    grad_attended = jnp.einsum(
        "rte,de->rtd", grad_branch, output_full, preferred_element_type=f32
    ).astype(bf16)
    grad_attended = grad_attended.reshape(row_count, local_len, head_count, head_size)
    grad_probs = jnp.einsum(
        "rihe,rjhe->rhij", grad_attended, value_heads, preferred_element_type=f32
    )
    row_delta = jnp.sum(probs * grad_probs, axis=-1)
    grad_scores = probs * (grad_probs - row_delta[..., None])
    bias_part = jnp.einsum(
        "hij,ijb->bh",
        jnp.sum(grad_scores, axis=0),
        onehot.astype(f32),
        precision=lax.Precision.HIGHEST,
    )
    scores_low = grad_scores.astype(bf16)
    grad_queries = jnp.einsum("rhij,rjhe->rihe", scores_low, key_heads, preferred_element_type=f32)
    grad_queries = grad_queries.reshape(row_count, local_len, model_width).astype(bf16)
    value_partial = jnp.einsum(
        "rhij,rihe->rjhe", probs_low, grad_attended, preferred_element_type=f32
    ).reshape(row_count, full_len, model_width)
    key_partial = jnp.einsum(
        "rhij,rihe->rjhe", scores_low, queries, preferred_element_type=f32
    ).reshape(row_count, full_len, model_width)
    key_summed, value_summed = (
        lax.psum_scatter(
            key_partial.astype(jnp.bfloat16), "seq", scatter_dimension=1, tiled=True
        ).astype(jnp.float32),
        lax.psum_scatter(
            value_partial.astype(jnp.bfloat16), "seq", scatter_dimension=1, tiled=True
        ).astype(jnp.float32),
    )
    grad_keys = key_summed.astype(bf16)
    grad_values = value_summed.astype(bf16)
    query_part = jnp.einsum("rtd,rte->de", normed_low, grad_queries, preferred_element_type=f32)
    key_part = jnp.einsum("rtd,rte->de", normed_low, grad_keys, preferred_element_type=f32)
    value_part = jnp.einsum("rtd,rte->de", normed_low, grad_values, preferred_element_type=f32)
    grad_normed_one = jnp.einsum(
        "rte,de->rtd", grad_queries, query_full, preferred_element_type=f32
    )
    grad_normed_one = grad_normed_one + jnp.einsum(
        "rte,de->rtd", grad_keys, key_full, preferred_element_type=f32
    )
    grad_normed_one = grad_normed_one + jnp.einsum(
        "rte,de->rtd", grad_values, value_full, preferred_element_type=f32
    )
    grad_input_norm, gain_one_grad = norm_back(
        input_wide, scale_one, gain_one_wide, grad_normed_one
    )
    input_grad = (grad_middle + grad_input_norm).astype(bf16)
    owned = (
        lax.psum_scatter(
            query_part.astype(jnp.bfloat16), "fsdp", scatter_dimension=0, tiled=True
        ).astype(jnp.float32),
        lax.psum_scatter(
            key_part.astype(jnp.bfloat16), "fsdp", scatter_dimension=0, tiled=True
        ).astype(jnp.float32),
        lax.psum_scatter(
            value_part.astype(jnp.bfloat16), "fsdp", scatter_dimension=0, tiled=True
        ).astype(jnp.float32),
        lax.psum_scatter(
            output_grad.astype(jnp.bfloat16), "fsdp", scatter_dimension=0, tiled=True
        ).astype(jnp.float32),
        lax.psum_scatter(
            expand_grad.astype(jnp.bfloat16), "fsdp", scatter_dimension=0, tiled=True
        ).astype(jnp.float32),
        lax.psum_scatter(
            contract_grad.astype(jnp.bfloat16), "fsdp", scatter_dimension=0, tiled=True
        ).astype(jnp.float32),
        lax.psum_scatter(
            gain_one_grad.astype(jnp.bfloat16), "fsdp", scatter_dimension=0, tiled=True
        ).astype(jnp.float32),
        lax.psum_scatter(
            gain_two_grad.astype(jnp.bfloat16), "fsdp", scatter_dimension=0, tiled=True
        ).astype(jnp.float32),
        lax.psum_scatter(
            bias_part.astype(jnp.bfloat16), "fsdp", scatter_dimension=0, tiled=True
        ).astype(jnp.float32),
    )
    summed = (
        lax.psum(owned[0].astype(jnp.bfloat16), "seq").astype(jnp.float32),
        lax.psum(owned[1].astype(jnp.bfloat16), "seq").astype(jnp.float32),
        lax.psum(owned[2].astype(jnp.bfloat16), "seq").astype(jnp.float32),
        lax.psum(owned[3].astype(jnp.bfloat16), "seq").astype(jnp.float32),
        lax.psum(owned[4].astype(jnp.bfloat16), "seq").astype(jnp.float32),
        lax.psum(owned[5].astype(jnp.bfloat16), "seq").astype(jnp.float32),
        lax.psum(owned[6].astype(jnp.bfloat16), "seq").astype(jnp.float32),
        lax.psum(owned[7].astype(jnp.bfloat16), "seq").astype(jnp.float32),
        lax.psum(owned[8].astype(jnp.bfloat16), "seq").astype(jnp.float32),
    )
    (
        query_grad,
        key_grad,
        value_grad,
        output_sum,
        expand_sum,
        contract_sum,
        gain_one_sum,
        gain_two_sum,
        bias_grad,
    ) = summed
    return (
        layer_output,
        input_grad,
        gain_one_sum,
        gain_two_sum,
        query_grad,
        key_grad,
        value_grad,
        output_sum,
        expand_sum,
        contract_sum,
        bias_grad,
    )


def solution(mesh):
    in_specs = (
        P("fsdp", "seq", None),
        P("fsdp", None),
        P("fsdp", None),
        P("fsdp", None),
        P("fsdp", None),
        P("fsdp", None),
        P("fsdp", None),
        P("fsdp"),
        P("fsdp"),
        P("fsdp", None),
        P("fsdp"),
        P("fsdp"),
        P("fsdp"),
        P("fsdp", "seq", None),
    )
    out_specs = (
        P("fsdp", "seq", None),
        P("fsdp", "seq", None),
        P("fsdp"),
        P("fsdp"),
        P("fsdp", None),
        P("fsdp", None),
        P("fsdp", None),
        P("fsdp", None),
        P("fsdp", None),
        P("fsdp", None),
        P("fsdp", None),
    )
    split = mesh.shape["fsdp"] == 16 and mesh.shape["seq"] == 2
    step = local_split if split else local
    return jax.shard_map(step, mesh=mesh, in_specs=in_specs, out_specs=out_specs, check_vma=False)
```
